32 devices in a mesh: dp: 8 (over y, x, core), tensor: 4 (over z).
Axes of the slice: x: 2, y: 2, z: 4, core: 2. Of those that a mesh axis runs over, the one named last changes fastest.
Arguments:
- tokens: bfloat16 [32768, 768], P(('dp', 'tensor')), may hold values from -6 to 6
- prior_logits: bfloat16 [32768, 12], P(('dp', 'tensor')), may hold values from -6 to 6
- expert_ids: int32 [32768, 2], P('dp'), may hold values from 0 to 11, as said below
- expert_ranks: int32 [32768, 2], P('dp'), may hold values from 0 to 768, as said below
- piece_starts: int32 [32, 2], P('dp'), may hold values from 0 to 768, as said below
- norm_attn: bfloat16 [768], replicated, may hold values from 0.5 to 1.5
- qkv_weight: bfloat16 [3, 768, 768], P(None, 'dp', 'tensor'), may hold values from -0.21875 to 0.21875
- out_weight: bfloat16 [768, 768], P('tensor', 'dp'), may hold values from -0.625 to 0.625
- norm_moe: bfloat16 [768], replicated, may hold values from 0.5 to 1.5
- router_weight: bfloat16 [768, 12], replicated, may hold values from -0.109375 to 0.109375
- residual_weight: bfloat16 [12, 12], replicated, may hold values from -0.875 to 0.875
- const_vectors: bfloat16 [2, 768], replicated, may hold values from -6 to 6
- const_gates: bfloat16 [2, 2, 768], replicated, may hold values from -0.21875 to 0.21875
- w_gate_up: bfloat16 [2, 8, 768, 2048], P(None, None, 'dp', 'tensor'), may hold values from -0.21875 to 0.21875
- w_down: bfloat16 [8, 2048, 768], P(None, 'tensor', 'dp'), may hold values from -1 to 1
- out_grad: bfloat16 [32768, 768], P(('dp', 'tensor')), may hold values from -6 to 6
Outputs:
- layer_out: bfloat16 [32768, 768], P(('dp', 'tensor'))
- input_grad: float32 [32768, 768], P(('dp', 'tensor'))
- prior_grad: float32 [32768, 12], P(('dp', 'tensor'))
- norm_attn_grad: float32 [768], replicated
- qkv_grad: float32 [3, 768, 768], P(None, 'dp', 'tensor')
- out_weight_grad: float32 [768, 768], P('tensor', 'dp')
- norm_moe_grad: float32 [768], replicated
- router_grad: float32 [768, 12], replicated
- residual_grad: float32 [12, 12], replicated
- const_vector_grad: float32 [2, 768], replicated
- const_gate_grad: float32 [2, 2, 768], replicated
- gate_up_grad: float32 [2, 8, 768, 2048], P(None, None, 'dp', 'tensor')
- down_grad: float32 [8, 2048, 768], P(None, 'tensor', 'dp')
The draws below stay inside these ranges and needn't reach their ends.
Inputs may be any that keep to these rules, and one draw needn't show every extreme that they name: `expert_ids`: each token names two different experts: ids below 8 are feed-forward experts, 8 the zero expert, 9 the copy expert, 10 and 11 the constant experts. In the tokens of each index of dp some feed-forward expert is named 2 * 768 times or more. `expert_ranks`: within the tokens of one index of dp, the choices that name one expert carry the ranks 0, 1, and so on, each once, up to 767; choices past the first 768 of an expert carry 768. `piece_starts`: each row gives the first positions of the 2 picture pieces of one sequence in rising order; the pieces do not intersect and do not pass the sequence's end.
All inputs are finite; a program needn't handle non-finite values.
Results may differ from the reference program's by a relative error of at most 0.018.
Values may be sent and summed in bfloat16 or wider, within the bound.
A program may use at most 320 MiB of HBM per device.

```python
import jax
import jax.numpy as jnp
from jax import lax

D = 768
H = 12
HD = 64
FF = 2048
NF = 8
NC = 2
NE = 12
SEQ = 1024
PIECE = 256
PIECES = 2
TOK_DEV = 4096
CAP = 768
TOKENS = 32768
SEQS = 32


def routing(key):
    groups = TOKENS // TOK_DEV

    def one_group(group_key):
        subkeys = jax.random.split(group_key, 5)
        busiest = jax.random.randint(subkeys[0], (), 0, NF)
        ordering = jax.random.permutation(subkeys[1], TOK_DEV)
        first_choice = jax.random.randint(subkeys[2], (TOK_DEV,), 0, NE)
        first_choice = jnp.where(ordering < 2 * CAP, busiest, first_choice)
        second = (first_choice + jax.random.randint(subkeys[3], (TOK_DEV,), 1, NE)) % NE
        choice_ids = jnp.stack([first_choice, second], axis=1).astype(jnp.int32)
        flat_ids = choice_ids.reshape(-1)
        priority = jax.random.permutation(subkeys[4], 2 * TOK_DEV)
        ordered = flat_ids[priority]
        onehot = (ordered[:, None] == jnp.arange(NE)[None, :]).astype(jnp.int32)
        before = jnp.cumsum(onehot, axis=0) - onehot
        rank_ordered = jnp.minimum(jnp.sum(before * onehot, axis=1), CAP)
        rank_vals = jnp.zeros((2 * TOK_DEV,), jnp.int32).at[priority].set(rank_ordered)
        return (choice_ids, rank_vals.reshape(TOK_DEV, 2).astype(jnp.int32))
    choice_ids, rank_vals = jax.vmap(one_group)(jax.random.split(key, groups))
    return (choice_ids.reshape(TOKENS, 2), rank_vals.reshape(TOKENS, 2))


def draw_expert_ids(key, part):
    choice_ids, rank_vals = routing(jax.random.fold_in(key, 11))
    return choice_ids


def draw_expert_ranks(key, part):
    choice_ids, rank_vals = routing(jax.random.fold_in(key, 11))
    return rank_vals


def draw_piece_starts(key, part):
    room = SEQ - PIECES * PIECE
    offsets = jax.random.randint(key, (SEQS, PIECES), 0, room + 1)
    ordered = jnp.sort(offsets, axis=1)
    ordered = ordered.at[0, 0].set(0).at[0, PIECES - 1].set(room)
    return (ordered + jnp.arange(PIECES, dtype=jnp.int32)[None, :] * PIECE).astype(jnp.int32)


def block_scale(stream_key, extent, pieces, least, high):
    level, own = 1.0, jax.random.fold_in(stream_key, 6)
    for axis_at, shards_of in pieces:
        steps = jnp.exp(jax.random.uniform(jax.random.fold_in(own, axis_at), (shards_of,), jnp.float32, least / len(pieces), high / len(pieces)))
        level = level * jnp.repeat(steps, extent[axis_at] // shards_of).reshape([-1 if axis == axis_at else 1 for axis in range(len(extent))])
    return level


def gaussian(key, dims, scale, limit, shards=(), held_as=jnp.bfloat16):
    result = scale * jax.random.normal(key, dims, jnp.float32)
    if shards:
        result = result * block_scale(key, dims, shards, -0.22, 0.18)
    return jnp.clip(result, -limit, limit).astype(held_as)


def setup_inputs(seed: int = 0) -> dict:
    streams_of = jax.random.split(jax.random.key(seed), 17)
    return {
        "tokens": gaussian(streams_of[0], (TOKENS, D), 1.0, 6.0, ((0, 32),)),
        "prior_logits": gaussian(streams_of[1], (TOKENS, NE), 1.0, 6.0, ((0, 32),)),
        "expert_ids": draw_expert_ids(jax.random.fold_in(streams_of[16], 71), 0),
        "expert_ranks": draw_expert_ranks(jax.random.fold_in(streams_of[16], 71), 0),
        "piece_starts": draw_piece_starts(jax.random.fold_in(streams_of[16], 71), 0),
        "norm_attn": jnp.clip(1.0 + 0.1 * jax.random.normal(streams_of[5], (D,), jnp.float32), 0.5, 1.5).astype(jnp.bfloat16),
        "qkv_weight": gaussian(streams_of[6], (3, D, D), D ** -0.5, 0.21875, ((1, 8), (2, 4))),
        "out_weight": gaussian(streams_of[7], (D, D), (D // 8) ** -0.5, 0.625, ((0, 4), (1, 8))),
        "norm_moe": jnp.clip(1.0 + 0.1 * jax.random.normal(streams_of[8], (D,), jnp.float32), 0.5, 1.5).astype(jnp.bfloat16),
        "router_weight": gaussian(streams_of[9], (D, NE), (4 * D) ** -0.5, 0.109375),
        "residual_weight": gaussian(streams_of[10], (NE, NE), (4 * NE) ** -0.5, 0.875),
        "const_vectors": gaussian(streams_of[11], (NC, D), 1.0, 6.0),
        "const_gates": gaussian(streams_of[12], (NC, 2, D), D ** -0.5, 0.21875),
        "w_gate_up": gaussian(streams_of[13], (2, NF, D, FF), D ** -0.5, 0.21875, ((2, 8), (3, 4))),
        "w_down": gaussian(streams_of[14], (NF, FF, D), (max(FF // 64, 1)) ** -0.5, 1.0, ((1, 4), (2, 8))),
        "out_grad": gaussian(streams_of[15], (TOKENS, D), 1.0, 6.0, ((0, 32),)),
    }


eps = 1e-06

@jax.custom_vjp
def low(v):
    return lax.optimization_barrier(v.astype(jnp.bfloat16)).astype(jnp.float32)

@jax.custom_vjp
def low_back(v):
    return v

def low_keep(v):
    return (low(v), None)

def low_pass(kept, grad):
    return (grad,)

def back_keep(v):
    return (v, None)

def back_low(kept, grad):
    return (low(grad),)
low.defvjp(low_keep, low_pass)
low_back.defvjp(back_keep, back_low)

def rms_scaled(values, gain):
    return values * lax.rsqrt(lax.optimization_barrier(jnp.mean(values * values, axis=-1, keepdims=True)) + eps) * gain

def rotary(positions, width):
    place = (jnp.arange(positions) % SEQ).astype(jnp.float32)
    freqs = jnp.power(10000.0, jnp.arange(width // 2).astype(jnp.float32) * (-2.0 / width))
    angles = place[:, None] * freqs[None, :]
    return (jnp.cos(angles)[:, None, :], jnp.sin(angles)[:, None, :])

def rotate(values, cosine, sine):
    half = values.shape[-1] // 2
    front = values[..., :half]
    behind = values[..., half:]
    return jnp.concatenate([front * cosine - behind * sine, behind * cosine + front * sine], axis=-1)

def visible(starts):
    position = jnp.arange(SEQ)
    piece_of = jnp.zeros((SEQ,), jnp.int32)
    for index in range(starts.shape[0]):
        inside = (position >= starts[index]) & (position < starts[index] + PIECE)
        piece_of = jnp.where(inside, index + 1, piece_of)
    causal = position[None, :] <= position[:, None]
    same_piece = (piece_of[:, None] > 0) & (piece_of[:, None] == piece_of[None, :])
    return causal | same_piece

def dispatch(route_ids, route_ranks):
    group_rows = route_ids.shape[0]
    retained = (route_ids < NF) & (route_ranks < CAP)
    target = jnp.where(retained, route_ids * CAP + route_ranks, NF * CAP).astype(jnp.int32)
    token_index = jnp.broadcast_to(jnp.arange(group_rows, dtype=jnp.int32)[:, None], route_ids.shape)
    slot_token = jnp.zeros((NF * CAP + 1,), jnp.int32).at[target.reshape(-1)].set(token_index.reshape(-1))[:NF * CAP]
    filled = jnp.zeros((NF * CAP + 1,), jnp.float32).at[target.reshape(-1)].set(1.0)[:NF * CAP]
    return (retained, target, slot_token, filled)

def attend_block(parts):
    query, keys, values, starts = parts
    scores = low_back(jnp.einsum('qhd,khd->hqk', query, keys, precision=lax.Precision.HIGHEST) * HD ** (-0.5))
    scores = jnp.where(visible(starts)[None], scores, -1e+30)
    shares = jax.nn.softmax(scores, axis=-1)
    return jnp.einsum('hqk,khd->qhd', low(shares), values, precision=lax.Precision.HIGHEST)

def other_experts(normed, route_ids, gates, vectors, gate_mats):
    copy_share = lax.optimization_barrier(jnp.sum(jnp.where(route_ids == NF + 1, gates, 0.0), axis=1))
    mixing = jax.nn.softmax(jnp.einsum('gd,cjd->gcj', normed, gate_mats, precision=lax.Precision.HIGHEST), axis=-1)
    const_out = mixing[:, :, 0:1] * normed[:, None, :] + mixing[:, :, 1:2] * vectors[None, :, :]
    const_share = jnp.stack([lax.optimization_barrier(jnp.sum(jnp.where(route_ids == NF + 2 + index, gates, 0.0), axis=1)) for index in range(NC)], axis=1)
    return copy_share[:, None] * normed + lax.optimization_barrier(jnp.sum(const_share[:, :, None] * const_out, axis=1))

def block_forward(route_ids, route_ranks, starts, tok_vals, prior_vals, norm_attn, qkv_weight, out_weight, norm_moe, router_weight, residual_weight, const_vectors, const_gates, w_gate_up, w_down):
    highest = lax.Precision.HIGHEST
    group_rows = tok_vals.shape[0]
    sequences = group_rows // SEQ
    seq_shape = (sequences, SEQ, H, HD)
    normed_attn = low(rms_scaled(tok_vals, norm_attn))
    projected = jnp.einsum('gd,cde->cge', normed_attn, qkv_weight, precision=highest)
    cosine, sine = rotary(group_rows, HD)
    query = low(rotate(low_back(projected[0]).reshape(group_rows, H, HD), cosine, sine))
    keys = low(rotate(low_back(projected[1]).reshape(group_rows, H, HD), cosine, sine))
    values = low(low_back(projected[2]))
    mixed = lax.map(jax.checkpoint(attend_block), (query.reshape(seq_shape), keys.reshape(seq_shape), values.reshape(seq_shape), starts))
    mixed = low(low_back(mixed.reshape(group_rows, H * HD)))
    resid = tok_vals + low_back(jnp.dot(mixed, out_weight, precision=highest))
    normed_moe = low(rms_scaled(resid, norm_moe))
    logits = jnp.dot(normed_moe, router_weight, precision=highest) + jnp.dot(prior_vals, residual_weight, precision=highest)
    shares = jax.nn.softmax(logits, axis=-1)
    gates = jnp.take_along_axis(shares, route_ids, axis=1)
    retained, target, slot_token, filled = dispatch(route_ids, route_ranks)
    expert_rows = (normed_moe[slot_token] * filled[:, None]).reshape(NF, CAP, H * HD)
    gate_up = low_back(jnp.einsum('ecd,sedf->secf', expert_rows, w_gate_up, precision=highest))
    hidden = low(jax.nn.silu(gate_up[0]) * gate_up[1])
    expert_out = low_back(jnp.einsum('ecf,efd->ecd', hidden, w_down, precision=highest)).reshape(NF * CAP, H * HD)
    picked = expert_out[jnp.minimum(target, NF * CAP - 1)]
    ffn_out = lax.optimization_barrier(jnp.sum(jnp.where(retained, gates, 0.0)[:, :, None] * picked, axis=1))
    branch = ffn_out + other_experts(normed_moe, route_ids, gates, const_vectors, const_gates)
    return resid + low_back(branch)

def reference(tokens, prior_logits, expert_ids, expert_ranks, piece_starts, norm_attn, qkv_weight, out_weight, norm_moe, router_weight, residual_weight, const_vectors, const_gates, w_gate_up, w_down, out_grad):
    groups = TOKENS // TOK_DEV
    weights = tuple((item.astype(jnp.float32) for item in (norm_attn, qkv_weight, out_weight, norm_moe, router_weight, residual_weight, const_vectors, const_gates, w_gate_up, w_down)))

    def group_step(totals, parts):
        tok_part, prior_part, id_part, rank_part, start_part, grad_part = parts

        def forward(tok_vals, prior_vals, *weight_vals):
            return block_forward(id_part, rank_part, start_part, tok_vals, prior_vals, *weight_vals)
        layer_vals, pullback = jax.vjp(forward, tok_part.astype(jnp.float32), prior_part.astype(jnp.float32), *weights)
        grads = pullback(grad_part.astype(jnp.float32))
        totals = tuple((left + right for left, right in zip(totals, grads[2:])))
        return (totals, (layer_vals.astype(jnp.bfloat16), grads[0], grads[1]))
    zeros = tuple((jnp.zeros(item.shape, jnp.float32) for item in weights))
    parts = (tokens.reshape(groups, TOK_DEV, D), prior_logits.reshape(groups, TOK_DEV, NE), expert_ids.reshape(groups, TOK_DEV, 2), expert_ranks.reshape(groups, TOK_DEV, 2), piece_starts.reshape(groups, TOK_DEV // SEQ, PIECES), out_grad.reshape(groups, TOK_DEV, D))
    totals, outputs = lax.scan(group_step, zeros, parts)
    layer_out, input_grad, prior_grad = outputs
    return (layer_out.reshape(TOKENS, D), input_grad.reshape(TOKENS, D), prior_grad.reshape(TOKENS, NE), totals[0], totals[1], totals[2], totals[3], totals[4], totals[5], totals[6], totals[7], totals[8], totals[9])
```

```python
import functools

import jax
import jax.numpy as jnp
import numpy as np
from jax import lax
from jax.experimental import pallas as pl
from jax.experimental.pallas import tpu as pltpu
from jax.sharding import PartitionSpec as P

HD = 64
NF = 8
NC = 2
SEQ = 1024
PIECE = 256
PIECES = 2
CAP = 768
EPS = 1e-06
QT = 256
LANES = 128
TM = 256
WIN = 256
Z0 = 16

bf16 = jnp.bfloat16
f32 = jnp.float32
i32 = jnp.int32

VM = pl.BlockSpec(memory_space=pltpu.VMEM)
SM = pl.BlockSpec(memory_space=pltpu.SMEM)
ANY = pl.BlockSpec(memory_space=pl.ANY)


def nn(a, b):
    return lax.dot_general(a, b, (((1,), (0,)), ((), ())), preferred_element_type=f32)


def nt(a, b):
    return lax.dot_general(a, b, (((1,), (1,)), ((), ())), preferred_element_type=f32)


def tn(a, b):
    return lax.dot_general(a, b, (((0,), (0,)), ((), ())), preferred_element_type=f32)


def split(x):
    hi = x.astype(bf16)
    return hi, (x - hi.astype(f32)).astype(bf16)


def lanes(rows):
    return lax.broadcasted_iota(i32, (rows, LANES), 1)


def rot(x, cosine, sine):
    first = lanes(x.shape[0]) % HD < HD // 2
    other = jnp.where(first, pltpu.roll(x, LANES - HD // 2, 1), pltpu.roll(x, HD // 2, 1))
    return x * cosine + other * sine


def head_masks():
    low = lax.broadcasted_iota(i32, (1, LANES), 1) < HD
    a = jnp.where(low, 1.0, 0.0)
    return a, 1.0 - a


def rotary_tables():
    place = np.arange(SEQ, dtype=np.float32)
    half = HD // 2
    freqs = np.power(np.float32(10000.0), np.arange(half, dtype=np.float32) * np.float32(-2.0 / HD)).astype(np.float32)
    angles = (place[:, None] * freqs[None, :]).astype(np.float32).astype(np.float64)
    c, s = np.cos(angles).astype(np.float32), np.sin(angles).astype(np.float32)
    return np.concatenate([c, c, c, c], 1), np.concatenate([-s, s, -s, s], 1)


def window_bias(starts_ref, tile, width, transposed):
    shape = (width, QT) if transposed else (QT, width)
    qpos = lax.broadcasted_iota(i32, shape, 1 if transposed else 0) + tile * QT
    kpos = lax.broadcasted_iota(i32, shape, 0 if transposed else 1) + tile * QT
    seen = jnp.where(kpos <= qpos, 1, 0)
    for piece in range(PIECES):
        s = starts_ref[0, piece]
        both = jnp.where(qpos >= s, 1, 0) * jnp.where(qpos < s + PIECE, 1, 0)
        both = both * jnp.where(kpos >= s, 1, 0) * jnp.where(kpos < s + PIECE, 1, 0)
        seen = jnp.maximum(seen, both)
    return jnp.where(seen > 0, 0.0, -1e30)


def fwd_kernel(
    starts_ref, tok_ref, prior_ref, ids_ref, ranks_ref, ga_ref, gm_ref, cos_ref, sin_ref, wqkv_ref, wo_ref, wr_ref,
    wres_ref, cv_ref,
    q_ref, k_ref, v_ref, mixed_ref, lse_ref, nattn_ref, resid_ref, nmoe_ref, base_ref, aux_ref, pay_ref,
    bias_ref,
):
    d = tok_ref.shape[1]
    pairs = d // LANES
    ntile = SEQ // QT
    ga, gm = ga_ref[...], gm_ref[...]
    mask_a, mask_b = head_masks()
    mask16 = (mask_a.astype(bf16), mask_b.astype(bf16))

    def project(i, carry):
        rows = pl.ds(pl.multiple_of(i * QT, QT), QT)
        x = tok_ref[rows, :].astype(f32)
        r1 = lax.rsqrt(jnp.mean(x * x, axis=-1, keepdims=True) + EPS)
        n = (x * r1 * ga).astype(bf16)
        nattn_ref[rows, :] = n
        cosine, sine = cos_ref[rows, :], sin_ref[rows, :]
        for c, out in ((0, q_ref), (1, k_ref), (2, v_ref)):
            proj = nn(n, wqkv_ref[c])
            for p in range(pairs):
                part = proj[:, p * LANES : (p + 1) * LANES]
                if c < 2:
                    part = rot(part, cosine, sine)
                part = part.astype(bf16)
                if c == 0:
                    part = part * jnp.array(HD**-0.5, bf16)
                out[rows, p * LANES : (p + 1) * LANES] = part
        return carry

    lax.fori_loop(0, ntile, project, 0)

    taken = jnp.zeros((1, LANES), f32)
    lower = jnp.where(
        lax.broadcasted_iota(i32, (QT, QT), 1) < lax.broadcasted_iota(i32, (QT, QT), 0), 1.0, 0.0
    ).astype(bf16)
    lane = lanes(QT)
    for i in range(ntile):
        lo = i * QT
        width = min(SEQ, lo + 2 * QT) - lo
        rows = pl.ds(lo, QT)
        bias_ref[:, :width] = window_bias(starts_ref, i, width, False)

        def pair(p, lse):
            cols = pl.ds(pl.multiple_of(p * LANES, LANES), LANES)
            q2 = q_ref[rows, cols]
            outs = []
            for h in range(2):
                qh = q2 * mask16[h]
                sb = nt(qh, k_ref[lo : lo + width, cols]) + bias_ref[:, :width]
                m = jnp.max(sb, axis=-1, keepdims=True)
                if lo:
                    sa = nt(qh, k_ref[0:lo, cols])
                    m = jnp.maximum(m, jnp.max(sa, axis=-1, keepdims=True))
                pb = jnp.exp(sb - m)
                total = jnp.sum(pb, axis=-1, keepdims=True)
                acc = nn(pb.astype(bf16), v_ref[lo : lo + width, cols])
                if lo:
                    pa = jnp.exp(sa - m)
                    total = total + jnp.sum(pa, axis=-1, keepdims=True)
                    acc = acc + nn(pa.astype(bf16), v_ref[0:lo, cols])
                outs.append(acc / total)
                lse = jnp.where(lane == 2 * p + h, m + jnp.log(total), lse)
            mixed_ref[rows, cols] = (outs[0] * mask_a + outs[1] * mask_b).astype(bf16)
            return lse

        lse = lax.fori_loop(0, pairs, pair, jnp.zeros((QT, LANES), f32))
        lse_ref[:, rows] = lse.T[0 : lse_ref.shape[0], :]

        x = tok_ref[rows, :].astype(f32)
        resid = x + nn(mixed_ref[rows, :], wo_ref[...])
        resid_ref[rows, :] = resid
        r2 = lax.rsqrt(jnp.mean(resid * resid, axis=-1, keepdims=True) + EPS)
        nm = (resid * r2 * gm).astype(bf16)
        nmoe_ref[rows, :] = nm
        raw = nn(nm, wr_ref[...])
        logits = raw + nn(prior_ref[rows, :], wres_ref[...])
        logits = jnp.where(lane < NF + 2 + NC, logits, -1e30)
        e = jnp.exp(logits - jnp.max(logits, axis=-1, keepdims=True))
        shares = e / jnp.sum(e, axis=-1, keepdims=True)
        id0, id1 = ids_ref[rows, 0:1], ids_ref[rows, 1:2]
        rk0, rk1 = ranks_ref[rows, 0:1], ranks_ref[rows, 1:2]
        hit0, hit1 = jnp.where(lane == id0, 1.0, 0.0), jnp.where(lane == id1, 1.0, 0.0)
        gates = shares * (hit0 + hit1)
        keep0, keep1 = jnp.where(rk0 < CAP, 1.0, 0.0), jnp.where(rk1 < CAP, 1.0, 0.0)
        kept = (hit0 * keep0 + hit1 * keep1) * jnp.where(lane < NF, 1.0, 0.0)
        pos = nn(lower, kept.astype(bf16)) + taken
        taken = taken + jnp.sum(kept, axis=0, keepdims=True)
        pay_ref[0:NF, rows] = jnp.where(kept > 0, shares, -1.0).T[0:NF, :]
        pay_ref[NF : 2 * NF, rows] = jnp.where(kept > 0, pos, -1.0).T[0:NF, :]
        nv = nm.astype(f32)
        aux = jnp.where(lane < NF + 2 + NC, shares, 0.0)
        direct = gates[:, NF + 1 : NF + 2]
        others = None
        for c in range(NC):
            z0, z1 = raw[:, Z0 + 2 * c : Z0 + 2 * c + 1], raw[:, Z0 + 2 * c + 1 : Z0 + 2 * c + 2]
            m0, m1 = 1.0 / (1.0 + jnp.exp(z1 - z0)), 1.0 / (1.0 + jnp.exp(z0 - z1))
            aux = jnp.where(lane == Z0 + 2 * c, m0, aux)
            aux = jnp.where(lane == Z0 + 2 * c + 1, m1, aux)
            w = gates[:, NF + 2 + c : NF + 3 + c]
            direct = direct + w * m0
            term = (w * m1) * cv_ref[c : c + 1, :]
            others = term if others is None else others + term
        aux_ref[rows, :] = aux
        base_ref[rows, :] = resid + direct * nv + others


def mid_kernel(
    dx_ref, gg_ref, og_ref, nmoe_ref, resid_ref, ids_ref, aux_ref, prior_ref, wr_ref, wres_ref, cv_ref, gm_ref,
    gmo_ref, gres_ref, pgrad_ref, nmg_ref, wrg_ref, resg_ref, cvg_ref,
):
    gm = gm_ref[...]
    lane = lanes(QT)
    nmg_ref[...] = jnp.zeros_like(nmg_ref)
    wrg_ref[...] = jnp.zeros_like(wrg_ref)
    resg_ref[...] = jnp.zeros_like(resg_ref)
    cvg_ref[...] = jnp.zeros_like(cvg_ref)

    def tile(i, carry):
        rows = pl.ds(pl.multiple_of(i * QT, QT), QT)
        g16, n16 = og_ref[rows, :], nmoe_ref[rows, :]
        g, nv = g16.astype(f32), n16.astype(f32)
        x = resid_ref[rows, :]
        r2 = lax.rsqrt(jnp.mean(x * x, axis=-1, keepdims=True) + EPS)
        aux = aux_ref[rows, :]
        shares = jnp.where(lane < NF + 2 + NC, aux, 0.0)
        id0, id1 = ids_ref[rows, 0:1], ids_ref[rows, 1:2]
        chosen = jnp.where(lane == id0, 1.0, 0.0) + jnp.where(lane == id1, 1.0, 0.0)
        gates = shares * chosen
        copy_inner = jnp.sum(g * nv, axis=-1, keepdims=True)
        inner = jnp.where(lane < NF, gg_ref[rows, :], 0.0)
        inner = jnp.where(lane == NF + 1, copy_inner, inner)
        direct = gates[:, NF + 1 : NF + 2]
        blend = jnp.zeros((QT, LANES), f32)
        cvw = jnp.zeros((QT, LANES), f32)
        for c in range(NC):
            m0, m1 = aux[:, Z0 + 2 * c : Z0 + 2 * c + 1], aux[:, Z0 + 2 * c + 1 : Z0 + 2 * c + 2]
            v_inner = jnp.sum(g * cv_ref[c : c + 1, :], axis=-1, keepdims=True)
            mean = m0 * copy_inner + m1 * v_inner
            inner = jnp.where(lane == NF + 2 + c, mean, inner)
            w = gates[:, NF + 2 + c : NF + 3 + c]
            direct = direct + w * m0
            blend = jnp.where(lane == Z0 + 2 * c, m0 * (w * copy_inner - w * mean), blend)
            blend = jnp.where(lane == Z0 + 2 * c + 1, m1 * (w * v_inner - w * mean), blend)
            cvw = jnp.where(lane == c, w * m1, cvw)
        grad_router = inner * chosen
        glog = shares * (grad_router - jnp.sum(shares * grad_router, axis=-1, keepdims=True))
        both_hi, both_lo = split(glog + blend)
        log_hi, log_lo = split(glog)
        cv_hi, cv_lo = split(cvw)
        pgrad_ref[rows, :] = nt(log_hi, wres_ref[...]) + nt(log_lo, wres_ref[...])
        wrg_ref[...] += tn(n16, both_hi) + tn(n16, both_lo)
        resg_ref[...] += tn(prior_ref[rows, :], log_hi) + tn(prior_ref[rows, :], log_lo)
        cvg_ref[...] += tn(g16, cv_hi) + tn(g16, cv_lo)
        gmi = dx_ref[rows, :].astype(f32) + direct * g + nt(both_hi, wr_ref[...]) + nt(both_lo, wr_ref[...])
        nmg_ref[...] += jnp.sum(gmi * x * r2, axis=0, keepdims=True)
        scaled = gmi * gm
        avg = jnp.mean(scaled * x, axis=-1, keepdims=True)
        gres = g + r2 * scaled - x * (r2 * r2 * r2 * avg)
        gres_ref[rows, :] = gres
        gmo_ref[rows, :] = gres.astype(bf16)
        return carry

    lax.fori_loop(0, SEQ // QT, tile, 0)


def bwd_kernel(
    starts_ref, gmo_ref, gres_ref, mixed_ref, q_ref, k_ref, v_ref, lse_ref, nattn_ref, tok_ref, ga_ref, cos_ref,
    sin_ref, wqkv_ref, wo_ref,
    igrad_ref, qkvg_ref, wog_ref, nag_ref,
    do_ref, delta_ref, bias_ref, gp_ref, dk_ref, dv_ref, dq_ref,
):
    d = tok_ref.shape[1]
    pairs = d // LANES
    ntile = SEQ // QT
    ga = ga_ref[...]
    mask_a, mask_b = head_masks()
    mask16 = (mask_a.astype(bf16), mask_b.astype(bf16))
    maskf = (mask_a, mask_b)
    heads = delta_ref.shape[0]
    pick = jnp.where(
        lax.broadcasted_iota(i32, (heads, d), 1) // HD == lax.broadcasted_iota(i32, (heads, d), 0), 1.0, 0.0
    ).astype(bf16)

    def start(i, carry):
        rows = pl.ds(pl.multiple_of(i * QT, QT), QT)
        do = nt(gmo_ref[rows, :], wo_ref[...]).astype(bf16)
        do_ref[rows, :] = do
        hi, lo = split(do.astype(f32) * mixed_ref[rows, :].astype(f32))
        delta_ref[:, rows] = nt(pick, hi) + nt(pick, lo)
        return carry

    lax.fori_loop(0, ntile, start, 0)
    wog_ref[...] = tn(mixed_ref[...], gmo_ref[...]).astype(wog_ref.dtype)
    for i in range(ntile):
        width = min(SEQ, (i + 2) * QT) - i * QT
        bias_ref[i, 0:width, :] = window_bias(starts_ref, i, width, True)

    def pair(p, carry):
        cols = pl.ds(pl.multiple_of(p * LANES, LANES), LANES)
        dk_ref[...] = jnp.zeros_like(dk_ref)
        dv_ref[...] = jnp.zeros_like(dv_ref)
        for i in range(ntile):
            lo = i * QT
            width = min(SEQ, lo + 2 * QT) - lo
            rows = pl.ds(lo, QT)
            q2, do2 = q_ref[rows, cols], do_ref[rows, cols]
            dq = jnp.zeros((QT, LANES), f32)
            for h in range(2):
                qh, doh = q2 * mask16[h], do2 * mask16[h]
                lse, delta = lse_ref[pl.ds(2 * p + h, 1), rows], delta_ref[pl.ds(2 * p + h, 1), rows]
                spans = [(lo, width, True)] + ([(0, lo, False)] if lo else [])
                for at, size, masked in spans:
                    k2 = k_ref[at : at + size, cols]
                    s = nt(k2, qh)
                    if masked:
                        s = s + bias_ref[i, 0:size, :]
                    prob = jnp.exp(s - lse)
                    ds = (prob * (nt(v_ref[at : at + size, cols], doh) - delta)).astype(bf16)
                    dv_ref[at : at + size, :] += nn(prob.astype(bf16), doh)
                    dk_ref[at : at + size, :] += nn(ds, qh)
                    dq = dq + tn(ds, k2) * maskf[h]
            dq_ref[rows, :] = dq * HD**-0.5
        cosine, sine = cos_ref[...], -sin_ref[...]
        gp_ref[0, :, cols] = rot(dq_ref[...], cosine, sine).astype(bf16)
        gp_ref[1, :, cols] = rot(dk_ref[...], cosine, sine).astype(bf16)
        gp_ref[2, :, cols] = dv_ref[...].astype(bf16)
        return carry

    lax.fori_loop(0, pairs, pair, 0)
    for c in range(3):
        qkvg_ref[c] = tn(nattn_ref[...], gp_ref[c]).astype(qkvg_ref.dtype)
    nag_ref[...] = jnp.zeros_like(nag_ref)

    def finish(i, carry):
        rows = pl.ds(pl.multiple_of(i * QT, QT), QT)
        gai = nt(gp_ref[0, rows, :], wqkv_ref[0]) + nt(gp_ref[1, rows, :], wqkv_ref[1])
        gai = gai + nt(gp_ref[2, rows, :], wqkv_ref[2])
        x = tok_ref[rows, :].astype(f32)
        r1 = lax.rsqrt(jnp.mean(x * x, axis=-1, keepdims=True) + EPS)
        nag_ref[...] += jnp.sum(gai * x * r1, axis=0, keepdims=True)
        scaled = gai * ga
        avg = jnp.mean(scaled * x, axis=-1, keepdims=True)
        igrad_ref[rows, :] = gres_ref[rows, :] + r1 * scaled - x * (r1 * r1 * r1 * avg)
        return carry

    lax.fori_loop(0, ntile, finish, 0)


def pack_kernel(
    meta_ref, pos_ref, gate_ref, x_ref, y_ref, xc_ref, yc_ref, gc_ref, xs, ys, gs, sems,
):
    g = pl.program_id(0)
    off, count = meta_ref[g], meta_ref[NF + 1 + g]
    pos, gate = pos_ref[0], gate_ref[0]
    group = pos.shape[1]

    def window(j, carry):
        at = pl.multiple_of(off + j * WIN, 16)
        slot = (lax.broadcasted_iota(i32, (WIN, group), 0) + j * WIN).astype(f32)
        hot = jnp.where(slot == pos, 1.0, 0.0)
        h16 = hot.astype(bf16)
        xs[pl.ds(at, WIN), :] = nn(h16, x_ref[0]).astype(bf16)
        ys[pl.ds(at, WIN), :] = nn(h16, y_ref[0]).astype(bf16)
        gs[pl.ds(at, WIN), :] = jnp.broadcast_to(jnp.sum(hot * gate, axis=1, keepdims=True), (WIN, LANES))
        return carry

    lax.fori_loop(0, (count + WIN - 1) // WIN, window, 0)

    @pl.when(g == NF - 1)
    def _():
        at = pl.multiple_of(meta_ref[NF], 16)
        for k in range(TM // WIN):
            xs[pl.ds(at + k * WIN, WIN), :] = jnp.zeros((WIN, xs.shape[1]), bf16)
            ys[pl.ds(at + k * WIN, WIN), :] = jnp.zeros((WIN, ys.shape[1]), bf16)
            gs[pl.ds(at + k * WIN, WIN), :] = jnp.zeros((WIN, LANES), f32)
        tiles = meta_ref[2 * NF + 1]

        def copies(t):
            rows = pl.ds(pl.multiple_of(t * TM, TM), TM)
            return [
                pltpu.make_async_copy(src.at[rows, :], dst.at[rows, :], sems.at[n, t])
                for n, (src, dst) in enumerate(((xs, xc_ref), (ys, yc_ref), (gs, gc_ref)))
            ]

        def begin(t, carry):
            for c in copies(t):
                c.start()
            return carry

        def end(t, carry):
            for c in copies(t):
                c.wait()
            return carry

        lax.fori_loop(0, tiles, begin, 0)
        lax.fori_loop(0, tiles, end, 0)


def ffn_kernel(meta_ref, x_ref, y_ref, gc_ref, w_ref, out_ref, dx_ref, gg_ref, dw_ref, acc):
    i = pl.program_id(0)

    @pl.when(i == 0)
    def _():
        acc[...] = jnp.zeros_like(acc)

    @pl.when(i < meta_ref[2 * NF + 1])
    def _():
        x = x_ref[...]
        gate = gc_ref[:, 0:1]
        dy = y_ref[...].astype(f32)
        ge = (gate * dy).astype(bf16)
        rows, d = x.shape
        x_t, ge_t = x.T, ge.T

        def chunk(c, carry):
            eo, dx = carry
            wg, wu, wd = w_ref[c, 0], w_ref[c, 1], w_ref[c, 2]
            gv, uv = nn(x, wg), nn(x, wu)
            gh = nn(ge, wd)
            sig = 1.0 / (1.0 + jnp.exp(-gv))
            act = gv * sig
            hid = (act * uv).astype(bf16)
            eo = eo + nt(hid, wd)
            gg = (gh * uv * (sig * (1.0 + gv * (1.0 - sig)))).astype(bf16)
            gu = (gh * act).astype(bf16)
            dx = dx + nt(gg, wg) + nt(gu, wu)
            acc[c, 0] += nn(x_t, gg)
            acc[c, 1] += nn(x_t, gu)
            acc[c, 2] += nn(ge_t, hid)
            return eo, dx

        zero = jnp.zeros((rows, d), f32)
        eo, dx = lax.fori_loop(0, w_ref.shape[0], chunk, (zero, zero))
        out_ref[...] = (gate * eo).astype(bf16)
        dx_ref[...] = dx.astype(bf16)
        gg_ref[...] = jnp.broadcast_to(jnp.sum(dy * eo, axis=1, keepdims=True), gg_ref.shape)

    @pl.when(i == pl.num_programs(0) - 1)
    def _():
        dw_ref[...] = acc[...].astype(bf16)


def unpack_kernel(
    meta_ref, pos_ref, yc_ref, dxc_ref, ggc_ref, out_ref, dx_ref, gg_ref, ys, xs, gs, sems,
):
    g = pl.program_id(0)
    off, count = meta_ref[g], meta_ref[NF + 1 + g]

    @pl.when(g == 0)
    def _():
        tiles = meta_ref[2 * NF + 1]

        def copies(t):
            rows = pl.ds(pl.multiple_of(t * TM, TM), TM)
            return [
                pltpu.make_async_copy(src.at[rows, :], dst.at[rows, :], sems.at[n, t])
                for n, (src, dst) in enumerate(((yc_ref, ys), (dxc_ref, xs), (ggc_ref, gs)))
            ]

        def begin(t, carry):
            for c in copies(t):
                c.start()
            return carry

        def end(t, carry):
            for c in copies(t):
                c.wait()
            return carry

        lax.fori_loop(0, tiles, begin, 0)
        lax.fori_loop(0, tiles, end, 0)

    pos = pos_ref[0]
    group = pos.shape[1]
    d = ys.shape[1]

    def window(j, first):
        at = pl.multiple_of(off + j * WIN, 16)
        index = lax.broadcasted_iota(i32, (WIN, group), 0) + j * WIN
        hot = jnp.where(index.astype(f32) == pos, 1.0, 0.0)
        h16 = hot.astype(bf16)
        live = lax.broadcasted_iota(i32, (WIN, d), 0) + j * WIN < count
        yv = jnp.where(live, ys[pl.ds(at, WIN), :].astype(f32), 0.0).astype(bf16)
        xv = jnp.where(live, xs[pl.ds(at, WIN), :].astype(f32), 0.0).astype(bf16)
        gv = jnp.where(live[:, 0:1], gs[pl.ds(at, WIN), 0:1], 0.0)
        py, px = tn(h16, yv).astype(bf16), tn(h16, xv).astype(bf16)
        pg = jnp.sum(hot * gv, axis=0, keepdims=True)
        if first:
            out_ref[0], dx_ref[0], gg_ref[0] = py, px, pg
        else:
            out_ref[0] += py
            dx_ref[0] += px
            gg_ref[0] += pg

    window(0, True)

    def more(j, carry):
        window(j, False)
        return carry

    lax.fori_loop(1, (count + WIN - 1) // WIN, more, 0)


def shape(dims, dtype):
    return jax.ShapeDtypeStruct(dims, dtype)


def cost(gflop, mbytes, mexp=0):
    return pl.CostEstimate(flops=int(gflop * 1e9), bytes_accessed=int(mbytes * 1e6), transcendentals=int(mexp * 1e6))


def experts(x_all, y_all, pos, gate, w_all):
    groups, group, d = x_all.shape
    count = (jnp.max(pos, axis=1) + 1.0).astype(i32)
    padded = (count + 15) // 16 * 16
    order = jnp.arange(NF)
    ends = jnp.sum(jnp.where(order[None, :] <= order[:, None], padded[None, :], 0), axis=1)
    tiles = jnp.maximum((ends[-1:] + TM - 1) // TM, 1)
    meta = jnp.concatenate([jnp.zeros((1,), i32), ends, count, tiles])
    room = NF * min(CAP, group) + TM + WIN
    room = (room + TM - 1) // TM * TM
    most = room // TM
    pos3, gate3 = pos.reshape(groups, 1, group), gate.reshape(groups, 1, group)
    params = pltpu.CompilerParams(vmem_limit_bytes=60 << 20, dimension_semantics=("arbitrary",))
    row_spec = pl.BlockSpec((1, 1, group), lambda g, *_: (g, 0, 0))
    tok_spec = pl.BlockSpec((1, group, d), lambda g, *_: (g, 0, 0))
    scratch = [
        pltpu.VMEM((room, d), bf16),
        pltpu.VMEM((room, d), bf16),
        pltpu.VMEM((room, LANES), f32),
        pltpu.SemaphoreType.DMA((3, most)),
    ]
    xc, yc, gc = pl.pallas_call(
        pack_kernel,
        out_shape=(shape((room, d), bf16), shape((room, d), bf16), shape((room, LANES), f32)),
        grid_spec=pltpu.PrefetchScalarGridSpec(
            num_scalar_prefetch=1,
            grid=(groups,),
            in_specs=[row_spec, row_spec, tok_spec, tok_spec],
            out_specs=(ANY, ANY, ANY),
            scratch_shapes=scratch,
        ),
        compiler_params=params,
        cost_estimate=cost(8, 30),
    )(meta, pos3, gate3, x_all, y_all)
    tile = lambda i, m: (jnp.minimum(i, m[2 * NF + 1] - 1), 0)
    zero4 = lambda i, m: (0, 0, 0, 0)
    out_c, dx_c, gg_c, dw = pl.pallas_call(
        ffn_kernel,
        out_shape=(
            shape((room, d), bf16), shape((room, d), bf16), shape((room, LANES), f32), shape(w_all.shape, bf16),
        ),
        grid_spec=pltpu.PrefetchScalarGridSpec(
            num_scalar_prefetch=1,
            grid=(most,),
            in_specs=[
                pl.BlockSpec((TM, d), tile),
                pl.BlockSpec((TM, d), tile),
                pl.BlockSpec((TM, LANES), tile),
                pl.BlockSpec(w_all.shape, zero4, pipeline_mode=pl.Buffered(1)),
            ],
            out_specs=(
                pl.BlockSpec((TM, d), tile),
                pl.BlockSpec((TM, d), tile),
                pl.BlockSpec((TM, LANES), tile),
                pl.BlockSpec(w_all.shape, zero4, pipeline_mode=pl.Buffered(1)),
            ),
            scratch_shapes=[pltpu.VMEM(w_all.shape, f32)],
        ),
        compiler_params=params,
        cost_estimate=cost(44, 30),
    )(meta, xc, yc, gc, w_all)
    out, dx, gg = pl.pallas_call(
        unpack_kernel,
        out_shape=(
            shape((groups, group, d), bf16), shape((groups, group, d), bf16), shape((groups, 1, group), f32),
        ),
        grid_spec=pltpu.PrefetchScalarGridSpec(
            num_scalar_prefetch=1,
            grid=(groups,),
            in_specs=[row_spec, ANY, ANY, ANY],
            out_specs=(tok_spec, tok_spec, row_spec),
            scratch_shapes=scratch,
        ),
        compiler_params=params,
        cost_estimate=cost(8, 30),
    )(meta, pos3, out_c, dx_c, gg_c)
    return out, dx, gg, dw


def on_device(
    dp,
    tensor,
    tokens,
    prior_logits,
    expert_ids,
    expert_ranks,
    piece_starts,
    norm_attn,
    qkv_weight,
    out_weight,
    norm_moe,
    router_weight,
    residual_weight,
    const_vectors,
    const_gates,
    w_gate_up,
    w_down,
    out_grad,
):
    rows, d = tokens.shape
    ne = router_weight.shape[1]
    packs = dp // NF
    groups = None if packs == 1 else [list(range(NF * r, NF * (r + 1))) for r in range(packs)]
    across = None if packs == 1 else [list(range(j, dp, NF)) for j in range(NF)]
    here = lax.axis_index("tensor")
    ids = lax.dynamic_slice_in_dim(expert_ids, here * rows, rows, 0)
    ranks = lax.dynamic_slice_in_dim(expert_ranks, here * rows, rows, 0)
    starts = lax.dynamic_slice_in_dim(piece_starts, here, 1, 0)
    ga, gm = norm_attn.astype(f32).reshape(1, d), norm_moe.astype(f32).reshape(1, d)
    cosine, sine = (jnp.asarray(t) for t in rotary_tables())
    prior = jnp.pad(prior_logits, ((0, 0), (0, LANES - ne)))
    wr = jnp.concatenate(
        [router_weight, jnp.zeros((d, Z0 - ne), bf16), const_gates.reshape(2 * NC, d).T,
         jnp.zeros((d, LANES - Z0 - 2 * NC), bf16)], axis=1)
    wres = jnp.pad(residual_weight, ((0, LANES - ne), (0, LANES - ne)))
    cv = const_vectors.astype(f32)

    wqkv = lax.all_gather(lax.all_gather(qkv_weight, "tensor", axis=2, tiled=True), "dp", axis=1, tiled=True)
    wo = lax.all_gather(lax.all_gather(out_weight, "tensor", axis=0, tiled=True), "dp", axis=1, tiled=True)

    shard = w_down.shape[1]
    w_local = jnp.concatenate([w_gate_up, w_down.transpose(0, 2, 1)[None]], axis=0)
    w_mine = lax.all_to_all(w_local, "dp", 1, 2, tiled=True, axis_index_groups=groups)
    w_mine = w_mine.reshape(3, w_local.shape[2] * NF, shard)
    if packs > 1:
        w_mine = lax.all_gather(w_mine, "dp", axis=1, tiled=True, axis_index_groups=across)
    w_all = lax.all_gather(w_mine, "tensor", axis=0, tiled=False)

    y_all = lax.all_gather(out_grad, "dp", axis=0, tiled=False, axis_index_groups=groups)

    heads = 16
    q, k, v, mixed, lse, nattn, resid, nmoe, base, aux, pay = pl.pallas_call(
        fwd_kernel,
        in_specs=[SM] + [VM] * 13,
        out_specs=[VM] * 11,
        out_shape=(
            shape((rows, d), bf16), shape((rows, d), bf16), shape((rows, d), bf16), shape((rows, d), bf16),
            shape((heads, rows), f32), shape((rows, d), bf16), shape((rows, d), f32), shape((rows, d), bf16),
            shape((rows, d), f32), shape((rows, LANES), f32), shape((2 * NF, rows), f32),
        ),
        scratch_shapes=[pltpu.VMEM((QT, 2 * QT), f32)],
        compiler_params=pltpu.CompilerParams(vmem_limit_bytes=60 << 20),
        cost_estimate=cost(40, 30, 10),
    )(starts, tokens, prior, ids, ranks, ga, gm, cosine, sine, wqkv, wo, wr, wres, cv)

    x_all = lax.all_gather(nmoe, "dp", axis=0, tiled=False, axis_index_groups=groups)
    payload = pay.reshape(2, NF, rows).transpose(1, 0, 2)
    payload = lax.all_to_all(payload, "dp", 0, 0, tiled=True, axis_index_groups=groups)
    out_p, dx_p, gg_p, dw = experts(x_all, y_all, payload[:, 1], payload[:, 0], w_all)
    gg = lax.all_to_all(gg_p.reshape(NF, rows), "dp", 0, 0, tiled=True, axis_index_groups=groups)
    gg = jnp.pad(gg, ((0, LANES - NF), (0, 0))).T
    scatter = functools.partial(
        lax.psum_scatter, axis_name="dp", scatter_dimension=0, tiled=True, axis_index_groups=groups
    )
    dx = scatter(dx_p.reshape(NF * rows, d))
    ffn = scatter(out_p.reshape(NF * rows, d))
    layer_out = (base + ffn.astype(f32)).astype(bf16)

    dw_mine = lax.psum_scatter(dw, "tensor", scatter_dimension=0, tiled=False)
    if packs > 1:
        dw_mine = lax.psum_scatter(dw_mine, "dp", scatter_dimension=1, tiled=True, axis_index_groups=across)
    dw_mine = dw_mine.reshape(3, NF, -1, shard)
    dw_mine = lax.all_to_all(dw_mine, "dp", 1, 1, tiled=True, axis_index_groups=groups).astype(f32)
    gate_up_grad, down_grad = dw_mine[0:2], dw_mine[2].transpose(0, 2, 1)

    gmo, gres, pgrad, nmg, wrg, resg, cvg = pl.pallas_call(
        mid_kernel,
        in_specs=[VM] * 12,
        out_specs=[VM] * 7,
        out_shape=(
            shape((rows, d), bf16), shape((rows, d), f32), shape((rows, LANES), f32), shape((1, d), f32),
            shape((d, LANES), f32), shape((LANES, LANES), f32), shape((d, LANES), f32),
        ),
        compiler_params=pltpu.CompilerParams(vmem_limit_bytes=60 << 20),
        cost_estimate=cost(2, 20),
    )(dx, gg, out_grad, nmoe, resid, ids, aux, prior, wr, wres, cv, gm)
    igrad, qkvg, wog, nag = pl.pallas_call(
        bwd_kernel,
        in_specs=[SM] + [VM] * 14,
        out_specs=[VM] * 4,
        out_shape=(
            shape((rows, d), f32), shape((3, d, d), bf16), shape((d, d), bf16), shape((1, d), f32),
        ),
        scratch_shapes=[
            pltpu.VMEM((rows, d), bf16),
            pltpu.VMEM((heads, rows), f32),
            pltpu.VMEM((rows // QT, 2 * QT, QT), f32),
            pltpu.VMEM((3, rows, d), bf16),
            pltpu.VMEM((rows, LANES), f32),
            pltpu.VMEM((rows, LANES), f32),
            pltpu.VMEM((rows, LANES), f32),
        ],
        compiler_params=pltpu.CompilerParams(vmem_limit_bytes=60 << 20),
        cost_estimate=cost(80, 40, 10),
    )(starts, gmo, gres, mixed, q, k, v, lse, nattn, tokens, ga, cosine, sine, wqkv, wo)

    qkvg = lax.psum_scatter(qkvg, "dp", scatter_dimension=1, tiled=True)
    qkvg = lax.psum_scatter(qkvg, "tensor", scatter_dimension=2, tiled=True).astype(f32)
    wog = lax.psum_scatter(wog, "dp", scatter_dimension=1, tiled=True)
    wog = lax.psum_scatter(wog, "tensor", scatter_dimension=0, tiled=True).astype(f32)
    small = lax.psum(
        (nag.reshape(d), nmg.reshape(d), wrg[:, 0 : Z0 + 2 * NC], resg[0:ne, 0:ne], cvg[:, 0:NC]), ("dp", "tensor")
    )
    return (
        layer_out,
        igrad,
        pgrad[:, 0:ne],
        small[0],
        qkvg,
        wog,
        small[1],
        small[2][:, 0:ne],
        small[3],
        small[4].T,
        small[2][:, Z0 : Z0 + 2 * NC].T.reshape(NC, 2, d),
        gate_up_grad,
        down_grad,
    )


def solution(mesh):
    body = functools.partial(on_device, mesh.shape["dp"], mesh.shape["tensor"])
    rows = P(("dp", "tensor"), None)
    return jax.shard_map(
        body,
        mesh=mesh,
        in_specs=(
            rows, rows, P("dp", None), P("dp", None), P("dp", None), P(), P(None, "dp", "tensor"), P("tensor", "dp"),
            P(), P(), P(), P(), P(), P(None, None, "dp", "tensor"), P(None, "tensor", "dp"), rows,
        ),
        out_specs=(
            rows, rows, rows, P(), P(None, "dp", "tensor"), P("tensor", "dp"), P(), P(), P(), P(), P(),
            P(None, None, "dp", "tensor"), P(None, "tensor", "dp"),
        ),
        check_vma=False,
    )
```

```python
import functools

import jax
import jax.numpy as jnp
import numpy as np
from jax import lax
from jax.experimental import pallas as pl
from jax.experimental.pallas import tpu as pltpu
from jax.sharding import PartitionSpec as P

HD = 64
NF = 8
NC = 2
SEQ = 1024
PIECE = 256
PIECES = 2
CAP = 768
EPS = 1e-06
QT = 256
LANES = 128
TM = 256
WIN = 256
Z0 = 16

bf16 = jnp.bfloat16
f32 = jnp.float32
i32 = jnp.int32

VM = pl.BlockSpec(memory_space=pltpu.VMEM)
SM = pl.BlockSpec(memory_space=pltpu.SMEM)
ANY = pl.BlockSpec(memory_space=pl.ANY)


def nn(a, b):
    return lax.dot_general(a, b, (((1,), (0,)), ((), ())), preferred_element_type=f32)


def nt(a, b):
    return lax.dot_general(a, b, (((1,), (1,)), ((), ())), preferred_element_type=f32)


def tn(a, b):
    return lax.dot_general(a, b, (((0,), (0,)), ((), ())), preferred_element_type=f32)


def split(x):
    hi = x.astype(bf16)
    return hi, (x - hi.astype(f32)).astype(bf16)


def lanes(rows):
    return lax.broadcasted_iota(i32, (rows, LANES), 1)


def rot(x, cosine, sine):
    first = lanes(x.shape[0]) % HD < HD // 2
    other = jnp.where(first, pltpu.roll(x, LANES - HD // 2, 1), pltpu.roll(x, HD // 2, 1))
    return x * cosine + other * sine


def head_masks():
    low = lax.broadcasted_iota(i32, (1, LANES), 1) < HD
    a = jnp.where(low, 1.0, 0.0)
    return a, 1.0 - a


def rotary_tables():
    place = np.arange(SEQ, dtype=np.float32)
    half = HD // 2
    freqs = np.power(np.float32(10000.0), np.arange(half, dtype=np.float32) * np.float32(-2.0 / HD)).astype(np.float32)
    angles = (place[:, None] * freqs[None, :]).astype(np.float32).astype(np.float64)
    c, s = np.cos(angles).astype(np.float32), np.sin(angles).astype(np.float32)
    return np.concatenate([c, c, c, c], 1), np.concatenate([-s, s, -s, s], 1)


def window_bias(starts_ref, tile, width, transposed):
    shape = (width, QT) if transposed else (QT, width)
    qpos = lax.broadcasted_iota(i32, shape, 1 if transposed else 0) + tile * QT
    kpos = lax.broadcasted_iota(i32, shape, 0 if transposed else 1) + tile * QT
    seen = jnp.where(kpos <= qpos, 1, 0)
    for piece in range(PIECES):
        s = starts_ref[0, piece]
        both = jnp.where(qpos >= s, 1, 0) * jnp.where(qpos < s + PIECE, 1, 0)
        both = both * jnp.where(kpos >= s, 1, 0) * jnp.where(kpos < s + PIECE, 1, 0)
        seen = jnp.maximum(seen, both)
    return jnp.where(seen > 0, 0.0, -1e30)


MESH = pl.DeviceIdType.MESH
GATHER_COPIES = 13
REDUCE_COPIES = 10


def flip(index, m):
    for bit in (1, 2, 4):
        if m & bit:
            index = index + bit - 2 * bit * (index // bit % 2)
    return index


def remote(src, dst, sems, n, axis, peer):
    return pltpu.make_async_remote_copy(
        src_ref=src,
        dst_ref=dst,
        send_sem=sems.at[0, n],
        recv_sem=sems.at[1, n],
        device_id={axis: peer},
        device_id_type=MESH,
    )


def greet(peers):
    barrier = pltpu.get_barrier_semaphore()
    for axis, peer in peers:
        pl.semaphore_signal(barrier, inc=1, device_id={axis: peer}, device_id_type=MESH)
    pl.semaphore_wait(barrier, len(peers))


def near_peers():
    me = lax.axis_index("dp")
    return [("dp", flip(me, m)) for m in (1, 2, 4)]


def far_peers(tensor):
    me = lax.axis_index("tensor")
    return [("tensor", (me + k) % tensor) for k in range(1, tensor)]


class Gather8:
    def __init__(self, src, dst, sems, own_sem):
        me = lax.axis_index("dp")
        slot = me % NF
        nx, ny, nc = flip(me, 2), flip(me, 4), flip(me, 1)
        sx, sy, sd = flip(slot, 2), flip(slot, 4), flip(slot, 6)
        self.own = pltpu.make_async_copy(src(None), dst(slot, None), own_sem)
        go = lambda n, s, d, peer: remote(s, d, sems, n, "dp", peer)
        on = lambda n, s, h, peer: go(n, dst(s, h), dst(s, h), peer)
        self.c = [
            go(0, src(0), dst(slot, 0), nx),
            go(1, src(1), dst(slot, 1), ny),
            go(2, src(1), dst(slot, 1), nx),
            go(3, src(0), dst(slot, 0), ny),
            go(4, src(None), dst(slot, None), nc),
            on(5, sx, 0, ny),
            on(6, sy, 1, nx),
            on(7, sx, 0, nc),
            on(8, sy, 1, nc),
            on(9, sx, 1, nc),
            on(10, sy, 0, nc),
            on(11, sd, 0, nc),
            on(12, sd, 1, nc),
        ]

    def begin(self):
        self.own.start()
        for n in range(5):
            self.c[n].start()

    def forward(self):
        for got, out in ((0, (5, 7)), (1, (6, 8))):
            self.c[got].wait_recv()
            for n in out:
                self.c[n].start()

    def share(self):
        for got, out in ((2, 9), (3, 10)):
            self.c[got].wait_recv()
            self.c[out].start()

    def last(self):
        for got, out in ((5, 11), (6, 12)):
            self.c[got].wait_recv()
            self.c[out].start()

    def end(self):
        for n in (4, 7, 8, 9, 10, 11, 12):
            self.c[n].wait_recv()
        for c in self.c:
            c.wait_send()
        self.own.wait()


def halves(ref, index, rows):
    half = rows // 2
    return lambda s, h: ref.at[s] if h is None else ref.at[s, pl.ds(h * half, half)]


def gather_kernel(src, dst, sems, own_sem):
    greet(near_peers())
    half = src.shape[0] // 2
    g = Gather8(
        lambda h: src if h is None else src.at[pl.ds(h * half, half)], halves(dst, 0, src.shape[0]), sems, own_sem
    )
    g.begin()
    g.forward()
    g.share()
    g.last()
    g.end()


def gather8(x, cid):
    return pl.pallas_call(
        gather_kernel,
        in_specs=[ANY],
        out_specs=ANY,
        out_shape=shape((NF, *x.shape), x.dtype),
        scratch_shapes=[pltpu.SemaphoreType.DMA((2, GATHER_COPIES)), pltpu.SemaphoreType.DMA],
        compiler_params=pltpu.CompilerParams(collective_id=cid, has_side_effects=True),
        cost_estimate=cost(50, 30),
    )(x)


def weights_kernel(tensor, w_ref, out_ref, zbuf, slab, sems, zsems, own_sem):
    here = lax.axis_index("tensor")
    k, r, f = w_ref.shape
    greet(near_peers() + far_peers(tensor))
    copies = [
        remote(w_ref, zbuf.at[here], zsems, n, axis, peer) for n, (axis, peer) in enumerate(far_peers(tensor))
    ]
    for c in copies:
        c.start()
    zbuf[here] = w_ref[...]
    for c in copies:
        c.wait_recv()
    for c in range(k):
        for t in range(0, tensor, 2):
            both = jnp.concatenate([zbuf[t, c].astype(f32), zbuf[t + 1, c].astype(f32)], axis=-1)
            slab[c, :, t * f : (t + 2) * f] = both.astype(bf16)
    part = lambda h: pl.ds(0, k) if h is None else pl.ds(h * (k // 2), k // 2)
    g = Gather8(
        lambda h: slab.at[part(h)],
        lambda s, h: out_ref.at[part(h), pl.ds(pl.multiple_of(s * r, r), r), :],
        sems,
        own_sem,
    )
    g.begin()
    g.forward()
    g.share()
    g.last()
    g.end()
    for c in copies:
        c.wait_send()


def gather_weights(w, tensor, cid):
    k, r, f = w.shape
    return pl.pallas_call(
        functools.partial(weights_kernel, tensor),
        in_specs=[VM],
        out_specs=ANY,
        out_shape=shape((k, NF * r, tensor * f), w.dtype),
        scratch_shapes=[
            pltpu.VMEM((tensor, k, r, f), bf16),
            pltpu.VMEM((k, r, tensor * f), bf16),
            pltpu.SemaphoreType.DMA((2, GATHER_COPIES)),
            pltpu.SemaphoreType.DMA((2, tensor - 1)),
            pltpu.SemaphoreType.DMA,
        ],
        compiler_params=pltpu.CompilerParams(collective_id=cid, has_side_effects=True),
        cost_estimate=cost(30, 10),
    )(w)


class Reduce8:
    def __init__(self, view, bufs, sems, lsems):
        self.own, self.away, self.qd, self.qx, self.qy, self.ind, self.inx, self.iny = bufs
        me = lax.axis_index("dp")
        slot = me % NF
        half = self.qd.shape[0] // 2
        a, b = pl.ds(0, half), pl.ds(half, half)
        self.a, self.b = a, b
        nx, ny, nc = flip(me, 2), flip(me, 4), flip(me, 1)
        mine = [flip(slot, m) for m in (6, 2, 4)] + [slot]
        self.loads = [pltpu.make_async_copy(view(s), self.own.at[n], lsems.at[n]) for n, s in enumerate(mine)]
        self.over = [remote(view(flip(s, 1)), self.away.at[n], sems, n, "dp", nc) for n, s in enumerate(mine)]
        go = lambda n, q, i, part, peer: remote(q.at[part], i.at[part], sems, n, "dp", peer)
        self.da, self.db = go(4, self.qd, self.ind, a, nx), go(5, self.qd, self.ind, b, ny)
        self.xa, self.yb = go(6, self.qx, self.inx, a, nx), go(7, self.qy, self.iny, b, ny)
        self.ya, self.xb = go(8, self.qy, self.iny, a, ny), go(9, self.qx, self.inx, b, nx)

    def load(self):
        for c in self.loads:
            c.start()

    def begin(self):
        for c in self.over:
            c.start()

    def add(self, out, n, part, more=None):
        total = self.own[n, part].astype(f32) + self.away[n, part].astype(f32)
        if more is not None:
            total = total + more[part].astype(f32)
        out[part] = total.astype(bf16)

    def ready(self, n):
        self.loads[n].wait()
        self.over[n].wait_recv()

    def first(self):
        self.ready(0)
        self.add(self.qd, 0, self.a)
        self.da.start()
        self.add(self.qd, 0, self.b)
        self.db.start()

    def second(self):
        self.ready(1)
        self.add(self.qx, 1, self.a)
        self.xa.start()
        self.ready(2)
        self.add(self.qy, 2, self.b)
        self.yb.start()

    def third(self):
        self.ready(3)
        self.da.wait_recv()
        self.add(self.qy, 2, self.a, self.ind)
        self.ya.start()
        self.db.wait_recv()
        self.add(self.qx, 1, self.b, self.ind)
        self.xb.start()

    def end(self, write):
        for part, first, second in ((self.a, self.xa, self.ya), (self.b, self.yb, self.xb)):
            first.wait_recv()
            second.wait_recv()
            total = self.own[3, part].astype(f32) + self.away[3, part].astype(f32)
            write(part, total + self.inx[part].astype(f32) + self.iny[part].astype(f32))

    def close(self):
        for c in self.over + [self.da, self.db, self.xa, self.yb, self.ya, self.xb]:
            c.wait_send()


def reduce_scratch(block):
    return [pltpu.VMEM((4, *block), bf16)] * 2 + [pltpu.VMEM(block, bf16)] * 6 + [
        pltpu.SemaphoreType.DMA((2, REDUCE_COPIES)),
        pltpu.SemaphoreType.DMA((4,)),
    ]


def reduce_kernel(p_ref, out_ref, *scratch):
    r = Reduce8(lambda s: p_ref.at[s], scratch[:8], *scratch[8:10])
    r.load()
    greet(near_peers())
    r.begin()
    r.first()
    r.second()
    r.third()

    def write(part, total):
        out_ref[part] = total.astype(out_ref.dtype)

    r.end(write)
    r.close()


def reduce8(p, cid):
    groups, rows, columns = p.shape
    block = (2, rows // 2, columns)
    out = pl.pallas_call(
        reduce_kernel,
        in_specs=[ANY],
        out_specs=VM,
        out_shape=shape(block, bf16),
        scratch_shapes=reduce_scratch(block),
        compiler_params=pltpu.CompilerParams(collective_id=cid, has_side_effects=True, vmem_limit_bytes=60 << 20),
        cost_estimate=cost(50, 30),
    )(p.reshape(groups, *block))
    return out.reshape(rows, columns)


def exchange_kernel(n, *refs):
    srcs, dst, sems, own_sems = refs[:n], refs[n], refs[n + 1], refs[n + 2]
    me = lax.axis_index("dp")
    slot = me % NF
    at, pieces = 0, []
    for src in srcs:
        pieces.append((src, pl.ds(at, src.shape[0])))
        at += src.shape[0]
    own = [
        pltpu.make_async_copy(src.at[:, slot], dst.at[part, slot], own_sems.at[i])
        for i, (src, part) in enumerate(pieces)
    ]
    for c in own:
        c.start()
    greet([("dp", flip(me, m)) for m in range(1, NF)])
    copies = []
    for m in (6, 7, 2, 3, 4, 5, 1):
        for i, (src, part) in enumerate(pieces):
            at = (m - 1) * n + i
            copies.append(remote(src.at[:, flip(slot, m)], dst.at[part, slot], sems, at, "dp", flip(me, m)))
    for c in copies:
        c.start()
    for c in copies:
        c.wait_recv()
    for c in copies:
        c.wait_send()
    for c in own:
        c.wait()


def exchange8(xs, cid):
    total = sum(x.shape[0] for x in xs)
    return pl.pallas_call(
        functools.partial(exchange_kernel, len(xs)),
        in_specs=[ANY] * len(xs),
        out_specs=ANY,
        out_shape=shape((total, *xs[0].shape[1:]), xs[0].dtype),
        scratch_shapes=[
            pltpu.SemaphoreType.DMA((2, (NF - 1) * len(xs))),
            pltpu.SemaphoreType.DMA((len(xs),)),
        ],
        compiler_params=pltpu.CompilerParams(collective_id=cid, has_side_effects=True),
        cost_estimate=cost(25, 10),
    )(*xs)


def final_kernel(
    tensor, g_ref, wrg_ref, cvg_ref, resg_ref, nmg_ref, nag_ref, out_ref, small_ref, zf, zs, zr, sbuf, srecv, *scratch
):
    here = lax.axis_index("tensor")
    me = lax.axis_index("dp")
    k, d, _ = g_ref.shape
    r, f = out_ref.shape[1:]
    zsems, ssems = scratch[10], scratch[11]
    red = Reduce8(lambda s: g_ref.at[:, pl.ds(pl.multiple_of(s * r, r), r), :], scratch[:8], *scratch[8:10])
    red.load()
    sbuf[0] = jnp.zeros_like(sbuf[0])
    sbuf[0, 0:24, :] = wrg_ref[0:24, :]
    sbuf[0, 24:32, :] = cvg_ref[0:8, :]
    sbuf[0, 32:33, :] = nmg_ref[...]
    sbuf[0, 33:34, :] = nag_ref[...]
    sbuf[0, 40:56, 0:LANES] = resg_ref[0:16, :]
    greet(near_peers() + far_peers(tensor))
    red.begin()
    rounds = [remote(sbuf.at[n], srecv.at[n], ssems, n, "dp", flip(me, m)) for n, m in enumerate((1, 2, 4))]
    rounds[0].start()
    red.first()
    rounds[0].wait_recv()
    sbuf[1] = sbuf[0] + srecv[0]
    rounds[1].start()
    red.second()
    rounds[1].wait_recv()
    sbuf[2] = sbuf[1] + srecv[1]
    rounds[2].start()
    red.third()
    rounds[2].wait_recv()
    sbuf[3] = sbuf[2] + srecv[2]
    far = [
        remote(sbuf.at[3], srecv.at[3 + here], ssems, 3 + n, axis, peer)
        for n, (axis, peer) in enumerate(far_peers(tensor))
    ]
    for c in far:
        c.start()

    def write(part, total):
        for t in range(tensor):
            zf[t, part] = total[:, :, t * f : (t + 1) * f]
            zs[t, part] = total[:, :, t * f : (t + 1) * f].astype(bf16)

    red.end(write)
    out_copies = [
        remote(zs.at[peer], zr.at[here], zsems, n, axis, peer) for n, (axis, peer) in enumerate(far_peers(tensor))
    ]
    for c in out_copies:
        c.start()
    srecv[3 + here] = sbuf[3]
    for c in far:
        c.wait_recv()
    total = srecv[3]
    for t in range(1, tensor):
        total = total + srecv[3 + t]
    small_ref[...] = total
    zr[here] = jnp.zeros(zr.shape[1:], bf16)
    for c in out_copies:
        c.wait_recv()
    total = zf[here]
    for t in range(tensor):
        total = total + zr[t].astype(f32)
    out_ref[...] = total
    red.close()
    for c in rounds + far + out_copies:
        c.wait_send()


def finish(g, wrg, cvg, resg, nmg, nag, tensor, cid):
    k, d, columns = g.shape
    r, f = d // NF, columns // tensor
    return pl.pallas_call(
        functools.partial(final_kernel, tensor),
        in_specs=[ANY] + [VM] * 5,
        out_specs=[VM] * 2,
        out_shape=(shape((k, r, f), f32), shape((56, d), f32)),
        scratch_shapes=[
            pltpu.VMEM((tensor, k, r, f), f32),
            pltpu.VMEM((tensor, k, r, f), bf16),
            pltpu.VMEM((tensor, k, r, f), bf16),
            pltpu.VMEM((4, 56, d), f32),
            pltpu.VMEM((3 + tensor, 56, d), f32),
            *reduce_scratch((k, r, columns)),
            pltpu.SemaphoreType.DMA((2, tensor - 1)),
            pltpu.SemaphoreType.DMA((2, 2 + tensor)),
        ],
        compiler_params=pltpu.CompilerParams(collective_id=cid, has_side_effects=True, vmem_limit_bytes=60 << 20),
        cost_estimate=cost(30, 10),
    )(g, wrg, cvg, resg, nmg, nag)


def fwd_kernel(
    starts_ref, tok_ref, prior_ref, ids_ref, ranks_ref, ga_ref, gm_ref, cos_ref, sin_ref, w_ref, wr_ref, wres_ref, cv_ref,
    og_ref,
    q_ref, k_ref, v_ref, mixed_ref, lse_ref, nattn_ref, resid_ref, nmoe_ref, base_ref, aux_ref, pay_ref, yall_ref,
    bias_ref, sems, own_sem,
):
    greet(near_peers())
    half = og_ref.shape[0] // 2
    spread = Gather8(
        lambda h: og_ref if h is None else og_ref.at[pl.ds(h * half, half)], halves(yall_ref, 0, og_ref.shape[0]), sems, own_sem
    )
    spread.begin()
    d = tok_ref.shape[1]
    pairs = d // LANES
    ntile = SEQ // QT
    ga, gm = ga_ref[...], gm_ref[...]
    mask_a, mask_b = head_masks()
    mask16 = (mask_a.astype(bf16), mask_b.astype(bf16))

    def project(i, carry):
        rows = pl.ds(pl.multiple_of(i * QT, QT), QT)
        x = tok_ref[rows, :].astype(f32)
        r1 = lax.rsqrt(jnp.mean(x * x, axis=-1, keepdims=True) + EPS)
        n = (x * r1 * ga).astype(bf16)
        nattn_ref[rows, :] = n
        cosine, sine = cos_ref[rows, :], sin_ref[rows, :]
        for c, out in ((0, q_ref), (1, k_ref), (2, v_ref)):
            proj = nn(n, w_ref[c])
            for p in range(pairs):
                part = proj[:, p * LANES : (p + 1) * LANES]
                if c < 2:
                    part = rot(part, cosine, sine)
                part = part.astype(bf16)
                if c == 0:
                    part = part * jnp.array(HD**-0.5, bf16)
                out[rows, p * LANES : (p + 1) * LANES] = part
        return carry

    lax.fori_loop(0, ntile, project, 0)

    taken = jnp.zeros((1, LANES), f32)
    lower = jnp.where(
        lax.broadcasted_iota(i32, (QT, QT), 1) < lax.broadcasted_iota(i32, (QT, QT), 0), 1.0, 0.0
    ).astype(bf16)
    lane = lanes(QT)
    for i in range(ntile):
        lo = i * QT
        width = min(SEQ, lo + 2 * QT) - lo
        rows = pl.ds(lo, QT)
        bias_ref[:, :width] = window_bias(starts_ref, i, width, False)

        def pair(p, lse):
            cols = pl.ds(pl.multiple_of(p * LANES, LANES), LANES)
            q2 = q_ref[rows, cols]
            outs = []
            for h in range(2):
                qh = q2 * mask16[h]
                sb = nt(qh, k_ref[lo : lo + width, cols]) + bias_ref[:, :width]
                m = jnp.max(sb, axis=-1, keepdims=True)
                if lo:
                    sa = nt(qh, k_ref[0:lo, cols])
                    m = jnp.maximum(m, jnp.max(sa, axis=-1, keepdims=True))
                pb = jnp.exp(sb - m)
                total = jnp.sum(pb, axis=-1, keepdims=True)
                acc = nn(pb.astype(bf16), v_ref[lo : lo + width, cols])
                if lo:
                    pa = jnp.exp(sa - m)
                    total = total + jnp.sum(pa, axis=-1, keepdims=True)
                    acc = acc + nn(pa.astype(bf16), v_ref[0:lo, cols])
                outs.append(acc / total)
                lse = jnp.where(lane == 2 * p + h, m + jnp.log(total), lse)
            mixed_ref[rows, cols] = (outs[0] * mask_a + outs[1] * mask_b).astype(bf16)
            return lse

        lse = lax.fori_loop(0, pairs, pair, jnp.zeros((QT, LANES), f32))
        lse_ref[:, rows] = lse.T[0 : lse_ref.shape[0], :]

        x = tok_ref[rows, :].astype(f32)
        resid = x + nt(mixed_ref[rows, :], w_ref[3])
        resid_ref[rows, :] = resid
        r2 = lax.rsqrt(jnp.mean(resid * resid, axis=-1, keepdims=True) + EPS)
        nm = (resid * r2 * gm).astype(bf16)
        nmoe_ref[rows, :] = nm
        raw = nn(nm, wr_ref[...])
        logits = raw + nn(prior_ref[rows, :], wres_ref[...])
        logits = jnp.where(lane < NF + 2 + NC, logits, -1e30)
        e = jnp.exp(logits - jnp.max(logits, axis=-1, keepdims=True))
        shares = e / jnp.sum(e, axis=-1, keepdims=True)
        id0, id1 = ids_ref[rows, 0:1], ids_ref[rows, 1:2]
        rk0, rk1 = ranks_ref[rows, 0:1], ranks_ref[rows, 1:2]
        hit0, hit1 = jnp.where(lane == id0, 1.0, 0.0), jnp.where(lane == id1, 1.0, 0.0)
        gates = shares * (hit0 + hit1)
        keep0, keep1 = jnp.where(rk0 < CAP, 1.0, 0.0), jnp.where(rk1 < CAP, 1.0, 0.0)
        kept = (hit0 * keep0 + hit1 * keep1) * jnp.where(lane < NF, 1.0, 0.0)
        pos = nn(lower, kept.astype(bf16)) + taken
        taken = taken + jnp.sum(kept, axis=0, keepdims=True)
        pay_ref[0:NF, rows] = jnp.where(kept > 0, shares, -1.0).T[0:NF, :]
        pay_ref[NF : 2 * NF, rows] = jnp.where(kept > 0, pos, -1.0).T[0:NF, :]
        nv = nm.astype(f32)
        aux = jnp.where(lane < NF + 2 + NC, shares, 0.0)
        direct = gates[:, NF + 1 : NF + 2]
        others = None
        for c in range(NC):
            z0, z1 = raw[:, Z0 + 2 * c : Z0 + 2 * c + 1], raw[:, Z0 + 2 * c + 1 : Z0 + 2 * c + 2]
            m0, m1 = 1.0 / (1.0 + jnp.exp(z1 - z0)), 1.0 / (1.0 + jnp.exp(z0 - z1))
            aux = jnp.where(lane == Z0 + 2 * c, m0, aux)
            aux = jnp.where(lane == Z0 + 2 * c + 1, m1, aux)
            w = gates[:, NF + 2 + c : NF + 3 + c]
            direct = direct + w * m0
            term = (w * m1) * cv_ref[c : c + 1, :]
            others = term if others is None else others + term
        aux_ref[rows, :] = aux
        base_ref[rows, :] = resid + direct * nv + others
        stages = (spread.forward, spread.share, spread.last, spread.end)
        if ntile == len(stages):
            stages[i]()
        elif i == ntile - 1:
            for stage in stages:
                stage()


def mid_kernel(
    dx_ref, gg_ref, og_ref, nmoe_ref, resid_ref, ids_ref, aux_ref, prior_ref, wr_ref, wres_ref, cv_ref, gm_ref,
    gmo_ref, gres_ref, pgrad_ref, nmg_ref, wrg_ref, resg_ref, cvg_ref,
):
    gm = gm_ref[...]
    lane = lanes(QT)
    nmg_ref[...] = jnp.zeros_like(nmg_ref)
    wrg_ref[...] = jnp.zeros_like(wrg_ref)
    resg_ref[...] = jnp.zeros_like(resg_ref)
    cvg_ref[...] = jnp.zeros_like(cvg_ref)

    def tile(i, carry):
        rows = pl.ds(pl.multiple_of(i * QT, QT), QT)
        g16, n16 = og_ref[rows, :], nmoe_ref[rows, :]
        g, nv = g16.astype(f32), n16.astype(f32)
        x = resid_ref[rows, :]
        r2 = lax.rsqrt(jnp.mean(x * x, axis=-1, keepdims=True) + EPS)
        aux = aux_ref[rows, :]
        shares = jnp.where(lane < NF + 2 + NC, aux, 0.0)
        id0, id1 = ids_ref[rows, 0:1], ids_ref[rows, 1:2]
        chosen = jnp.where(lane == id0, 1.0, 0.0) + jnp.where(lane == id1, 1.0, 0.0)
        gates = shares * chosen
        copy_inner = jnp.sum(g * nv, axis=-1, keepdims=True)
        inner = jnp.where(lane < NF, gg_ref[rows, :], 0.0)
        inner = jnp.where(lane == NF + 1, copy_inner, inner)
        direct = gates[:, NF + 1 : NF + 2]
        blend = jnp.zeros((QT, LANES), f32)
        cvw = jnp.zeros((QT, LANES), f32)
        for c in range(NC):
            m0, m1 = aux[:, Z0 + 2 * c : Z0 + 2 * c + 1], aux[:, Z0 + 2 * c + 1 : Z0 + 2 * c + 2]
            v_inner = jnp.sum(g * cv_ref[c : c + 1, :], axis=-1, keepdims=True)
            mean = m0 * copy_inner + m1 * v_inner
            inner = jnp.where(lane == NF + 2 + c, mean, inner)
            w = gates[:, NF + 2 + c : NF + 3 + c]
            direct = direct + w * m0
            blend = jnp.where(lane == Z0 + 2 * c, m0 * (w * copy_inner - w * mean), blend)
            blend = jnp.where(lane == Z0 + 2 * c + 1, m1 * (w * v_inner - w * mean), blend)
            cvw = jnp.where(lane == c, w * m1, cvw)
        grad_router = inner * chosen
        glog = shares * (grad_router - jnp.sum(shares * grad_router, axis=-1, keepdims=True))
        both_hi, both_lo = split(glog + blend)
        log_hi, log_lo = split(glog)
        cv_hi, cv_lo = split(cvw)
        pgrad_ref[rows, :] = nt(log_hi, wres_ref[...]) + nt(log_lo, wres_ref[...])
        wrg_ref[...] += tn(both_hi, n16) + tn(both_lo, n16)
        resg_ref[...] += tn(prior_ref[rows, :], log_hi) + tn(prior_ref[rows, :], log_lo)
        cvg_ref[...] += tn(cv_hi, g16) + tn(cv_lo, g16)
        gmi = dx_ref[rows, :].astype(f32) + direct * g + nt(both_hi, wr_ref[...]) + nt(both_lo, wr_ref[...])
        nmg_ref[...] += jnp.sum(gmi * x * r2, axis=0, keepdims=True)
        scaled = gmi * gm
        avg = jnp.mean(scaled * x, axis=-1, keepdims=True)
        gres = g + r2 * scaled - x * (r2 * r2 * r2 * avg)
        gres_ref[rows, :] = gres
        gmo_ref[rows, :] = gres.astype(bf16)
        return carry

    lax.fori_loop(0, SEQ // QT, tile, 0)


def bwd_kernel(
    starts_ref, gmo_ref, gres_ref, mixed_ref, q_ref, k_ref, v_ref, lse_ref, nattn_ref, tok_ref, ga_ref, cos_ref,
    sin_ref, w_ref,
    igrad_ref, wg_ref, nag_ref,
    do_ref, delta_ref, bias_ref, gp_ref, dk_ref, dv_ref, dq_ref,
):
    d = tok_ref.shape[1]
    pairs = d // LANES
    ntile = SEQ // QT
    ga = ga_ref[...]
    mask_a, mask_b = head_masks()
    mask16 = (mask_a.astype(bf16), mask_b.astype(bf16))
    maskf = (mask_a, mask_b)
    heads = delta_ref.shape[0]
    pick = jnp.where(
        lax.broadcasted_iota(i32, (heads, d), 1) // HD == lax.broadcasted_iota(i32, (heads, d), 0), 1.0, 0.0
    ).astype(bf16)

    def start(i, carry):
        rows = pl.ds(pl.multiple_of(i * QT, QT), QT)
        do = nn(gmo_ref[rows, :], w_ref[3]).astype(bf16)
        do_ref[rows, :] = do
        hi, lo = split(do.astype(f32) * mixed_ref[rows, :].astype(f32))
        delta_ref[:, rows] = nt(pick, hi) + nt(pick, lo)
        return carry

    lax.fori_loop(0, ntile, start, 0)
    wg_ref[3] = tn(gmo_ref[...], mixed_ref[...]).astype(wg_ref.dtype)
    for i in range(ntile):
        width = min(SEQ, (i + 2) * QT) - i * QT
        bias_ref[i, 0:width, :] = window_bias(starts_ref, i, width, True)

    def pair(p, carry):
        cols = pl.ds(pl.multiple_of(p * LANES, LANES), LANES)
        dk_ref[...] = jnp.zeros_like(dk_ref)
        dv_ref[...] = jnp.zeros_like(dv_ref)
        for i in range(ntile):
            lo = i * QT
            width = min(SEQ, lo + 2 * QT) - lo
            rows = pl.ds(lo, QT)
            q2, do2 = q_ref[rows, cols], do_ref[rows, cols]
            dq = jnp.zeros((QT, LANES), f32)
            for h in range(2):
                qh, doh = q2 * mask16[h], do2 * mask16[h]
                lse, delta = lse_ref[pl.ds(2 * p + h, 1), rows], delta_ref[pl.ds(2 * p + h, 1), rows]
                spans = [(lo, width, True)] + ([(0, lo, False)] if lo else [])
                for at, size, masked in spans:
                    k2 = k_ref[at : at + size, cols]
                    s = nt(k2, qh)
                    if masked:
                        s = s + bias_ref[i, 0:size, :]
                    prob = jnp.exp(s - lse)
                    ds = (prob * (nt(v_ref[at : at + size, cols], doh) - delta)).astype(bf16)
                    dv_ref[at : at + size, :] += nn(prob.astype(bf16), doh)
                    dk_ref[at : at + size, :] += nn(ds, qh)
                    dq = dq + tn(ds, k2) * maskf[h]
            dq_ref[rows, :] = dq * HD**-0.5
        cosine, sine = cos_ref[...], -sin_ref[...]
        gp_ref[0, :, cols] = rot(dq_ref[...], cosine, sine).astype(bf16)
        gp_ref[1, :, cols] = rot(dk_ref[...], cosine, sine).astype(bf16)
        gp_ref[2, :, cols] = dv_ref[...].astype(bf16)
        return carry

    lax.fori_loop(0, pairs, pair, 0)
    for c in range(3):
        wg_ref[c] = tn(nattn_ref[...], gp_ref[c]).astype(wg_ref.dtype)
    nag_ref[...] = jnp.zeros_like(nag_ref)

    def finish(i, carry):
        rows = pl.ds(pl.multiple_of(i * QT, QT), QT)
        gai = nt(gp_ref[0, rows, :], w_ref[0]) + nt(gp_ref[1, rows, :], w_ref[1])
        gai = gai + nt(gp_ref[2, rows, :], w_ref[2])
        x = tok_ref[rows, :].astype(f32)
        r1 = lax.rsqrt(jnp.mean(x * x, axis=-1, keepdims=True) + EPS)
        nag_ref[...] += jnp.sum(gai * x * r1, axis=0, keepdims=True)
        scaled = gai * ga
        avg = jnp.mean(scaled * x, axis=-1, keepdims=True)
        igrad_ref[rows, :] = gres_ref[rows, :] + r1 * scaled - x * (r1 * r1 * r1 * avg)
        return carry

    lax.fori_loop(0, ntile, finish, 0)


def pack_kernel(
    meta_ref, pos_ref, gate_ref, x_ref, y_ref, xc_ref, yc_ref, gc_ref, xs, ys, gs, sems,
):
    g = pl.program_id(0)
    off, count = meta_ref[g], meta_ref[NF + 1 + g]
    pos, gate = pos_ref[0], gate_ref[0]
    group = pos.shape[1]

    def window(j, carry):
        at = pl.multiple_of(off + j * WIN, 16)
        slot = (lax.broadcasted_iota(i32, (WIN, group), 0) + j * WIN).astype(f32)
        hot = jnp.where(slot == pos, 1.0, 0.0)
        h16 = hot.astype(bf16)
        xs[pl.ds(at, WIN), :] = nn(h16, x_ref[0]).astype(bf16)
        ys[pl.ds(at, WIN), :] = nn(h16, y_ref[0]).astype(bf16)
        gs[pl.ds(at, WIN), :] = jnp.broadcast_to(jnp.sum(hot * gate, axis=1, keepdims=True), (WIN, LANES))
        return carry

    lax.fori_loop(0, (count + WIN - 1) // WIN, window, 0)

    @pl.when(g == NF - 1)
    def _():
        at = pl.multiple_of(meta_ref[NF], 16)
        for k in range(TM // WIN):
            xs[pl.ds(at + k * WIN, WIN), :] = jnp.zeros((WIN, xs.shape[1]), bf16)
            ys[pl.ds(at + k * WIN, WIN), :] = jnp.zeros((WIN, ys.shape[1]), bf16)
            gs[pl.ds(at + k * WIN, WIN), :] = jnp.zeros((WIN, LANES), f32)
        tiles = meta_ref[2 * NF + 1]

        def copies(t):
            rows = pl.ds(pl.multiple_of(t * TM, TM), TM)
            return [
                pltpu.make_async_copy(src.at[rows, :], dst.at[rows, :], sems.at[n, t])
                for n, (src, dst) in enumerate(((xs, xc_ref), (ys, yc_ref), (gs, gc_ref)))
            ]

        def begin(t, carry):
            for c in copies(t):
                c.start()
            return carry

        def end(t, carry):
            for c in copies(t):
                c.wait()
            return carry

        lax.fori_loop(0, tiles, begin, 0)
        lax.fori_loop(0, tiles, end, 0)


def ffn_kernel(meta_ref, x_ref, y_ref, gc_ref, w_ref, out_ref, dx_ref, gg_ref, dw_ref, acc):
    i = pl.program_id(0)

    @pl.when(i == 0)
    def _():
        acc[...] = jnp.zeros_like(acc)

    @pl.when(i < meta_ref[2 * NF + 1])
    def _():
        x = x_ref[...]
        gate = gc_ref[:, 0:1]
        dy = y_ref[...].astype(f32)
        ge = (gate * dy).astype(bf16)
        rows, d = x.shape
        x_t, ge_t = x.T, ge.T

        def chunk(c, carry):
            eo, dx = carry
            wg, wu, wd = w_ref[c, 0], w_ref[c, 1], w_ref[c, 2]
            gv, uv = nn(x, wg), nn(x, wu)
            gh = nn(ge, wd)
            sig = 1.0 / (1.0 + jnp.exp(-gv))
            act = gv * sig
            hid = (act * uv).astype(bf16)
            eo = eo + nt(hid, wd)
            gg = (gh * uv * (sig * (1.0 + gv * (1.0 - sig)))).astype(bf16)
            gu = (gh * act).astype(bf16)
            dx = dx + nt(gg, wg) + nt(gu, wu)
            acc[c, 0] += nn(x_t, gg)
            acc[c, 1] += nn(x_t, gu)
            acc[c, 2] += nn(ge_t, hid)
            return eo, dx

        zero = jnp.zeros((rows, d), f32)
        eo, dx = lax.fori_loop(0, w_ref.shape[0], chunk, (zero, zero))
        out_ref[...] = (gate * eo).astype(bf16)
        dx_ref[...] = dx.astype(bf16)
        gg_ref[...] = jnp.broadcast_to(jnp.sum(dy * eo, axis=1, keepdims=True), gg_ref.shape)

    @pl.when(i == pl.num_programs(0) - 1)
    def _():
        dw_ref[...] = acc[...].astype(bf16)


def unpack_kernel(
    meta_ref, pos_ref, yc_ref, dxc_ref, ggc_ref, out_ref, dx_ref, gg_ref, ys, xs, gs, sems,
):
    g = pl.program_id(0)
    off, count = meta_ref[g], meta_ref[NF + 1 + g]

    @pl.when(g == 0)
    def _():
        tiles = meta_ref[2 * NF + 1]

        def copies(t):
            rows = pl.ds(pl.multiple_of(t * TM, TM), TM)
            return [
                pltpu.make_async_copy(src.at[rows, :], dst.at[rows, :], sems.at[n, t])
                for n, (src, dst) in enumerate(((yc_ref, ys), (dxc_ref, xs), (ggc_ref, gs)))
            ]

        def begin(t, carry):
            for c in copies(t):
                c.start()
            return carry

        def end(t, carry):
            for c in copies(t):
                c.wait()
            return carry

        lax.fori_loop(0, tiles, begin, 0)
        lax.fori_loop(0, tiles, end, 0)

    pos = pos_ref[0]
    group = pos.shape[1]
    d = ys.shape[1]

    def window(j, first):
        at = pl.multiple_of(off + j * WIN, 16)
        index = lax.broadcasted_iota(i32, (WIN, group), 0) + j * WIN
        hot = jnp.where(index.astype(f32) == pos, 1.0, 0.0)
        h16 = hot.astype(bf16)
        live = lax.broadcasted_iota(i32, (WIN, d), 0) + j * WIN < count
        yv = jnp.where(live, ys[pl.ds(at, WIN), :].astype(f32), 0.0).astype(bf16)
        xv = jnp.where(live, xs[pl.ds(at, WIN), :].astype(f32), 0.0).astype(bf16)
        gv = jnp.where(live[:, 0:1], gs[pl.ds(at, WIN), 0:1], 0.0)
        py, px = tn(h16, yv).astype(bf16), tn(h16, xv).astype(bf16)
        pg = jnp.sum(hot * gv, axis=0, keepdims=True)
        if first:
            out_ref[0], dx_ref[0], gg_ref[0] = py, px, pg
        else:
            out_ref[0] += py
            dx_ref[0] += px
            gg_ref[0] += pg

    window(0, True)

    def more(j, carry):
        window(j, False)
        return carry

    lax.fori_loop(1, (count + WIN - 1) // WIN, more, 0)


def shape(dims, dtype):
    return jax.ShapeDtypeStruct(dims, dtype)


def cost(gflop, mbytes, mexp=0):
    return pl.CostEstimate(flops=int(gflop * 1e9), bytes_accessed=int(mbytes * 1e6), transcendentals=int(mexp * 1e6))


def experts(x_all, y_all, pos, gate, w_all):
    groups, group, d = x_all.shape
    count = (jnp.max(pos, axis=1) + 1.0).astype(i32)
    padded = (count + 15) // 16 * 16
    order = jnp.arange(NF)
    ends = jnp.sum(jnp.where(order[None, :] <= order[:, None], padded[None, :], 0), axis=1)
    tiles = jnp.maximum((ends[-1:] + TM - 1) // TM, 1)
    meta = jnp.concatenate([jnp.zeros((1,), i32), ends, count, tiles])
    room = NF * min(CAP, group) + TM + WIN
    room = (room + TM - 1) // TM * TM
    most = room // TM
    pos3, gate3 = pos.reshape(groups, 1, group), gate.reshape(groups, 1, group)
    params = pltpu.CompilerParams(vmem_limit_bytes=60 << 20, dimension_semantics=("arbitrary",))
    row_spec = pl.BlockSpec((1, 1, group), lambda g, *_: (g, 0, 0))
    tok_spec = pl.BlockSpec((1, group, d), lambda g, *_: (g, 0, 0))
    scratch = [
        pltpu.VMEM((room, d), bf16),
        pltpu.VMEM((room, d), bf16),
        pltpu.VMEM((room, LANES), f32),
        pltpu.SemaphoreType.DMA((3, most)),
    ]
    xc, yc, gc = pl.pallas_call(
        pack_kernel,
        out_shape=(shape((room, d), bf16), shape((room, d), bf16), shape((room, LANES), f32)),
        grid_spec=pltpu.PrefetchScalarGridSpec(
            num_scalar_prefetch=1,
            grid=(groups,),
            in_specs=[row_spec, row_spec, tok_spec, tok_spec],
            out_specs=(ANY, ANY, ANY),
            scratch_shapes=scratch,
        ),
        compiler_params=params,
        cost_estimate=cost(8, 30),
    )(meta, pos3, gate3, x_all, y_all)
    tile = lambda i, m: (jnp.minimum(i, m[2 * NF + 1] - 1), 0)
    zero4 = lambda i, m: (0, 0, 0, 0)
    out_c, dx_c, gg_c, dw = pl.pallas_call(
        ffn_kernel,
        out_shape=(
            shape((room, d), bf16), shape((room, d), bf16), shape((room, LANES), f32), shape(w_all.shape, bf16),
        ),
        grid_spec=pltpu.PrefetchScalarGridSpec(
            num_scalar_prefetch=1,
            grid=(most,),
            in_specs=[
                pl.BlockSpec((TM, d), tile),
                pl.BlockSpec((TM, d), tile),
                pl.BlockSpec((TM, LANES), tile),
                pl.BlockSpec(w_all.shape, zero4, pipeline_mode=pl.Buffered(1)),
            ],
            out_specs=(
                pl.BlockSpec((TM, d), tile),
                pl.BlockSpec((TM, d), tile),
                pl.BlockSpec((TM, LANES), tile),
                pl.BlockSpec(w_all.shape, zero4, pipeline_mode=pl.Buffered(1)),
            ),
            scratch_shapes=[pltpu.VMEM(w_all.shape, f32)],
        ),
        compiler_params=params,
        cost_estimate=cost(44, 30),
    )(meta, xc, yc, gc, w_all)
    out, dx, gg = pl.pallas_call(
        unpack_kernel,
        out_shape=(
            shape((groups, group, d), bf16), shape((groups, group, d), bf16), shape((groups, 1, group), f32),
        ),
        grid_spec=pltpu.PrefetchScalarGridSpec(
            num_scalar_prefetch=1,
            grid=(groups,),
            in_specs=[row_spec, ANY, ANY, ANY],
            out_specs=(tok_spec, tok_spec, row_spec),
            scratch_shapes=scratch,
        ),
        compiler_params=params,
        cost_estimate=cost(8, 30),
    )(meta, pos3, out_c, dx_c, gg_c)
    return out, dx, gg, dw


def on_device(
    dp,
    tensor,
    tokens,
    prior_logits,
    expert_ids,
    expert_ranks,
    piece_starts,
    norm_attn,
    qkv_weight,
    out_weight,
    norm_moe,
    router_weight,
    residual_weight,
    const_vectors,
    const_gates,
    w_gate_up,
    w_down,
    out_grad,
):
    rows, d = tokens.shape
    ne = router_weight.shape[1]
    packs = dp // NF
    groups = None if packs == 1 else [list(range(NF * r, NF * (r + 1))) for r in range(packs)]
    across = None if packs == 1 else [list(range(j, dp, NF)) for j in range(NF)]
    here = lax.axis_index("tensor")
    ids = lax.dynamic_slice_in_dim(expert_ids, here * rows, rows, 0)
    ranks = lax.dynamic_slice_in_dim(expert_ranks, here * rows, rows, 0)
    starts = lax.dynamic_slice_in_dim(piece_starts, here, 1, 0)
    ga, gm = norm_attn.astype(f32).reshape(1, d), norm_moe.astype(f32).reshape(1, d)
    cosine, sine = (jnp.asarray(t) for t in rotary_tables())
    prior = jnp.pad(prior_logits, ((0, 0), (0, LANES - ne)))
    wr = jnp.concatenate(
        [router_weight, jnp.zeros((d, Z0 - ne), bf16), const_gates.reshape(2 * NC, d).T,
         jnp.zeros((d, LANES - Z0 - 2 * NC), bf16)], axis=1)
    wres = jnp.pad(residual_weight, ((0, LANES - ne), (0, LANES - ne)))
    cv = const_vectors.astype(f32)

    w_attn = jnp.concatenate([qkv_weight, out_weight.T[None]], axis=0)
    w_down_t = w_down.transpose(0, 2, 1)[None]
    shard = w_down.shape[1]
    w_mine = exchange8([w_gate_up, w_down_t], 1)
    w_mine = w_mine.reshape(3, -1, shard)
    if packs > 1:
        w_mine = lax.all_gather(w_mine, "dp", axis=1, tiled=True, axis_index_groups=across)
    w_all = lax.all_gather(w_mine, "tensor", axis=0, tiled=False)
    if packs > 1:
        w_attn = lax.all_gather(w_attn, "tensor", axis=2, tiled=True)
        w_attn = lax.all_gather(w_attn, "dp", axis=1, tiled=True)
    else:
        w_attn = gather_weights(w_attn, tensor, 2)

    heads = 16
    q, k, v, mixed, lse, nattn, resid, nmoe, base, aux, pay, y_all = pl.pallas_call(
        fwd_kernel,
        in_specs=[SM] + [VM] * 12 + [ANY],
        out_specs=[VM] * 11 + [ANY],
        out_shape=(
            shape((rows, d), bf16), shape((rows, d), bf16), shape((rows, d), bf16), shape((rows, d), bf16),
            shape((heads, rows), f32), shape((rows, d), bf16), shape((rows, d), f32), shape((rows, d), bf16),
            shape((rows, d), f32), shape((rows, LANES), f32), shape((2 * NF, rows), f32), shape((NF, rows, d), bf16),
        ),
        scratch_shapes=[
            pltpu.VMEM((QT, 2 * QT), f32),
            pltpu.SemaphoreType.DMA((2, GATHER_COPIES)),
            pltpu.SemaphoreType.DMA,
        ],
        compiler_params=pltpu.CompilerParams(collective_id=3, has_side_effects=True, vmem_limit_bytes=60 << 20),
        cost_estimate=cost(40, 30, 10),
    )(starts, tokens, prior, ids, ranks, ga, gm, cosine, sine, w_attn, wr, wres, cv, out_grad)

    x_all = gather8(nmoe, 4)
    payload = pay.reshape(2, NF, rows).transpose(1, 0, 2)
    payload = lax.all_to_all(payload, "dp", 0, 0, tiled=True, axis_index_groups=groups)
    out_p, dx_p, gg_p, dw = experts(x_all, y_all, payload[:, 1], payload[:, 0], w_all)
    gg = lax.all_to_all(gg_p.reshape(NF, rows), "dp", 0, 0, tiled=True, axis_index_groups=groups)
    gg = jnp.pad(gg, ((0, LANES - NF), (0, 0))).T
    scatter = functools.partial(
        lax.psum_scatter, axis_name="dp", scatter_dimension=0, tiled=True, axis_index_groups=groups
    )
    dx = reduce8(dx_p, 5)
    ffn = scatter(out_p.reshape(NF * rows, d))
    layer_out = (base + ffn.astype(f32)).astype(bf16)

    dw_mine = lax.psum_scatter(dw, "tensor", scatter_dimension=0, tiled=False)
    if packs > 1:
        dw_mine = lax.psum_scatter(dw_mine, "dp", scatter_dimension=1, tiled=True, axis_index_groups=across)
    dw_mine = dw_mine.reshape(3, NF, -1, shard)
    dw_mine = exchange8([dw_mine], 6).astype(f32)
    gate_up_grad, down_grad = dw_mine[0:2], dw_mine[2].transpose(0, 2, 1)

    gmo, gres, pgrad, nmg, wrg, resg, cvg = pl.pallas_call(
        mid_kernel,
        in_specs=[VM] * 12,
        out_specs=[VM] * 7,
        out_shape=(
            shape((rows, d), bf16), shape((rows, d), f32), shape((rows, LANES), f32), shape((1, d), f32),
            shape((LANES, d), f32), shape((LANES, LANES), f32), shape((LANES, d), f32),
        ),
        compiler_params=pltpu.CompilerParams(vmem_limit_bytes=60 << 20),
        cost_estimate=cost(2, 20),
    )(dx, gg, out_grad, nmoe, resid, ids, aux, prior, wr, wres, cv, gm)
    igrad, wg, nag = pl.pallas_call(
        bwd_kernel,
        in_specs=[SM] + [VM] * 13,
        out_specs=[VM] * 3,
        out_shape=(shape((rows, d), f32), shape((4, d, d), bf16), shape((1, d), f32)),
        scratch_shapes=[
            pltpu.VMEM((rows, d), bf16),
            pltpu.VMEM((heads, rows), f32),
            pltpu.VMEM((rows // QT, 2 * QT, QT), f32),
            pltpu.VMEM((3, rows, d), bf16),
            pltpu.VMEM((rows, LANES), f32),
            pltpu.VMEM((rows, LANES), f32),
            pltpu.VMEM((rows, LANES), f32),
        ],
        compiler_params=pltpu.CompilerParams(vmem_limit_bytes=60 << 20),
        cost_estimate=cost(80, 40, 10),
    )(starts, gmo, gres, mixed, q, k, v, lse, nattn, tokens, ga, cosine, sine, w_attn)

    if packs > 1:
        wg = lax.psum_scatter(wg, "dp", scatter_dimension=1, tiled=True)
        wg = lax.psum_scatter(wg, "tensor", scatter_dimension=2, tiled=True).astype(f32)
        wrg, cvg, resg, nmg, nag = lax.psum((wrg, cvg, resg, nmg, nag), ("dp", "tensor"))
    else:
        wg, small = finish(wg, wrg, cvg, resg, nmg, nag, tensor, 7)
        wrg, cvg, resg, nmg, nag = small[0:24], small[24:32], small[40:56, 0:LANES], small[32], small[33]
    return (
        layer_out,
        igrad,
        pgrad[:, 0:ne],
        nag.reshape(d),
        wg[0:3],
        wg[3].T,
        nmg.reshape(d),
        wrg[0:ne].T,
        resg[0:ne, 0:ne],
        cvg[0:NC],
        wrg[Z0 : Z0 + 2 * NC].reshape(NC, 2, d),
        gate_up_grad,
        down_grad,
    )


def solution(mesh):
    body = functools.partial(on_device, mesh.shape["dp"], mesh.shape["tensor"])
    rows = P(("dp", "tensor"), None)
    return jax.shard_map(
        body,
        mesh=mesh,
        in_specs=(
            rows, rows, P("dp", None), P("dp", None), P("dp", None), P(), P(None, "dp", "tensor"), P("tensor", "dp"),
            P(), P(), P(), P(), P(), P(None, None, "dp", "tensor"), P(None, "tensor", "dp"), rows,
        ),
        out_specs=(
            rows, rows, rows, P(), P(None, "dp", "tensor"), P("tensor", "dp"), P(), P(), P(), P(), P(),
            P(None, None, "dp", "tensor"), P(None, "tensor", "dp"),
        ),
        check_vma=False,
    )
```

```python
import functools

import jax
import jax.numpy as jnp
import numpy as np
from jax import lax
from jax.experimental import pallas as pl
from jax.experimental.pallas import tpu as pltpu
from jax.sharding import PartitionSpec as P

HD = 64
NF = 8
NC = 2
SEQ = 1024
PIECE = 256
PIECES = 2
CAP = 768
EPS = 1e-06
QT = 256
LANES = 128
TM = 256
ROOM = 256
Z0 = 16

bf16 = jnp.bfloat16
f32 = jnp.float32
i32 = jnp.int32

VM = pl.BlockSpec(memory_space=pltpu.VMEM)
SM = pl.BlockSpec(memory_space=pltpu.SMEM)
ANY = pl.BlockSpec(memory_space=pl.ANY)


def nn(a, b):
    return lax.dot_general(a, b, (((1,), (0,)), ((), ())), preferred_element_type=f32)


def nt(a, b):
    return lax.dot_general(a, b, (((1,), (1,)), ((), ())), preferred_element_type=f32)


def tn(a, b):
    return lax.dot_general(a, b, (((0,), (0,)), ((), ())), preferred_element_type=f32)


def split(x):
    hi = x.astype(bf16)
    return hi, (x - hi.astype(f32)).astype(bf16)


def lanes(rows):
    return lax.broadcasted_iota(i32, (rows, LANES), 1)


def rot(x, cosine, sine):
    first = lanes(x.shape[0]) % HD < HD // 2
    other = jnp.where(first, pltpu.roll(x, LANES - HD // 2, 1), pltpu.roll(x, HD // 2, 1))
    return x * cosine + other * sine


def head_masks():
    low = lax.broadcasted_iota(i32, (1, LANES), 1) < HD
    a = jnp.where(low, 1.0, 0.0)
    return a, 1.0 - a


def rotary_tables():
    place = np.arange(SEQ, dtype=np.float32)
    half = HD // 2
    freqs = np.power(np.float32(10000.0), np.arange(half, dtype=np.float32) * np.float32(-2.0 / HD)).astype(np.float32)
    angles = (place[:, None] * freqs[None, :]).astype(np.float32).astype(np.float64)
    c, s = np.cos(angles).astype(np.float32), np.sin(angles).astype(np.float32)
    return np.concatenate([c, c, c, c], 1), np.concatenate([-s, s, -s, s], 1)


def window_bias(starts_ref, tile, width, transposed):
    shape = (width, QT) if transposed else (QT, width)
    qpos = lax.broadcasted_iota(i32, shape, 1 if transposed else 0) + tile * QT
    kpos = lax.broadcasted_iota(i32, shape, 0 if transposed else 1) + tile * QT
    seen = jnp.where(kpos <= qpos, 1, 0)
    for piece in range(PIECES):
        s = starts_ref[0, piece]
        both = jnp.where(qpos >= s, 1, 0) * jnp.where(qpos < s + PIECE, 1, 0)
        both = both * jnp.where(kpos >= s, 1, 0) * jnp.where(kpos < s + PIECE, 1, 0)
        seen = jnp.maximum(seen, both)
    return jnp.where(seen > 0, 0.0, -1e30)


MESH = pl.DeviceIdType.MESH
GATHER_COPIES = 13
REDUCE_COPIES = 10


def flip(index, m):
    for bit in (1, 2, 4):
        if m & bit:
            index = index + bit - 2 * bit * (index // bit % 2)
    return index


def remote(src, dst, sems, n, axis, peer):
    return pltpu.make_async_remote_copy(
        src_ref=src,
        dst_ref=dst,
        send_sem=sems.at[0, n],
        recv_sem=sems.at[1, n],
        device_id={axis: peer},
        device_id_type=MESH,
    )


def greet(peers):
    barrier = pltpu.get_barrier_semaphore()
    for axis, peer in peers:
        pl.semaphore_signal(barrier, inc=1, device_id={axis: peer}, device_id_type=MESH)
    pl.semaphore_wait(barrier, len(peers))


def near_peers():
    me = lax.axis_index("dp")
    return [("dp", flip(me, m)) for m in (1, 2, 4)]


def far_peers(tensor):
    me = lax.axis_index("tensor")
    return [("tensor", (me + k) % tensor) for k in range(1, tensor)]


class Gather8:
    def __init__(self, src, dst, sems, own_sem):
        me = lax.axis_index("dp")
        slot = me % NF
        nx, ny, nc = flip(me, 2), flip(me, 4), flip(me, 1)
        sx, sy, sd = flip(slot, 2), flip(slot, 4), flip(slot, 6)
        self.own = pltpu.make_async_copy(src(None), dst(slot, None), own_sem)
        go = lambda n, s, d, peer: remote(s, d, sems, n, "dp", peer)
        on = lambda n, s, h, peer: go(n, dst(s, h), dst(s, h), peer)
        self.c = [
            go(0, src(0), dst(slot, 0), nx),
            go(1, src(1), dst(slot, 1), ny),
            go(2, src(1), dst(slot, 1), nx),
            go(3, src(0), dst(slot, 0), ny),
            go(4, src(None), dst(slot, None), nc),
            on(5, sx, 0, ny),
            on(6, sy, 1, nx),
            on(7, sx, 0, nc),
            on(8, sy, 1, nc),
            on(9, sx, 1, nc),
            on(10, sy, 0, nc),
            on(11, sd, 0, nc),
            on(12, sd, 1, nc),
        ]

    def begin(self):
        self.own.start()
        for n in range(5):
            self.c[n].start()

    def forward(self):
        for got, out in ((0, (5, 7)), (1, (6, 8))):
            self.c[got].wait_recv()
            for n in out:
                self.c[n].start()

    def share(self):
        for got, out in ((2, 9), (3, 10)):
            self.c[got].wait_recv()
            self.c[out].start()

    def last(self):
        for got, out in ((5, 11), (6, 12)):
            self.c[got].wait_recv()
            self.c[out].start()

    def end(self):
        for n in (4, 7, 8, 9, 10, 11, 12):
            self.c[n].wait_recv()
        for c in self.c:
            c.wait_send()
        self.own.wait()


def halves(ref, index, rows):
    half = rows // 2
    return lambda s, h: ref.at[s] if h is None else ref.at[s, pl.ds(h * half, half)]


def all_peers():
    me = lax.axis_index("dp")
    return [("dp", flip(me, m)) for m in range(1, NF)]


class Swap8:
    def __init__(self, src, dst, sems, own_sems):
        me = lax.axis_index("dp")
        slot = me % NF
        count = src.shape[0] // NF
        self.own = [
            pltpu.make_async_copy(src.at[NF * i + slot], dst.at[NF * i + slot], own_sems.at[i]) for i in range(count)
        ]
        self.c = [
            remote(
                src.at[NF * i + flip(slot, m)], dst.at[NF * i + slot], sems, (m - 1) * count + i, "dp", flip(me, m)
            )
            for m in range(1, NF)
            for i in range(count)
        ]

    def begin(self):
        for c in self.own + self.c:
            c.start()

    def end(self):
        for c in self.c:
            c.wait_recv()
        for c in self.c:
            c.wait_send()
        for c in self.own:
            c.wait()


def weights_kernel(slab, gu_ref, dn_ref, out_ref, wx_ref, sems, own_sem, *scratch):
    k, r, _ = slab.shape
    greet(all_peers())
    part = lambda h: pl.ds(0, k) if h is None else pl.ds(h * (k // 2), k // 2)
    g = Gather8(
        lambda h: slab.at[part(h)],
        lambda s, h: out_ref.at[part(h), pl.ds(pl.multiple_of(s * r, r), r), :],
        sems,
        own_sem,
    )
    swap = Exchange8([gu_ref, dn_ref], wx_ref, 1, *scratch)
    g.begin()
    swap.begin()
    g.forward()
    g.share()
    g.last()
    g.end()
    swap.end()


def gather_weights(w, gate_up, down, cid):
    k, r, f = w.shape
    return pl.pallas_call(
        weights_kernel,
        in_specs=[ANY] * 3,
        out_specs=[ANY] * 2,
        out_shape=(shape((k, NF * r, f), w.dtype), half_shape(gate_up)),
        scratch_shapes=[
            pltpu.SemaphoreType.DMA((2, GATHER_COPIES)),
            pltpu.SemaphoreType.DMA,
            *exchange_scratch(2),
        ],
        compiler_params=pltpu.CompilerParams(collective_id=cid, has_side_effects=True),
        cost_estimate=cost(35, 10),
    )(w, gate_up, down)


def half_kernel(gu_ref, dn_ref, wx_ref, *scratch):
    greet(all_peers())
    swap = Exchange8([gu_ref, dn_ref], wx_ref, 1, *scratch)
    swap.begin()
    swap.end()


def exchange_half(gate_up, down, cid):
    return pl.pallas_call(
        half_kernel,
        in_specs=[ANY] * 2,
        out_specs=ANY,
        out_shape=half_shape(gate_up),
        scratch_shapes=exchange_scratch(2),
        compiler_params=pltpu.CompilerParams(collective_id=cid, has_side_effects=True),
        cost_estimate=cost(25, 10),
    )(gate_up, down)


class Reduce8:
    def __init__(self, view, bufs, sems, lsems):
        self.own, self.away, self.ind, self.inx, self.iny = bufs
        me = lax.axis_index("dp")
        slot = me % NF
        half = self.ind.shape[0] // 2
        a, b = pl.ds(0, half), pl.ds(half, half)
        self.a, self.b = a, b
        nx, ny, nc = flip(me, 2), flip(me, 4), flip(me, 1)
        mine = [flip(slot, m) for m in (6, 2, 4)] + [slot]
        self.loads = [pltpu.make_async_copy(view(s), self.own.at[n % 2], lsems.at[n]) for n, s in enumerate(mine)]
        self.over = [remote(view(flip(s, 1)), self.away.at[n], sems, n, "dp", nc) for n, s in enumerate(mine)]
        go = lambda n, k, i, part, peer: remote(self.away.at[k, part], i.at[part], sems, n, "dp", peer)
        self.da, self.db = go(4, 0, self.ind, a, nx), go(5, 0, self.ind, b, ny)
        self.xa, self.yb = go(6, 1, self.inx, a, nx), go(7, 2, self.iny, b, ny)
        self.ya, self.xb = go(8, 2, self.iny, a, ny), go(9, 1, self.inx, b, nx)

    def load(self):
        self.loads[0].start()
        self.loads[1].start()

    def begin(self):
        for c in self.over:
            c.start()

    def add(self, n, part):
        self.away[n, part] = (self.own[n % 2, part].astype(f32) + self.away[n, part].astype(f32)).astype(bf16)

    def more(self, n, part):
        self.away[n, part] = (self.away[n, part].astype(f32) + self.ind[part].astype(f32)).astype(bf16)

    def ready(self, n):
        self.loads[n].wait()
        self.over[n].wait_recv()

    def first(self):
        self.ready(0)
        self.add(0, self.a)
        self.da.start()
        self.add(0, self.b)
        self.db.start()
        self.loads[2].start()

    def second(self):
        self.ready(1)
        self.add(1, self.a)
        self.xa.start()
        self.add(1, self.b)
        self.loads[3].start()
        self.ready(2)
        self.add(2, self.b)
        self.yb.start()
        self.add(2, self.a)

    def third(self):
        self.da.wait_recv()
        self.more(2, self.a)
        self.ya.start()
        self.db.wait_recv()
        self.more(1, self.b)
        self.xb.start()

    def end(self, write):
        self.ready(3)
        for part, first, second in ((self.a, self.xa, self.ya), (self.b, self.yb, self.xb)):
            first.wait_recv()
            second.wait_recv()
            total = self.own[1, part].astype(f32) + self.away[3, part].astype(f32)
            write(part, total + self.inx[part].astype(f32) + self.iny[part].astype(f32))

    def close(self):
        for c in self.over + [self.da, self.db, self.xa, self.yb, self.ya, self.xb]:
            c.wait_send()


def reduce_scratch(block):
    return [pltpu.VMEM((2, *block), bf16), pltpu.VMEM((4, *block), bf16)] + [pltpu.VMEM(block, bf16)] * 3 + [
        pltpu.SemaphoreType.DMA((2, REDUCE_COPIES)),
        pltpu.SemaphoreType.DMA((4,)),
    ]


class Exchange8:
    def __init__(self, srcs, dst, part, sems, own_sems):
        me = lax.axis_index("dp")
        slot = me % NF
        width = dst.shape[-1]

        def piece(src, e):
            return src.at[:, e] if part is None else src.at[:, e, :, pl.ds(part * width, width)]

        at, pieces = 0, []
        for src in srcs:
            pieces.append((src, pl.ds(at, src.shape[0])))
            at += src.shape[0]
        self.own = [
            pltpu.make_async_copy(piece(src, slot), dst.at[rows, slot], own_sems.at[i])
            for i, (src, rows) in enumerate(pieces)
        ]
        self.c = [
            remote(
                piece(src, flip(slot, m)), dst.at[rows, slot], sems, (m - 1) * len(srcs) + i, "dp", flip(me, m)
            )
            for m in (6, 7, 2, 3, 4, 5, 1)
            for i, (src, rows) in enumerate(pieces)
        ]

    def begin(self):
        for c in self.c + self.own:
            c.start()

    def end(self):
        for c in self.c:
            c.wait_recv()
        for c in self.c:
            c.wait_send()
        for c in self.own:
            c.wait()


class Send8:
    order = (6, 7, 2, 3, 4, 5, 1)

    def __init__(self, src, dst, sems, own_sem, packed):
        me = lax.axis_index("dp")
        slot = me % NF
        at = lambda m: src.at[m] if packed else src.at[flip(slot, m)]
        self.slot = slot
        self.own = pltpu.make_async_copy(at(0), dst.at[slot], own_sem)
        self.c = {m: remote(at(m), dst.at[slot], sems, m - 1, "dp", flip(me, m)) for m in self.order}

    def start(self, m):
        (self.c[m] if m else self.own).start()

    def begin(self):
        for m in (*self.order, 0):
            self.start(m)

    def got(self, m):
        if m:
            self.c[m].wait_recv()
        else:
            self.own.wait()

    def close(self):
        for c in self.c.values():
            c.wait_send()


def send_scratch():
    return [pltpu.SemaphoreType.DMA((2, NF - 1)), pltpu.SemaphoreType.DMA]


def half_shape(gate_up):
    _, groups, r, f = gate_up.shape
    return shape((3, groups, r, f // 2), bf16)


def exchange_scratch(n):
    return [pltpu.SemaphoreType.DMA((2, (NF - 1) * n)), pltpu.SemaphoreType.DMA((n,))]


def prologue_kernel(tensor, gu_ref, dn_ref, w_ref, out_ref, slab_ref, zbuf, zsems, *scratch):
    here = lax.axis_index("tensor")
    k, _, f = w_ref.shape
    greet(all_peers() + far_peers(tensor))
    copies = [
        remote(w_ref, zbuf.at[here], zsems, n, axis, peer) for n, (axis, peer) in enumerate(far_peers(tensor))
    ]
    for c in copies:
        c.start()
    swap = Exchange8([gu_ref, dn_ref], out_ref, 0, *scratch)
    swap.begin()
    zbuf[here] = w_ref[...]
    for c in copies:
        c.wait_recv()
    for c in range(k):
        for t in range(0, tensor, 2):
            both = jnp.concatenate([zbuf[t, c].astype(f32), zbuf[t + 1, c].astype(f32)], axis=-1)
            slab_ref[c, :, t * f : (t + 2) * f] = both.astype(bf16)
    swap.end()
    for c in copies:
        c.wait_send()


def prologue(gate_up, down, w, tensor, cid):
    k, r, f = w.shape
    return pl.pallas_call(
        functools.partial(prologue_kernel, tensor),
        in_specs=[ANY, ANY, VM],
        out_specs=[ANY, VM],
        out_shape=(half_shape(gate_up), shape((k, r, tensor * f), bf16)),
        scratch_shapes=[
            pltpu.VMEM((tensor, k, r, f), bf16),
            pltpu.SemaphoreType.DMA((2, tensor - 1)),
            *exchange_scratch(2),
        ],
        compiler_params=pltpu.CompilerParams(collective_id=cid, has_side_effects=True),
        cost_estimate=cost(25, 10),
    )(gate_up, down, w)


def exchange_kernel(a_ref, b_ref, a_out, b_out, *scratch):
    greet(all_peers())
    swaps = [Exchange8([a_ref], a_out, None, *scratch[0:2]), Exchange8([b_ref], b_out, None, *scratch[2:4])]
    for swap in swaps:
        swap.begin()
    for swap in swaps:
        swap.end()


def exchange8(a, b, cid):
    return pl.pallas_call(
        exchange_kernel,
        in_specs=[ANY] * 2,
        out_specs=[ANY] * 2,
        out_shape=(shape(a.shape, a.dtype), shape(b.shape, b.dtype)),
        scratch_shapes=exchange_scratch(1) + exchange_scratch(1),
        compiler_params=pltpu.CompilerParams(collective_id=cid, has_side_effects=True),
        cost_estimate=cost(25, 10),
    )(a, b)


def final_kernel(
    tensor, g_ref, dwa_ref, dwb_ref, wrg_ref, cvg_ref, resg_ref, nmg_ref, nag_ref, count_ref, out_ref, small_ref, dwax_ref,
    dwbx_ref, zf, zs, zr, sbuf, srecv, *scratch,
):
    here = lax.axis_index("tensor")
    me = lax.axis_index("dp")
    k, d, _ = g_ref.shape
    r, f = out_ref.shape[1:]
    zsems, ssems = scratch[7], scratch[8]
    red = Reduce8(lambda s: g_ref.at[:, pl.ds(pl.multiple_of(s * r, r), r), :], scratch[:5], *scratch[5:7])
    swaps = [
        Exchange8([dwa_ref], dwax_ref, None, *scratch[9:11]), Exchange8([dwb_ref], dwbx_ref, None, *scratch[11:13])
    ]
    red.load()
    sbuf[0] = jnp.zeros_like(sbuf[0])
    sbuf[0, 0:24, :] = wrg_ref[0:24, :]
    sbuf[0, 24:26, :] = cvg_ref[0:2, :]
    sbuf[0, 26:27, :] = nmg_ref[...]
    sbuf[0, 27:28, :] = nag_ref[...]
    sbuf[0, 28:29, 0:LANES] = jnp.where(count_ref[...] > ROOM, 1.0, 0.0)
    sbuf[0, 32:48, 0:LANES] = resg_ref[0:16, :]
    greet(all_peers() + far_peers(tensor))
    red.begin()
    rounds = [remote(sbuf.at[n], srecv.at[n], ssems, n, "dp", flip(me, m)) for n, m in enumerate((1, 2, 4))]
    rounds[0].start()
    red.first()
    for swap in swaps:
        swap.begin()
    rounds[0].wait_recv()
    sbuf[1] = sbuf[0] + srecv[0]
    rounds[1].start()
    red.second()
    rounds[1].wait_recv()
    sbuf[2] = sbuf[1] + srecv[1]
    rounds[2].start()
    red.third()
    rounds[2].wait_recv()
    sbuf[3] = sbuf[2] + srecv[2]
    far = [
        remote(sbuf.at[3], srecv.at[3 + here], ssems, 3 + n, axis, peer)
        for n, (axis, peer) in enumerate(far_peers(tensor))
    ]
    for c in far:
        c.start()

    def write(part, total):
        for t in range(tensor):
            zf[t, part] = total[:, :, t * f : (t + 1) * f]
            zs[t, part] = total[:, :, t * f : (t + 1) * f].astype(bf16)

    red.end(write)
    out_copies = [
        remote(zs.at[peer], zr.at[here], zsems, n, axis, peer) for n, (axis, peer) in enumerate(far_peers(tensor))
    ]
    for c in out_copies:
        c.start()
    srecv[3 + here] = sbuf[3]
    for c in far:
        c.wait_recv()
    total = srecv[3]
    for t in range(1, tensor):
        total = total + srecv[3 + t]
    small_ref[...] = total
    zr[here] = jnp.zeros(zr.shape[1:], bf16)
    for c in out_copies:
        c.wait_recv()
    total = zf[here]
    for t in range(tensor):
        total = total + zr[t].astype(f32)
    out_ref[...] = total
    red.close()
    for c in rounds + far + out_copies:
        c.wait_send()
    for swap in swaps:
        swap.end()


def finish(g, dwa, dwb, wrg, cvg, resg, nmg, nag, count, tensor, cid):
    k, d, columns = g.shape
    r, f = d // NF, columns // tensor
    return pl.pallas_call(
        functools.partial(final_kernel, tensor),
        in_specs=[ANY] * 3 + [VM] * 6,
        out_specs=[VM] * 2 + [ANY] * 2,
        out_shape=(shape((k, r, f), f32), shape((48, d), f32), shape(dwa.shape, bf16), shape(dwb.shape, bf16)),
        scratch_shapes=[
            pltpu.VMEM((tensor, k, r, f), f32),
            pltpu.VMEM((tensor, k, r, f), bf16),
            pltpu.VMEM((tensor, k, r, f), bf16),
            pltpu.VMEM((4, 48, d), f32),
            pltpu.VMEM((3 + tensor, 48, d), f32),
            *reduce_scratch((k, r, columns)),
            pltpu.SemaphoreType.DMA((2, tensor - 1)),
            pltpu.SemaphoreType.DMA((2, 2 + tensor)),
            *exchange_scratch(1),
            *exchange_scratch(1),
        ],
        compiler_params=pltpu.CompilerParams(collective_id=cid, has_side_effects=True, vmem_limit_bytes=60 << 20),
        cost_estimate=cost(30, 10),
    )(g, dwa, dwb, wrg, cvg, resg, nmg, nag, count)


def fwd_kernel(
    starts_ref, tok_ref, prior_ref, ids_ref, ranks_ref, ga_ref, gm_ref, cos_ref, sin_ref, w_ref, wr_ref, wres_ref, cv_ref,
    og_ref,
    q_ref, k_ref, v_ref, mixed_ref, lse_ref, nattn_ref, resid_ref, nmoe_ref, base_ref, aux_ref, pos_ref, count_ref, xr_ref,
    yr_ref, payr_ref,
    bias_ref, gate_ref, xs, ys, pay, *scratch,
):
    greet(all_peers())
    send_x, send_y = Send8(xs, xr_ref, *scratch[0:2], True), Send8(ys, yr_ref, *scratch[2:4], True)
    swap = Swap8(pay, payr_ref, *scratch[4:6])
    lane = lanes(QT)
    lower = jnp.where(
        lax.broadcasted_iota(i32, (QT, QT), 1) < lax.broadcasted_iota(i32, (QT, QT), 0), 1.0, 0.0
    ).astype(bf16)

    def hits(rows):
        id0, id1 = ids_ref[rows, 0:1], ids_ref[rows, 1:2]
        rk0, rk1 = ranks_ref[rows, 0:1], ranks_ref[rows, 1:2]
        hit0, hit1 = jnp.where(lane == id0, 1.0, 0.0), jnp.where(lane == id1, 1.0, 0.0)
        keep0, keep1 = jnp.where(rk0 < CAP, 1.0, 0.0), jnp.where(rk1 < CAP, 1.0, 0.0)
        return hit0 + hit1, (hit0 * keep0 + hit1 * keep1) * jnp.where(lane < NF, 1.0, 0.0)

    def places(i, taken):
        rows = pl.ds(pl.multiple_of(i * QT, QT), QT)
        _, kept = hits(rows)
        pos = nn(lower, kept.astype(bf16)) + taken
        pos_ref[:, 0, rows] = jnp.where(kept > 0, pos, -1.0).T[0:NF, :]
        return taken + jnp.sum(kept, axis=0, keepdims=True)

    count_ref[...] = lax.fori_loop(0, SEQ // QT, places, jnp.zeros((1, LANES), f32))
    for m in (*Send8.order, 0):
        ys[m] = nn(hot_rows(pos_ref[flip(send_y.slot, m)]), og_ref[...]).astype(bf16)
        send_y.start(m)
    d = tok_ref.shape[1]
    pairs = d // LANES
    ntile = SEQ // QT
    ga, gm = ga_ref[...], gm_ref[...]
    mask_a, mask_b = head_masks()
    mask16 = (mask_a.astype(bf16), mask_b.astype(bf16))

    def project(i, carry):
        rows = pl.ds(pl.multiple_of(i * QT, QT), QT)
        x = tok_ref[rows, :].astype(f32)
        r1 = lax.rsqrt(jnp.mean(x * x, axis=-1, keepdims=True) + EPS)
        n = (x * r1 * ga).astype(bf16)
        nattn_ref[rows, :] = n
        cosine, sine = cos_ref[rows, :], sin_ref[rows, :]
        for c, out in ((0, q_ref), (1, k_ref), (2, v_ref)):
            proj = nn(n, w_ref[c])
            for p in range(pairs):
                part = proj[:, p * LANES : (p + 1) * LANES]
                if c < 2:
                    part = rot(part, cosine, sine)
                part = part.astype(bf16)
                if c == 0:
                    part = part * jnp.array(HD**-0.5, bf16)
                out[rows, p * LANES : (p + 1) * LANES] = part
        return carry

    lax.fori_loop(0, ntile, project, 0)

    for i in range(ntile):
        lo = i * QT
        width = min(SEQ, lo + 2 * QT) - lo
        rows = pl.ds(lo, QT)
        bias_ref[:, :width] = window_bias(starts_ref, i, width, False)

        def pair(p, lse):
            cols = pl.ds(pl.multiple_of(p * LANES, LANES), LANES)
            q2 = q_ref[rows, cols]
            outs = []
            for h in range(2):
                qh = q2 * mask16[h]
                sb = nt(qh, k_ref[lo : lo + width, cols]) + bias_ref[:, :width]
                m = jnp.max(sb, axis=-1, keepdims=True)
                if lo:
                    sa = nt(qh, k_ref[0:lo, cols])
                    m = jnp.maximum(m, jnp.max(sa, axis=-1, keepdims=True))
                pb = jnp.exp(sb - m)
                total = jnp.sum(pb, axis=-1, keepdims=True)
                acc = nn(pb.astype(bf16), v_ref[lo : lo + width, cols])
                if lo:
                    pa = jnp.exp(sa - m)
                    total = total + jnp.sum(pa, axis=-1, keepdims=True)
                    acc = acc + nn(pa.astype(bf16), v_ref[0:lo, cols])
                outs.append(acc / total)
                lse = jnp.where(lane == 2 * p + h, m + jnp.log(total), lse)
            mixed_ref[rows, cols] = (outs[0] * mask_a + outs[1] * mask_b).astype(bf16)
            return lse

        lse = lax.fori_loop(0, pairs, pair, jnp.zeros((QT, LANES), f32))
        lse_ref[:, rows] = lse.T[0 : lse_ref.shape[0], :]

        x = tok_ref[rows, :].astype(f32)
        resid = x + nt(mixed_ref[rows, :], w_ref[3])
        resid_ref[rows, :] = resid
        r2 = lax.rsqrt(jnp.mean(resid * resid, axis=-1, keepdims=True) + EPS)
        nm = (resid * r2 * gm).astype(bf16)
        nmoe_ref[rows, :] = nm
        raw = nn(nm, wr_ref[...])
        logits = raw + nn(prior_ref[rows, :], wres_ref[...])
        logits = jnp.where(lane < NF + 2 + NC, logits, -1e30)
        e = jnp.exp(logits - jnp.max(logits, axis=-1, keepdims=True))
        shares = e / jnp.sum(e, axis=-1, keepdims=True)
        chosen, kept = hits(rows)
        gates = shares * chosen
        gate_ref[:, 0, rows] = (shares * kept).T[0:NF, :]
        nv = nm.astype(f32)
        aux = jnp.where(lane < NF + 2 + NC, shares, 0.0)
        direct = gates[:, NF + 1 : NF + 2]
        others = None
        for c in range(NC):
            z0, z1 = raw[:, Z0 + 2 * c : Z0 + 2 * c + 1], raw[:, Z0 + 2 * c + 1 : Z0 + 2 * c + 2]
            m0, m1 = 1.0 / (1.0 + jnp.exp(z1 - z0)), 1.0 / (1.0 + jnp.exp(z0 - z1))
            aux = jnp.where(lane == Z0 + 2 * c, m0, aux)
            aux = jnp.where(lane == Z0 + 2 * c + 1, m1, aux)
            w = gates[:, NF + 2 + c : NF + 3 + c]
            direct = direct + w * m0
            term = (w * m1) * cv_ref[c : c + 1, :]
            others = term if others is None else others + term
        aux_ref[rows, :] = aux
        base_ref[rows, :] = resid + direct * nv + others

    for m in (*Send8.order, 0):
        e = flip(send_x.slot, m)
        place = pos_ref[e]
        hot = hot_rows(place)
        xs[m] = nn(hot, nmoe_ref[...]).astype(bf16)
        send_x.start(m)
        pay[e] = jnp.sum(nt(split_rows(gate_ref[e]), hot), axis=0, keepdims=True)
        filled = jnp.minimum(jnp.max(place, axis=1, keepdims=True) + 1.0, float(ROOM))
        pay[NF + e] = jnp.broadcast_to(filled, (1, ROOM))
    swap.begin()
    for send in (send_y, send_x):
        for m in (*Send8.order, 0):
            send.got(m)
        send.close()
    swap.end()


def mid_kernel(
    dxb_ref, ggb_ref, pos_ref, og_ref, nmoe_ref, resid_ref, ids_ref, aux_ref, prior_ref, wr_ref, wres_ref, cv_ref, gm_ref,
    gmo_ref, gres_ref, pgrad_ref, nmg_ref, wrg_ref, resg_ref, cvg_ref,
    dxr, ggr, dx_ref, gg_ref, *scratch,
):
    greet(all_peers())
    send, swap = Send8(dxb_ref, dxr, *scratch[0:2], False), Swap8(ggb_ref, ggr, *scratch[2:4])
    swap.begin()
    send.begin()
    swap.end()
    for n, m in enumerate((0, 1, 2, 3, 4, 5, 6, 7)):
        send.got(m)
        e = flip(send.slot, m)
        hot = hot_rows(pos_ref[e])
        gg_ref[pl.ds(e, 1), :] = jnp.sum(nn(split_rows(ggr[e]), hot), axis=0, keepdims=True)
        part = tn(hot, dxr[e])
        if n:
            dx_ref[...] += part
        else:
            dx_ref[...] = part
    send.close()
    gm = gm_ref[...]
    lane = lanes(QT)
    nmg_ref[...] = jnp.zeros_like(nmg_ref)
    wrg_ref[...] = jnp.zeros_like(wrg_ref)
    resg_ref[...] = jnp.zeros_like(resg_ref)
    cvg_ref[...] = jnp.zeros_like(cvg_ref)

    def tile(i, carry):
        rows = pl.ds(pl.multiple_of(i * QT, QT), QT)
        g16, n16 = og_ref[rows, :], nmoe_ref[rows, :]
        g, nv = g16.astype(f32), n16.astype(f32)
        x = resid_ref[rows, :]
        r2 = lax.rsqrt(jnp.mean(x * x, axis=-1, keepdims=True) + EPS)
        aux = aux_ref[rows, :]
        shares = jnp.where(lane < NF + 2 + NC, aux, 0.0)
        id0, id1 = ids_ref[rows, 0:1], ids_ref[rows, 1:2]
        chosen = jnp.where(lane == id0, 1.0, 0.0) + jnp.where(lane == id1, 1.0, 0.0)
        gates = shares * chosen
        copy_inner = jnp.sum(g * nv, axis=-1, keepdims=True)
        inner = jnp.concatenate([gg_ref[:, rows], jnp.zeros((LANES - NF, QT), f32)], axis=0).T
        inner = jnp.where(lane == NF + 1, copy_inner, inner)
        direct = gates[:, NF + 1 : NF + 2]
        blend = jnp.zeros((QT, LANES), f32)
        cvw = jnp.zeros((QT, LANES), f32)
        for c in range(NC):
            m0, m1 = aux[:, Z0 + 2 * c : Z0 + 2 * c + 1], aux[:, Z0 + 2 * c + 1 : Z0 + 2 * c + 2]
            v_inner = jnp.sum(g * cv_ref[c : c + 1, :], axis=-1, keepdims=True)
            mean = m0 * copy_inner + m1 * v_inner
            inner = jnp.where(lane == NF + 2 + c, mean, inner)
            w = gates[:, NF + 2 + c : NF + 3 + c]
            direct = direct + w * m0
            blend = jnp.where(lane == Z0 + 2 * c, m0 * (w * copy_inner - w * mean), blend)
            blend = jnp.where(lane == Z0 + 2 * c + 1, m1 * (w * v_inner - w * mean), blend)
            cvw = jnp.where(lane == c, w * m1, cvw)
        grad_router = inner * chosen
        glog = shares * (grad_router - jnp.sum(shares * grad_router, axis=-1, keepdims=True))
        both_hi, both_lo = split(glog + blend)
        log_hi, log_lo = split(glog)
        cv_hi, cv_lo = split(cvw)
        pgrad_ref[rows, :] = nt(log_hi, wres_ref[...]) + nt(log_lo, wres_ref[...])
        wrg_ref[...] += tn(both_hi, n16) + tn(both_lo, n16)
        resg_ref[...] += tn(prior_ref[rows, :], log_hi) + tn(prior_ref[rows, :], log_lo)
        cvg_ref[...] += tn(cv_hi, g16) + tn(cv_lo, g16)
        gmi = dx_ref[rows, :] + direct * g + nt(both_hi, wr_ref[...]) + nt(both_lo, wr_ref[...])
        nmg_ref[...] += jnp.sum(gmi * x * r2, axis=0, keepdims=True)
        scaled = gmi * gm
        avg = jnp.mean(scaled * x, axis=-1, keepdims=True)
        gres = g + r2 * scaled - x * (r2 * r2 * r2 * avg)
        gres_ref[rows, :] = gres
        gmo_ref[rows, :] = gres.astype(bf16)
        return carry

    lax.fori_loop(0, SEQ // QT, tile, 0)


def bwd_kernel(
    starts_ref, gmo_ref, gres_ref, mixed_ref, q_ref, k_ref, v_ref, lse_ref, nattn_ref, tok_ref, ga_ref, cos_ref,
    sin_ref, w_ref, outb_ref, pos_ref, base_ref,
    igrad_ref, wg_ref, nag_ref, layer_ref,
    do_ref, delta_ref, bias_ref, gp_ref, dk_ref, dv_ref, dq_ref, outr, *scratch,
):
    greet(all_peers())
    send = Send8(outb_ref, outr, *scratch, False)
    send.begin()
    d = tok_ref.shape[1]
    pairs = d // LANES
    ntile = SEQ // QT
    ga = ga_ref[...]
    mask_a, mask_b = head_masks()
    mask16 = (mask_a.astype(bf16), mask_b.astype(bf16))
    maskf = (mask_a, mask_b)
    heads = delta_ref.shape[0]
    pick = jnp.where(
        lax.broadcasted_iota(i32, (heads, d), 1) // HD == lax.broadcasted_iota(i32, (heads, d), 0), 1.0, 0.0
    ).astype(bf16)

    def start(i, carry):
        rows = pl.ds(pl.multiple_of(i * QT, QT), QT)
        do = nn(gmo_ref[rows, :], w_ref[3]).astype(bf16)
        do_ref[rows, :] = do
        hi, lo = split(do.astype(f32) * mixed_ref[rows, :].astype(f32))
        delta_ref[:, rows] = nt(pick, hi) + nt(pick, lo)
        return carry

    lax.fori_loop(0, ntile, start, 0)
    wg_ref[3] = tn(gmo_ref[...], mixed_ref[...]).astype(wg_ref.dtype)
    for i in range(ntile):
        width = min(SEQ, (i + 2) * QT) - i * QT
        bias_ref[i, 0:width, :] = window_bias(starts_ref, i, width, True)

    def pair(p, carry):
        cols = pl.ds(pl.multiple_of(p * LANES, LANES), LANES)
        dk_ref[...] = jnp.zeros_like(dk_ref)
        dv_ref[...] = jnp.zeros_like(dv_ref)
        for i in range(ntile):
            lo = i * QT
            width = min(SEQ, lo + 2 * QT) - lo
            rows = pl.ds(lo, QT)
            q2, do2 = q_ref[rows, cols], do_ref[rows, cols]
            dq = jnp.zeros((QT, LANES), f32)
            for h in range(2):
                qh, doh = q2 * mask16[h], do2 * mask16[h]
                lse, delta = lse_ref[pl.ds(2 * p + h, 1), rows], delta_ref[pl.ds(2 * p + h, 1), rows]
                spans = [(lo, width, True)] + ([(0, lo, False)] if lo else [])
                for at, size, masked in spans:
                    k2 = k_ref[at : at + size, cols]
                    s = nt(k2, qh)
                    if masked:
                        s = s + bias_ref[i, 0:size, :]
                    prob = jnp.exp(s - lse)
                    ds = (prob * (nt(v_ref[at : at + size, cols], doh) - delta)).astype(bf16)
                    dv_ref[at : at + size, :] += nn(prob.astype(bf16), doh)
                    dk_ref[at : at + size, :] += nn(ds, qh)
                    dq = dq + tn(ds, k2) * maskf[h]
            dq_ref[rows, :] = dq * HD**-0.5
        cosine, sine = cos_ref[...], -sin_ref[...]
        gp_ref[0, :, cols] = rot(dq_ref[...], cosine, sine).astype(bf16)
        gp_ref[1, :, cols] = rot(dk_ref[...], cosine, sine).astype(bf16)
        gp_ref[2, :, cols] = dv_ref[...].astype(bf16)
        return carry

    lax.fori_loop(0, pairs, pair, 0)
    for c in range(3):
        wg_ref[c] = tn(nattn_ref[...], gp_ref[c]).astype(wg_ref.dtype)
    nag_ref[...] = jnp.zeros_like(nag_ref)
    for m in range(NF):
        send.got(m)

    def finish(i, carry):
        rows = pl.ds(pl.multiple_of(i * QT, QT), QT)
        layer = base_ref[rows, :]
        for e in range(NF):
            layer = layer + tn(hot_rows(pos_ref[e, :, rows]), outr[e])
        layer_ref[rows, :] = layer.astype(bf16)
        gai = nt(gp_ref[0, rows, :], w_ref[0]) + nt(gp_ref[1, rows, :], w_ref[1])
        gai = gai + nt(gp_ref[2, rows, :], w_ref[2])
        x = tok_ref[rows, :].astype(f32)
        r1 = lax.rsqrt(jnp.mean(x * x, axis=-1, keepdims=True) + EPS)
        nag_ref[...] += jnp.sum(gai * x * r1, axis=0, keepdims=True)
        scaled = gai * ga
        avg = jnp.mean(scaled * x, axis=-1, keepdims=True)
        igrad_ref[rows, :] = gres_ref[rows, :] + r1 * scaled - x * (r1 * r1 * r1 * avg)
        return carry

    lax.fori_loop(0, ntile, finish, 0)
    send.close()


def ffn_tile(x, gate, y, w_ref, acc, eo, dx):
    dy = y.astype(f32)
    ge = (gate * dy).astype(bf16)
    x_t, ge_t = x.T, ge.T
    for c in range(w_ref.shape[0]):
        wg, wu, wd = w_ref[c, 0], w_ref[c, 1], w_ref[c, 2]
        gv, uv = nn(x, wg), nn(x, wu)
        gh = nn(ge, wd)
        sig = 1.0 / (1.0 + jnp.exp(-gv))
        act = gv * sig
        hid = (act * uv).astype(bf16)
        eo = eo + nt(hid, wd)
        gg = (gh * uv * (sig * (1.0 + gv * (1.0 - sig)))).astype(bf16)
        gu = (gh * act).astype(bf16)
        dx = dx + nt(gg, wg) + nt(gu, wu)
        acc[c, 0] += nn(x_t, gg)
        acc[c, 1] += nn(x_t, gu)
        acc[c, 2] += nn(ge_t, hid)
    return eo, dx


def first_kernel(pay_ref, x_ref, y_ref, w_ref, xc_ref, yc_ref, gc_ref, eo_ref, dx_ref, dw_ref, meta_ref, acc):
    d = x_ref.shape[2]
    gates = [pay_ref[g] for g in range(NF)] + [jnp.zeros((LANES - NF, ROOM), f32)]
    columns = jnp.concatenate(gates, axis=0).T
    off = jnp.int32(0)
    for g in range(NF):
        rows = pl.ds(pl.multiple_of(off, 16), ROOM)
        xc_ref[rows, :] = x_ref[g]
        yc_ref[rows, :] = y_ref[g]
        gc_ref[rows, :] = jnp.broadcast_to(columns[:, g : g + 1], (ROOM, LANES))
        meta_ref[g] = off
        off = off + (jnp.max(pay_ref[NF + g]).astype(i32) + 15) // 16 * 16
    rows = pl.ds(pl.multiple_of(off, 16), TM)
    xc_ref[rows, :] = jnp.zeros((TM, d), bf16)
    yc_ref[rows, :] = jnp.zeros((TM, d), bf16)
    gc_ref[rows, :] = jnp.zeros((TM, LANES), f32)
    tiles = jnp.maximum((off + TM - 1) // TM, 1)
    meta_ref[NF] = tiles
    acc[...] = jnp.zeros_like(acc)
    zero = jnp.zeros((TM, d), f32)

    def tile(t, carry):
        rows = pl.ds(pl.multiple_of(t * TM, TM), TM)
        eo_ref[rows, :], dx_ref[rows, :] = ffn_tile(
            xc_ref[rows, :], gc_ref[rows, 0:1], yc_ref[rows, :], w_ref, acc, zero, zero
        )
        return carry

    lax.fori_loop(0, tiles, tile, 0)
    dw_ref[...] = acc[...].astype(bf16)


def second_kernel(
    meta_ref, xc_ref, yc_ref, gc_ref, eo_ref, dx_ref, w_ref, outb_ref, dxb_ref, ggb_ref, dw_ref, outs, dxs, ggs, acc
):
    d = xc_ref.shape[1]
    tiles = meta_ref[NF]
    acc[...] = jnp.zeros_like(acc)
    rows = pl.ds(pl.multiple_of(tiles * TM, TM), ROOM)
    outs[rows, :] = jnp.zeros((ROOM, d), bf16)
    dxs[rows, :] = jnp.zeros((ROOM, d), bf16)
    ggs[rows, :] = jnp.zeros((ROOM, LANES), f32)

    def tile(t, carry):
        rows = pl.ds(pl.multiple_of(t * TM, TM), TM)
        gate, y = gc_ref[rows, 0:1], yc_ref[rows, :]
        eo, dx = ffn_tile(xc_ref[rows, :], gate, y, w_ref, acc, eo_ref[rows, :], dx_ref[rows, :])
        outs[rows, :] = (gate * eo).astype(bf16)
        dxs[rows, :] = dx.astype(bf16)
        ggs[rows, :] = jnp.broadcast_to(jnp.sum(y.astype(f32) * eo, axis=1, keepdims=True), (TM, LANES))
        return carry

    lax.fori_loop(0, tiles, tile, 0)
    lane = lanes(ROOM)
    columns = jnp.zeros((ROOM, LANES), f32)
    for g in range(NF):
        rows = pl.ds(pl.multiple_of(meta_ref[g], 16), ROOM)
        outb_ref[g] = outs[rows, :]
        dxb_ref[g] = dxs[rows, :]
        columns = jnp.where(lane == g, ggs[rows, :], columns)
    ggb_ref[:, 0, :] = columns.T[0:NF, :]
    dw_ref[...] = acc[...].astype(bf16)


def experts_first(pay, x, y, w):
    groups, _, d = x.shape
    total = groups * ROOM + TM
    return pl.pallas_call(
        first_kernel,
        in_specs=[VM] * 4,
        out_specs=[VM] * 6 + [SM],
        out_shape=(
            shape((total, d), bf16), shape((total, d), bf16), shape((total, LANES), f32), shape((total, d), f32),
            shape((total, d), f32), shape(w.shape, bf16), shape((NF + 1,), i32),
        ),
        scratch_shapes=[pltpu.VMEM(w.shape, f32)],
        compiler_params=pltpu.CompilerParams(vmem_limit_bytes=60 << 20),
        cost_estimate=cost(22, 25),
    )(pay, x, y, w)


def experts_second(meta, xc, yc, gc, eo, dx, w):
    total, d = xc.shape
    blocks = shape((NF, ROOM, d), bf16)
    room = total + ROOM
    return pl.pallas_call(
        second_kernel,
        in_specs=[SM] + [VM] * 6,
        out_specs=[VM] * 4,
        out_shape=(blocks, blocks, shape((NF, 1, ROOM), f32), shape(w.shape, bf16)),
        scratch_shapes=[
            pltpu.VMEM((room, d), bf16),
            pltpu.VMEM((room, d), bf16),
            pltpu.VMEM((room, LANES), f32),
            pltpu.VMEM(w.shape, f32),
        ],
        compiler_params=pltpu.CompilerParams(vmem_limit_bytes=60 << 20),
        cost_estimate=cost(22, 25),
    )(meta, xc, yc, gc, eo, dx, w)


def hot_rows(pos):
    slot = lax.broadcasted_iota(i32, (ROOM, pos.shape[1]), 0).astype(f32)
    return jnp.where(slot == pos, 1.0, 0.0).astype(bf16)


def split_rows(row):
    hi = row.astype(bf16).astype(f32)
    mid = (row - hi).astype(bf16).astype(f32)
    at = lax.broadcasted_iota(i32, (8, row.shape[1]), 0)
    out = jnp.where(at == 0, hi, jnp.where(at == 1, mid, jnp.where(at == 2, row - hi - mid, 0.0)))
    return out.astype(bf16)


def shape(dims, dtype):
    return jax.ShapeDtypeStruct(dims, dtype)


def cost(gflop, mbytes, mexp=0):
    return pl.CostEstimate(flops=int(gflop * 1e9), bytes_accessed=int(mbytes * 1e6), transcendentals=int(mexp * 1e6))


def rms_factor(values):
    return lax.rsqrt(jnp.mean(values * values, axis=-1, keepdims=True) + EPS)


def norm_back(grad, values, factor, gain):
    scaled = grad * gain
    inner = jnp.mean(scaled * values, axis=-1, keepdims=True)
    return factor * scaled - values * factor * factor * factor * inner


def rotary(positions, width):
    place = (jnp.arange(positions) % SEQ).astype(jnp.float32)
    freqs = jnp.power(10000.0, jnp.arange(width // 2).astype(jnp.float32) * (-2.0 / width))
    angles = place[:, None] * freqs[None, :]
    return (jnp.cos(angles)[:, None, :], jnp.sin(angles)[:, None, :])


def rotate(values, cosine, sine):
    half = values.shape[-1] // 2
    front = values[..., :half]
    behind = values[..., half:]
    return jnp.concatenate(
        [front * cosine - behind * sine, behind * cosine + front * sine], axis=-1
    )


def visible(starts):
    position = jnp.arange(SEQ)
    piece_of = jnp.zeros((SEQ,), jnp.int32)
    for index in range(starts.shape[0]):
        inside = (position >= starts[index]) & (position < starts[index] + PIECE)
        piece_of = jnp.where(inside, index + 1, piece_of)
    causal = position[None, :] <= position[:, None]
    same_piece = (piece_of[:, None] > 0) & (piece_of[:, None] == piece_of[None, :])
    return causal | same_piece


def dispatch(route_ids, route_ranks):
    group_rows = route_ids.shape[0]
    retained = (route_ids < NF) & (route_ranks < CAP)
    target = jnp.where(retained, route_ids * CAP + route_ranks, NF * CAP)
    token_index = jnp.broadcast_to(
        jnp.arange(group_rows, dtype=jnp.int32)[:, None], route_ids.shape
    )
    slot_token = (
        jnp.zeros((NF * CAP + 1,), jnp.int32)
        .at[target.reshape(-1)]
        .set(token_index.reshape(-1))[: NF * CAP]
    )
    filled = jnp.zeros((NF * CAP + 1,), jnp.float32).at[target.reshape(-1)].set(1.0)[: NF * CAP]
    return (retained, target, slot_token, filled)


def masked_scores(query, keys, starts):
    scores = jnp.einsum("qhd,khd->hqk", query, keys, preferred_element_type=jnp.float32) * HD ** (
        -0.5
    )
    return jnp.where(visible(starts)[None], scores, -1e30)


def attend_block(parts):
    query, keys, values, starts = parts
    scores = masked_scores(query, keys, starts)
    row_max = jnp.max(scores, axis=-1, keepdims=True)
    denominator = jnp.sum(jnp.exp(scores - row_max), axis=-1, keepdims=True)
    log_total = row_max + jnp.log(denominator)
    shares = jnp.exp(scores - log_total).astype(jnp.bfloat16)
    mixed = jnp.einsum("hqk,khd->qhd", shares, values, preferred_element_type=jnp.float32)
    return (mixed.astype(jnp.bfloat16), log_total)


def attend_back(parts):
    query, keys, values, starts, log_total, grad_out = parts
    shares = jnp.exp(masked_scores(query, keys, starts) - log_total)
    grad_shares = jnp.einsum("qhd,khd->hqk", grad_out, values, preferred_element_type=jnp.float32)
    centre = jnp.sum(shares * grad_shares, axis=-1, keepdims=True)
    grad_scores = (shares * (grad_shares - centre)).astype(jnp.bfloat16)
    factor = HD ** (-0.5)
    grad_query = (
        jnp.einsum("hqk,khd->qhd", grad_scores, keys, preferred_element_type=jnp.float32) * factor
    )
    grad_keys = (
        jnp.einsum("hqk,qhd->khd", grad_scores, query, preferred_element_type=jnp.float32) * factor
    )
    grad_values = jnp.einsum(
        "hqk,qhd->khd", shares.astype(jnp.bfloat16), grad_out, preferred_element_type=jnp.float32
    )
    return (grad_query, grad_keys, grad_values)


def plain_on_device(
    tokens,
    prior_logits,
    expert_ids,
    expert_ranks,
    piece_starts,
    norm_attn,
    qkv_weight,
    out_weight,
    norm_moe,
    router_weight,
    residual_weight,
    const_vectors,
    const_gates,
    w_gate_up,
    w_down,
    out_grad,
):
    highest = lax.Precision.HIGHEST
    local_rows = tokens.shape[0]
    group_rows = expert_ids.shape[0]
    sequences = group_rows // SEQ
    head_count = qkv_weight.shape[2] // HD
    row_start = lax.axis_index("tensor") * local_rows
    seq_shape = (sequences, SEQ, head_count, HD)
    gain_attn = norm_attn.astype(jnp.float32)
    gain_moe = norm_moe.astype(jnp.float32)
    tok_vals = tokens.astype(jnp.float32)
    factor_attn = rms_factor(tok_vals)
    normed_attn = (tok_vals * factor_attn * gain_attn).astype(jnp.bfloat16)
    attn_rows = lax.all_gather(normed_attn, "tensor", axis=0, tiled=True)
    qkv_full, out_full = (
        lax.all_gather(qkv_weight, "dp", axis=1, tiled=True),
        lax.all_gather(out_weight, "dp", axis=1, tiled=True),
    )
    projected = jnp.einsum("gd,cde->cge", attn_rows, qkv_full, preferred_element_type=jnp.float32)
    cosine, sine = rotary(group_rows, HD)
    query = (
        rotate(projected[0].reshape(group_rows, head_count, HD), cosine, sine)
        .astype(jnp.bfloat16)
        .reshape(seq_shape)
    )
    keys = (
        rotate(projected[1].reshape(group_rows, head_count, HD), cosine, sine)
        .astype(jnp.bfloat16)
        .reshape(seq_shape)
    )
    values = projected[2].astype(jnp.bfloat16).reshape(seq_shape)
    mixed, log_total = lax.map(attend_block, (query, keys, values, piece_starts))
    mixed_rows = mixed.reshape(group_rows, head_count * HD)
    attn_part = jnp.dot(mixed_rows, out_full, preferred_element_type=jnp.float32)
    attn_out = lax.psum_scatter(attn_part, "tensor", scatter_dimension=0, tiled=True)
    resid = tok_vals + attn_out
    factor_moe = rms_factor(resid)
    normed_moe = (resid * factor_moe * gain_moe).astype(jnp.bfloat16)
    moe_rows, prior_rows = (
        lax.all_gather(normed_moe, "tensor", axis=0, tiled=True),
        lax.all_gather(prior_logits, "tensor", axis=0, tiled=True),
    )
    logits = jnp.dot(moe_rows, router_weight, preferred_element_type=jnp.float32) + jnp.dot(
        prior_rows, residual_weight, preferred_element_type=jnp.float32
    )
    shares = jax.nn.softmax(logits, axis=-1)
    gates = jnp.take_along_axis(shares, expert_ids, axis=1)
    retained, target, slot_token, filled = dispatch(expert_ids, expert_ranks)
    picker = jnp.minimum(target, NF * CAP - 1)
    slot_gate = (
        jnp.zeros((NF * CAP + 1,), jnp.float32)
        .at[target.reshape(-1)]
        .set(gates.reshape(-1))[: NF * CAP]
        * filled
    )
    expert_rows = (moe_rows[slot_token] * filled[:, None].astype(jnp.bfloat16)).reshape(NF, CAP, -1)
    gate_full, down_full = (
        lax.all_gather(w_gate_up, "dp", axis=2, tiled=True),
        lax.all_gather(w_down, "dp", axis=2, tiled=True),
    )
    gate_up = jnp.einsum(
        "ecd,sedf->secf", expert_rows, gate_full, preferred_element_type=jnp.float32
    )
    sigmoid_vals = jax.nn.sigmoid(gate_up[0])
    activated = gate_up[0] * sigmoid_vals
    hidden = (activated * gate_up[1]).astype(jnp.bfloat16)
    expert_out = jnp.einsum(
        "ecf,efd->ecd", hidden, down_full, preferred_element_type=jnp.float32
    ).reshape(NF * CAP, -1)
    retained_gates = jnp.where(retained, gates, 0.0)
    combined = jnp.sum(retained_gates[:, :, None] * expert_out[picker], axis=1)
    ffn_out = lax.psum_scatter(
        combined.astype(jnp.bfloat16), "tensor", scatter_dimension=0, tiled=True
    ).astype(jnp.float32)
    local_ids = lax.dynamic_slice_in_dim(expert_ids, row_start, local_rows, 0)
    local_shares = lax.dynamic_slice_in_dim(shares, row_start, local_rows, 0)
    local_gates = lax.dynamic_slice_in_dim(gates, row_start, local_rows, 0)
    normed_vals = normed_moe.astype(jnp.float32)
    vectors = const_vectors.astype(jnp.float32)
    gate_mats = const_gates.astype(jnp.float32)
    const_count = vectors.shape[0]
    copy_share = jnp.sum(jnp.where(local_ids == NF + 1, local_gates, 0.0), axis=1)
    const_share = jnp.stack(
        [
            jnp.sum(jnp.where(local_ids == NF + 2 + index, local_gates, 0.0), axis=1)
            for index in range(const_count)
        ],
        axis=1,
    )
    mixing = jax.nn.softmax(
        jnp.einsum("gd,cjd->gcj", normed_vals, gate_mats, precision=highest), axis=-1
    )
    const_out = (
        mixing[:, :, 0:1] * normed_vals[:, None, :] + mixing[:, :, 1:2] * vectors[None, :, :]
    )
    others = copy_share[:, None] * normed_vals + jnp.sum(
        const_share[:, :, None] * const_out, axis=1
    )
    layer_out = (resid + ffn_out + others).astype(jnp.bfloat16)
    grad_out = out_grad.astype(jnp.float32)
    grad_moe_rows = lax.all_gather(out_grad, "tensor", axis=0, tiled=True)
    gate_back, down_back = (
        lax.all_gather(w_gate_up, "dp", axis=2, tiled=True),
        lax.all_gather(w_down, "dp", axis=2, tiled=True),
    )
    slot_grads = grad_moe_rows[slot_token].astype(jnp.float32)
    grad_expert = (slot_gate[:, None] * slot_grads).astype(jnp.bfloat16).reshape(NF, CAP, -1)
    slot_inner = jnp.sum(slot_grads * expert_out, axis=-1)
    gate_grad_ffn = jnp.where(retained, slot_inner[picker], 0.0)
    down_grad = jnp.einsum("ecf,ecd->efd", hidden, grad_expert, preferred_element_type=jnp.float32)
    grad_hidden = jnp.einsum(
        "ecd,efd->ecf", grad_expert, down_back, preferred_element_type=jnp.float32
    )
    slope = sigmoid_vals * (1.0 + gate_up[0] * (1.0 - sigmoid_vals))
    grad_gate_up = jnp.stack([grad_hidden * gate_up[1] * slope, grad_hidden * activated]).astype(
        jnp.bfloat16
    )
    gate_up_grad = jnp.einsum(
        "ecd,secf->sedf", expert_rows, grad_gate_up, preferred_element_type=jnp.float32
    )
    slot_input_grad = jnp.einsum(
        "secf,sedf->ecd", grad_gate_up, gate_back, preferred_element_type=jnp.float32
    ).reshape(NF * CAP, -1)
    grad_ffn_in = jnp.sum(jnp.where(retained[:, :, None], slot_input_grad[picker], 0.0), axis=1)
    gate_up_grad, down_grad = (
        lax.psum_scatter(gate_up_grad, "dp", scatter_dimension=2, tiled=True),
        lax.psum_scatter(down_grad, "dp", scatter_dimension=2, tiled=True),
    )
    grad_ffn_in, gate_grad_ffn = (
        lax.psum_scatter(grad_ffn_in, "tensor", scatter_dimension=0, tiled=True),
        lax.psum_scatter(gate_grad_ffn, "tensor", scatter_dimension=0, tiled=True),
    )
    copy_inner = jnp.sum(grad_out * normed_vals, axis=-1)
    const_inner = jnp.sum(grad_out[:, None, :] * const_out, axis=-1)
    choice_inner = jnp.where(local_ids == NF + 1, copy_inner[:, None], 0.0)
    for index in range(const_count):
        choice_inner = choice_inner + jnp.where(
            local_ids == NF + 2 + index, const_inner[:, index : index + 1], 0.0
        )
    gate_grad = gate_grad_ffn + choice_inner
    expert_range = jnp.arange(shares.shape[1])
    onehot = (local_ids[:, :, None] == expert_range[None, None, :]).astype(jnp.float32)
    grad_router = jnp.sum(onehot * gate_grad[:, :, None], axis=1)
    grad_logits = local_shares * (
        grad_router - jnp.sum(local_shares * grad_router, axis=-1, keepdims=True)
    )
    prior_vals = prior_logits.astype(jnp.float32)
    router_grad = jnp.dot(normed_vals.T, grad_logits, precision=highest)
    residual_grad = jnp.dot(prior_vals.T, grad_logits, precision=highest)
    prior_grad = jnp.dot(grad_logits, residual_weight.astype(jnp.float32).T, precision=highest)
    vector_inner = jnp.dot(grad_out, vectors.T, precision=highest)
    grad_mixing = const_share[:, :, None] * jnp.stack(
        [jnp.broadcast_to(copy_inner[:, None], vector_inner.shape), vector_inner], axis=-1
    )
    grad_blend = mixing * (grad_mixing - jnp.sum(mixing * grad_mixing, axis=-1, keepdims=True))
    const_gate_grad = jnp.einsum("gcj,gd->cjd", grad_blend, normed_vals, precision=highest)
    const_vector_grad = jnp.einsum(
        "gc,gd->cd", const_share * mixing[:, :, 1], grad_out, precision=highest
    )
    direct_share = copy_share + jnp.sum(const_share * mixing[:, :, 0], axis=1)
    grad_moe_in = (
        grad_ffn_in
        + jnp.dot(grad_logits, router_weight.astype(jnp.float32).T, precision=highest)
        + direct_share[:, None] * grad_out
        + jnp.einsum("gcj,cjd->gd", grad_blend, gate_mats, precision=highest)
    )
    norm_moe_grad = jnp.sum(grad_moe_in * resid * factor_moe, axis=0)
    grad_resid = grad_out + norm_back(grad_moe_in, resid, factor_moe, gain_moe)
    grad_mixed_out = grad_resid.astype(jnp.bfloat16)
    grad_attn_rows = lax.all_gather(grad_mixed_out, "tensor", axis=0, tiled=True)
    out_weight_grad = jnp.dot(mixed_rows.T, grad_attn_rows, preferred_element_type=jnp.float32)
    grad_mixed = jnp.dot(grad_attn_rows, out_full.T, preferred_element_type=jnp.float32).astype(
        jnp.bfloat16
    )
    grad_query, grad_keys, grad_values = lax.map(
        attend_back, (query, keys, values, piece_starts, log_total, grad_mixed.reshape(seq_shape))
    )
    grad_query = rotate(grad_query.reshape(group_rows, head_count, HD), cosine, -sine).reshape(
        group_rows, -1
    )
    grad_keys = rotate(grad_keys.reshape(group_rows, head_count, HD), cosine, -sine).reshape(
        group_rows, -1
    )
    grad_proj = jnp.stack([grad_query, grad_keys, grad_values.reshape(group_rows, -1)]).astype(
        jnp.bfloat16
    )
    qkv_grad = jnp.einsum("gd,cge->cde", attn_rows, grad_proj, preferred_element_type=jnp.float32)
    qkv_grad, out_weight_grad = (
        lax.psum_scatter(qkv_grad, "dp", scatter_dimension=1, tiled=True),
        lax.psum_scatter(out_weight_grad, "dp", scatter_dimension=1, tiled=True),
    )
    grad_attn_part = jnp.einsum(
        "cge,cde->gd", grad_proj, qkv_full, preferred_element_type=jnp.float32
    )
    grad_attn_in = lax.psum_scatter(
        grad_attn_part.astype(jnp.bfloat16), "tensor", scatter_dimension=0, tiled=True
    ).astype(jnp.float32)
    norm_attn_grad = jnp.sum(grad_attn_in * tok_vals * factor_attn, axis=0)
    input_grad = grad_resid + norm_back(grad_attn_in, tok_vals, factor_attn, gain_attn)
    summed = lax.psum(
        (
            norm_attn_grad,
            norm_moe_grad,
            router_grad,
            residual_grad,
            const_vector_grad,
            const_gate_grad,
        ),
        ("dp", "tensor"),
    )
    return (
        layer_out,
        input_grad,
        prior_grad,
        summed[0],
        qkv_grad,
        out_weight_grad,
        summed[1],
        summed[2],
        summed[3],
        summed[4],
        summed[5],
        gate_up_grad,
        down_grad,
    )


def on_device(
    dp,
    tensor,
    tokens,
    prior_logits,
    expert_ids,
    expert_ranks,
    piece_starts,
    norm_attn,
    qkv_weight,
    out_weight,
    norm_moe,
    router_weight,
    residual_weight,
    const_vectors,
    const_gates,
    w_gate_up,
    w_down,
    out_grad,
):
    rows, d = tokens.shape
    ne = router_weight.shape[1]
    packs = dp // NF
    groups = None if packs == 1 else [list(range(NF * r, NF * (r + 1))) for r in range(packs)]
    across = None if packs == 1 else [list(range(j, dp, NF)) for j in range(NF)]
    here = lax.axis_index("tensor")
    ids = lax.dynamic_slice_in_dim(expert_ids, here * rows, rows, 0)
    ranks = lax.dynamic_slice_in_dim(expert_ranks, here * rows, rows, 0)
    starts = lax.dynamic_slice_in_dim(piece_starts, here, 1, 0)
    ga, gm = norm_attn.astype(f32).reshape(1, d), norm_moe.astype(f32).reshape(1, d)
    cosine, sine = (jnp.asarray(t) for t in rotary_tables())
    prior = jnp.pad(prior_logits, ((0, 0), (0, LANES - ne)))
    wr = jnp.concatenate(
        [router_weight, jnp.zeros((d, Z0 - ne), bf16), const_gates.reshape(2 * NC, d).T,
         jnp.zeros((d, LANES - Z0 - 2 * NC), bf16)], axis=1)
    wres = jnp.pad(residual_weight, ((0, LANES - ne), (0, LANES - ne)))
    cv = const_vectors.astype(f32)

    w_attn = jnp.concatenate([qkv_weight, out_weight.T[None]], axis=0)
    w_down_t = w_down.transpose(0, 2, 1)[None]
    shard = w_down.shape[1]
    w_first, slab = prologue(w_gate_up, w_down_t, w_attn, tensor, 1)
    if packs > 1:
        w_attn = lax.all_gather(slab, "dp", axis=1, tiled=True)
        w_second = exchange_half(w_gate_up, w_down_t, 2)
    else:
        w_attn, w_second = gather_weights(slab, w_gate_up, w_down_t, 2)

    def whole(w):
        w = w.reshape(3, -1, w.shape[3])
        if packs > 1:
            w = lax.all_gather(w, "dp", axis=1, tiled=True, axis_index_groups=across)
        return lax.all_gather(w, "tensor", axis=0, tiled=False)

    w_first, w_second = whole(w_first), whole(w_second)

    heads = 16
    blocks = shape((NF, ROOM, d), bf16)
    q, k, v, mixed, lse, nattn, resid, nmoe, base, aux, pos, count, x_b, y_b, pay = pl.pallas_call(
        fwd_kernel,
        in_specs=[SM] + [VM] * 13,
        out_specs=[VM] * 12 + [ANY] * 3,
        out_shape=(
            shape((rows, d), bf16), shape((rows, d), bf16), shape((rows, d), bf16), shape((rows, d), bf16),
            shape((heads, rows), f32), shape((rows, d), bf16), shape((rows, d), f32), shape((rows, d), bf16),
            shape((rows, d), f32), shape((rows, LANES), f32), shape((NF, 1, rows), f32), shape((1, LANES), f32),
            blocks, blocks, shape((2 * NF, 1, ROOM), f32),
        ),
        scratch_shapes=[
            pltpu.VMEM((QT, 2 * QT), f32),
            pltpu.VMEM((NF, 1, rows), f32),
            pltpu.VMEM((NF, ROOM, d), bf16),
            pltpu.VMEM((NF, ROOM, d), bf16),
            pltpu.VMEM((2 * NF, 1, ROOM), f32),
            *send_scratch(),
            *send_scratch(),
            pltpu.SemaphoreType.DMA((2, 2 * (NF - 1))),
            pltpu.SemaphoreType.DMA((2,)),
        ],
        compiler_params=pltpu.CompilerParams(collective_id=3, has_side_effects=True, vmem_limit_bytes=60 << 20),
        cost_estimate=cost(40, 30, 10),
    )(starts, tokens, prior, ids, ranks, ga, gm, cosine, sine, w_attn, wr, wres, cv, out_grad)

    xc, yc, gc, eo, dx, dw_a, meta = experts_first(pay, x_b, y_b, w_first)
    out_b, dx_b, gg_b, dw_b = experts_second(meta, xc, yc, gc, eo, dx, w_second)

    def owned(dw):
        dw = lax.psum_scatter(dw, "tensor", scatter_dimension=0, tiled=False)
        if packs > 1:
            dw = lax.psum_scatter(dw, "dp", scatter_dimension=1, tiled=True, axis_index_groups=across)
        return dw.reshape(3, NF, -1, dw.shape[-1])

    dw_a = owned(dw_a)

    gmo, gres, pgrad, nmg, wrg, resg, cvg = pl.pallas_call(
        mid_kernel,
        in_specs=[ANY] * 2 + [VM] * 11,
        out_specs=[VM] * 7,
        out_shape=(
            shape((rows, d), bf16), shape((rows, d), f32), shape((rows, LANES), f32), shape((1, d), f32),
            shape((LANES, d), f32), shape((LANES, LANES), f32), shape((LANES, d), f32),
        ),
        scratch_shapes=[
            pltpu.VMEM((NF, ROOM, d), bf16),
            pltpu.VMEM((NF, 1, ROOM), f32),
            pltpu.VMEM((rows, d), f32),
            pltpu.VMEM((NF, rows), f32),
            *send_scratch(),
            pltpu.SemaphoreType.DMA((2, NF - 1)),
            pltpu.SemaphoreType.DMA((1,)),
        ],
        compiler_params=pltpu.CompilerParams(collective_id=4, has_side_effects=True, vmem_limit_bytes=60 << 20),
        cost_estimate=cost(4, 4),
    )(dx_b, gg_b, pos, out_grad, nmoe, resid, ids, aux, prior, wr, wres, cv, gm)
    dw_a, dw_b, gmo = lax.optimization_barrier((dw_a, dw_b, gmo))
    dw_b = owned(dw_b)
    igrad, wg, nag, layer_out = pl.pallas_call(
        bwd_kernel,
        in_specs=[SM] + [VM] * 13 + [ANY] + [VM] * 2,
        out_specs=[VM] * 4,
        out_shape=(shape((rows, d), f32), shape((4, d, d), bf16), shape((1, d), f32), shape((rows, d), bf16)),
        scratch_shapes=[
            pltpu.VMEM((rows, d), bf16),
            pltpu.VMEM((heads, rows), f32),
            pltpu.VMEM((rows // QT, 2 * QT, QT), f32),
            pltpu.VMEM((3, rows, d), bf16),
            pltpu.VMEM((rows, LANES), f32),
            pltpu.VMEM((rows, LANES), f32),
            pltpu.VMEM((rows, LANES), f32),
            pltpu.VMEM((NF, ROOM, d), bf16),
            *send_scratch(),
        ],
        compiler_params=pltpu.CompilerParams(collective_id=5, has_side_effects=True, vmem_limit_bytes=60 << 20),
        cost_estimate=cost(8, 4),
    )(starts, gmo, gres, mixed, q, k, v, lse, nattn, tokens, ga, cosine, sine, w_attn, out_b, pos, base)

    if packs > 1:
        wg = lax.psum_scatter(wg, "dp", scatter_dimension=1, tiled=True)
        wg = lax.psum_scatter(wg, "tensor", scatter_dimension=2, tiled=True).astype(f32)
        over = jnp.where(count > ROOM, 1.0, 0.0)
        wrg, cvg, resg, nmg, nag, over = lax.psum((wrg, cvg, resg, nmg, nag, over), ("dp", "tensor"))
        dw_a, dw_b = exchange8(dw_a, dw_b, 6)
    else:
        wg, small, dw_a, dw_b = finish(wg, dw_a, dw_b, wrg, cvg, resg, nmg, nag, count, tensor, 7)
        wrg, cvg, resg, nmg, nag = small[0:24], small[24:26], small[32:48, 0:LANES], small[26], small[27]
        over = small[28:29, 0:LANES]
    overflow = jnp.sum(over) > 0

    def roomy(args):
        return plain_on_device(*args)

    def packed(args):
        dw = jnp.concatenate([dw_a, dw_b], axis=-1).astype(f32)
        return (
            layer_out,
            igrad,
            pgrad[:, 0:ne],
            nag.reshape(d),
            wg[0:3],
            wg[3].T,
            nmg.reshape(d),
            wrg[0:ne].T,
            resg[0:ne, 0:ne],
            cvg[0:NC],
            wrg[Z0 : Z0 + 2 * NC].reshape(NC, 2, d),
            dw[0:2],
            dw[2].transpose(0, 2, 1),
        )

    args = (
        tokens, prior_logits, expert_ids, expert_ranks, piece_starts, norm_attn, qkv_weight, out_weight, norm_moe,
        router_weight, residual_weight, const_vectors, const_gates, w_gate_up, w_down, out_grad,
    )
    return lax.cond(overflow, roomy, packed, args)


def solution(mesh):
    body = functools.partial(on_device, mesh.shape["dp"], mesh.shape["tensor"])
    rows = P(("dp", "tensor"), None)
    return jax.shard_map(
        body,
        mesh=mesh,
        in_specs=(
            rows, rows, P("dp", None), P("dp", None), P("dp", None), P(), P(None, "dp", "tensor"), P("tensor", "dp"),
            P(), P(), P(), P(), P(), P(None, None, "dp", "tensor"), P(None, "tensor", "dp"), rows,
        ),
        out_specs=(
            rows, rows, rows, P(), P(None, "dp", "tensor"), P("tensor", "dp"), P(), P(), P(), P(), P(),
            P(None, None, "dp", "tensor"), P(None, "tensor", "dp"),
        ),
        check_vma=False,
    )
```

```python
import functools

import jax
import jax.numpy as jnp
import numpy as np
from jax import lax
from jax.experimental import pallas as pl
from jax.experimental.pallas import tpu as pltpu
from jax.sharding import PartitionSpec as P

HD = 64
NF = 8
NC = 2
SEQ = 1024
PIECE = 256
PIECES = 2
CAP = 768
EPS = 1e-06
QT = 256
LANES = 128
TM = 256
ROOM = 256
Z0 = 16
CHOSEN = 32
RES = 6

bf16 = jnp.bfloat16
f32 = jnp.float32
i32 = jnp.int32

VM = pl.BlockSpec(memory_space=pltpu.VMEM)
SM = pl.BlockSpec(memory_space=pltpu.SMEM)
ANY = pl.BlockSpec(memory_space=pl.ANY)


def nn(a, b):
    return lax.dot_general(a, b, (((1,), (0,)), ((), ())), preferred_element_type=f32)


def nt(a, b):
    return lax.dot_general(a, b, (((1,), (1,)), ((), ())), preferred_element_type=f32)


def tn(a, b):
    return lax.dot_general(a, b, (((0,), (0,)), ((), ())), preferred_element_type=f32)


def split(x):
    hi = x.astype(bf16)
    return hi, (x - hi.astype(f32)).astype(bf16)


def lanes(rows):
    return lax.broadcasted_iota(i32, (rows, LANES), 1)


def rot(x, cosine, sine):
    first = lanes(x.shape[0]) % HD < HD // 2
    other = jnp.where(first, pltpu.roll(x, LANES - HD // 2, 1), pltpu.roll(x, HD // 2, 1))
    return x * cosine + other * sine


def head_masks():
    low = lax.broadcasted_iota(i32, (1, LANES), 1) < HD
    a = jnp.where(low, 1.0, 0.0)
    return a, 1.0 - a


def rotary_tables():
    place = np.arange(SEQ, dtype=np.float32)
    half = HD // 2
    freqs = np.power(np.float32(10000.0), np.arange(half, dtype=np.float32) * np.float32(-2.0 / HD)).astype(np.float32)
    angles = (place[:, None] * freqs[None, :]).astype(np.float32).astype(np.float64)
    c, s = np.cos(angles).astype(np.float32), np.sin(angles).astype(np.float32)
    return np.concatenate([c, c, c, c], 1), np.concatenate([-s, s, -s, s], 1)


def window_bias(starts_ref, tile, width, transposed):
    shape = (width, QT) if transposed else (QT, width)
    qpos = lax.broadcasted_iota(i32, shape, 1 if transposed else 0) + tile * QT
    kpos = lax.broadcasted_iota(i32, shape, 0 if transposed else 1) + tile * QT
    seen = jnp.where(kpos <= qpos, 1, 0)
    for piece in range(PIECES):
        s = starts_ref[lax.axis_index("tensor"), piece]
        both = jnp.where(qpos >= s, 1, 0) * jnp.where(qpos < s + PIECE, 1, 0)
        both = both * jnp.where(kpos >= s, 1, 0) * jnp.where(kpos < s + PIECE, 1, 0)
        seen = jnp.maximum(seen, both)
    return jnp.where(seen > 0, 0.0, -1e30)


MESH = pl.DeviceIdType.MESH
GATHER_COPIES = 13
REDUCE_COPIES = 10


def flip(index, m):
    for bit in (1, 2, 4):
        if m & bit:
            index = index + bit - 2 * bit * (index // bit % 2)
    return index


def remote(src, dst, sems, n, axis, peer):
    return pltpu.make_async_remote_copy(
        src_ref=src,
        dst_ref=dst,
        send_sem=sems.at[0, n],
        recv_sem=sems.at[1, n],
        device_id={axis: peer},
        device_id_type=MESH,
    )


def greet(peers):
    barrier = pltpu.get_barrier_semaphore()
    for axis, peer in peers:
        pl.semaphore_signal(barrier, inc=1, device_id={axis: peer}, device_id_type=MESH)
    pl.semaphore_wait(barrier, len(peers))


def near_peers():
    me = lax.axis_index("dp")
    return [("dp", flip(me, m)) for m in (1, 2, 4)]


def far_peers(tensor):
    me = lax.axis_index("tensor")
    return [("tensor", (me + k) % tensor) for k in range(1, tensor)]


class Gather8:
    def __init__(self, src, dst, sems, own_sem):
        me = lax.axis_index("dp")
        slot = me % NF
        nx, ny, nc = flip(me, 2), flip(me, 4), flip(me, 1)
        sx, sy, sd = flip(slot, 2), flip(slot, 4), flip(slot, 6)
        self.own = pltpu.make_async_copy(src(None), dst(slot, None), own_sem)
        go = lambda n, s, d, peer: remote(s, d, sems, n, "dp", peer)
        on = lambda n, s, h, peer: go(n, dst(s, h), dst(s, h), peer)
        self.c = [
            go(0, src(0), dst(slot, 0), nx),
            go(1, src(1), dst(slot, 1), ny),
            go(2, src(1), dst(slot, 1), nx),
            go(3, src(0), dst(slot, 0), ny),
            go(4, src(None), dst(slot, None), nc),
            on(5, sx, 0, ny),
            on(6, sy, 1, nx),
            on(7, sx, 0, nc),
            on(8, sy, 1, nc),
            on(9, sx, 1, nc),
            on(10, sy, 0, nc),
            on(11, sd, 0, nc),
            on(12, sd, 1, nc),
        ]

    def begin(self):
        self.own.start()
        for n in range(5):
            self.c[n].start()

    def forward(self):
        for got, out in ((0, (5, 7)), (1, (6, 8))):
            self.c[got].wait_recv()
            for n in out:
                self.c[n].start()

    def share(self):
        for got, out in ((2, 9), (3, 10)):
            self.c[got].wait_recv()
            self.c[out].start()

    def last(self):
        for got, out in ((5, 11), (6, 12)):
            self.c[got].wait_recv()
            self.c[out].start()

    def end(self):
        for n in (4, 7, 8, 9, 10, 11, 12):
            self.c[n].wait_recv()
        for c in self.c:
            c.wait_send()
        self.own.wait()


def halves(ref, index, rows):
    half = rows // 2
    return lambda s, h: ref.at[s] if h is None else ref.at[s, pl.ds(h * half, half)]


def all_peers():
    me = lax.axis_index("dp")
    return [("dp", flip(me, m)) for m in range(1, NF)]


class Swap8:
    def __init__(self, src, dst, sems, own_sems):
        me = lax.axis_index("dp")
        slot = me % NF
        count = src.shape[0] // NF
        self.own = [
            pltpu.make_async_copy(src.at[NF * i + slot], dst.at[NF * i + slot], own_sems.at[i]) for i in range(count)
        ]
        self.c = [
            remote(
                src.at[NF * i + flip(slot, m)], dst.at[NF * i + slot], sems, (m - 1) * count + i, "dp", flip(me, m)
            )
            for m in range(1, NF)
            for i in range(count)
        ]

    def begin(self):
        for c in self.own + self.c:
            c.start()

    def end(self):
        for c in self.c:
            c.wait_recv()
        for c in self.c:
            c.wait_send()
        for c in self.own:
            c.wait()


def routes(ids_ref, ranks_ref, i):
    start = lax.axis_index("tensor") * SEQ + i * QT
    cols = pl.ds(pl.multiple_of(start, QT), QT)
    at = lax.broadcasted_iota(i32, (16, QT), 0)
    hit0, hit1 = (jnp.where(at == ids_ref[n : n + 1, cols], 1.0, 0.0) for n in range(2))
    keep0, keep1 = (jnp.where(ranks_ref[n : n + 1, cols] < CAP, 1.0, 0.0) for n in range(2))
    return hit0 + hit1, (hit0 * keep0 + hit1 * keep1) * jnp.where(at < NF, 1.0, 0.0)


def weights_kernel(
    gather, slab, gu_ref, dn_ref, ids_ref, ranks_ref, og_ref, out_ref, wx_ref, pos_ref, count_ref, ys_ref, sems, own_sem,
    *scratch,
):
    k, r, _ = slab.shape
    greet(all_peers())
    part = lambda h: pl.ds(0, k) if h is None else pl.ds(h * (k // 2), k // 2)
    if gather:
        g = Gather8(
            lambda h: slab.at[part(h)],
            lambda s, h: out_ref.at[part(h), pl.ds(pl.multiple_of(s * r, r), r), :],
            sems,
            own_sem,
        )
        g.begin()
    swap = Exchange8([gu_ref, dn_ref], wx_ref, 1, *scratch)
    swap.begin()
    upper = jnp.where(
        lax.broadcasted_iota(i32, (QT, QT), 0) < lax.broadcasted_iota(i32, (QT, QT), 1), 1.0, 0.0
    ).astype(bf16)
    taken = jnp.zeros((16, 1), f32)
    for i in range(SEQ // QT):
        _, kept = routes(ids_ref, ranks_ref, i)
        pos = jnp.where(kept > 0, nn(kept.astype(bf16), upper) + taken, -1.0)
        pos_ref[:, 0, i * QT : (i + 1) * QT] = pos[0:NF, :]
        taken = taken + jnp.sum(kept, axis=1, keepdims=True)
    count_ref[...] = jnp.broadcast_to(taken, (16, LANES))
    slot = lax.axis_index("dp") % NF

    def pack(*blocks):
        for m in blocks:
            ys_ref[m] = nn(hot_rows(pos_ref[flip(slot, m)]), og_ref[...]).astype(bf16)

    pack(0, 1)
    if gather:
        g.forward()
    pack(2, 3)
    if gather:
        g.share()
    pack(4, 5)
    if gather:
        g.last()
    pack(6, 7)
    if gather:
        g.end()
    swap.end()


def gather_weights(w, gate_up, down, ids, ranks, og, gather, cid):
    k, r, f = w.shape
    return pl.pallas_call(
        functools.partial(weights_kernel, gather),
        in_specs=[ANY] * 3 + [VM] * 3,
        out_specs=[ANY] * 2 + [VM] * 3,
        out_shape=(
            shape((k, NF * r, f), w.dtype), half_shape(gate_up), shape((NF, 1, og.shape[0]), f32),
            shape((16, LANES), f32), shape((NF, ROOM, og.shape[1]), bf16),
        ),
        scratch_shapes=[
            pltpu.SemaphoreType.DMA((2, GATHER_COPIES)),
            pltpu.SemaphoreType.DMA,
            *exchange_scratch(2),
        ],
        compiler_params=pltpu.CompilerParams(collective_id=cid, has_side_effects=True, vmem_limit_bytes=40 << 20),
        cost_estimate=cost(35, 10),
    )(w, gate_up, down, ids, ranks, og)


class Reduce8:
    def __init__(self, view, bufs, sems, lsems):
        self.own, self.away, self.ind, self.inx, self.iny = bufs
        me = lax.axis_index("dp")
        slot = me % NF
        half = self.ind.shape[0] // 2
        a, b = pl.ds(0, half), pl.ds(half, half)
        self.a, self.b = a, b
        nx, ny, nc = flip(me, 2), flip(me, 4), flip(me, 1)
        mine = [flip(slot, m) for m in (6, 2, 4)] + [slot]
        self.loads = [pltpu.make_async_copy(view(s), self.own.at[n % 2], lsems.at[n]) for n, s in enumerate(mine)]
        self.over = [remote(view(flip(s, 1)), self.away.at[n], sems, n, "dp", nc) for n, s in enumerate(mine)]
        go = lambda n, k, i, part, peer: remote(self.away.at[k, part], i.at[part], sems, n, "dp", peer)
        self.da, self.db = go(4, 0, self.ind, a, nx), go(5, 0, self.ind, b, ny)
        self.xa, self.yb = go(6, 1, self.inx, a, nx), go(7, 2, self.iny, b, ny)
        self.ya, self.xb = go(8, 2, self.iny, a, ny), go(9, 1, self.inx, b, nx)

    def load(self):
        self.loads[0].start()
        self.loads[1].start()

    def begin(self):
        for c in self.over:
            c.start()

    def add(self, n, part):
        self.away[n, part] = (self.own[n % 2, part].astype(f32) + self.away[n, part].astype(f32)).astype(bf16)

    def more(self, n, part):
        self.away[n, part] = (self.away[n, part].astype(f32) + self.ind[part].astype(f32)).astype(bf16)

    def ready(self, n):
        self.loads[n].wait()
        self.over[n].wait_recv()

    def first(self):
        self.ready(0)
        self.add(0, self.a)
        self.da.start()
        self.add(0, self.b)
        self.db.start()
        self.loads[2].start()

    def second(self):
        self.ready(1)
        self.add(1, self.a)
        self.xa.start()
        self.add(1, self.b)
        self.loads[3].start()
        self.ready(2)
        self.add(2, self.b)
        self.yb.start()
        self.add(2, self.a)

    def third(self):
        self.da.wait_recv()
        self.more(2, self.a)
        self.ya.start()
        self.db.wait_recv()
        self.more(1, self.b)
        self.xb.start()

    def end(self, write):
        self.ready(3)
        for part, first, second in ((self.a, self.xa, self.ya), (self.b, self.yb, self.xb)):
            first.wait_recv()
            second.wait_recv()
            total = self.own[1, part].astype(f32) + self.away[3, part].astype(f32)
            write(part, total + self.inx[part].astype(f32) + self.iny[part].astype(f32))

    def close(self):
        for c in self.over + [self.da, self.db, self.xa, self.yb, self.ya, self.xb]:
            c.wait_send()


def reduce_scratch(block):
    return [pltpu.VMEM((2, *block), bf16), pltpu.VMEM((4, *block), bf16)] + [pltpu.VMEM(block, bf16)] * 3 + [
        pltpu.SemaphoreType.DMA((2, REDUCE_COPIES)),
        pltpu.SemaphoreType.DMA((4,)),
    ]


class Exchange8:
    def __init__(self, srcs, dst, part, sems, own_sems):
        me = lax.axis_index("dp")
        slot = me % NF
        width = dst.shape[-1]

        def piece(src, e):
            return src.at[:, e] if part is None else src.at[:, e, :, pl.ds(part * width, width)]

        at, pieces = 0, []
        for src in srcs:
            pieces.append((src, pl.ds(at, src.shape[0])))
            at += src.shape[0]
        self.own = [
            pltpu.make_async_copy(piece(src, slot), dst.at[rows, slot], own_sems.at[i])
            for i, (src, rows) in enumerate(pieces)
        ]
        self.c = [
            remote(
                piece(src, flip(slot, m)), dst.at[rows, slot], sems, (m - 1) * len(srcs) + i, "dp", flip(me, m)
            )
            for m in (6, 7, 2, 3, 4, 5, 1)
            for i, (src, rows) in enumerate(pieces)
        ]

    def begin(self):
        for c in self.c + self.own:
            c.start()

    def end(self):
        for c in self.c:
            c.wait_recv()
        for c in self.c:
            c.wait_send()
        for c in self.own:
            c.wait()


class Send8:
    order = (6, 7, 2, 3, 4, 5, 1)

    def __init__(self, src, dst, sems, own_sem, packed):
        me = lax.axis_index("dp")
        slot = me % NF
        at = lambda m: src.at[m] if packed else src.at[flip(slot, m)]
        self.slot = slot
        self.own = pltpu.make_async_copy(at(0), dst.at[slot], own_sem)
        self.c = {m: remote(at(m), dst.at[slot], sems, m - 1, "dp", flip(me, m)) for m in self.order}

    def start(self, m):
        (self.c[m] if m else self.own).start()

    def begin(self):
        for m in (*self.order, 0):
            self.start(m)

    def got(self, m):
        if m:
            self.c[m].wait_recv()
        else:
            self.own.wait()

    def close(self):
        for c in self.c.values():
            c.wait_send()


def send_scratch():
    return [pltpu.SemaphoreType.DMA((2, NF - 1)), pltpu.SemaphoreType.DMA]


def half_shape(gate_up):
    _, groups, r, f = gate_up.shape
    return shape((3, groups, r, f // 2), bf16)


def exchange_scratch(n):
    return [pltpu.SemaphoreType.DMA((2, (NF - 1) * n)), pltpu.SemaphoreType.DMA((n,))]


def prologue_kernel(tensor, gu_ref, dn_ref, w_ref, out_ref, slab_ref, zbuf, zsems, *scratch):
    here = lax.axis_index("tensor")
    k, _, f = w_ref.shape
    greet(all_peers() + far_peers(tensor))
    copies = [
        remote(w_ref, zbuf.at[here], zsems, n, axis, peer) for n, (axis, peer) in enumerate(far_peers(tensor))
    ]
    for c in copies:
        c.start()
    swap = Exchange8([gu_ref, dn_ref], out_ref, 0, *scratch)
    swap.begin()
    zbuf[here] = w_ref[...]
    for c in copies:
        c.wait_recv()
    for c in range(k):
        for t in range(0, tensor, 2):
            both = jnp.concatenate([zbuf[t, c].astype(f32), zbuf[t + 1, c].astype(f32)], axis=-1)
            slab_ref[c, :, t * f : (t + 2) * f] = both.astype(bf16)
    swap.end()
    for c in copies:
        c.wait_send()


def prologue(gate_up, down, w, tensor, cid):
    k, r, f = w.shape
    return pl.pallas_call(
        functools.partial(prologue_kernel, tensor),
        in_specs=[ANY, ANY, VM],
        out_specs=[ANY, VM],
        out_shape=(half_shape(gate_up), shape((k, r, tensor * f), bf16)),
        scratch_shapes=[
            pltpu.VMEM((tensor, k, r, f), bf16),
            pltpu.SemaphoreType.DMA((2, tensor - 1)),
            *exchange_scratch(2),
        ],
        compiler_params=pltpu.CompilerParams(collective_id=cid, has_side_effects=True),
        cost_estimate=cost(25, 10),
    )(gate_up, down, w)


def exchange_kernel(src, dst, *scratch):
    greet(all_peers())
    swap = Exchange8([src], dst, None, *scratch)
    swap.begin()
    swap.end()


def exchange8(x, cid):
    return pl.pallas_call(
        exchange_kernel,
        in_specs=[ANY],
        out_specs=ANY,
        out_shape=shape(x.shape, x.dtype),
        scratch_shapes=exchange_scratch(1),
        compiler_params=pltpu.CompilerParams(collective_id=cid, has_side_effects=True),
        cost_estimate=cost(18, 10),
    )(x)


class Near:
    def __init__(self, have, got, sems):
        me = lax.axis_index("dp")
        self.have, self.got = have, got
        self.c = [remote(have.at[n], got.at[n], sems, n, "dp", flip(me, m)) for n, m in enumerate((1, 2, 4))]

    def begin(self):
        self.c[0].start()

    def step(self, n):
        self.c[n].wait_recv()
        self.have[n + 1] = self.have[n] + self.got[n]
        if n < 2:
            self.c[n + 1].start()

    def close(self):
        for c in self.c:
            c.wait_send()


def near_scratch(dims):
    return [pltpu.VMEM((4, *dims), f32), pltpu.VMEM((3, *dims), f32), pltpu.SemaphoreType.DMA((2, 3))]


class Far:
    def __init__(self, tensor, have, got, sems):
        self.tensor, self.have, self.got, self.here = tensor, have, got, lax.axis_index("tensor")
        self.c = [
            remote(have, got.at[self.here], sems, n, axis, peer) for n, (axis, peer) in enumerate(far_peers(tensor))
        ]

    def begin(self):
        for c in self.c:
            c.start()
        self.got[self.here] = self.have[...]

    def end(self):
        for c in self.c:
            c.wait_recv()
        total = self.got[0]
        for t in range(1, self.tensor):
            total = total + self.got[t]
        for c in self.c:
            c.wait_send()
        return total


def far_scratch(tensor, dims):
    return [pltpu.VMEM((tensor, *dims), f32), pltpu.SemaphoreType.DMA((2, tensor - 1))]


def final_kernel(
    tensor, comm, g_ref, gp_any, gres_any, tok_any, w_any, yr_any, base_any, pos_ref, par_ref, small_ref,
    out_ref, nag_ref, igrad_ref, layer_ref, total_ref,
    gp_ref, gres_ref, tok_ref, w_ref, yr_ref, base_ref, lsems, zf, zs, zr, *scratch,
):
    k, d, _ = g_ref.shape
    ntile = SEQ // QT
    pairs = (
        (gp_any, gp_ref), (w_any.at[pl.ds(0, 3)], w_ref), (tok_any, tok_ref), (gres_any, gres_ref), (yr_any, yr_ref),
        (base_any, base_ref),
    )
    loads = [pltpu.make_async_copy(src, dst, lsems.at[n]) for n, (src, dst) in enumerate(pairs)]
    if comm:
        here = lax.axis_index("tensor")
        r, f = out_ref.shape[1:]
        red = Reduce8(lambda s: g_ref.at[:, pl.ds(pl.multiple_of(s * r, r), r), :], scratch[:5], *scratch[5:7])
        zsems = scratch[7]
        sums = Near(*scratch[8:11])
        gains, smalls = Far(tensor, sums.have.at[3], *scratch[11:13]), Far(tensor, small_ref, *scratch[13:15])
        red.load()
        greet(near_peers() + far_peers(tensor))
        red.begin()
        smalls.begin()
    for c in loads:
        c.start()
    ga = par_ref[24:25, :].astype(f32)
    if comm:
        red.first()
        red.second()
    for c in loads[:4]:
        c.wait()
    nag = jnp.zeros((1, d), f32)
    for i in range(ntile):
        rows = pl.ds(i * QT, QT)
        gai = nt(gp_ref[0, rows, :], w_ref[0]) + nt(gp_ref[1, rows, :], w_ref[1])
        gai = gai + nt(gp_ref[2, rows, :], w_ref[2])
        x = tok_ref[rows, :].astype(f32)
        r1 = lax.rsqrt(jnp.mean(x * x, axis=-1, keepdims=True) + EPS)
        nag = nag + jnp.sum(gai * x * r1, axis=0, keepdims=True)
        scaled = gai * ga
        avg = jnp.mean(scaled * x, axis=-1, keepdims=True)
        igrad_ref[rows, :] = gres_ref[rows, :] + r1 * scaled - x * (r1 * r1 * r1 * avg)
        if comm and i == 0:
            red.third()
    if comm:
        sums.have[0] = nag
        sums.begin()
    else:
        nag_ref[...] = nag
        total_ref[...] = small_ref[...]
    for c in loads[4:]:
        c.wait()

    def layer(i):
        rows = pl.ds(i * QT, QT)
        total = base_ref[rows, :]
        for e in range(NF):
            total = total + tn(hot_rows(pos_ref[e, :, rows]), yr_ref[e])
        layer_ref[rows, :] = total.astype(bf16)

    def write(part, total):
        for t in range(tensor):
            zf[t, part] = total[:, :, t * f : (t + 1) * f]
            zs[t, part] = total[:, :, t * f : (t + 1) * f].astype(bf16)

    if not comm:
        for i in range(ntile):
            layer(i)
        return
    layer(0)
    sums.step(0)
    red.end(write)
    out_copies = [
        remote(zs.at[peer], zr.at[here], zsems, n, axis, peer) for n, (axis, peer) in enumerate(far_peers(tensor))
    ]
    for c in out_copies:
        c.start()
    sums.step(1)
    for i in range(1, ntile - 1):
        layer(i)
    sums.step(2)
    gains.begin()
    layer(ntile - 1)
    nag_ref[...] = gains.end()
    total_ref[...] = smalls.end()
    sums.close()
    zr[here] = jnp.zeros(zr.shape[1:], bf16)
    for c in out_copies:
        c.wait_recv()
    total = zf[here]
    for t in range(tensor):
        total = total + zr[t].astype(f32)
    out_ref[...] = total
    red.close()
    for c in out_copies:
        c.wait_send()


def finish(g, gp, gres, tokens, w, yr, base, pos, params, small, tensor, comm, cid):
    k, d, columns = g.shape
    rows = tokens.shape[0]
    r, f = (d // NF if comm else 8), columns // tensor
    once = pltpu.CompilerParams(vmem_limit_bytes=60 << 20)
    if comm:
        once = pltpu.CompilerParams(collective_id=cid, has_side_effects=True, vmem_limit_bytes=60 << 20)
    return pl.pallas_call(
        functools.partial(final_kernel, tensor, comm),
        in_specs=[ANY] * 7 + [VM] * 3,
        out_specs=[VM] * 5,
        out_shape=(
            shape((k, r, f), f32), shape((1, d), f32), shape((rows, d), f32), shape((rows, d), bf16),
            shape(small.shape, f32),
        ),
        scratch_shapes=[
            pltpu.VMEM(gp.shape, bf16),
            pltpu.VMEM((rows, d), f32),
            pltpu.VMEM((rows, d), bf16),
            pltpu.VMEM((3, d, columns), bf16),
            pltpu.VMEM(yr.shape, bf16),
            pltpu.VMEM((rows, d), f32),
            pltpu.SemaphoreType.DMA((6,)),
            pltpu.VMEM((tensor, k, r, f), f32),
            pltpu.VMEM((tensor, k, r, f), bf16),
            pltpu.VMEM((tensor, k, r, f), bf16),
            *reduce_scratch((k, r, columns)),
            pltpu.SemaphoreType.DMA((2, tensor - 1)),
            *near_scratch((1, d)),
            *far_scratch(tensor, (1, d)),
            *far_scratch(tensor, small.shape),
        ],
        compiler_params=once,
        cost_estimate=cost(8, 4),
    )(g, gp, gres, tokens, w, yr, base, pos, params, small)


def fwd_kernel(
    starts_ref, tok_ref, prior_ref, ids_ref, ranks_ref, par_ref, cos_ref, sin_ref, w_ref, pos_ref, ys,
    q_ref, k_ref, v_ref, mixed_ref, lse_ref, nattn_ref, resid_ref, nmoe_ref, base_ref, aux_ref, xr_ref, yr_ref, payr_ref,
    bias_ref, gate_ref, xs, pay, wr_ref, *scratch,
):
    greet(all_peers())
    send_x, send_y = Send8(xs, xr_ref, *scratch[0:2], True), Send8(ys, yr_ref, *scratch[2:4], True)
    swap = Swap8(pay, payr_ref, *scratch[4:6])
    send_y.begin()
    lane = lanes(QT)
    router_rows(par_ref, wr_ref)
    wres = par_ref[32:48, 0:LANES]
    d = tok_ref.shape[1]
    pairs = d // LANES
    ntile = SEQ // QT
    ga, gm = par_ref[24:25, :].astype(f32), par_ref[25:26, :].astype(f32)
    cv = par_ref[26:28, :].astype(f32)
    mask_a, mask_b = head_masks()
    mask16 = (mask_a.astype(bf16), mask_b.astype(bf16))

    def project(i, carry):
        rows = pl.ds(pl.multiple_of(i * QT, QT), QT)
        x = tok_ref[rows, :].astype(f32)
        r1 = lax.rsqrt(jnp.mean(x * x, axis=-1, keepdims=True) + EPS)
        n = (x * r1 * ga).astype(bf16)
        nattn_ref[rows, :] = n
        cosine, sine = cos_ref[rows, :], sin_ref[rows, :]
        for c, out in ((0, q_ref), (1, k_ref), (2, v_ref)):
            proj = nn(n, w_ref[c])
            for p in range(pairs):
                part = proj[:, p * LANES : (p + 1) * LANES]
                if c < 2:
                    part = rot(part, cosine, sine)
                part = part.astype(bf16)
                if c == 0:
                    part = part * jnp.array(HD**-0.5, bf16)
                out[rows, p * LANES : (p + 1) * LANES] = part
        return carry

    lax.fori_loop(0, ntile, project, 0)

    for i in range(ntile):
        lo = i * QT
        width = min(SEQ, lo + 2 * QT) - lo
        rows = pl.ds(lo, QT)
        bias_ref[:, :width] = window_bias(starts_ref, i, width, False)

        def pair(p, lse):
            cols = pl.ds(pl.multiple_of(p * LANES, LANES), LANES)
            q2 = q_ref[rows, cols]
            outs = []
            for h in range(2):
                qh = q2 * mask16[h]
                sb = nt(qh, k_ref[lo : lo + width, cols]) + bias_ref[:, :width]
                m = jnp.max(sb, axis=-1, keepdims=True)
                if lo:
                    sa = nt(qh, k_ref[0:lo, cols])
                    m = jnp.maximum(m, jnp.max(sa, axis=-1, keepdims=True))
                pb = jnp.exp(sb - m)
                total = jnp.sum(pb, axis=-1, keepdims=True)
                acc = nn(pb.astype(bf16), v_ref[lo : lo + width, cols])
                if lo:
                    pa = jnp.exp(sa - m)
                    total = total + jnp.sum(pa, axis=-1, keepdims=True)
                    acc = acc + nn(pa.astype(bf16), v_ref[0:lo, cols])
                outs.append(acc / total)
                lse = jnp.where(lane == 2 * p + h, m + jnp.log(total), lse)
            mixed_ref[rows, cols] = (outs[0] * mask_a + outs[1] * mask_b).astype(bf16)
            return lse

        lse = lax.fori_loop(0, pairs, pair, jnp.zeros((QT, LANES), f32))
        lse_ref[:, rows] = lse.T[0 : lse_ref.shape[0], :]

        x = tok_ref[rows, :].astype(f32)
        resid = x + nt(mixed_ref[rows, :], w_ref[3])
        resid_ref[rows, :] = resid
        r2 = lax.rsqrt(jnp.mean(resid * resid, axis=-1, keepdims=True) + EPS)
        nm = (resid * r2 * gm).astype(bf16)
        nmoe_ref[rows, :] = nm
        raw = nt(nm, wr_ref[...])
        logits = raw + tn(prior_ref[:, rows], wres)
        logits = jnp.where(lane < NF + 2 + NC, logits, -1e30)
        e = jnp.exp(logits - jnp.max(logits, axis=-1, keepdims=True))
        shares = e / jnp.sum(e, axis=-1, keepdims=True)
        chosen, kept = routes(ids_ref, ranks_ref, i)
        gate_ref[:, 0, rows] = shares.T[0:NF, :] * kept[0:NF, :]
        chosen = jnp.concatenate([chosen, jnp.zeros((LANES - 16, QT), f32)], axis=0).T
        gates = shares * chosen
        nv = nm.astype(f32)
        aux = jnp.where(lane < NF + 2 + NC, shares, 0.0) + pltpu.roll(chosen, CHOSEN, 1)
        direct = gates[:, NF + 1 : NF + 2]
        others = None
        for c in range(NC):
            z0, z1 = raw[:, Z0 + 2 * c : Z0 + 2 * c + 1], raw[:, Z0 + 2 * c + 1 : Z0 + 2 * c + 2]
            m0, m1 = 1.0 / (1.0 + jnp.exp(z1 - z0)), 1.0 / (1.0 + jnp.exp(z0 - z1))
            aux = jnp.where(lane == Z0 + 2 * c, m0, aux)
            aux = jnp.where(lane == Z0 + 2 * c + 1, m1, aux)
            w = gates[:, NF + 2 + c : NF + 3 + c]
            direct = direct + w * m0
            term = (w * m1) * cv[c : c + 1, :]
            others = term if others is None else others + term
        aux_ref[rows, :] = aux
        base_ref[rows, :] = resid + direct * nv + others

    for m in (*Send8.order, 0):
        e = flip(send_x.slot, m)
        place = pos_ref[e]
        hot = hot_rows(place)
        xs[m] = nn(hot, nmoe_ref[...]).astype(bf16)
        send_x.start(m)
        pay[e] = jnp.sum(nt(split_rows(gate_ref[e]), hot), axis=0, keepdims=True)
        filled = jnp.minimum(jnp.max(place, axis=1, keepdims=True) + 1.0, float(ROOM))
        pay[NF + e] = jnp.broadcast_to(filled, (1, ROOM))
    swap.begin()
    for send in (send_y, send_x):
        for m in (*Send8.order, 0):
            send.got(m)
        send.close()
    swap.end()


def mid_kernel(
    dxb_ref, ggb_ref, pos_ref, og_ref, nmoe_ref, resid_ref, aux_ref, prior_ref, par_ref, count_ref,
    gmo_ref, gres_ref, pgrad_ref, small_ref,
    dxr, ggr, dx_ref, gg_ref, inner_ref, extra_ref, wr_ref, resg_ref, *scratch,
):
    greet(all_peers())
    send, swap = Send8(dxb_ref, dxr, *scratch[0:2], False), Swap8(ggb_ref, ggr, *scratch[2:4])
    swap.begin()
    send.begin()
    gm, cv = par_ref[25:26, :].astype(f32), par_ref[26:28, :].astype(f32)
    wres = par_ref[32:48, 0:LANES]
    router_rows(par_ref, wr_ref)
    lane = lanes(QT)
    small_ref[...] = jnp.zeros_like(small_ref)
    resg_ref[...] = jnp.zeros_like(resg_ref)
    small_ref[28:29, 0:LANES] = jnp.max(jnp.where(count_ref[...] > ROOM, 1.0, 0.0), axis=0, keepdims=True)

    def ahead(i, carry):
        rows = pl.ds(pl.multiple_of(i * QT, QT), QT)
        g16 = og_ref[rows, :]
        g, nv = g16.astype(f32), nmoe_ref[rows, :].astype(f32)
        x = resid_ref[rows, :]
        aux = aux_ref[rows, :]
        chosen = jnp.where(lane < 16, pltpu.roll(aux, LANES - CHOSEN, 1), 0.0)
        gates = jnp.where(lane < NF + 2 + NC, aux, 0.0) * chosen
        copy_inner = jnp.sum(g * nv, axis=-1, keepdims=True)
        inner = jnp.where(lane == NF + 1, copy_inner, 0.0)
        direct = gates[:, NF + 1 : NF + 2]
        extra = jnp.where(lane == 1, lax.rsqrt(jnp.mean(x * x, axis=-1, keepdims=True) + EPS), 0.0)
        cvw = jnp.zeros((QT, LANES), f32)
        for c in range(NC):
            m0, m1 = aux[:, Z0 + 2 * c : Z0 + 2 * c + 1], aux[:, Z0 + 2 * c + 1 : Z0 + 2 * c + 2]
            v_inner = jnp.sum(g * cv[c : c + 1, :], axis=-1, keepdims=True)
            mean = m0 * copy_inner + m1 * v_inner
            inner = jnp.where(lane == NF + 2 + c, mean, inner)
            w = gates[:, NF + 2 + c : NF + 3 + c]
            direct = direct + w * m0
            extra = jnp.where(lane == Z0 + 2 * c, m0 * (w * copy_inner - w * mean), extra)
            extra = jnp.where(lane == Z0 + 2 * c + 1, m1 * (w * v_inner - w * mean), extra)
            cvw = jnp.where(lane == c, w * m1, cvw)
        inner_ref[rows, :] = inner
        extra_ref[rows, :] = jnp.where(lane == 0, direct, extra)
        cv_hi, cv_lo = split(cvw)
        small_ref[24:26, :] += tn(cv_hi, g16)[0:NC] + tn(cv_lo, g16)[0:NC]
        return carry

    lax.fori_loop(0, SEQ // QT, ahead, 0)
    swap.end()
    for n, m in enumerate((0, 1, 2, 3, 4, 5, 6, 7)):
        send.got(m)
        e = flip(send.slot, m)
        hot = hot_rows(pos_ref[e])
        gg_ref[pl.ds(e, 1), :] = jnp.sum(nn(split_rows(ggr[e]), hot), axis=0, keepdims=True)
        part = tn(hot, dxr[e])
        if n:
            dx_ref[...] += part
        else:
            dx_ref[...] = part
    send.close()

    def tile(i, carry):
        rows = pl.ds(pl.multiple_of(i * QT, QT), QT)
        g, n16 = og_ref[rows, :].astype(f32), nmoe_ref[rows, :]
        x = resid_ref[rows, :]
        aux, extra = aux_ref[rows, :], extra_ref[rows, :]
        direct, r2 = extra[:, 0:1], extra[:, 1:2]
        shares = jnp.where(lane < NF + 2 + NC, aux, 0.0)
        chosen = jnp.where(lane < 16, pltpu.roll(aux, LANES - CHOSEN, 1), 0.0)
        inner = jnp.concatenate([gg_ref[:, rows], jnp.zeros((LANES - NF, QT), f32)], axis=0).T
        grad_router = (inner + inner_ref[rows, :]) * chosen
        glog = shares * (grad_router - jnp.sum(shares * grad_router, axis=-1, keepdims=True))
        both_hi, both_lo = split(glog + jnp.where(lane >= Z0, extra, 0.0))
        log_hi, log_lo = split(glog)
        pgrad_ref[:, rows] = nt(wres, log_hi) + nt(wres, log_lo)
        small_ref[0:24, :] += tn(both_hi, n16)[0:24] + tn(both_lo, n16)[0:24]
        resg_ref[...] += nn(prior_ref[:, rows], log_hi) + nn(prior_ref[:, rows], log_lo)
        gmi = dx_ref[rows, :] + direct * g + nn(both_hi, wr_ref[...]) + nn(both_lo, wr_ref[...])
        small_ref[26:27, :] += jnp.sum(gmi * x * r2, axis=0, keepdims=True)
        scaled = gmi * gm
        avg = jnp.mean(scaled * x, axis=-1, keepdims=True)
        gres = g + r2 * scaled - x * (r2 * r2 * r2 * avg)
        gres_ref[rows, :] = gres
        gmo_ref[rows, :] = gres.astype(bf16)
        return carry

    lax.fori_loop(0, SEQ // QT, tile, 0)
    for n in range(NF + 2 + NC):
        at = n % RES * LANES
        small_ref[29 + n // RES : 30 + n // RES, at : at + LANES] = resg_ref[n : n + 1, :]


def bwd_kernel(
    starts_ref, gmo_ref, mixed_ref, q_ref, k_ref, v_ref, lse_ref, nattn_ref, cos_ref, sin_ref, wo_ref, small_ref,
    outb_ref, dw_ref,
    wg_ref, gp_ref, outr_ref, total_ref, dwx_ref,
    do_ref, delta_ref, bias_ref, dk_ref, dv_ref, dq_ref, *scratch,
):
    send = Send8(outb_ref, outr_ref, *scratch[0:2], False)
    sums = Near(*scratch[2:5])
    sums.have[0] = small_ref[...]
    greet(all_peers())
    sums.begin()
    send.begin()
    swap = Exchange8([dw_ref], dwx_ref, None, *scratch[5:7])
    swap.begin()
    d = mixed_ref.shape[1]
    pairs = d // LANES
    ntile = SEQ // QT
    mask_a, mask_b = head_masks()
    mask16 = (mask_a.astype(bf16), mask_b.astype(bf16))
    maskf = (mask_a, mask_b)
    heads = delta_ref.shape[0]
    pick = jnp.where(
        lax.broadcasted_iota(i32, (heads, d), 1) // HD == lax.broadcasted_iota(i32, (heads, d), 0), 1.0, 0.0
    ).astype(bf16)

    def start(i, carry):
        rows = pl.ds(pl.multiple_of(i * QT, QT), QT)
        do = nn(gmo_ref[rows, :], wo_ref[0]).astype(bf16)
        do_ref[rows, :] = do
        hi, lo = split(do.astype(f32) * mixed_ref[rows, :].astype(f32))
        delta_ref[:, rows] = nt(pick, hi) + nt(pick, lo)
        return carry

    lax.fori_loop(0, ntile, start, 0)
    sums.step(0)
    wg_ref[3] = tn(gmo_ref[...], mixed_ref[...]).astype(wg_ref.dtype)
    for i in range(ntile):
        width = min(SEQ, (i + 2) * QT) - i * QT
        bias_ref[i, 0:width, :] = window_bias(starts_ref, i, width, True)

    def pair(p, carry):
        cols = pl.ds(pl.multiple_of(p * LANES, LANES), LANES)
        dk_ref[...] = jnp.zeros_like(dk_ref)
        dv_ref[...] = jnp.zeros_like(dv_ref)
        for i in range(ntile):
            lo = i * QT
            width = min(SEQ, lo + 2 * QT) - lo
            rows = pl.ds(lo, QT)
            q2, do2 = q_ref[rows, cols], do_ref[rows, cols]
            dq = jnp.zeros((QT, LANES), f32)
            for h in range(2):
                qh, doh = q2 * mask16[h], do2 * mask16[h]
                lse, delta = lse_ref[pl.ds(2 * p + h, 1), rows], delta_ref[pl.ds(2 * p + h, 1), rows]
                spans = [(lo, width, True)] + ([(0, lo, False)] if lo else [])
                for at, size, masked in spans:
                    k2 = k_ref[at : at + size, cols]
                    s = nt(k2, qh)
                    if masked:
                        s = s + bias_ref[i, 0:size, :]
                    prob = jnp.exp(s - lse)
                    ds = (prob * (nt(v_ref[at : at + size, cols], doh) - delta)).astype(bf16)
                    dv_ref[at : at + size, :] += nn(prob.astype(bf16), doh)
                    dk_ref[at : at + size, :] += nn(ds, qh)
                    dq = dq + tn(ds, k2) * maskf[h]
            dq_ref[rows, :] = dq * HD**-0.5
        cosine, sine = cos_ref[...], -sin_ref[...]
        gp_ref[0, :, cols] = rot(dq_ref[...], cosine, sine).astype(bf16)
        gp_ref[1, :, cols] = rot(dk_ref[...], cosine, sine).astype(bf16)
        gp_ref[2, :, cols] = dv_ref[...].astype(bf16)
        return carry

    sums.step(1)
    lax.fori_loop(0, pairs, pair, 0)
    sums.step(2)
    for c in range(3):
        wg_ref[c] = tn(nattn_ref[...], gp_ref[c]).astype(wg_ref.dtype)
    for m in range(NF):
        send.got(m)
    send.close()
    swap.end()
    total_ref[...] = sums.have[3]
    sums.close()


def ffn_tile(x, gate, y, w_ref, acc, eo, dx):
    dy = y.astype(f32)
    ge = (gate * dy).astype(bf16)
    x_t, ge_t = x.T, ge.T
    for c in range(w_ref.shape[0]):
        wg, wu, wd = w_ref[c, 0], w_ref[c, 1], w_ref[c, 2]
        gv, uv = nn(x, wg), nn(x, wu)
        gh = nn(ge, wd)
        sig = 1.0 / (1.0 + jnp.exp(-gv))
        act = gv * sig
        hid = (act * uv).astype(bf16)
        eo = eo + nt(hid, wd)
        gg = (gh * uv * (sig * (1.0 + gv * (1.0 - sig)))).astype(bf16)
        gu = (gh * act).astype(bf16)
        dx = dx + nt(gg, wg) + nt(gu, wu)
        acc[c, 0] += nn(x_t, gg)
        acc[c, 1] += nn(x_t, gu)
        acc[c, 2] += nn(ge_t, hid)
    return eo, dx


def first_kernel(pay_ref, x_ref, y_ref, w_ref, xc_ref, yc_ref, gc_ref, eo_ref, dx_ref, dw_ref, meta_ref, acc):
    d = x_ref.shape[2]
    gates = [pay_ref[g] for g in range(NF)] + [jnp.zeros((LANES - NF, ROOM), f32)]
    columns = jnp.concatenate(gates, axis=0).T
    off = jnp.int32(0)
    for g in range(NF):
        rows = pl.ds(pl.multiple_of(off, 16), ROOM)
        xc_ref[rows, :] = x_ref[g]
        yc_ref[rows, :] = y_ref[g]
        gc_ref[rows, :] = jnp.broadcast_to(columns[:, g : g + 1], (ROOM, LANES))
        meta_ref[g] = off
        off = off + (jnp.max(pay_ref[NF + g]).astype(i32) + 15) // 16 * 16
    rows = pl.ds(pl.multiple_of(off, 16), TM)
    xc_ref[rows, :] = jnp.zeros((TM, d), bf16)
    yc_ref[rows, :] = jnp.zeros((TM, d), bf16)
    gc_ref[rows, :] = jnp.zeros((TM, LANES), f32)
    tiles = jnp.maximum((off + TM - 1) // TM, 1)
    meta_ref[NF] = tiles
    acc[...] = jnp.zeros_like(acc)
    zero = jnp.zeros((TM, d), f32)

    def tile(t, carry):
        rows = pl.ds(pl.multiple_of(t * TM, TM), TM)
        eo_ref[rows, :], dx_ref[rows, :] = ffn_tile(
            xc_ref[rows, :], gc_ref[rows, 0:1], yc_ref[rows, :], w_ref, acc, zero, zero
        )
        return carry

    lax.fori_loop(0, tiles, tile, 0)
    dw_ref[...] = acc[...].astype(bf16)


def second_kernel(
    meta_ref, xc_any, yc_any, gc_any, eo_any, dx_any, w_any, outb_ref, dxb_ref, ggb_ref, dw_ref,
    xc_ref, yc_ref, gc_ref, eo_ref, dx_ref, w_ref, outs, dxs, ggs, acc, sems, wsem,
):
    d = xc_ref.shape[1]
    tiles = meta_ref[NF]
    weights = pltpu.make_async_copy(w_any, w_ref, wsem)
    weights.start()

    def copies(t):
        rows = pl.ds(pl.multiple_of(t * TM, TM), TM)
        pairs = ((xc_any, xc_ref), (yc_any, yc_ref), (gc_any, gc_ref), (eo_any, eo_ref), (dx_any, dx_ref))
        return [pltpu.make_async_copy(a.at[rows, :], b.at[rows, :], sems.at[n, t]) for n, (a, b) in enumerate(pairs)]

    def begin(t, carry):
        for c in copies(t):
            c.start()
        return carry

    lax.fori_loop(0, tiles, begin, 0)
    acc[...] = jnp.zeros_like(acc)
    rows = pl.ds(pl.multiple_of(tiles * TM, TM), ROOM)
    outs[rows, :] = jnp.zeros((ROOM, d), bf16)
    dxs[rows, :] = jnp.zeros((ROOM, d), bf16)
    ggs[rows, :] = jnp.zeros((ROOM, LANES), f32)
    weights.wait()

    def tile(t, carry):
        rows = pl.ds(pl.multiple_of(t * TM, TM), TM)
        for c in copies(t):
            c.wait()
        gate, y = gc_ref[rows, 0:1], yc_ref[rows, :]
        eo, dx = ffn_tile(xc_ref[rows, :], gate, y, w_ref, acc, eo_ref[rows, :], dx_ref[rows, :])
        outs[rows, :] = (gate * eo).astype(bf16)
        dxs[rows, :] = dx.astype(bf16)
        ggs[rows, :] = jnp.broadcast_to(jnp.sum(y.astype(f32) * eo, axis=1, keepdims=True), (TM, LANES))
        return carry

    lax.fori_loop(0, tiles, tile, 0)
    lane = lanes(ROOM)
    columns = jnp.zeros((ROOM, LANES), f32)
    for g in range(NF):
        rows = pl.ds(pl.multiple_of(meta_ref[g], 16), ROOM)
        outb_ref[g] = outs[rows, :]
        dxb_ref[g] = dxs[rows, :]
        columns = jnp.where(lane == g, ggs[rows, :], columns)
    ggb_ref[:, 0, :] = columns.T[0:NF, :]
    dw_ref[...] = acc[...].astype(bf16)


def experts_first(pay, x, y, w):
    groups, _, d = x.shape
    total = groups * ROOM + TM
    return pl.pallas_call(
        first_kernel,
        in_specs=[VM] * 4,
        out_specs=[VM] * 6 + [SM],
        out_shape=(
            shape((total, d), bf16), shape((total, d), bf16), shape((total, LANES), f32), shape((total, d), f32),
            shape((total, d), f32), shape(w.shape, bf16), shape((NF + 1,), i32),
        ),
        scratch_shapes=[pltpu.VMEM(w.shape, f32)],
        compiler_params=pltpu.CompilerParams(vmem_limit_bytes=60 << 20),
        cost_estimate=cost(22, 25),
    )(pay, x, y, w)


def experts_second(meta, xc, yc, gc, eo, dx, w):
    total, d = xc.shape
    blocks = shape((NF, ROOM, d), bf16)
    room = total + ROOM
    return pl.pallas_call(
        second_kernel,
        in_specs=[SM] + [ANY] * 6,
        out_specs=[VM] * 4,
        out_shape=(blocks, blocks, shape((NF, 1, ROOM), f32), shape(w.shape, bf16)),
        scratch_shapes=[
            pltpu.VMEM((total, d), bf16),
            pltpu.VMEM((total, d), bf16),
            pltpu.VMEM((total, LANES), f32),
            pltpu.VMEM((total, d), f32),
            pltpu.VMEM((total, d), f32),
            pltpu.VMEM(w.shape, bf16),
            pltpu.VMEM((room, d), bf16),
            pltpu.VMEM((room, d), bf16),
            pltpu.VMEM((room, LANES), f32),
            pltpu.VMEM(w.shape, f32),
            pltpu.SemaphoreType.DMA((5, total // TM)),
            pltpu.SemaphoreType.DMA,
        ],
        compiler_params=pltpu.CompilerParams(vmem_limit_bytes=60 << 20),
        cost_estimate=cost(22, 25),
    )(meta, xc, yc, gc, eo, dx, w)


def router_rows(par_ref, wr_ref):
    wr_ref[...] = jnp.zeros_like(wr_ref)
    wr_ref[0:16, :] = par_ref[0:16, :]
    wr_ref[16:32, :] = jnp.where(
        lax.broadcasted_iota(i32, (16, par_ref.shape[1]), 0) < 2 * NC, par_ref[16:32, :].astype(f32), 0.0
    ).astype(bf16)


def hot_rows(pos):
    slot = lax.broadcasted_iota(i32, (ROOM, pos.shape[1]), 0).astype(f32)
    return jnp.where(slot == pos, 1.0, 0.0).astype(bf16)


def split_rows(row):
    hi = row.astype(bf16).astype(f32)
    mid = (row - hi).astype(bf16).astype(f32)
    at = lax.broadcasted_iota(i32, (8, row.shape[1]), 0)
    out = jnp.where(at == 0, hi, jnp.where(at == 1, mid, jnp.where(at == 2, row - hi - mid, 0.0)))
    return out.astype(bf16)


def shape(dims, dtype):
    return jax.ShapeDtypeStruct(dims, dtype)


def cost(gflop, mbytes, mexp=0):
    return pl.CostEstimate(flops=int(gflop * 1e9), bytes_accessed=int(mbytes * 1e6), transcendentals=int(mexp * 1e6))


def rms_factor(values):
    return lax.rsqrt(jnp.mean(values * values, axis=-1, keepdims=True) + EPS)


def norm_back(grad, values, factor, gain):
    scaled = grad * gain
    inner = jnp.mean(scaled * values, axis=-1, keepdims=True)
    return factor * scaled - values * factor * factor * factor * inner


def rotary(positions, width):
    place = (jnp.arange(positions) % SEQ).astype(jnp.float32)
    freqs = jnp.power(10000.0, jnp.arange(width // 2).astype(jnp.float32) * (-2.0 / width))
    angles = place[:, None] * freqs[None, :]
    return (jnp.cos(angles)[:, None, :], jnp.sin(angles)[:, None, :])


def rotate(values, cosine, sine):
    half = values.shape[-1] // 2
    front = values[..., :half]
    behind = values[..., half:]
    return jnp.concatenate(
        [front * cosine - behind * sine, behind * cosine + front * sine], axis=-1
    )


def visible(starts):
    position = jnp.arange(SEQ)
    piece_of = jnp.zeros((SEQ,), jnp.int32)
    for index in range(starts.shape[0]):
        inside = (position >= starts[index]) & (position < starts[index] + PIECE)
        piece_of = jnp.where(inside, index + 1, piece_of)
    causal = position[None, :] <= position[:, None]
    same_piece = (piece_of[:, None] > 0) & (piece_of[:, None] == piece_of[None, :])
    return causal | same_piece


def dispatch(route_ids, route_ranks):
    group_rows = route_ids.shape[0]
    retained = (route_ids < NF) & (route_ranks < CAP)
    target = jnp.where(retained, route_ids * CAP + route_ranks, NF * CAP)
    token_index = jnp.broadcast_to(
        jnp.arange(group_rows, dtype=jnp.int32)[:, None], route_ids.shape
    )
    slot_token = (
        jnp.zeros((NF * CAP + 1,), jnp.int32)
        .at[target.reshape(-1)]
        .set(token_index.reshape(-1))[: NF * CAP]
    )
    filled = jnp.zeros((NF * CAP + 1,), jnp.float32).at[target.reshape(-1)].set(1.0)[: NF * CAP]
    return (retained, target, slot_token, filled)


def masked_scores(query, keys, starts):
    scores = jnp.einsum("qhd,khd->hqk", query, keys, preferred_element_type=jnp.float32) * HD ** (
        -0.5
    )
    return jnp.where(visible(starts)[None], scores, -1e30)


def attend_block(parts):
    query, keys, values, starts = parts
    scores = masked_scores(query, keys, starts)
    row_max = jnp.max(scores, axis=-1, keepdims=True)
    denominator = jnp.sum(jnp.exp(scores - row_max), axis=-1, keepdims=True)
    log_total = row_max + jnp.log(denominator)
    shares = jnp.exp(scores - log_total).astype(jnp.bfloat16)
    mixed = jnp.einsum("hqk,khd->qhd", shares, values, preferred_element_type=jnp.float32)
    return (mixed.astype(jnp.bfloat16), log_total)


def attend_back(parts):
    query, keys, values, starts, log_total, grad_out = parts
    shares = jnp.exp(masked_scores(query, keys, starts) - log_total)
    grad_shares = jnp.einsum("qhd,khd->hqk", grad_out, values, preferred_element_type=jnp.float32)
    centre = jnp.sum(shares * grad_shares, axis=-1, keepdims=True)
    grad_scores = (shares * (grad_shares - centre)).astype(jnp.bfloat16)
    factor = HD ** (-0.5)
    grad_query = (
        jnp.einsum("hqk,khd->qhd", grad_scores, keys, preferred_element_type=jnp.float32) * factor
    )
    grad_keys = (
        jnp.einsum("hqk,qhd->khd", grad_scores, query, preferred_element_type=jnp.float32) * factor
    )
    grad_values = jnp.einsum(
        "hqk,qhd->khd", shares.astype(jnp.bfloat16), grad_out, preferred_element_type=jnp.float32
    )
    return (grad_query, grad_keys, grad_values)


def plain_on_device(
    tokens,
    prior_logits,
    expert_ids,
    expert_ranks,
    piece_starts,
    norm_attn,
    qkv_weight,
    out_weight,
    norm_moe,
    router_weight,
    residual_weight,
    const_vectors,
    const_gates,
    w_gate_up,
    w_down,
    out_grad,
):
    highest = lax.Precision.HIGHEST
    local_rows = tokens.shape[0]
    group_rows = expert_ids.shape[0]
    sequences = group_rows // SEQ
    head_count = qkv_weight.shape[2] // HD
    row_start = lax.axis_index("tensor") * local_rows
    seq_shape = (sequences, SEQ, head_count, HD)
    gain_attn = norm_attn.astype(jnp.float32)
    gain_moe = norm_moe.astype(jnp.float32)
    tok_vals = tokens.astype(jnp.float32)
    factor_attn = rms_factor(tok_vals)
    normed_attn = (tok_vals * factor_attn * gain_attn).astype(jnp.bfloat16)
    attn_rows = lax.all_gather(normed_attn, "tensor", axis=0, tiled=True)
    qkv_full, out_full = (
        lax.all_gather(qkv_weight, "dp", axis=1, tiled=True),
        lax.all_gather(out_weight, "dp", axis=1, tiled=True),
    )
    projected = jnp.einsum("gd,cde->cge", attn_rows, qkv_full, preferred_element_type=jnp.float32)
    cosine, sine = rotary(group_rows, HD)
    query = (
        rotate(projected[0].reshape(group_rows, head_count, HD), cosine, sine)
        .astype(jnp.bfloat16)
        .reshape(seq_shape)
    )
    keys = (
        rotate(projected[1].reshape(group_rows, head_count, HD), cosine, sine)
        .astype(jnp.bfloat16)
        .reshape(seq_shape)
    )
    values = projected[2].astype(jnp.bfloat16).reshape(seq_shape)
    mixed, log_total = lax.map(attend_block, (query, keys, values, piece_starts))
    mixed_rows = mixed.reshape(group_rows, head_count * HD)
    attn_part = jnp.dot(mixed_rows, out_full, preferred_element_type=jnp.float32)
    attn_out = lax.psum_scatter(attn_part, "tensor", scatter_dimension=0, tiled=True)
    resid = tok_vals + attn_out
    factor_moe = rms_factor(resid)
    normed_moe = (resid * factor_moe * gain_moe).astype(jnp.bfloat16)
    moe_rows, prior_rows = (
        lax.all_gather(normed_moe, "tensor", axis=0, tiled=True),
        lax.all_gather(prior_logits, "tensor", axis=0, tiled=True),
    )
    logits = jnp.dot(moe_rows, router_weight, preferred_element_type=jnp.float32) + jnp.dot(
        prior_rows, residual_weight, preferred_element_type=jnp.float32
    )
    shares = jax.nn.softmax(logits, axis=-1)
    gates = jnp.take_along_axis(shares, expert_ids, axis=1)
    retained, target, slot_token, filled = dispatch(expert_ids, expert_ranks)
    picker = jnp.minimum(target, NF * CAP - 1)
    slot_gate = (
        jnp.zeros((NF * CAP + 1,), jnp.float32)
        .at[target.reshape(-1)]
        .set(gates.reshape(-1))[: NF * CAP]
        * filled
    )
    expert_rows = (moe_rows[slot_token] * filled[:, None].astype(jnp.bfloat16)).reshape(NF, CAP, -1)
    gate_full, down_full = (
        lax.all_gather(w_gate_up, "dp", axis=2, tiled=True),
        lax.all_gather(w_down, "dp", axis=2, tiled=True),
    )
    gate_up = jnp.einsum(
        "ecd,sedf->secf", expert_rows, gate_full, preferred_element_type=jnp.float32
    )
    sigmoid_vals = jax.nn.sigmoid(gate_up[0])
    activated = gate_up[0] * sigmoid_vals
    hidden = (activated * gate_up[1]).astype(jnp.bfloat16)
    expert_out = jnp.einsum(
        "ecf,efd->ecd", hidden, down_full, preferred_element_type=jnp.float32
    ).reshape(NF * CAP, -1)
    retained_gates = jnp.where(retained, gates, 0.0)
    combined = jnp.sum(retained_gates[:, :, None] * expert_out[picker], axis=1)
    ffn_out = lax.psum_scatter(
        combined.astype(jnp.bfloat16), "tensor", scatter_dimension=0, tiled=True
    ).astype(jnp.float32)
    local_ids = lax.dynamic_slice_in_dim(expert_ids, row_start, local_rows, 0)
    local_shares = lax.dynamic_slice_in_dim(shares, row_start, local_rows, 0)
    local_gates = lax.dynamic_slice_in_dim(gates, row_start, local_rows, 0)
    normed_vals = normed_moe.astype(jnp.float32)
    vectors = const_vectors.astype(jnp.float32)
    gate_mats = const_gates.astype(jnp.float32)
    const_count = vectors.shape[0]
    copy_share = jnp.sum(jnp.where(local_ids == NF + 1, local_gates, 0.0), axis=1)
    const_share = jnp.stack(
        [
            jnp.sum(jnp.where(local_ids == NF + 2 + index, local_gates, 0.0), axis=1)
            for index in range(const_count)
        ],
        axis=1,
    )
    mixing = jax.nn.softmax(
        jnp.einsum("gd,cjd->gcj", normed_vals, gate_mats, precision=highest), axis=-1
    )
    const_out = (
        mixing[:, :, 0:1] * normed_vals[:, None, :] + mixing[:, :, 1:2] * vectors[None, :, :]
    )
    others = copy_share[:, None] * normed_vals + jnp.sum(
        const_share[:, :, None] * const_out, axis=1
    )
    layer_out = (resid + ffn_out + others).astype(jnp.bfloat16)
    grad_out = out_grad.astype(jnp.float32)
    grad_moe_rows = lax.all_gather(out_grad, "tensor", axis=0, tiled=True)
    gate_back, down_back = (
        lax.all_gather(w_gate_up, "dp", axis=2, tiled=True),
        lax.all_gather(w_down, "dp", axis=2, tiled=True),
    )
    slot_grads = grad_moe_rows[slot_token].astype(jnp.float32)
    grad_expert = (slot_gate[:, None] * slot_grads).astype(jnp.bfloat16).reshape(NF, CAP, -1)
    slot_inner = jnp.sum(slot_grads * expert_out, axis=-1)
    gate_grad_ffn = jnp.where(retained, slot_inner[picker], 0.0)
    down_grad = jnp.einsum("ecf,ecd->efd", hidden, grad_expert, preferred_element_type=jnp.float32)
    grad_hidden = jnp.einsum(
        "ecd,efd->ecf", grad_expert, down_back, preferred_element_type=jnp.float32
    )
    slope = sigmoid_vals * (1.0 + gate_up[0] * (1.0 - sigmoid_vals))
    grad_gate_up = jnp.stack([grad_hidden * gate_up[1] * slope, grad_hidden * activated]).astype(
        jnp.bfloat16
    )
    gate_up_grad = jnp.einsum(
        "ecd,secf->sedf", expert_rows, grad_gate_up, preferred_element_type=jnp.float32
    )
    slot_input_grad = jnp.einsum(
        "secf,sedf->ecd", grad_gate_up, gate_back, preferred_element_type=jnp.float32
    ).reshape(NF * CAP, -1)
    grad_ffn_in = jnp.sum(jnp.where(retained[:, :, None], slot_input_grad[picker], 0.0), axis=1)
    gate_up_grad, down_grad = (
        lax.psum_scatter(gate_up_grad, "dp", scatter_dimension=2, tiled=True),
        lax.psum_scatter(down_grad, "dp", scatter_dimension=2, tiled=True),
    )
    grad_ffn_in, gate_grad_ffn = (
        lax.psum_scatter(grad_ffn_in, "tensor", scatter_dimension=0, tiled=True),
        lax.psum_scatter(gate_grad_ffn, "tensor", scatter_dimension=0, tiled=True),
    )
    copy_inner = jnp.sum(grad_out * normed_vals, axis=-1)
    const_inner = jnp.sum(grad_out[:, None, :] * const_out, axis=-1)
    choice_inner = jnp.where(local_ids == NF + 1, copy_inner[:, None], 0.0)
    for index in range(const_count):
        choice_inner = choice_inner + jnp.where(
            local_ids == NF + 2 + index, const_inner[:, index : index + 1], 0.0
        )
    gate_grad = gate_grad_ffn + choice_inner
    expert_range = jnp.arange(shares.shape[1])
    onehot = (local_ids[:, :, None] == expert_range[None, None, :]).astype(jnp.float32)
    grad_router = jnp.sum(onehot * gate_grad[:, :, None], axis=1)
    grad_logits = local_shares * (
        grad_router - jnp.sum(local_shares * grad_router, axis=-1, keepdims=True)
    )
    prior_vals = prior_logits.astype(jnp.float32)
    router_grad = jnp.dot(normed_vals.T, grad_logits, precision=highest)
    residual_grad = jnp.dot(prior_vals.T, grad_logits, precision=highest)
    prior_grad = jnp.dot(grad_logits, residual_weight.astype(jnp.float32).T, precision=highest)
    vector_inner = jnp.dot(grad_out, vectors.T, precision=highest)
    grad_mixing = const_share[:, :, None] * jnp.stack(
        [jnp.broadcast_to(copy_inner[:, None], vector_inner.shape), vector_inner], axis=-1
    )
    grad_blend = mixing * (grad_mixing - jnp.sum(mixing * grad_mixing, axis=-1, keepdims=True))
    const_gate_grad = jnp.einsum("gcj,gd->cjd", grad_blend, normed_vals, precision=highest)
    const_vector_grad = jnp.einsum(
        "gc,gd->cd", const_share * mixing[:, :, 1], grad_out, precision=highest
    )
    direct_share = copy_share + jnp.sum(const_share * mixing[:, :, 0], axis=1)
    grad_moe_in = (
        grad_ffn_in
        + jnp.dot(grad_logits, router_weight.astype(jnp.float32).T, precision=highest)
        + direct_share[:, None] * grad_out
        + jnp.einsum("gcj,cjd->gd", grad_blend, gate_mats, precision=highest)
    )
    norm_moe_grad = jnp.sum(grad_moe_in * resid * factor_moe, axis=0)
    grad_resid = grad_out + norm_back(grad_moe_in, resid, factor_moe, gain_moe)
    grad_mixed_out = grad_resid.astype(jnp.bfloat16)
    grad_attn_rows = lax.all_gather(grad_mixed_out, "tensor", axis=0, tiled=True)
    out_weight_grad = jnp.dot(mixed_rows.T, grad_attn_rows, preferred_element_type=jnp.float32)
    grad_mixed = jnp.dot(grad_attn_rows, out_full.T, preferred_element_type=jnp.float32).astype(
        jnp.bfloat16
    )
    grad_query, grad_keys, grad_values = lax.map(
        attend_back, (query, keys, values, piece_starts, log_total, grad_mixed.reshape(seq_shape))
    )
    grad_query = rotate(grad_query.reshape(group_rows, head_count, HD), cosine, -sine).reshape(
        group_rows, -1
    )
    grad_keys = rotate(grad_keys.reshape(group_rows, head_count, HD), cosine, -sine).reshape(
        group_rows, -1
    )
    grad_proj = jnp.stack([grad_query, grad_keys, grad_values.reshape(group_rows, -1)]).astype(
        jnp.bfloat16
    )
    qkv_grad = jnp.einsum("gd,cge->cde", attn_rows, grad_proj, preferred_element_type=jnp.float32)
    qkv_grad, out_weight_grad = (
        lax.psum_scatter(qkv_grad, "dp", scatter_dimension=1, tiled=True),
        lax.psum_scatter(out_weight_grad, "dp", scatter_dimension=1, tiled=True),
    )
    grad_attn_part = jnp.einsum(
        "cge,cde->gd", grad_proj, qkv_full, preferred_element_type=jnp.float32
    )
    grad_attn_in = lax.psum_scatter(
        grad_attn_part.astype(jnp.bfloat16), "tensor", scatter_dimension=0, tiled=True
    ).astype(jnp.float32)
    norm_attn_grad = jnp.sum(grad_attn_in * tok_vals * factor_attn, axis=0)
    input_grad = grad_resid + norm_back(grad_attn_in, tok_vals, factor_attn, gain_attn)
    summed = lax.psum(
        (
            norm_attn_grad,
            norm_moe_grad,
            router_grad,
            residual_grad,
            const_vector_grad,
            const_gate_grad,
        ),
        ("dp", "tensor"),
    )
    return (
        layer_out,
        input_grad,
        prior_grad,
        summed[0],
        qkv_grad,
        out_weight_grad,
        summed[1],
        summed[2],
        summed[3],
        summed[4],
        summed[5],
        gate_up_grad,
        down_grad,
    )


def on_device(
    dp,
    tensor,
    tokens,
    prior_logits,
    expert_ids,
    expert_ranks,
    piece_starts,
    norm_attn,
    qkv_weight,
    out_weight,
    norm_moe,
    router_weight,
    residual_weight,
    const_vectors,
    const_gates,
    w_gate_up,
    w_down,
    out_grad,
):
    rows, d = tokens.shape
    ne = router_weight.shape[1]
    packs = dp // NF
    groups = None if packs == 1 else [list(range(NF * r, NF * (r + 1))) for r in range(packs)]
    across = None if packs == 1 else [list(range(j, dp, NF)) for j in range(NF)]
    ids, ranks = expert_ids.T, expert_ranks.T
    cosine, sine = (jnp.asarray(t) for t in rotary_tables())
    prior = jnp.pad(prior_logits.T, ((0, 16 - ne), (0, 0)))
    zeros = lambda n: jnp.zeros((n, d), bf16)
    params = jnp.concatenate(
        [
            router_weight.T, zeros(Z0 - ne), const_gates.reshape(2 * NC, d), zeros(8 - 2 * NC), norm_attn[None],
            norm_moe[None], const_vectors, zeros(6 - NC), jnp.pad(residual_weight, ((0, 16 - ne), (0, d - ne))),
        ],
        axis=0,
    )

    w_attn = jnp.concatenate([qkv_weight, out_weight.T[None]], axis=0)
    w_down_t = w_down.transpose(0, 2, 1)[None]
    shard = w_down.shape[1]
    w_first, slab = prologue(w_gate_up, w_down_t, w_attn, tensor, 1)
    w_full, w_second, pos, count, ys = gather_weights(
        slab, w_gate_up, w_down_t, ids, ranks, out_grad, packs == 1, 2
    )
    w_attn = lax.all_gather(slab, "dp", axis=1, tiled=True) if packs > 1 else w_full

    def whole(w):
        w = w.reshape(3, -1, w.shape[3])
        if packs > 1:
            w = lax.all_gather(w, "dp", axis=1, tiled=True, axis_index_groups=across)
        return lax.all_gather(w, "tensor", axis=0, tiled=False)

    w_first, w_second = whole(w_first), whole(w_second)

    heads = 16
    blocks = shape((NF, ROOM, d), bf16)
    q, k, v, mixed, lse, nattn, resid, nmoe, base, aux, x_b, y_b, pay = pl.pallas_call(
        fwd_kernel,
        in_specs=[SM] + [VM] * 9 + [ANY],
        out_specs=[VM] * 10 + [ANY] * 3,
        out_shape=(
            shape((rows, d), bf16), shape((rows, d), bf16), shape((rows, d), bf16), shape((rows, d), bf16),
            shape((heads, rows), f32), shape((rows, d), bf16), shape((rows, d), f32), shape((rows, d), bf16),
            shape((rows, d), f32), shape((rows, LANES), f32), blocks, blocks, shape((2 * NF, 1, ROOM), f32),
        ),
        scratch_shapes=[
            pltpu.VMEM((QT, 2 * QT), f32),
            pltpu.VMEM((NF, 1, rows), f32),
            pltpu.VMEM((NF, ROOM, d), bf16),
            pltpu.VMEM((2 * NF, 1, ROOM), f32),
            pltpu.VMEM((LANES, d), bf16),
            *send_scratch(),
            *send_scratch(),
            pltpu.SemaphoreType.DMA((2, 2 * (NF - 1))),
            pltpu.SemaphoreType.DMA((2,)),
        ],
        compiler_params=pltpu.CompilerParams(collective_id=3, has_side_effects=True, vmem_limit_bytes=60 << 20),
        cost_estimate=cost(40, 30, 10),
    )(piece_starts, tokens, prior, ids, ranks, params, cosine, sine, w_attn, pos, ys)

    xc, yc, gc, eo, dx, dw_a, meta = experts_first(pay, x_b, y_b, w_first)
    out_b, dx_b, gg_b, dw_b = experts_second(meta, xc, yc, gc, eo, dx, w_second)

    def owned(dw):
        dw = lax.psum_scatter(dw, "tensor", scatter_dimension=0, tiled=False)
        if packs > 1:
            dw = lax.psum_scatter(dw, "dp", scatter_dimension=1, tiled=True, axis_index_groups=across)
        return dw.reshape(3, NF, -1, dw.shape[-1])

    dw_a = owned(dw_a)

    gmo, gres, pgrad, small = pl.pallas_call(
        mid_kernel,
        in_specs=[ANY] * 2 + [VM] * 8,
        out_specs=[VM] * 4,
        out_shape=(shape((rows, d), bf16), shape((rows, d), f32), shape((16, rows), f32), shape((32, d), f32)),
        scratch_shapes=[
            pltpu.VMEM((NF, ROOM, d), bf16),
            pltpu.VMEM((NF, 1, ROOM), f32),
            pltpu.VMEM((rows, d), f32),
            pltpu.VMEM((NF, rows), f32),
            pltpu.VMEM((rows, LANES), f32),
            pltpu.VMEM((rows, LANES), f32),
            pltpu.VMEM((LANES, d), bf16),
            pltpu.VMEM((16, LANES), f32),
            *send_scratch(),
            pltpu.SemaphoreType.DMA((2, NF - 1)),
            pltpu.SemaphoreType.DMA((1,)),
        ],
        compiler_params=pltpu.CompilerParams(collective_id=4, has_side_effects=True, vmem_limit_bytes=60 << 20),
        cost_estimate=cost(4, 4),
    )(dx_b, gg_b, pos, out_grad, nmoe, resid, aux, prior, params, count)
    dw_a, dw_b, gmo = lax.optimization_barrier((dw_a, dw_b, gmo))
    dw_b = owned(dw_b)
    wg, gp, yr, small, dw_a = pl.pallas_call(
        bwd_kernel,
        grid=(1,),
        in_specs=[SM] + [VM] * 9 + [pl.BlockSpec((1, d, d), lambda i: (3, 0, 0)), VM, ANY, ANY],
        out_specs=[VM] * 2 + [ANY, VM, ANY],
        out_shape=(shape((4, d, d), bf16), shape((3, rows, d), bf16), blocks, shape((32, d), f32), shape(dw_a.shape, bf16)),
        scratch_shapes=[
            pltpu.VMEM((rows, d), bf16),
            pltpu.VMEM((heads, rows), f32),
            pltpu.VMEM((rows // QT, 2 * QT, QT), f32),
            pltpu.VMEM((rows, LANES), f32),
            pltpu.VMEM((rows, LANES), f32),
            pltpu.VMEM((rows, LANES), f32),
            *send_scratch(),
            *near_scratch((32, d)),
            *exchange_scratch(1),
        ],
        compiler_params=pltpu.CompilerParams(collective_id=5, has_side_effects=True, vmem_limit_bytes=60 << 20),
        cost_estimate=cost(8, 4),
    )(piece_starts, gmo, mixed, q, k, v, lse, nattn, cosine, sine, w_attn, small, out_b, dw_a)
    alone = packs == 1
    mine, nag, igrad, layer_out, small = finish(
        wg, gp, gres, tokens, w_attn, yr, base, pos, params, small, tensor, alone, 6
    )
    if alone:
        wg = mine
    else:
        wg = lax.psum_scatter(wg, "dp", scatter_dimension=1, tiled=True)
        wg = lax.psum_scatter(wg, "tensor", scatter_dimension=2, tiled=True).astype(f32)
        nag = lax.psum(nag, ("dp", "tensor"))
        small = lax.psum(lax.psum(small, "tensor"), "dp", axis_index_groups=across)
    dw_b = exchange8(dw_b, 7)
    wrg, cvg, nmg = small[0:24], small[24:26], small[26]
    resg = small[29:31].reshape(2 * RES, LANES)
    overflow = jnp.sum(small[28:29, 0:LANES]) > 0

    def roomy(args):
        return plain_on_device(*args)

    def packed(args):
        dw = jnp.concatenate([dw_a, dw_b], axis=-1).astype(f32)
        return (
            layer_out,
            igrad,
            pgrad[0:ne].T,
            nag.reshape(d),
            wg[0:3],
            wg[3].T,
            nmg.reshape(d),
            wrg[0:ne].T,
            resg[0:ne, 0:ne],
            cvg[0:NC],
            wrg[Z0 : Z0 + 2 * NC].reshape(NC, 2, d),
            dw[0:2],
            dw[2].transpose(0, 2, 1),
        )

    args = (
        tokens, prior_logits, expert_ids, expert_ranks, piece_starts, norm_attn, qkv_weight, out_weight, norm_moe,
        router_weight, residual_weight, const_vectors, const_gates, w_gate_up, w_down, out_grad,
    )
    return lax.cond(overflow, roomy, packed, args)


def solution(mesh):
    body = functools.partial(on_device, mesh.shape["dp"], mesh.shape["tensor"])
    rows = P(("dp", "tensor"), None)
    return jax.shard_map(
        body,
        mesh=mesh,
        in_specs=(
            rows, rows, P("dp", None), P("dp", None), P("dp", None), P(), P(None, "dp", "tensor"), P("tensor", "dp"),
            P(), P(), P(), P(), P(), P(None, None, "dp", "tensor"), P(None, "tensor", "dp"), rows,
        ),
        out_specs=(
            rows, rows, rows, P(), P(None, "dp", "tensor"), P("tensor", "dp"), P(), P(), P(), P(), P(),
            P(None, None, "dp", "tensor"), P(None, "tensor", "dp"),
        ),
        check_vma=False,
    )
```

```python
import functools

import jax
import jax.numpy as jnp
import numpy as np
from jax import lax
from jax.experimental import pallas as pl
from jax.experimental.pallas import tpu as pltpu
from jax.sharding import PartitionSpec as P

HD = 64
NF = 8
NC = 2
SEQ = 1024
PIECE = 256
PIECES = 2
CAP = 768
EPS = 1e-06
QT = 256
LANES = 128
TM = 256
ROOM = 256
Z0 = 16
CHOSEN = 32
RES = 6

bf16 = jnp.bfloat16
f32 = jnp.float32
i32 = jnp.int32

VM = pl.BlockSpec(memory_space=pltpu.VMEM)
SM = pl.BlockSpec(memory_space=pltpu.SMEM)
ANY = pl.BlockSpec(memory_space=pl.ANY)


def nn(a, b):
    return lax.dot_general(a, b, (((1,), (0,)), ((), ())), preferred_element_type=f32)


def nt(a, b):
    return lax.dot_general(a, b, (((1,), (1,)), ((), ())), preferred_element_type=f32)


def tn(a, b):
    return lax.dot_general(a, b, (((0,), (0,)), ((), ())), preferred_element_type=f32)


def split(x):
    hi = x.astype(bf16)
    return hi, (x - hi.astype(f32)).astype(bf16)


def lanes(rows):
    return lax.broadcasted_iota(i32, (rows, LANES), 1)


def rot(x, cosine, sine):
    first = lanes(x.shape[0]) % HD < HD // 2
    other = jnp.where(first, pltpu.roll(x, LANES - HD // 2, 1), pltpu.roll(x, HD // 2, 1))
    return x * cosine + other * sine


def head_masks():
    low = lax.broadcasted_iota(i32, (1, LANES), 1) < HD
    a = jnp.where(low, 1.0, 0.0)
    return a, 1.0 - a


def rotary_tables():
    place = np.arange(SEQ, dtype=np.float32)
    half = HD // 2
    freqs = np.power(np.float32(10000.0), np.arange(half, dtype=np.float32) * np.float32(-2.0 / HD)).astype(np.float32)
    angles = (place[:, None] * freqs[None, :]).astype(np.float32).astype(np.float64)
    c, s = np.cos(angles).astype(np.float32), np.sin(angles).astype(np.float32)
    return np.concatenate([c, c, c, c], 1), np.concatenate([-s, s, -s, s], 1)


def window_bias(starts_ref, tile, width, transposed):
    shape = (width, QT) if transposed else (QT, width)
    qpos = lax.broadcasted_iota(i32, shape, 1 if transposed else 0) + tile * QT
    kpos = lax.broadcasted_iota(i32, shape, 0 if transposed else 1) + tile * QT
    seen = jnp.where(kpos <= qpos, 1, 0)
    for piece in range(PIECES):
        s = starts_ref[lax.axis_index("tensor"), piece]
        both = jnp.where(qpos >= s, 1, 0) * jnp.where(qpos < s + PIECE, 1, 0)
        both = both * jnp.where(kpos >= s, 1, 0) * jnp.where(kpos < s + PIECE, 1, 0)
        seen = jnp.maximum(seen, both)
    return jnp.where(seen > 0, 0.0, -1e30)


MESH = pl.DeviceIdType.MESH
GATHER_COPIES = 13
REDUCE_COPIES = 10


def flip(index, m):
    for bit in (1, 2, 4):
        if m & bit:
            index = index + bit - 2 * bit * (index // bit % 2)
    return index


def remote(src, dst, sems, n, axis, peer):
    return pltpu.make_async_remote_copy(
        src_ref=src,
        dst_ref=dst,
        send_sem=sems.at[0, n],
        recv_sem=sems.at[1, n],
        device_id={axis: peer},
        device_id_type=MESH,
    )


def greet(peers):
    barrier = pltpu.get_barrier_semaphore()
    for axis, peer in peers:
        pl.semaphore_signal(barrier, inc=1, device_id={axis: peer}, device_id_type=MESH)
    pl.semaphore_wait(barrier, len(peers))


def near_peers():
    me = lax.axis_index("dp")
    return [("dp", flip(me, m)) for m in (1, 2, 4)]


def far_peers(tensor):
    me = lax.axis_index("tensor")
    return [("tensor", (me + k) % tensor) for k in range(1, tensor)]


class Gather8:
    def __init__(self, src, dst, sems, own_sem):
        me = lax.axis_index("dp")
        slot = me % NF
        nx, ny, nc = flip(me, 2), flip(me, 4), flip(me, 1)
        sx, sy, sd = flip(slot, 2), flip(slot, 4), flip(slot, 6)
        self.own = pltpu.make_async_copy(src(None), dst(slot, None), own_sem)
        go = lambda n, s, d, peer: remote(s, d, sems, n, "dp", peer)
        on = lambda n, s, h, peer: go(n, dst(s, h), dst(s, h), peer)
        self.c = [
            go(0, src(0), dst(slot, 0), nx),
            go(1, src(1), dst(slot, 1), ny),
            go(2, src(1), dst(slot, 1), nx),
            go(3, src(0), dst(slot, 0), ny),
            go(4, src(None), dst(slot, None), nc),
            on(5, sx, 0, ny),
            on(6, sy, 1, nx),
            on(7, sx, 0, nc),
            on(8, sy, 1, nc),
            on(9, sx, 1, nc),
            on(10, sy, 0, nc),
            on(11, sd, 0, nc),
            on(12, sd, 1, nc),
        ]

    def begin(self):
        self.own.start()
        for n in range(5):
            self.c[n].start()

    def forward(self):
        for got, out in ((0, (5, 7)), (1, (6, 8))):
            self.c[got].wait_recv()
            for n in out:
                self.c[n].start()

    def share(self):
        for got, out in ((2, 9), (3, 10)):
            self.c[got].wait_recv()
            self.c[out].start()

    def last(self):
        for got, out in ((5, 11), (6, 12)):
            self.c[got].wait_recv()
            self.c[out].start()

    def end(self):
        for n in (4, 7, 8, 9, 10, 11, 12):
            self.c[n].wait_recv()
        for c in self.c:
            c.wait_send()
        self.own.wait()


def halves(ref, index, rows):
    half = rows // 2
    return lambda s, h: ref.at[s] if h is None else ref.at[s, pl.ds(h * half, half)]


def all_peers():
    me = lax.axis_index("dp")
    return [("dp", flip(me, m)) for m in range(1, NF)]


class Swap8:
    def __init__(self, src, dst, sems, own_sems):
        me = lax.axis_index("dp")
        slot = me % NF
        count = src.shape[0] // NF
        self.own = [
            pltpu.make_async_copy(src.at[NF * i + slot], dst.at[NF * i + slot], own_sems.at[i]) for i in range(count)
        ]
        self.c = [
            remote(
                src.at[NF * i + flip(slot, m)], dst.at[NF * i + slot], sems, (m - 1) * count + i, "dp", flip(me, m)
            )
            for m in range(1, NF)
            for i in range(count)
        ]

    def begin(self):
        for c in self.own + self.c:
            c.start()

    def end(self):
        for c in self.c:
            c.wait_recv()
        for c in self.c:
            c.wait_send()
        for c in self.own:
            c.wait()


def routes(ids_ref, ranks_ref, i):
    start = lax.axis_index("tensor") * SEQ + i * QT
    cols = pl.ds(pl.multiple_of(start, QT), QT)
    at = lax.broadcasted_iota(i32, (16, QT), 0)
    hit0, hit1 = (jnp.where(at == ids_ref[n : n + 1, cols], 1.0, 0.0) for n in range(2))
    keep0, keep1 = (jnp.where(ranks_ref[n : n + 1, cols] < CAP, 1.0, 0.0) for n in range(2))
    return hit0 + hit1, (hit0 * keep0 + hit1 * keep1) * jnp.where(at < NF, 1.0, 0.0)


def weights_kernel(
    gather, slab, gu_ref, dn_ref, ids_ref, ranks_ref, og_ref, out_ref, wx_ref, pos_ref, count_ref, ys_ref, sems, own_sem,
    *scratch,
):
    k, r, _ = slab.shape
    greet(all_peers())
    part = lambda h: pl.ds(0, k) if h is None else pl.ds(h * (k // 2), k // 2)
    if gather:
        g = Gather8(
            lambda h: slab.at[part(h)],
            lambda s, h: out_ref.at[part(h), pl.ds(pl.multiple_of(s * r, r), r), :],
            sems,
            own_sem,
        )
        g.begin()
    swap = Exchange8([gu_ref, dn_ref], wx_ref, 1, *scratch)
    swap.begin()
    upper = jnp.where(
        lax.broadcasted_iota(i32, (QT, QT), 0) < lax.broadcasted_iota(i32, (QT, QT), 1), 1.0, 0.0
    ).astype(bf16)
    taken = jnp.zeros((16, 1), f32)
    for i in range(SEQ // QT):
        _, kept = routes(ids_ref, ranks_ref, i)
        pos = jnp.where(kept > 0, nn(kept.astype(bf16), upper) + taken, -1.0)
        pos_ref[:, 0, i * QT : (i + 1) * QT] = pos[0:NF, :]
        taken = taken + jnp.sum(kept, axis=1, keepdims=True)
    count_ref[...] = jnp.broadcast_to(taken, (16, LANES))
    slot = lax.axis_index("dp") % NF

    def pack(*blocks):
        for m in blocks:
            ys_ref[m] = nn(hot_rows(pos_ref[flip(slot, m)]), og_ref[...]).astype(bf16)

    pack(0, 1)
    if gather:
        g.forward()
    pack(2, 3)
    if gather:
        g.share()
    pack(4, 5)
    if gather:
        g.last()
    pack(6, 7)
    if gather:
        g.end()
    swap.end()


def gather_weights(w, gate_up, down, ids, ranks, og, gather, cid):
    k, r, f = w.shape
    return pl.pallas_call(
        functools.partial(weights_kernel, gather),
        in_specs=[ANY] * 3 + [VM] * 3,
        out_specs=[ANY] * 2 + [VM] * 3,
        out_shape=(
            shape((k, NF * r, f), w.dtype), half_shape(gate_up), shape((NF, 1, og.shape[0]), f32),
            shape((16, LANES), f32), shape((NF, ROOM, og.shape[1]), bf16),
        ),
        scratch_shapes=[
            pltpu.SemaphoreType.DMA((2, GATHER_COPIES)),
            pltpu.SemaphoreType.DMA,
            *exchange_scratch(2),
        ],
        compiler_params=pltpu.CompilerParams(collective_id=cid, has_side_effects=True, vmem_limit_bytes=60 << 20),
        cost_estimate=cost(35, 10),
    )(w, gate_up, down, ids, ranks, og)


class Reduce8:
    def __init__(self, view, bufs, sems, lsems):
        self.own, self.away, self.ind, self.inx, self.iny = bufs
        me = lax.axis_index("dp")
        slot = me % NF
        half = self.ind.shape[0] // 2
        a, b = pl.ds(0, half), pl.ds(half, half)
        self.a, self.b = a, b
        nx, ny, nc = flip(me, 2), flip(me, 4), flip(me, 1)
        mine = [flip(slot, m) for m in (6, 2, 4)] + [slot]
        self.loads = [pltpu.make_async_copy(view(s), self.own.at[n % 2], lsems.at[n]) for n, s in enumerate(mine)]
        self.over = [remote(view(flip(s, 1)), self.away.at[n], sems, n, "dp", nc) for n, s in enumerate(mine)]
        go = lambda n, k, i, part, peer: remote(self.away.at[k, part], i.at[part], sems, n, "dp", peer)
        self.da, self.db = go(4, 0, self.ind, a, nx), go(5, 0, self.ind, b, ny)
        self.xa, self.yb = go(6, 1, self.inx, a, nx), go(7, 2, self.iny, b, ny)
        self.ya, self.xb = go(8, 2, self.iny, a, ny), go(9, 1, self.inx, b, nx)

    def load(self):
        self.loads[0].start()
        self.loads[1].start()

    def begin(self):
        for c in self.over:
            c.start()

    def add(self, n, part):
        self.away[n, part] = (self.own[n % 2, part].astype(f32) + self.away[n, part].astype(f32)).astype(bf16)

    def more(self, n, part):
        self.away[n, part] = (self.away[n, part].astype(f32) + self.ind[part].astype(f32)).astype(bf16)

    def ready(self, n):
        self.loads[n].wait()
        self.over[n].wait_recv()

    def first(self):
        self.ready(0)
        self.add(0, self.a)
        self.da.start()
        self.add(0, self.b)
        self.db.start()
        self.loads[2].start()

    def second(self):
        self.ready(1)
        self.add(1, self.a)
        self.xa.start()
        self.add(1, self.b)
        self.loads[3].start()
        self.ready(2)
        self.add(2, self.b)
        self.yb.start()
        self.add(2, self.a)

    def third(self):
        self.da.wait_recv()
        self.more(2, self.a)
        self.ya.start()
        self.db.wait_recv()
        self.more(1, self.b)
        self.xb.start()

    def end(self, write):
        self.ready(3)
        for part, first, second in ((self.a, self.xa, self.ya), (self.b, self.yb, self.xb)):
            first.wait_recv()
            second.wait_recv()
            total = self.own[1, part].astype(f32) + self.away[3, part].astype(f32)
            write(part, total + self.inx[part].astype(f32) + self.iny[part].astype(f32))

    def close(self):
        for c in self.over + [self.da, self.db, self.xa, self.yb, self.ya, self.xb]:
            c.wait_send()


def reduce_scratch(block):
    return [pltpu.VMEM((2, *block), bf16), pltpu.VMEM((4, *block), bf16)] + [pltpu.VMEM(block, bf16)] * 3 + [
        pltpu.SemaphoreType.DMA((2, REDUCE_COPIES)),
        pltpu.SemaphoreType.DMA((4,)),
    ]


class Exchange8:
    def __init__(self, srcs, dst, part, sems, own_sems):
        me = lax.axis_index("dp")
        slot = me % NF
        width = dst.shape[-1]

        def piece(src, e):
            return src.at[:, e] if part is None else src.at[:, e, :, pl.ds(part * width, width)]

        at, pieces = 0, []
        for src in srcs:
            pieces.append((src, pl.ds(at, src.shape[0])))
            at += src.shape[0]
        self.own = [
            pltpu.make_async_copy(piece(src, slot), dst.at[rows, slot], own_sems.at[i])
            for i, (src, rows) in enumerate(pieces)
        ]
        self.c = [
            remote(
                piece(src, flip(slot, m)), dst.at[rows, slot], sems, (m - 1) * len(srcs) + i, "dp", flip(me, m)
            )
            for m in (6, 7, 2, 3, 4, 5, 1)
            for i, (src, rows) in enumerate(pieces)
        ]

    def begin(self):
        for c in self.c + self.own:
            c.start()

    def end(self):
        for c in self.c:
            c.wait_recv()
        for c in self.c:
            c.wait_send()
        for c in self.own:
            c.wait()


class Send8:
    order = (6, 7, 2, 3, 4, 5, 1)

    def __init__(self, src, dst, sems, own_sem, packed):
        me = lax.axis_index("dp")
        slot = me % NF
        at = lambda m: src.at[m] if packed else src.at[flip(slot, m)]
        self.slot = slot
        self.own = pltpu.make_async_copy(at(0), dst.at[slot], own_sem)
        self.c = {m: remote(at(m), dst.at[slot], sems, m - 1, "dp", flip(me, m)) for m in self.order}

    def start(self, m):
        (self.c[m] if m else self.own).start()

    def begin(self):
        for m in (*self.order, 0):
            self.start(m)

    def got(self, m):
        if m:
            self.c[m].wait_recv()
        else:
            self.own.wait()

    def close(self):
        for c in self.c.values():
            c.wait_send()


def send_scratch():
    return [pltpu.SemaphoreType.DMA((2, NF - 1)), pltpu.SemaphoreType.DMA]


def half_shape(gate_up):
    _, groups, r, f = gate_up.shape
    return shape((3, groups, r, f // 2), bf16)


def exchange_scratch(n):
    return [pltpu.SemaphoreType.DMA((2, (NF - 1) * n)), pltpu.SemaphoreType.DMA((n,))]


def prologue_kernel(tensor, gu_ref, dn_ref, w_ref, wo_ref, out_ref, slab_ref, zbuf, zsems, *scratch):
    here = lax.axis_index("tensor")
    k, f = slab_ref.shape[0], w_ref.shape[2]
    greet(all_peers() + far_peers(tensor))
    copies = []
    for n, (axis, peer) in enumerate(far_peers(tensor)):
        copies.append(remote(w_ref, zbuf.at[here, pl.ds(0, k - 1)], zsems, 2 * n, axis, peer))
        copies.append(remote(wo_ref, zbuf.at[here, k - 1], zsems, 2 * n + 1, axis, peer))
    for c in copies:
        c.start()
    swap = Exchange8([gu_ref, dn_ref], out_ref, 0, *scratch)
    swap.begin()
    zbuf[here, 0 : k - 1] = w_ref[...]
    zbuf[here, k - 1] = wo_ref[...]
    for c in copies:
        c.wait_recv()
    for c in range(k):
        for t in range(0, tensor, 2):
            both = jnp.concatenate([zbuf[t, c].astype(f32), zbuf[t + 1, c].astype(f32)], axis=-1)
            slab_ref[c, :, t * f : (t + 2) * f] = both.astype(bf16)
    swap.end()
    for c in copies:
        c.wait_send()


def prologue(gate_up, down, w, wo, tensor, cid):
    k, r, f = w.shape
    k = k + 1
    return pl.pallas_call(
        functools.partial(prologue_kernel, tensor),
        in_specs=[ANY, ANY, VM, VM],
        out_specs=[ANY, VM],
        out_shape=(half_shape(gate_up), shape((k, r, tensor * f), bf16)),
        scratch_shapes=[
            pltpu.VMEM((tensor, k, r, f), bf16),
            pltpu.SemaphoreType.DMA((2, 2 * (tensor - 1))),
            *exchange_scratch(2),
        ],
        compiler_params=pltpu.CompilerParams(collective_id=cid, has_side_effects=True),
        cost_estimate=cost(25, 10),
    )(gate_up, down, w, wo)


def exchange_kernel(src, dst, *scratch):
    greet(all_peers())
    swap = Exchange8([src], dst, None, *scratch)
    swap.begin()
    swap.end()


def exchange8(x, cid):
    return pl.pallas_call(
        exchange_kernel,
        in_specs=[ANY],
        out_specs=ANY,
        out_shape=shape(x.shape, x.dtype),
        scratch_shapes=exchange_scratch(1),
        compiler_params=pltpu.CompilerParams(collective_id=cid, has_side_effects=True),
        cost_estimate=cost(18, 10),
    )(x)


class Near:
    def __init__(self, have, got, sems):
        me = lax.axis_index("dp")
        self.have, self.got = have, got
        self.c = [remote(have.at[n], got.at[n], sems, n, "dp", flip(me, m)) for n, m in enumerate((1, 2, 4))]

    def begin(self):
        self.c[0].start()

    def step(self, n):
        self.c[n].wait_recv()
        self.have[n + 1] = self.have[n] + self.got[n]
        if n < 2:
            self.c[n + 1].start()

    def close(self):
        for c in self.c:
            c.wait_send()


def near_scratch(dims):
    return [pltpu.VMEM((4, *dims), f32), pltpu.VMEM((3, *dims), f32), pltpu.SemaphoreType.DMA((2, 3))]


class Far:
    def __init__(self, tensor, value, have, got, sems):
        self.tensor, self.value, self.have, self.got, self.here = tensor, value, have, got, lax.axis_index("tensor")
        self.c = [
            remote(have, got.at[self.here], sems, n, axis, peer) for n, (axis, peer) in enumerate(far_peers(tensor))
        ]

    def begin(self):
        self.have[...] = self.value[...].astype(bf16)
        for c in self.c:
            c.start()
        self.got[self.here] = self.have[...]

    def end(self):
        for c in self.c:
            c.wait_recv()
        total = self.got[0].astype(f32)
        for t in range(1, self.tensor):
            total = total + self.got[t].astype(f32)
        for c in self.c:
            c.wait_send()
        return total


def far_scratch(tensor, dims):
    return [pltpu.VMEM(dims, bf16), pltpu.VMEM((tensor, *dims), bf16), pltpu.SemaphoreType.DMA((2, tensor - 1))]


def final_kernel(
    tensor, comm, g_ref, gp_any, gres_any, tok_any, w_any, yr_any, base_any, pos_ref, par_ref, small_ref,
    zs_ref, igrad_ref, layer_ref, total_ref, nag_ref,
    gp_ref, gres_ref, tok_ref, w_ref, yr_ref, base_ref, lsems, *scratch,
):
    k, d, _ = g_ref.shape
    ntile = SEQ // QT
    pairs = (
        (gp_any, gp_ref), (w_any.at[pl.ds(0, 3)], w_ref), (tok_any, tok_ref), (gres_any, gres_ref), (yr_any, yr_ref),
        (base_any, base_ref),
    )
    loads = [pltpu.make_async_copy(src, dst, lsems.at[n]) for n, (src, dst) in enumerate(pairs)]
    if comm:
        r, f = zs_ref.shape[2:]
        red = Reduce8(lambda s: g_ref.at[:, pl.ds(pl.multiple_of(s * r, r), r), :], scratch[:5], *scratch[5:7])
        sums, smalls = Near(*scratch[7:10]), Far(tensor, small_ref, *scratch[10:13])
        red.load()
        greet(near_peers() + far_peers(tensor))
        red.begin()
        smalls.begin()
    for c in loads:
        c.start()
    ga = par_ref[24:25, :].astype(f32)
    if comm:
        red.first()
        red.second()
    for c in loads[:4]:
        c.wait()
    nag = jnp.zeros((1, d), f32)
    for i in range(ntile):
        rows = pl.ds(i * QT, QT)
        gai = nt(gp_ref[0, rows, :], w_ref[0]) + nt(gp_ref[1, rows, :], w_ref[1])
        gai = gai + nt(gp_ref[2, rows, :], w_ref[2])
        x = tok_ref[rows, :].astype(f32)
        r1 = lax.rsqrt(jnp.mean(x * x, axis=-1, keepdims=True) + EPS)
        nag = nag + jnp.sum(gai * x * r1, axis=0, keepdims=True)
        scaled = gai * ga
        avg = jnp.mean(scaled * x, axis=-1, keepdims=True)
        igrad_ref[rows, :] = gres_ref[rows, :] + r1 * scaled - x * (r1 * r1 * r1 * avg)
        if comm and i == 0:
            red.third()
    if comm:
        sums.have[0] = nag
        sums.begin()
    else:
        nag_ref[...] = nag
        total_ref[...] = small_ref[...]
    for c in loads[4:]:
        c.wait()

    def layer(i):
        rows = pl.ds(i * QT, QT)
        total = base_ref[rows, :]
        for e in range(NF):
            total = total + tn(hot_rows(pos_ref[e, :, rows]), yr_ref[e])
        layer_ref[rows, :] = total.astype(bf16)

    def write(part, total):
        for t in range(tensor):
            zs_ref[t, part] = total[:, :, t * f : (t + 1) * f].astype(bf16)

    for i in range(ntile):
        layer(i)
        if comm and i < 3:
            sums.step(i)
    if not comm:
        return
    for i in range(ntile, 3):
        sums.step(i)
    nag_ref[...] = sums.have[3]
    red.end(write)
    total_ref[...] = smalls.end()
    red.close()
    sums.close()


def last_kernel(tensor, zs_ref, small_ref, dw_ref, out_ref, total_ref, dwx_ref, zr, zsems, *scratch):
    here = lax.axis_index("tensor")
    smalls = Far(tensor, small_ref, *scratch[0:3])
    swap = Exchange8([dw_ref], dwx_ref, None, *scratch[3:5])
    greet(all_peers() + far_peers(tensor))
    copies = [
        remote(zs_ref.at[peer], zr.at[here], zsems, n, axis, peer) for n, (axis, peer) in enumerate(far_peers(tensor))
    ]
    for c in copies:
        c.start()
    smalls.begin()
    swap.begin()
    zr[here] = zs_ref[here]
    for c in copies:
        c.wait_recv()
    total = zr[0].astype(f32)
    for t in range(1, tensor):
        total = total + zr[t].astype(f32)
    out_ref[...] = total
    total_ref[...] = smalls.end()
    for c in copies:
        c.wait_send()
    swap.end()


def last(zs, small, dw, tensor, cid):
    return pl.pallas_call(
        functools.partial(last_kernel, tensor),
        in_specs=[VM] * 2 + [ANY],
        out_specs=[VM] * 2 + [ANY],
        out_shape=(shape(zs.shape[1:], f32), shape(small.shape, f32), shape(dw.shape, dw.dtype)),
        scratch_shapes=[
            pltpu.VMEM(zs.shape, bf16),
            pltpu.SemaphoreType.DMA((2, tensor - 1)),
            *far_scratch(tensor, small.shape),
            *exchange_scratch(1),
        ],
        compiler_params=pltpu.CompilerParams(collective_id=cid, has_side_effects=True, vmem_limit_bytes=60 << 20),
        cost_estimate=cost(18, 10),
    )(zs, small, dw)


def finish(g, gp, gres, tokens, w, yr, base, pos, params, small, tensor, comm, cid):
    k, d, columns = g.shape
    rows = tokens.shape[0]
    r, f = (d // NF if comm else 8), columns // tensor
    once = pltpu.CompilerParams(vmem_limit_bytes=60 << 20)
    if comm:
        once = pltpu.CompilerParams(collective_id=cid, has_side_effects=True, vmem_limit_bytes=60 << 20)
    return pl.pallas_call(
        functools.partial(final_kernel, tensor, comm),
        in_specs=[ANY] * 7 + [VM] * 3,
        out_specs=[VM] * 5,
        out_shape=(
            shape((tensor, k, r, f), bf16), shape((rows, d), f32), shape((rows, d), bf16), shape(small.shape, f32),
            shape((1, d), f32),
        ),
        scratch_shapes=[
            pltpu.VMEM(gp.shape, bf16),
            pltpu.VMEM((rows, d), f32),
            pltpu.VMEM((rows, d), bf16),
            pltpu.VMEM((3, d, columns), bf16),
            pltpu.VMEM(yr.shape, bf16),
            pltpu.VMEM((rows, d), f32),
            pltpu.SemaphoreType.DMA((6,)),
            *reduce_scratch((k, r, columns)),
            *near_scratch((1, d)),
            *far_scratch(tensor, small.shape),
        ],
        compiler_params=once,
        cost_estimate=cost(8, 4),
    )(g, gp, gres, tokens, w, yr, base, pos, params, small)


def fwd_kernel(
    starts_ref, tok_ref, prior_ref, ids_ref, ranks_ref, par_ref, cos_ref, sin_ref, w_ref, pos_ref, ys,
    q_ref, k_ref, v_ref, mixed_ref, lse_ref, nattn_ref, resid_ref, nmoe_ref, base_ref, aux_ref, xr_ref, yr_ref, payr_ref,
    bias_ref, gate_ref, xs, pay, wr_ref, *scratch,
):
    greet(all_peers())
    send_x, send_y = Send8(xs, xr_ref, *scratch[0:2], True), Send8(ys, yr_ref, *scratch[2:4], True)
    swap = Swap8(pay, payr_ref, *scratch[4:6])
    send_y.begin()
    lane = lanes(QT)
    router_rows(par_ref, wr_ref)
    wres = par_ref[32:48, 0:LANES]
    d = tok_ref.shape[1]
    pairs = d // LANES
    ntile = SEQ // QT
    ga, gm = par_ref[24:25, :].astype(f32), par_ref[25:26, :].astype(f32)
    cv = par_ref[26:28, :].astype(f32)
    mask_a, mask_b = head_masks()
    mask16 = (mask_a.astype(bf16), mask_b.astype(bf16))

    def project(i, carry):
        rows = pl.ds(pl.multiple_of(i * QT, QT), QT)
        x = tok_ref[rows, :].astype(f32)
        r1 = lax.rsqrt(jnp.mean(x * x, axis=-1, keepdims=True) + EPS)
        n = (x * r1 * ga).astype(bf16)
        nattn_ref[rows, :] = n
        cosine, sine = cos_ref[rows, :], sin_ref[rows, :]
        for c, out in ((0, q_ref), (1, k_ref), (2, v_ref)):
            proj = nn(n, w_ref[c])
            for p in range(pairs):
                part = proj[:, p * LANES : (p + 1) * LANES]
                if c < 2:
                    part = rot(part, cosine, sine)
                part = part.astype(bf16)
                if c == 0:
                    part = part * jnp.array(HD**-0.5, bf16)
                out[rows, p * LANES : (p + 1) * LANES] = part
        return carry

    lax.fori_loop(0, ntile, project, 0)

    for i in range(ntile):
        lo = i * QT
        width = min(SEQ, lo + 2 * QT) - lo
        rows = pl.ds(lo, QT)
        bias_ref[:, :width] = window_bias(starts_ref, i, width, False)

        def pair(p, lse):
            cols = pl.ds(pl.multiple_of(p * LANES, LANES), LANES)
            q2 = q_ref[rows, cols]
            outs = []
            for h in range(2):
                qh = q2 * mask16[h]
                sb = nt(qh, k_ref[lo : lo + width, cols]) + bias_ref[:, :width]
                m = jnp.max(sb, axis=-1, keepdims=True)
                if lo:
                    sa = nt(qh, k_ref[0:lo, cols])
                    m = jnp.maximum(m, jnp.max(sa, axis=-1, keepdims=True))
                pb = jnp.exp(sb - m)
                total = jnp.sum(pb, axis=-1, keepdims=True)
                acc = nn(pb.astype(bf16), v_ref[lo : lo + width, cols])
                if lo:
                    pa = jnp.exp(sa - m)
                    total = total + jnp.sum(pa, axis=-1, keepdims=True)
                    acc = acc + nn(pa.astype(bf16), v_ref[0:lo, cols])
                outs.append(acc / total)
                lse = jnp.where(lane == 2 * p + h, m + jnp.log(total), lse)
            mixed_ref[rows, cols] = (outs[0] * mask_a + outs[1] * mask_b).astype(bf16)
            return lse

        lse = lax.fori_loop(0, pairs, pair, jnp.zeros((QT, LANES), f32))
        lse_ref[:, rows] = lse.T[0 : lse_ref.shape[0], :]

        x = tok_ref[rows, :].astype(f32)
        resid = x + nt(mixed_ref[rows, :], w_ref[3])
        resid_ref[rows, :] = resid
        r2 = lax.rsqrt(jnp.mean(resid * resid, axis=-1, keepdims=True) + EPS)
        nm = (resid * r2 * gm).astype(bf16)
        nmoe_ref[rows, :] = nm
        raw = nt(nm, wr_ref[...])
        logits = raw + tn(prior_ref[:, rows], wres)
        logits = jnp.where(lane < NF + 2 + NC, logits, -1e30)
        e = jnp.exp(logits - jnp.max(logits, axis=-1, keepdims=True))
        shares = e / jnp.sum(e, axis=-1, keepdims=True)
        chosen, kept = routes(ids_ref, ranks_ref, i)
        gate_ref[:, 0, rows] = shares.T[0:NF, :] * kept[0:NF, :]
        chosen = jnp.concatenate([chosen, jnp.zeros((LANES - 16, QT), f32)], axis=0).T
        gates = shares * chosen
        nv = nm.astype(f32)
        aux = jnp.where(lane < NF + 2 + NC, shares, 0.0) + pltpu.roll(chosen, CHOSEN, 1)
        direct = gates[:, NF + 1 : NF + 2]
        others = None
        for c in range(NC):
            z0, z1 = raw[:, Z0 + 2 * c : Z0 + 2 * c + 1], raw[:, Z0 + 2 * c + 1 : Z0 + 2 * c + 2]
            m0, m1 = 1.0 / (1.0 + jnp.exp(z1 - z0)), 1.0 / (1.0 + jnp.exp(z0 - z1))
            aux = jnp.where(lane == Z0 + 2 * c, m0, aux)
            aux = jnp.where(lane == Z0 + 2 * c + 1, m1, aux)
            w = gates[:, NF + 2 + c : NF + 3 + c]
            direct = direct + w * m0
            term = (w * m1) * cv[c : c + 1, :]
            others = term if others is None else others + term
        aux_ref[rows, :] = aux
        base_ref[rows, :] = resid + direct * nv + others

    for m in (*Send8.order, 0):
        e = flip(send_x.slot, m)
        place = pos_ref[e]
        hot = hot_rows(place)
        xs[m] = nn(hot, nmoe_ref[...]).astype(bf16)
        send_x.start(m)
        pay[e] = jnp.sum(nt(split_rows(gate_ref[e]), hot), axis=0, keepdims=True)
        filled = jnp.minimum(jnp.max(place, axis=1, keepdims=True) + 1.0, float(ROOM))
        pay[NF + e] = jnp.broadcast_to(filled, (1, ROOM))
    swap.begin()
    for send in (send_y, send_x):
        for m in (*Send8.order, 0):
            send.got(m)
        send.close()
    swap.end()


def mid_kernel(
    dxb_ref, ggb_ref, og_any, nmoe_any, resid_any, aux_any, pos_ref, prior_ref, par_ref, count_ref,
    gmo_ref, gres_ref, pgrad_ref, small_ref,
    dxr, ggr, dx_ref, gg_ref, inner_ref, extra_ref, wr_ref, resg_ref, og_ref, nmoe_ref, resid_ref, aux_ref, lsems, *scratch,
):
    pairs = ((og_any, og_ref), (nmoe_any, nmoe_ref), (resid_any, resid_ref), (aux_any, aux_ref))
    loads = [pltpu.make_async_copy(a, b, lsems.at[n]) for n, (a, b) in enumerate(pairs)]
    for c in loads:
        c.start()
    greet(all_peers())
    send, swap = Send8(dxb_ref, dxr, *scratch[0:2], False), Swap8(ggb_ref, ggr, *scratch[2:4])
    swap.begin()
    send.begin()
    gm, cv = par_ref[25:26, :].astype(f32), par_ref[26:28, :].astype(f32)
    wres = par_ref[32:48, 0:LANES]
    router_rows(par_ref, wr_ref)
    lane = lanes(QT)
    small_ref[...] = jnp.zeros_like(small_ref)
    resg_ref[...] = jnp.zeros_like(resg_ref)
    small_ref[28:29, 0:LANES] = jnp.max(jnp.where(count_ref[...] > ROOM, 1.0, 0.0), axis=0, keepdims=True)

    def ahead(i, carry):
        rows = pl.ds(pl.multiple_of(i * QT, QT), QT)
        g16 = og_ref[rows, :]
        g, nv = g16.astype(f32), nmoe_ref[rows, :].astype(f32)
        x = resid_ref[rows, :]
        aux = aux_ref[rows, :]
        chosen = jnp.where(lane < 16, pltpu.roll(aux, LANES - CHOSEN, 1), 0.0)
        gates = jnp.where(lane < NF + 2 + NC, aux, 0.0) * chosen
        copy_inner = jnp.sum(g * nv, axis=-1, keepdims=True)
        inner = jnp.where(lane == NF + 1, copy_inner, 0.0)
        direct = gates[:, NF + 1 : NF + 2]
        extra = jnp.where(lane == 1, lax.rsqrt(jnp.mean(x * x, axis=-1, keepdims=True) + EPS), 0.0)
        cvw = jnp.zeros((QT, LANES), f32)
        for c in range(NC):
            m0, m1 = aux[:, Z0 + 2 * c : Z0 + 2 * c + 1], aux[:, Z0 + 2 * c + 1 : Z0 + 2 * c + 2]
            v_inner = jnp.sum(g * cv[c : c + 1, :], axis=-1, keepdims=True)
            mean = m0 * copy_inner + m1 * v_inner
            inner = jnp.where(lane == NF + 2 + c, mean, inner)
            w = gates[:, NF + 2 + c : NF + 3 + c]
            direct = direct + w * m0
            extra = jnp.where(lane == Z0 + 2 * c, m0 * (w * copy_inner - w * mean), extra)
            extra = jnp.where(lane == Z0 + 2 * c + 1, m1 * (w * v_inner - w * mean), extra)
            cvw = jnp.where(lane == c, w * m1, cvw)
        inner_ref[rows, :] = inner
        extra_ref[rows, :] = jnp.where(lane == 0, direct, extra)
        cv_hi, cv_lo = split(cvw)
        small_ref[24:26, :] += tn(cv_hi, g16)[0:NC] + tn(cv_lo, g16)[0:NC]
        return carry

    for c in loads:
        c.wait()
    lax.fori_loop(0, SEQ // QT, ahead, 0)
    swap.end()
    for n, m in enumerate((0, 1, 2, 3, 4, 5, 6, 7)):
        send.got(m)
        e = flip(send.slot, m)
        hot = hot_rows(pos_ref[e])
        gg_ref[pl.ds(e, 1), :] = jnp.sum(nn(split_rows(ggr[e]), hot), axis=0, keepdims=True)
        part = tn(hot, dxr[e])
        if n:
            dx_ref[...] += part
        else:
            dx_ref[...] = part
    send.close()

    def tile(i, carry):
        rows = pl.ds(pl.multiple_of(i * QT, QT), QT)
        g, n16 = og_ref[rows, :].astype(f32), nmoe_ref[rows, :]
        x = resid_ref[rows, :]
        aux, extra = aux_ref[rows, :], extra_ref[rows, :]
        direct, r2 = extra[:, 0:1], extra[:, 1:2]
        shares = jnp.where(lane < NF + 2 + NC, aux, 0.0)
        chosen = jnp.where(lane < 16, pltpu.roll(aux, LANES - CHOSEN, 1), 0.0)
        inner = jnp.concatenate([gg_ref[:, rows], jnp.zeros((LANES - NF, QT), f32)], axis=0).T
        grad_router = (inner + inner_ref[rows, :]) * chosen
        glog = shares * (grad_router - jnp.sum(shares * grad_router, axis=-1, keepdims=True))
        both_hi, both_lo = split(glog + jnp.where(lane >= Z0, extra, 0.0))
        log_hi, log_lo = split(glog)
        pgrad_ref[:, rows] = nt(wres, log_hi) + nt(wres, log_lo)
        small_ref[0:24, :] += tn(both_hi, n16)[0:24] + tn(both_lo, n16)[0:24]
        resg_ref[...] += nn(prior_ref[:, rows], log_hi) + nn(prior_ref[:, rows], log_lo)
        gmi = dx_ref[rows, :] + direct * g + nn(both_hi, wr_ref[...]) + nn(both_lo, wr_ref[...])
        small_ref[26:27, :] += jnp.sum(gmi * x * r2, axis=0, keepdims=True)
        scaled = gmi * gm
        avg = jnp.mean(scaled * x, axis=-1, keepdims=True)
        gres = g + r2 * scaled - x * (r2 * r2 * r2 * avg)
        gres_ref[rows, :] = gres
        gmo_ref[rows, :] = gres.astype(bf16)
        return carry

    lax.fori_loop(0, SEQ // QT, tile, 0)
    for n in range(NF + 2 + NC):
        at = n % RES * LANES
        small_ref[29 + n // RES : 30 + n // RES, at : at + LANES] = resg_ref[n : n + 1, :]


def bwd_kernel(
    starts_ref, gmo_ref, mixed_ref, q_any, k_any, v_any, lse_ref, nattn_any, cos_any, sin_any, w_any, small_ref,
    outb_ref, dw_ref,
    wg_ref, gp_ref, outr_ref, total_ref, dwx_ref,
    do_ref, delta_ref, bias_ref, dk_ref, dv_ref, dq_ref, wo_ref, wsem, q_ref, k_ref, v_ref, nattn_ref, cos_ref, sin_ref, lsems,
    *scratch,
):
    late = ((q_any, q_ref), (k_any, k_ref), (v_any, v_ref), (cos_any, cos_ref), (sin_any, sin_ref), (nattn_any, nattn_ref))
    loads = [pltpu.make_async_copy(a, b, lsems.at[n]) for n, (a, b) in enumerate(late)]
    load = pltpu.make_async_copy(w_any.at[pl.ds(3, 1)], wo_ref, wsem)
    load.start()
    send = Send8(outb_ref, outr_ref, *scratch[0:2], False)
    sums = Near(*scratch[2:5])
    sums.have[0] = small_ref[...]
    greet(all_peers())
    sums.begin()
    send.begin()
    swap = Exchange8([dw_ref], dwx_ref, None, *scratch[5:7])
    swap.begin()
    for c in loads:
        c.start()
    d = mixed_ref.shape[1]
    pairs = d // LANES
    ntile = SEQ // QT
    mask_a, mask_b = head_masks()
    mask16 = (mask_a.astype(bf16), mask_b.astype(bf16))
    maskf = (mask_a, mask_b)
    heads = delta_ref.shape[0]
    pick = jnp.where(
        lax.broadcasted_iota(i32, (heads, d), 1) // HD == lax.broadcasted_iota(i32, (heads, d), 0), 1.0, 0.0
    ).astype(bf16)

    load.wait()

    def start(i, carry):
        rows = pl.ds(pl.multiple_of(i * QT, QT), QT)
        do = nn(gmo_ref[rows, :], wo_ref[0]).astype(bf16)
        do_ref[rows, :] = do
        hi, lo = split(do.astype(f32) * mixed_ref[rows, :].astype(f32))
        delta_ref[:, rows] = nt(pick, hi) + nt(pick, lo)
        return carry

    lax.fori_loop(0, ntile, start, 0)
    sums.step(0)
    wg_ref[3] = tn(gmo_ref[...], mixed_ref[...]).astype(wg_ref.dtype)
    for i in range(ntile):
        width = min(SEQ, (i + 2) * QT) - i * QT
        bias_ref[i, 0:width, :] = window_bias(starts_ref, i, width, True)

    def pair(p, carry):
        cols = pl.ds(pl.multiple_of(p * LANES, LANES), LANES)
        dk_ref[...] = jnp.zeros_like(dk_ref)
        dv_ref[...] = jnp.zeros_like(dv_ref)
        for i in range(ntile):
            lo = i * QT
            width = min(SEQ, lo + 2 * QT) - lo
            rows = pl.ds(lo, QT)
            q2, do2 = q_ref[rows, cols], do_ref[rows, cols]
            dq = jnp.zeros((QT, LANES), f32)
            for h in range(2):
                qh, doh = q2 * mask16[h], do2 * mask16[h]
                lse, delta = lse_ref[pl.ds(2 * p + h, 1), rows], delta_ref[pl.ds(2 * p + h, 1), rows]
                spans = [(lo, width, True)] + ([(0, lo, False)] if lo else [])
                for at, size, masked in spans:
                    k2 = k_ref[at : at + size, cols]
                    s = nt(k2, qh)
                    if masked:
                        s = s + bias_ref[i, 0:size, :]
                    prob = jnp.exp(s - lse)
                    ds = (prob * (nt(v_ref[at : at + size, cols], doh) - delta)).astype(bf16)
                    dv_ref[at : at + size, :] += nn(prob.astype(bf16), doh)
                    dk_ref[at : at + size, :] += nn(ds, qh)
                    dq = dq + tn(ds, k2) * maskf[h]
            dq_ref[rows, :] = dq * HD**-0.5
        cosine, sine = cos_ref[...], -sin_ref[...]
        gp_ref[0, :, cols] = rot(dq_ref[...], cosine, sine).astype(bf16)
        gp_ref[1, :, cols] = rot(dk_ref[...], cosine, sine).astype(bf16)
        gp_ref[2, :, cols] = dv_ref[...].astype(bf16)
        return carry

    for c in loads:
        c.wait()
    lax.fori_loop(0, pairs, pair, 0)
    sums.step(1)
    for c in range(3):
        wg_ref[c] = tn(nattn_ref[...], gp_ref[c]).astype(wg_ref.dtype)
    for m in range(NF):
        send.got(m)
    send.close()
    swap.end()
    sums.step(2)
    total_ref[...] = sums.have[3]
    sums.close()


def ffn_tile(x, gate, y, w_ref, acc, eo, dx):
    dy = y.astype(f32)
    ge = (gate * dy).astype(bf16)
    x_t, ge_t = x.T, ge.T
    for c in range(w_ref.shape[0]):
        wg, wu, wd = w_ref[c, 0], w_ref[c, 1], w_ref[c, 2]
        gv, uv = nn(x, wg), nn(x, wu)
        gh = nn(ge, wd)
        sig = 1.0 / (1.0 + jnp.exp(-gv))
        act = gv * sig
        hid = (act * uv).astype(bf16)
        eo = eo + nt(hid, wd)
        gg = (gh * uv * (sig * (1.0 + gv * (1.0 - sig)))).astype(bf16)
        gu = (gh * act).astype(bf16)
        dx = dx + nt(gg, wg) + nt(gu, wu)
        acc[c, 0] += nn(x_t, gg)
        acc[c, 1] += nn(x_t, gu)
        acc[c, 2] += nn(ge_t, hid)
    return eo, dx


def first_kernel(pay_ref, x_ref, y_ref, w_ref, xc_ref, yc_ref, gc_ref, eo_ref, dx_ref, dw_ref, meta_ref, acc):
    d = x_ref.shape[2]
    gates = [pay_ref[g] for g in range(NF)] + [jnp.zeros((LANES - NF, ROOM), f32)]
    columns = jnp.concatenate(gates, axis=0).T
    off = jnp.int32(0)
    for g in range(NF):
        rows = pl.ds(pl.multiple_of(off, 16), ROOM)
        xc_ref[rows, :] = x_ref[g]
        yc_ref[rows, :] = y_ref[g]
        gc_ref[rows, :] = jnp.broadcast_to(columns[:, g : g + 1], (ROOM, LANES))
        meta_ref[g] = off
        off = off + (jnp.max(pay_ref[NF + g]).astype(i32) + 15) // 16 * 16
    rows = pl.ds(pl.multiple_of(off, 16), TM)
    xc_ref[rows, :] = jnp.zeros((TM, d), bf16)
    yc_ref[rows, :] = jnp.zeros((TM, d), bf16)
    gc_ref[rows, :] = jnp.zeros((TM, LANES), f32)
    tiles = jnp.maximum((off + TM - 1) // TM, 1)
    meta_ref[NF] = tiles
    acc[...] = jnp.zeros_like(acc)
    zero = jnp.zeros((TM, d), f32)

    def tile(t, carry):
        rows = pl.ds(pl.multiple_of(t * TM, TM), TM)
        eo_ref[rows, :], dx_ref[rows, :] = ffn_tile(
            xc_ref[rows, :], gc_ref[rows, 0:1], yc_ref[rows, :], w_ref, acc, zero, zero
        )
        return carry

    lax.fori_loop(0, tiles, tile, 0)
    dw_ref[...] = acc[...].astype(bf16)


def second_kernel(
    meta_ref, xc_any, yc_any, gc_any, eo_any, dx_any, w_any, outb_ref, dxb_ref, ggb_ref, dw_ref,
    xc_ref, yc_ref, gc_ref, eo_ref, dx_ref, w_ref, outs, dxs, ggs, acc, sems, wsem,
):
    d = xc_ref.shape[1]
    tiles = meta_ref[NF]
    weights = pltpu.make_async_copy(w_any, w_ref, wsem)
    weights.start()

    def copies(t):
        rows = pl.ds(pl.multiple_of(t * TM, TM), TM)
        pairs = ((xc_any, xc_ref), (yc_any, yc_ref), (gc_any, gc_ref), (eo_any, eo_ref), (dx_any, dx_ref))
        return [pltpu.make_async_copy(a.at[rows, :], b.at[rows, :], sems.at[n, t]) for n, (a, b) in enumerate(pairs)]

    def begin(t, carry):
        for c in copies(t):
            c.start()
        return carry

    lax.fori_loop(0, tiles, begin, 0)
    acc[...] = jnp.zeros_like(acc)
    rows = pl.ds(pl.multiple_of(tiles * TM, TM), ROOM)
    outs[rows, :] = jnp.zeros((ROOM, d), bf16)
    dxs[rows, :] = jnp.zeros((ROOM, d), bf16)
    ggs[rows, :] = jnp.zeros((ROOM, LANES), f32)
    weights.wait()

    def tile(t, carry):
        rows = pl.ds(pl.multiple_of(t * TM, TM), TM)
        for c in copies(t):
            c.wait()
        gate, y = gc_ref[rows, 0:1], yc_ref[rows, :]
        eo, dx = ffn_tile(xc_ref[rows, :], gate, y, w_ref, acc, eo_ref[rows, :], dx_ref[rows, :])
        outs[rows, :] = (gate * eo).astype(bf16)
        dxs[rows, :] = dx.astype(bf16)
        ggs[rows, :] = jnp.broadcast_to(jnp.sum(y.astype(f32) * eo, axis=1, keepdims=True), (TM, LANES))
        return carry

    lax.fori_loop(0, tiles, tile, 0)
    lane = lanes(ROOM)
    columns = jnp.zeros((ROOM, LANES), f32)
    for g in range(NF):
        rows = pl.ds(pl.multiple_of(meta_ref[g], 16), ROOM)
        outb_ref[g] = outs[rows, :]
        dxb_ref[g] = dxs[rows, :]
        columns = jnp.where(lane == g, ggs[rows, :], columns)
    ggb_ref[:, 0, :] = columns.T[0:NF, :]
    dw_ref[...] = acc[...].astype(bf16)


def experts_first(pay, x, y, w):
    groups, _, d = x.shape
    total = groups * ROOM + TM
    return pl.pallas_call(
        first_kernel,
        in_specs=[VM] * 4,
        out_specs=[VM] * 6 + [SM],
        out_shape=(
            shape((total, d), bf16), shape((total, d), bf16), shape((total, LANES), f32), shape((total, d), f32),
            shape((total, d), f32), shape(w.shape, bf16), shape((NF + 1,), i32),
        ),
        scratch_shapes=[pltpu.VMEM(w.shape, f32)],
        compiler_params=pltpu.CompilerParams(vmem_limit_bytes=60 << 20),
        cost_estimate=cost(22, 25),
    )(pay, x, y, w)


def experts_second(meta, xc, yc, gc, eo, dx, w):
    total, d = xc.shape
    blocks = shape((NF, ROOM, d), bf16)
    room = total + ROOM
    return pl.pallas_call(
        second_kernel,
        in_specs=[SM] + [ANY] * 6,
        out_specs=[VM] * 4,
        out_shape=(blocks, blocks, shape((NF, 1, ROOM), f32), shape(w.shape, bf16)),
        scratch_shapes=[
            pltpu.VMEM((total, d), bf16),
            pltpu.VMEM((total, d), bf16),
            pltpu.VMEM((total, LANES), f32),
            pltpu.VMEM((total, d), f32),
            pltpu.VMEM((total, d), f32),
            pltpu.VMEM(w.shape, bf16),
            pltpu.VMEM((room, d), bf16),
            pltpu.VMEM((room, d), bf16),
            pltpu.VMEM((room, LANES), f32),
            pltpu.VMEM(w.shape, f32),
            pltpu.SemaphoreType.DMA((5, total // TM)),
            pltpu.SemaphoreType.DMA,
        ],
        compiler_params=pltpu.CompilerParams(vmem_limit_bytes=60 << 20),
        cost_estimate=cost(22, 25),
    )(meta, xc, yc, gc, eo, dx, w)


def emit_kernel(a_ref, b_ref, wg_ref, small_ref, nag_ref, gu_ref, dn_ref, qkv_ref, wo_ref, rt_ref, rg_ref, cv_ref, cg_ref, na_ref, nm_ref):
    half = a_ref.shape[3]
    for n, ref in ((0, a_ref), (1, b_ref)):
        at = slice(n * half, (n + 1) * half)
        gu_ref[:, 0, :, at] = ref[0:2, 0].astype(f32)
        dn_ref[0, :, at] = ref[2, 0].astype(f32)

    @pl.when(pl.program_id(0) == 0)
    def _():
        qkv_ref[...] = wg_ref[0:3]
        r, f = wg_ref.shape[1:]
        wide = jnp.concatenate([wg_ref[3], jnp.zeros((r, -f % LANES), f32)], axis=1)
        wo_ref[...] = jnp.concatenate([wide, jnp.zeros((-r % LANES, wide.shape[1]), f32)], axis=0).T[0:f, 0:r]
        ne = rg_ref.shape[0]
        rt_ref[...] = small_ref[0:ne, :]
        for c in range(NC):
            cg_ref[c] = small_ref[Z0 + 2 * c : Z0 + 2 * c + 2, :]
        cv_ref[...] = small_ref[24 : 24 + NC, :]
        nm_ref[...] = small_ref[26, :]
        na_ref[...] = nag_ref[0, :]
        for n in range(ne):
            at = n % RES * LANES
            rg_ref[n : n + 1, :] = small_ref[29 + n // RES : 30 + n // RES, at : at + LANES][:, 0:ne]


def emit(dw_a, dw_b, wg, small, nag, ne):
    _, groups, r, half = dw_a.shape
    d = small.shape[1]
    piece = pl.BlockSpec((3, 1, r, half), lambda e: (0, e, 0, 0))
    whole = lambda *dims: pl.BlockSpec(dims, lambda e: (0,) * len(dims))
    rest = [(3, *wg.shape[1:]), wg.shape[:0:-1], (ne, d), (ne, ne), (NC, d), (NC, 2, d), (d,), (d,)]
    return pl.pallas_call(
        emit_kernel,
        grid=(groups,),
        in_specs=[piece, piece, whole(*wg.shape), whole(*small.shape), whole(1, d)],
        out_specs=[
            pl.BlockSpec((2, 1, r, 2 * half), lambda e: (0, e, 0, 0)), pl.BlockSpec((1, r, 2 * half), lambda e: (e, 0, 0)),
            *(whole(*dims) for dims in rest),
        ],
        out_shape=(
            shape((2, groups, r, 2 * half), f32), shape((groups, r, 2 * half), f32), *(shape(dims, f32) for dims in rest),
        ),
        cost_estimate=cost(1, 8),
    )(dw_a, dw_b, wg, small, nag)


def router_rows(par_ref, wr_ref):
    wr_ref[...] = jnp.zeros_like(wr_ref)
    wr_ref[0:16, :] = par_ref[0:16, :]
    wr_ref[16:32, :] = jnp.where(
        lax.broadcasted_iota(i32, (16, par_ref.shape[1]), 0) < 2 * NC, par_ref[16:32, :].astype(f32), 0.0
    ).astype(bf16)


def hot_rows(pos):
    slot = lax.broadcasted_iota(i32, (ROOM, pos.shape[1]), 0).astype(f32)
    return jnp.where(slot == pos, 1.0, 0.0).astype(bf16)


def split_rows(row):
    hi = row.astype(bf16).astype(f32)
    mid = (row - hi).astype(bf16).astype(f32)
    at = lax.broadcasted_iota(i32, (8, row.shape[1]), 0)
    out = jnp.where(at == 0, hi, jnp.where(at == 1, mid, jnp.where(at == 2, row - hi - mid, 0.0)))
    return out.astype(bf16)


def shape(dims, dtype):
    return jax.ShapeDtypeStruct(dims, dtype)


def cost(gflop, mbytes, mexp=0):
    return pl.CostEstimate(flops=int(gflop * 1e9), bytes_accessed=int(mbytes * 1e6), transcendentals=int(mexp * 1e6))


def rms_factor(values):
    return lax.rsqrt(jnp.mean(values * values, axis=-1, keepdims=True) + EPS)


def norm_back(grad, values, factor, gain):
    scaled = grad * gain
    inner = jnp.mean(scaled * values, axis=-1, keepdims=True)
    return factor * scaled - values * factor * factor * factor * inner


def rotary(positions, width):
    place = (jnp.arange(positions) % SEQ).astype(jnp.float32)
    freqs = jnp.power(10000.0, jnp.arange(width // 2).astype(jnp.float32) * (-2.0 / width))
    angles = place[:, None] * freqs[None, :]
    return (jnp.cos(angles)[:, None, :], jnp.sin(angles)[:, None, :])


def rotate(values, cosine, sine):
    half = values.shape[-1] // 2
    front = values[..., :half]
    behind = values[..., half:]
    return jnp.concatenate(
        [front * cosine - behind * sine, behind * cosine + front * sine], axis=-1
    )


def visible(starts):
    position = jnp.arange(SEQ)
    piece_of = jnp.zeros((SEQ,), jnp.int32)
    for index in range(starts.shape[0]):
        inside = (position >= starts[index]) & (position < starts[index] + PIECE)
        piece_of = jnp.where(inside, index + 1, piece_of)
    causal = position[None, :] <= position[:, None]
    same_piece = (piece_of[:, None] > 0) & (piece_of[:, None] == piece_of[None, :])
    return causal | same_piece


def dispatch(route_ids, route_ranks):
    group_rows = route_ids.shape[0]
    retained = (route_ids < NF) & (route_ranks < CAP)
    target = jnp.where(retained, route_ids * CAP + route_ranks, NF * CAP)
    token_index = jnp.broadcast_to(
        jnp.arange(group_rows, dtype=jnp.int32)[:, None], route_ids.shape
    )
    slot_token = (
        jnp.zeros((NF * CAP + 1,), jnp.int32)
        .at[target.reshape(-1)]
        .set(token_index.reshape(-1))[: NF * CAP]
    )
    filled = jnp.zeros((NF * CAP + 1,), jnp.float32).at[target.reshape(-1)].set(1.0)[: NF * CAP]
    return (retained, target, slot_token, filled)


def masked_scores(query, keys, starts):
    scores = jnp.einsum("qhd,khd->hqk", query, keys, preferred_element_type=jnp.float32) * HD ** (
        -0.5
    )
    return jnp.where(visible(starts)[None], scores, -1e30)


def attend_block(parts):
    query, keys, values, starts = parts
    scores = masked_scores(query, keys, starts)
    row_max = jnp.max(scores, axis=-1, keepdims=True)
    denominator = jnp.sum(jnp.exp(scores - row_max), axis=-1, keepdims=True)
    log_total = row_max + jnp.log(denominator)
    shares = jnp.exp(scores - log_total).astype(jnp.bfloat16)
    mixed = jnp.einsum("hqk,khd->qhd", shares, values, preferred_element_type=jnp.float32)
    return (mixed.astype(jnp.bfloat16), log_total)


def attend_back(parts):
    query, keys, values, starts, log_total, grad_out = parts
    shares = jnp.exp(masked_scores(query, keys, starts) - log_total)
    grad_shares = jnp.einsum("qhd,khd->hqk", grad_out, values, preferred_element_type=jnp.float32)
    centre = jnp.sum(shares * grad_shares, axis=-1, keepdims=True)
    grad_scores = (shares * (grad_shares - centre)).astype(jnp.bfloat16)
    factor = HD ** (-0.5)
    grad_query = (
        jnp.einsum("hqk,khd->qhd", grad_scores, keys, preferred_element_type=jnp.float32) * factor
    )
    grad_keys = (
        jnp.einsum("hqk,qhd->khd", grad_scores, query, preferred_element_type=jnp.float32) * factor
    )
    grad_values = jnp.einsum(
        "hqk,qhd->khd", shares.astype(jnp.bfloat16), grad_out, preferred_element_type=jnp.float32
    )
    return (grad_query, grad_keys, grad_values)


def plain_on_device(
    tokens,
    prior_logits,
    expert_ids,
    expert_ranks,
    piece_starts,
    norm_attn,
    qkv_weight,
    out_weight,
    norm_moe,
    router_weight,
    residual_weight,
    const_vectors,
    const_gates,
    w_gate_up,
    w_down,
    out_grad,
):
    highest = lax.Precision.HIGHEST
    local_rows = tokens.shape[0]
    group_rows = expert_ids.shape[0]
    sequences = group_rows // SEQ
    head_count = qkv_weight.shape[2] // HD
    row_start = lax.axis_index("tensor") * local_rows
    seq_shape = (sequences, SEQ, head_count, HD)
    gain_attn = norm_attn.astype(jnp.float32)
    gain_moe = norm_moe.astype(jnp.float32)
    tok_vals = tokens.astype(jnp.float32)
    factor_attn = rms_factor(tok_vals)
    normed_attn = (tok_vals * factor_attn * gain_attn).astype(jnp.bfloat16)
    attn_rows = lax.all_gather(normed_attn, "tensor", axis=0, tiled=True)
    qkv_full, out_full = (
        lax.all_gather(qkv_weight, "dp", axis=1, tiled=True),
        lax.all_gather(out_weight, "dp", axis=1, tiled=True),
    )
    projected = jnp.einsum("gd,cde->cge", attn_rows, qkv_full, preferred_element_type=jnp.float32)
    cosine, sine = rotary(group_rows, HD)
    query = (
        rotate(projected[0].reshape(group_rows, head_count, HD), cosine, sine)
        .astype(jnp.bfloat16)
        .reshape(seq_shape)
    )
    keys = (
        rotate(projected[1].reshape(group_rows, head_count, HD), cosine, sine)
        .astype(jnp.bfloat16)
        .reshape(seq_shape)
    )
    values = projected[2].astype(jnp.bfloat16).reshape(seq_shape)
    mixed, log_total = lax.map(attend_block, (query, keys, values, piece_starts))
    mixed_rows = mixed.reshape(group_rows, head_count * HD)
    attn_part = jnp.dot(mixed_rows, out_full, preferred_element_type=jnp.float32)
    attn_out = lax.psum_scatter(attn_part, "tensor", scatter_dimension=0, tiled=True)
    resid = tok_vals + attn_out
    factor_moe = rms_factor(resid)
    normed_moe = (resid * factor_moe * gain_moe).astype(jnp.bfloat16)
    moe_rows, prior_rows = (
        lax.all_gather(normed_moe, "tensor", axis=0, tiled=True),
        lax.all_gather(prior_logits, "tensor", axis=0, tiled=True),
    )
    logits = jnp.dot(moe_rows, router_weight, preferred_element_type=jnp.float32) + jnp.dot(
        prior_rows, residual_weight, preferred_element_type=jnp.float32
    )
    shares = jax.nn.softmax(logits, axis=-1)
    gates = jnp.take_along_axis(shares, expert_ids, axis=1)
    retained, target, slot_token, filled = dispatch(expert_ids, expert_ranks)
    picker = jnp.minimum(target, NF * CAP - 1)
    slot_gate = (
        jnp.zeros((NF * CAP + 1,), jnp.float32)
        .at[target.reshape(-1)]
        .set(gates.reshape(-1))[: NF * CAP]
        * filled
    )
    expert_rows = (moe_rows[slot_token] * filled[:, None].astype(jnp.bfloat16)).reshape(NF, CAP, -1)
    gate_full, down_full = (
        lax.all_gather(w_gate_up, "dp", axis=2, tiled=True),
        lax.all_gather(w_down, "dp", axis=2, tiled=True),
    )
    gate_up = jnp.einsum(
        "ecd,sedf->secf", expert_rows, gate_full, preferred_element_type=jnp.float32
    )
    sigmoid_vals = jax.nn.sigmoid(gate_up[0])
    activated = gate_up[0] * sigmoid_vals
    hidden = (activated * gate_up[1]).astype(jnp.bfloat16)
    expert_out = jnp.einsum(
        "ecf,efd->ecd", hidden, down_full, preferred_element_type=jnp.float32
    ).reshape(NF * CAP, -1)
    retained_gates = jnp.where(retained, gates, 0.0)
    combined = jnp.sum(retained_gates[:, :, None] * expert_out[picker], axis=1)
    ffn_out = lax.psum_scatter(
        combined.astype(jnp.bfloat16), "tensor", scatter_dimension=0, tiled=True
    ).astype(jnp.float32)
    local_ids = lax.dynamic_slice_in_dim(expert_ids, row_start, local_rows, 0)
    local_shares = lax.dynamic_slice_in_dim(shares, row_start, local_rows, 0)
    local_gates = lax.dynamic_slice_in_dim(gates, row_start, local_rows, 0)
    normed_vals = normed_moe.astype(jnp.float32)
    vectors = const_vectors.astype(jnp.float32)
    gate_mats = const_gates.astype(jnp.float32)
    const_count = vectors.shape[0]
    copy_share = jnp.sum(jnp.where(local_ids == NF + 1, local_gates, 0.0), axis=1)
    const_share = jnp.stack(
        [
            jnp.sum(jnp.where(local_ids == NF + 2 + index, local_gates, 0.0), axis=1)
            for index in range(const_count)
        ],
        axis=1,
    )
    mixing = jax.nn.softmax(
        jnp.einsum("gd,cjd->gcj", normed_vals, gate_mats, precision=highest), axis=-1
    )
    const_out = (
        mixing[:, :, 0:1] * normed_vals[:, None, :] + mixing[:, :, 1:2] * vectors[None, :, :]
    )
    others = copy_share[:, None] * normed_vals + jnp.sum(
        const_share[:, :, None] * const_out, axis=1
    )
    layer_out = (resid + ffn_out + others).astype(jnp.bfloat16)
    grad_out = out_grad.astype(jnp.float32)
    grad_moe_rows = lax.all_gather(out_grad, "tensor", axis=0, tiled=True)
    gate_back, down_back = (
        lax.all_gather(w_gate_up, "dp", axis=2, tiled=True),
        lax.all_gather(w_down, "dp", axis=2, tiled=True),
    )
    slot_grads = grad_moe_rows[slot_token].astype(jnp.float32)
    grad_expert = (slot_gate[:, None] * slot_grads).astype(jnp.bfloat16).reshape(NF, CAP, -1)
    slot_inner = jnp.sum(slot_grads * expert_out, axis=-1)
    gate_grad_ffn = jnp.where(retained, slot_inner[picker], 0.0)
    down_grad = jnp.einsum("ecf,ecd->efd", hidden, grad_expert, preferred_element_type=jnp.float32)
    grad_hidden = jnp.einsum(
        "ecd,efd->ecf", grad_expert, down_back, preferred_element_type=jnp.float32
    )
    slope = sigmoid_vals * (1.0 + gate_up[0] * (1.0 - sigmoid_vals))
    grad_gate_up = jnp.stack([grad_hidden * gate_up[1] * slope, grad_hidden * activated]).astype(
        jnp.bfloat16
    )
    gate_up_grad = jnp.einsum(
        "ecd,secf->sedf", expert_rows, grad_gate_up, preferred_element_type=jnp.float32
    )
    slot_input_grad = jnp.einsum(
        "secf,sedf->ecd", grad_gate_up, gate_back, preferred_element_type=jnp.float32
    ).reshape(NF * CAP, -1)
    grad_ffn_in = jnp.sum(jnp.where(retained[:, :, None], slot_input_grad[picker], 0.0), axis=1)
    gate_up_grad, down_grad = (
        lax.psum_scatter(gate_up_grad, "dp", scatter_dimension=2, tiled=True),
        lax.psum_scatter(down_grad, "dp", scatter_dimension=2, tiled=True),
    )
    grad_ffn_in, gate_grad_ffn = (
        lax.psum_scatter(grad_ffn_in, "tensor", scatter_dimension=0, tiled=True),
        lax.psum_scatter(gate_grad_ffn, "tensor", scatter_dimension=0, tiled=True),
    )
    copy_inner = jnp.sum(grad_out * normed_vals, axis=-1)
    const_inner = jnp.sum(grad_out[:, None, :] * const_out, axis=-1)
    choice_inner = jnp.where(local_ids == NF + 1, copy_inner[:, None], 0.0)
    for index in range(const_count):
        choice_inner = choice_inner + jnp.where(
            local_ids == NF + 2 + index, const_inner[:, index : index + 1], 0.0
        )
    gate_grad = gate_grad_ffn + choice_inner
    expert_range = jnp.arange(shares.shape[1])
    onehot = (local_ids[:, :, None] == expert_range[None, None, :]).astype(jnp.float32)
    grad_router = jnp.sum(onehot * gate_grad[:, :, None], axis=1)
    grad_logits = local_shares * (
        grad_router - jnp.sum(local_shares * grad_router, axis=-1, keepdims=True)
    )
    prior_vals = prior_logits.astype(jnp.float32)
    router_grad = jnp.dot(normed_vals.T, grad_logits, precision=highest)
    residual_grad = jnp.dot(prior_vals.T, grad_logits, precision=highest)
    prior_grad = jnp.dot(grad_logits, residual_weight.astype(jnp.float32).T, precision=highest)
    vector_inner = jnp.dot(grad_out, vectors.T, precision=highest)
    grad_mixing = const_share[:, :, None] * jnp.stack(
        [jnp.broadcast_to(copy_inner[:, None], vector_inner.shape), vector_inner], axis=-1
    )
    grad_blend = mixing * (grad_mixing - jnp.sum(mixing * grad_mixing, axis=-1, keepdims=True))
    const_gate_grad = jnp.einsum("gcj,gd->cjd", grad_blend, normed_vals, precision=highest)
    const_vector_grad = jnp.einsum(
        "gc,gd->cd", const_share * mixing[:, :, 1], grad_out, precision=highest
    )
    direct_share = copy_share + jnp.sum(const_share * mixing[:, :, 0], axis=1)
    grad_moe_in = (
        grad_ffn_in
        + jnp.dot(grad_logits, router_weight.astype(jnp.float32).T, precision=highest)
        + direct_share[:, None] * grad_out
        + jnp.einsum("gcj,cjd->gd", grad_blend, gate_mats, precision=highest)
    )
    norm_moe_grad = jnp.sum(grad_moe_in * resid * factor_moe, axis=0)
    grad_resid = grad_out + norm_back(grad_moe_in, resid, factor_moe, gain_moe)
    grad_mixed_out = grad_resid.astype(jnp.bfloat16)
    grad_attn_rows = lax.all_gather(grad_mixed_out, "tensor", axis=0, tiled=True)
    out_weight_grad = jnp.dot(mixed_rows.T, grad_attn_rows, preferred_element_type=jnp.float32)
    grad_mixed = jnp.dot(grad_attn_rows, out_full.T, preferred_element_type=jnp.float32).astype(
        jnp.bfloat16
    )
    grad_query, grad_keys, grad_values = lax.map(
        attend_back, (query, keys, values, piece_starts, log_total, grad_mixed.reshape(seq_shape))
    )
    grad_query = rotate(grad_query.reshape(group_rows, head_count, HD), cosine, -sine).reshape(
        group_rows, -1
    )
    grad_keys = rotate(grad_keys.reshape(group_rows, head_count, HD), cosine, -sine).reshape(
        group_rows, -1
    )
    grad_proj = jnp.stack([grad_query, grad_keys, grad_values.reshape(group_rows, -1)]).astype(
        jnp.bfloat16
    )
    qkv_grad = jnp.einsum("gd,cge->cde", attn_rows, grad_proj, preferred_element_type=jnp.float32)
    qkv_grad, out_weight_grad = (
        lax.psum_scatter(qkv_grad, "dp", scatter_dimension=1, tiled=True),
        lax.psum_scatter(out_weight_grad, "dp", scatter_dimension=1, tiled=True),
    )
    grad_attn_part = jnp.einsum(
        "cge,cde->gd", grad_proj, qkv_full, preferred_element_type=jnp.float32
    )
    grad_attn_in = lax.psum_scatter(
        grad_attn_part.astype(jnp.bfloat16), "tensor", scatter_dimension=0, tiled=True
    ).astype(jnp.float32)
    norm_attn_grad = jnp.sum(grad_attn_in * tok_vals * factor_attn, axis=0)
    input_grad = grad_resid + norm_back(grad_attn_in, tok_vals, factor_attn, gain_attn)
    summed = lax.psum(
        (
            norm_attn_grad,
            norm_moe_grad,
            router_grad,
            residual_grad,
            const_vector_grad,
            const_gate_grad,
        ),
        ("dp", "tensor"),
    )
    return (
        layer_out,
        input_grad,
        prior_grad,
        summed[0],
        qkv_grad,
        out_weight_grad,
        summed[1],
        summed[2],
        summed[3],
        summed[4],
        summed[5],
        gate_up_grad,
        down_grad,
    )


def on_device(
    dp,
    tensor,
    tokens,
    prior_logits,
    expert_ids,
    expert_ranks,
    piece_starts,
    norm_attn,
    qkv_weight,
    out_weight,
    norm_moe,
    router_weight,
    residual_weight,
    const_vectors,
    const_gates,
    w_gate_up,
    w_down,
    out_grad,
):
    rows, d = tokens.shape
    ne = router_weight.shape[1]
    packs = dp // NF
    groups = None if packs == 1 else [list(range(NF * r, NF * (r + 1))) for r in range(packs)]
    across = None if packs == 1 else [list(range(j, dp, NF)) for j in range(NF)]
    ids, ranks = expert_ids.T, expert_ranks.T
    cosine, sine = (jnp.asarray(t) for t in rotary_tables())
    prior = jnp.pad(prior_logits.T, ((0, 16 - ne), (0, 0)))
    zeros = lambda n: jnp.zeros((n, d), bf16)
    params = jnp.concatenate(
        [
            router_weight.T, zeros(Z0 - ne), const_gates.reshape(2 * NC, d), zeros(8 - 2 * NC), norm_attn[None],
            norm_moe[None], const_vectors, zeros(6 - NC), jnp.pad(residual_weight, ((0, 16 - ne), (0, d - ne))),
        ],
        axis=0,
    )

    w_down_t = w_down.transpose(0, 2, 1)[None]
    shard = w_down.shape[1]
    w_first, slab = prologue(w_gate_up, w_down_t, qkv_weight, out_weight.T, tensor, 1)
    w_full, w_second, pos, count, ys = gather_weights(
        slab, w_gate_up, w_down_t, ids, ranks, out_grad, packs == 1, 2
    )
    w_attn = lax.all_gather(slab, "dp", axis=1, tiled=True) if packs > 1 else w_full

    def whole(w):
        w = w.reshape(3, -1, w.shape[3])
        if packs > 1:
            w = lax.all_gather(w, "dp", axis=1, tiled=True, axis_index_groups=across)
        return lax.all_gather(w, "tensor", axis=0, tiled=False)

    w_first, w_second = whole(w_first), whole(w_second)

    heads = 16
    blocks = shape((NF, ROOM, d), bf16)
    q, k, v, mixed, lse, nattn, resid, nmoe, base, aux, x_b, y_b, pay = pl.pallas_call(
        fwd_kernel,
        in_specs=[SM] + [VM] * 9 + [ANY],
        out_specs=[VM] * 10 + [ANY] * 3,
        out_shape=(
            shape((rows, d), bf16), shape((rows, d), bf16), shape((rows, d), bf16), shape((rows, d), bf16),
            shape((heads, rows), f32), shape((rows, d), bf16), shape((rows, d), f32), shape((rows, d), bf16),
            shape((rows, d), f32), shape((rows, LANES), f32), blocks, blocks, shape((2 * NF, 1, ROOM), f32),
        ),
        scratch_shapes=[
            pltpu.VMEM((QT, 2 * QT), f32),
            pltpu.VMEM((NF, 1, rows), f32),
            pltpu.VMEM((NF, ROOM, d), bf16),
            pltpu.VMEM((2 * NF, 1, ROOM), f32),
            pltpu.VMEM((LANES, d), bf16),
            *send_scratch(),
            *send_scratch(),
            pltpu.SemaphoreType.DMA((2, 2 * (NF - 1))),
            pltpu.SemaphoreType.DMA((2,)),
        ],
        compiler_params=pltpu.CompilerParams(collective_id=3, has_side_effects=True, vmem_limit_bytes=60 << 20),
        cost_estimate=cost(40, 30, 10),
    )(piece_starts, tokens, prior, ids, ranks, params, cosine, sine, w_attn, pos, ys)

    xc, yc, gc, eo, dx, dw_a, meta = experts_first(pay, x_b, y_b, w_first)
    out_b, dx_b, gg_b, dw_b = experts_second(meta, xc, yc, gc, eo, dx, w_second)

    def owned(dw):
        dw = lax.psum_scatter(dw, "tensor", scatter_dimension=0, tiled=False)
        if packs > 1:
            dw = lax.psum_scatter(dw, "dp", scatter_dimension=1, tiled=True, axis_index_groups=across)
        return dw.reshape(3, NF, -1, dw.shape[-1])

    dw_a = owned(dw_a)

    gmo, gres, pgrad, small = pl.pallas_call(
        mid_kernel,
        in_specs=[ANY] * 6 + [VM] * 4,
        out_specs=[VM] * 4,
        out_shape=(shape((rows, d), bf16), shape((rows, d), f32), shape((16, rows), f32), shape((32, d), f32)),
        scratch_shapes=[
            pltpu.VMEM((NF, ROOM, d), bf16),
            pltpu.VMEM((NF, 1, ROOM), f32),
            pltpu.VMEM((rows, d), f32),
            pltpu.VMEM((NF, rows), f32),
            pltpu.VMEM((rows, LANES), f32),
            pltpu.VMEM((rows, LANES), f32),
            pltpu.VMEM((LANES, d), bf16),
            pltpu.VMEM((16, LANES), f32),
            pltpu.VMEM((rows, d), bf16),
            pltpu.VMEM((rows, d), bf16),
            pltpu.VMEM((rows, d), f32),
            pltpu.VMEM((rows, LANES), f32),
            pltpu.SemaphoreType.DMA((4,)),
            *send_scratch(),
            pltpu.SemaphoreType.DMA((2, NF - 1)),
            pltpu.SemaphoreType.DMA((1,)),
        ],
        compiler_params=pltpu.CompilerParams(collective_id=4, has_side_effects=True, vmem_limit_bytes=60 << 20),
        cost_estimate=cost(4, 4),
    )(dx_b, gg_b, out_grad, nmoe, resid, aux, pos, prior, params, count)
    dw_a, dw_b, gmo = lax.optimization_barrier((dw_a, dw_b, gmo))
    dw_b = owned(dw_b)
    wg, gp, yr, small, dw_a = pl.pallas_call(
        bwd_kernel,
        in_specs=[SM, VM, VM, ANY, ANY, ANY, VM] + [ANY] * 4 + [VM, ANY, ANY],
        out_specs=[VM] * 2 + [ANY, VM, ANY],
        out_shape=(shape((4, d, d), bf16), shape((3, rows, d), bf16), blocks, shape((32, d), f32), shape(dw_a.shape, bf16)),
        scratch_shapes=[
            pltpu.VMEM((rows, d), bf16),
            pltpu.VMEM((heads, rows), f32),
            pltpu.VMEM((rows // QT, 2 * QT, QT), f32),
            pltpu.VMEM((rows, LANES), f32),
            pltpu.VMEM((rows, LANES), f32),
            pltpu.VMEM((rows, LANES), f32),
            pltpu.VMEM((1, d, d), bf16),
            pltpu.SemaphoreType.DMA,
            *[pltpu.VMEM((rows, d), bf16)] * 3,
            pltpu.VMEM((rows, d), bf16),
            *[pltpu.VMEM((rows, LANES), f32)] * 2,
            pltpu.SemaphoreType.DMA((6,)),
            *send_scratch(),
            *near_scratch((32, d)),
            *exchange_scratch(1),
        ],
        compiler_params=pltpu.CompilerParams(collective_id=5, has_side_effects=True, vmem_limit_bytes=60 << 20),
        cost_estimate=cost(8, 4),
    )(piece_starts, gmo, mixed, q, k, v, lse, nattn, cosine, sine, w_attn, small, out_b, dw_a)
    alone = packs == 1
    zs, igrad, layer_out, small, nag = finish(
        wg, gp, gres, tokens, w_attn, yr, base, pos, params, small, tensor, alone, 6
    )
    if alone:
        wg, nag, dw_b = last(zs, nag, dw_b, tensor, 7)
    else:
        wg = lax.psum_scatter(wg, "dp", scatter_dimension=1, tiled=True)
        wg = lax.psum_scatter(wg, "tensor", scatter_dimension=2, tiled=True).astype(f32)
        nag = lax.psum(nag, ("dp", "tensor"))
        small = lax.psum(lax.psum(small, "tensor"), "dp", axis_index_groups=across)
        dw_b = exchange8(dw_b, 7)
    overflow = jnp.sum(small[28:29, 0:LANES]) > 0

    def roomy(args):
        return plain_on_device(*args)

    def packed(args):
        gate_up, down, qkv, wo, router, residual, vectors, blends, gain_attn, gain_moe = emit(dw_a, dw_b, wg, small, nag, ne)
        return (
            layer_out,
            igrad,
            pgrad[0:ne].T,
            gain_attn,
            qkv,
            wo,
            gain_moe,
            router.T,
            residual,
            vectors,
            blends,
            gate_up,
            down.transpose(0, 2, 1),
        )

    args = (
        tokens, prior_logits, expert_ids, expert_ranks, piece_starts, norm_attn, qkv_weight, out_weight, norm_moe,
        router_weight, residual_weight, const_vectors, const_gates, w_gate_up, w_down, out_grad,
    )
    return lax.cond(overflow, roomy, packed, args)


def solution(mesh):
    body = functools.partial(on_device, mesh.shape["dp"], mesh.shape["tensor"])
    rows = P(("dp", "tensor"), None)
    return jax.shard_map(
        body,
        mesh=mesh,
        in_specs=(
            rows, rows, P("dp", None), P("dp", None), P("dp", None), P(), P(None, "dp", "tensor"), P("tensor", "dp"),
            P(), P(), P(), P(), P(), P(None, None, "dp", "tensor"), P(None, "tensor", "dp"), rows,
        ),
        out_specs=(
            rows, rows, rows, P(), P(None, "dp", "tensor"), P("tensor", "dp"), P(), P(), P(), P(), P(),
            P(None, None, "dp", "tensor"), P(None, "tensor", "dp"),
        ),
        check_vma=False,
    )
```

```python
import functools

import jax
import jax.numpy as jnp
import numpy as np
from jax import lax
from jax.experimental import pallas as pl
from jax.experimental.pallas import tpu as pltpu
from jax.sharding import PartitionSpec as P

HD = 64
NF = 8
NC = 2
SEQ = 1024
PIECE = 256
PIECES = 2
CAP = 768
EPS = 1e-06
QT = 256
LANES = 128
TM = 256
ROOM = 256
Z0 = 16
CHOSEN = 32
RES = 6

bf16 = jnp.bfloat16
f32 = jnp.float32
i32 = jnp.int32

VM = pl.BlockSpec(memory_space=pltpu.VMEM)
SM = pl.BlockSpec(memory_space=pltpu.SMEM)
ANY = pl.BlockSpec(memory_space=pl.ANY)


def nn(a, b):
    return lax.dot_general(a, b, (((1,), (0,)), ((), ())), preferred_element_type=f32)


def nt(a, b):
    return lax.dot_general(a, b, (((1,), (1,)), ((), ())), preferred_element_type=f32)


def tn(a, b):
    return lax.dot_general(a, b, (((0,), (0,)), ((), ())), preferred_element_type=f32)


def split(x):
    hi = x.astype(bf16)
    return hi, (x - hi.astype(f32)).astype(bf16)


def lanes(rows):
    return lax.broadcasted_iota(i32, (rows, LANES), 1)


def rot(x, cosine, sine):
    first = lanes(x.shape[0]) % HD < HD // 2
    other = jnp.where(first, pltpu.roll(x, LANES - HD // 2, 1), pltpu.roll(x, HD // 2, 1))
    return x * cosine + other * sine


def head_masks():
    low = lax.broadcasted_iota(i32, (1, LANES), 1) < HD
    a = jnp.where(low, 1.0, 0.0)
    return a, 1.0 - a


def rotary_tables():
    place = np.arange(SEQ, dtype=np.float32)
    half = HD // 2
    freqs = np.power(np.float32(10000.0), np.arange(half, dtype=np.float32) * np.float32(-2.0 / HD)).astype(np.float32)
    angles = (place[:, None] * freqs[None, :]).astype(np.float32).astype(np.float64)
    c, s = np.cos(angles).astype(np.float32), np.sin(angles).astype(np.float32)
    return np.concatenate([c, c, c, c], 1), np.concatenate([-s, s, -s, s], 1)


def window_bias(starts_ref, tile, width, transposed):
    shape = (width, QT) if transposed else (QT, width)
    qpos = lax.broadcasted_iota(i32, shape, 1 if transposed else 0) + tile * QT
    kpos = lax.broadcasted_iota(i32, shape, 0 if transposed else 1) + tile * QT
    seen = jnp.where(kpos <= qpos, 1, 0)
    for piece in range(PIECES):
        s = starts_ref[lax.axis_index("tensor"), piece]
        both = jnp.where(qpos >= s, 1, 0) * jnp.where(qpos < s + PIECE, 1, 0)
        both = both * jnp.where(kpos >= s, 1, 0) * jnp.where(kpos < s + PIECE, 1, 0)
        seen = jnp.maximum(seen, both)
    return jnp.where(seen > 0, 0.0, -1e30)


MESH = pl.DeviceIdType.MESH
GATHER_COPIES = 13
REDUCE_COPIES = 10


def flip(index, m):
    for bit in (1, 2, 4):
        if m & bit:
            index = index + bit - 2 * bit * (index // bit % 2)
    return index


def remote(src, dst, sems, n, axis, peer):
    return pltpu.make_async_remote_copy(
        src_ref=src,
        dst_ref=dst,
        send_sem=sems.at[0, n],
        recv_sem=sems.at[1, n],
        device_id={axis: peer},
        device_id_type=MESH,
    )


def greet(peers):
    barrier = pltpu.get_barrier_semaphore()
    for axis, peer in peers:
        pl.semaphore_signal(barrier, inc=1, device_id={axis: peer}, device_id_type=MESH)
    pl.semaphore_wait(barrier, len(peers))


def near_peers():
    me = lax.axis_index("dp")
    return [("dp", flip(me, m)) for m in (1, 2, 4)]


def far_peers(tensor):
    me = lax.axis_index("tensor")
    return [("tensor", (me + k) % tensor) for k in range(1, tensor)]


class Gather8:
    def __init__(self, src, dst, sems, own_sem):
        me = lax.axis_index("dp")
        slot = me % NF
        nx, ny, nc = flip(me, 2), flip(me, 4), flip(me, 1)
        sx, sy, sd = flip(slot, 2), flip(slot, 4), flip(slot, 6)
        self.own = pltpu.make_async_copy(src(None), dst(slot, None), own_sem)
        go = lambda n, s, d, peer: remote(s, d, sems, n, "dp", peer)
        on = lambda n, s, h, peer: go(n, dst(s, h), dst(s, h), peer)
        self.c = [
            go(0, src(0), dst(slot, 0), nx),
            go(1, src(1), dst(slot, 1), ny),
            go(2, src(1), dst(slot, 1), nx),
            go(3, src(0), dst(slot, 0), ny),
            go(4, src(None), dst(slot, None), nc),
            on(5, sx, 0, ny),
            on(6, sy, 1, nx),
            on(7, sx, 0, nc),
            on(8, sy, 1, nc),
            on(9, sx, 1, nc),
            on(10, sy, 0, nc),
            on(11, sd, 0, nc),
            on(12, sd, 1, nc),
        ]

    def begin(self):
        self.own.start()
        for n in range(5):
            self.c[n].start()

    def forward(self):
        for got, out in ((0, (5, 7)), (1, (6, 8))):
            self.c[got].wait_recv()
            for n in out:
                self.c[n].start()

    def share(self):
        for got, out in ((2, 9), (3, 10)):
            self.c[got].wait_recv()
            self.c[out].start()

    def last(self):
        for got, out in ((5, 11), (6, 12)):
            self.c[got].wait_recv()
            self.c[out].start()

    def end(self):
        for n in (4, 7, 8, 9, 10, 11, 12):
            self.c[n].wait_recv()
        for c in self.c:
            c.wait_send()
        self.own.wait()


def halves(ref, index, rows):
    half = rows // 2
    return lambda s, h: ref.at[s] if h is None else ref.at[s, pl.ds(h * half, half)]


def all_peers():
    me = lax.axis_index("dp")
    return [("dp", flip(me, m)) for m in range(1, NF)]


class Swap8:
    def __init__(self, src, dst, sems, own_sems):
        me = lax.axis_index("dp")
        slot = me % NF
        count = src.shape[0] // NF
        self.own = [
            pltpu.make_async_copy(src.at[NF * i + slot], dst.at[NF * i + slot], own_sems.at[i]) for i in range(count)
        ]
        self.c = [
            remote(
                src.at[NF * i + flip(slot, m)], dst.at[NF * i + slot], sems, (m - 1) * count + i, "dp", flip(me, m)
            )
            for m in range(1, NF)
            for i in range(count)
        ]

    def begin(self):
        for c in self.own + self.c:
            c.start()

    def end(self):
        for c in self.c:
            c.wait_recv()
        for c in self.c:
            c.wait_send()
        for c in self.own:
            c.wait()


def routes(ids_ref, ranks_ref, i):
    start = lax.axis_index("tensor") * SEQ + i * QT
    cols = pl.ds(pl.multiple_of(start, QT), QT)
    at = lax.broadcasted_iota(i32, (16, QT), 0)
    hit0, hit1 = (jnp.where(at == ids_ref[n : n + 1, cols], 1.0, 0.0) for n in range(2))
    keep0, keep1 = (jnp.where(ranks_ref[n : n + 1, cols] < CAP, 1.0, 0.0) for n in range(2))
    return hit0 + hit1, (hit0 * keep0 + hit1 * keep1) * jnp.where(at < NF, 1.0, 0.0)


def weights_kernel(
    gather, zq_ref, zo_ref, gu_ref, dn_ref, ids_ref, ranks_ref, og_ref, out_ref, wx_ref, pos_ref, count_ref, ys_ref, slab, sems,
    own_sem, *scratch,
):
    k, r, _ = slab.shape
    tensor, _, _, f = zq_ref.shape
    for t in range(0, tensor, 2):
        at = slice(t * f, (t + 2) * f)
        for c in range(k - 1):
            slab[c, :, at] = jnp.concatenate([zq_ref[n, c].astype(f32) for n in (t, t + 1)], axis=1).astype(bf16)
        both = jnp.concatenate([zo_ref[n].astype(f32) for n in (t, t + 1)], axis=0)
        wide = jnp.concatenate([both, jnp.zeros((2 * f, -r % LANES), f32)], axis=1)
        slab[k - 1, :, at] = wide.T[0:r, :].astype(bf16)
    greet(all_peers())
    part = lambda h: pl.ds(0, k) if h is None else pl.ds(h * (k // 2), k // 2)
    if gather:
        g = Gather8(
            lambda h: slab.at[part(h)],
            lambda s, h: out_ref.at[part(h), pl.ds(pl.multiple_of(s * r, r), r), :],
            sems,
            own_sem,
        )
        g.begin()
    swap = Exchange8([gu_ref, dn_ref], wx_ref, 1, *scratch)
    swap.begin()
    upper = jnp.where(
        lax.broadcasted_iota(i32, (QT, QT), 0) < lax.broadcasted_iota(i32, (QT, QT), 1), 1.0, 0.0
    ).astype(bf16)
    taken = jnp.zeros((16, 1), f32)
    for i in range(SEQ // QT):
        _, kept = routes(ids_ref, ranks_ref, i)
        pos = jnp.where(kept > 0, nn(kept.astype(bf16), upper) + taken, -1.0)
        pos_ref[:, 0, i * QT : (i + 1) * QT] = pos[0:NF, :]
        taken = taken + jnp.sum(kept, axis=1, keepdims=True)
    count_ref[...] = jnp.broadcast_to(taken, (16, LANES))
    slot = lax.axis_index("dp") % NF

    def pack(*blocks):
        for m in blocks:
            ys_ref[m] = nn(hot_rows(pos_ref[flip(slot, m)]), og_ref[...]).astype(bf16)

    pack(0, 1)
    if gather:
        g.forward()
    pack(2, 3)
    if gather:
        g.share()
    pack(4, 5)
    if gather:
        g.last()
    pack(6, 7)
    if gather:
        g.end()
    swap.end()


def gather_weights(zq, zo, gate_up, down, ids, ranks, og, gather, cid):
    tensor, k, r, f = zq.shape
    k, f = k + 1, tensor * f
    return pl.pallas_call(
        functools.partial(weights_kernel, gather),
        in_specs=[VM] * 2 + [ANY] * 2 + [VM] * 3,
        out_specs=[ANY] * 2 + [VM] * 4,
        out_shape=(
            shape((k, NF * r, f), bf16), half_shape(gate_up), shape((NF, 1, og.shape[0]), f32),
            shape((16, LANES), f32), shape((NF, ROOM, og.shape[1]), bf16),
            shape((k, r, f), bf16),
        ),
        scratch_shapes=[
            pltpu.SemaphoreType.DMA((2, GATHER_COPIES)),
            pltpu.SemaphoreType.DMA,
            *exchange_scratch(2),
        ],
        compiler_params=pltpu.CompilerParams(collective_id=cid, has_side_effects=True, vmem_limit_bytes=60 << 20),
        cost_estimate=cost(35, 10),
    )(zq, zo, gate_up, down, ids, ranks, og)


class Reduce8:
    def __init__(self, view, bufs, sems, lsems):
        self.own, self.away, self.ind, self.inx, self.iny = bufs
        me = lax.axis_index("dp")
        slot = me % NF
        half = self.ind.shape[0] // 2
        a, b = pl.ds(0, half), pl.ds(half, half)
        self.a, self.b = a, b
        nx, ny, nc = flip(me, 2), flip(me, 4), flip(me, 1)
        mine = [flip(slot, m) for m in (6, 2, 4)] + [slot]
        self.loads = [pltpu.make_async_copy(view(s), self.own.at[n % 2], lsems.at[n]) for n, s in enumerate(mine)]
        self.over = [remote(view(flip(s, 1)), self.away.at[n], sems, n, "dp", nc) for n, s in enumerate(mine)]
        go = lambda n, k, i, part, peer: remote(self.away.at[k, part], i.at[part], sems, n, "dp", peer)
        self.da, self.db = go(4, 0, self.ind, a, nx), go(5, 0, self.ind, b, ny)
        self.xa, self.yb = go(6, 1, self.inx, a, nx), go(7, 2, self.iny, b, ny)
        self.ya, self.xb = go(8, 2, self.iny, a, ny), go(9, 1, self.inx, b, nx)

    def load(self):
        self.loads[0].start()
        self.loads[1].start()

    def begin(self):
        for c in self.over:
            c.start()

    def add(self, n, part):
        self.away[n, part] = (self.own[n % 2, part].astype(f32) + self.away[n, part].astype(f32)).astype(bf16)

    def more(self, n, part):
        self.away[n, part] = (self.away[n, part].astype(f32) + self.ind[part].astype(f32)).astype(bf16)

    def ready(self, n):
        self.loads[n].wait()
        self.over[n].wait_recv()

    def first(self):
        self.ready(0)
        self.add(0, self.a)
        self.da.start()
        self.add(0, self.b)
        self.db.start()
        self.loads[2].start()

    def second(self):
        self.ready(1)
        self.add(1, self.a)
        self.xa.start()
        self.add(1, self.b)
        self.loads[3].start()
        self.ready(2)
        self.add(2, self.b)
        self.yb.start()
        self.add(2, self.a)

    def third(self):
        self.da.wait_recv()
        self.more(2, self.a)
        self.ya.start()
        self.db.wait_recv()
        self.more(1, self.b)
        self.xb.start()

    def end(self, write):
        self.ready(3)
        for part, first, second in ((self.a, self.xa, self.ya), (self.b, self.yb, self.xb)):
            first.wait_recv()
            second.wait_recv()
            total = self.own[1, part].astype(f32) + self.away[3, part].astype(f32)
            write(part, total + self.inx[part].astype(f32) + self.iny[part].astype(f32))

    def close(self):
        for c in self.over + [self.da, self.db, self.xa, self.yb, self.ya, self.xb]:
            c.wait_send()


def reduce_scratch(block):
    return [pltpu.VMEM((2, *block), bf16), pltpu.VMEM((4, *block), bf16)] + [pltpu.VMEM(block, bf16)] * 3 + [
        pltpu.SemaphoreType.DMA((2, REDUCE_COPIES)),
        pltpu.SemaphoreType.DMA((4,)),
    ]


class Exchange8:
    def __init__(self, srcs, dst, part, sems, own_sems):
        me = lax.axis_index("dp")
        slot = me % NF
        width = dst.shape[-1]

        def piece(src, e):
            return src.at[:, e] if part is None else src.at[:, e, :, pl.ds(part * width, width)]

        at, pieces = 0, []
        for src in srcs:
            pieces.append((src, pl.ds(at, src.shape[0])))
            at += src.shape[0]
        self.own = [
            pltpu.make_async_copy(piece(src, slot), dst.at[rows, slot], own_sems.at[i])
            for i, (src, rows) in enumerate(pieces)
        ]
        self.c = [
            remote(
                piece(src, flip(slot, m)), dst.at[rows, slot], sems, (m - 1) * len(srcs) + i, "dp", flip(me, m)
            )
            for m in (6, 7, 2, 3, 4, 5, 1)
            for i, (src, rows) in enumerate(pieces)
        ]

    def begin(self):
        for c in self.c + self.own:
            c.start()

    def end(self):
        for c in self.c:
            c.wait_recv()
        for c in self.c:
            c.wait_send()
        for c in self.own:
            c.wait()


class Send8:
    order = (6, 7, 2, 3, 4, 5, 1)

    def __init__(self, src, dst, sems, own_sem, packed):
        me = lax.axis_index("dp")
        slot = me % NF
        at = lambda m: src.at[m] if packed else src.at[flip(slot, m)]
        self.slot = slot
        self.own = pltpu.make_async_copy(at(0), dst.at[slot], own_sem)
        self.c = {m: remote(at(m), dst.at[slot], sems, m - 1, "dp", flip(me, m)) for m in self.order}

    def start(self, m):
        (self.c[m] if m else self.own).start()

    def begin(self):
        for m in (*self.order, 0):
            self.start(m)

    def got(self, m):
        if m:
            self.c[m].wait_recv()
        else:
            self.own.wait()

    def close(self):
        for c in self.c.values():
            c.wait_send()


def send_scratch():
    return [pltpu.SemaphoreType.DMA((2, NF - 1)), pltpu.SemaphoreType.DMA]


def half_shape(gate_up):
    _, groups, r, f = gate_up.shape
    return shape((3, groups, r, f // 2), bf16)


def exchange_scratch(n):
    return [pltpu.SemaphoreType.DMA((2, (NF - 1) * n)), pltpu.SemaphoreType.DMA((n,))]


def prologue_kernel(tensor, gu_ref, dn_ref, w_ref, wo_ref, out_ref, zq_ref, zo_ref, zsems, own_sems, *scratch):
    here = lax.axis_index("tensor")
    pairs = ((w_ref, zq_ref.at[here]), (wo_ref, zo_ref.at[here]))
    own = [pltpu.make_async_copy(src, dst, own_sems.at[i]) for i, (src, dst) in enumerate(pairs)]
    for c in own:
        c.start()
    greet(all_peers() + far_peers(tensor))
    copies = [
        remote(src, dst, zsems, 2 * n + i, axis, peer)
        for n, (axis, peer) in enumerate(far_peers(tensor))
        for i, (src, dst) in enumerate(pairs)
    ]
    for c in copies:
        c.start()
    swap = Exchange8([gu_ref, dn_ref], out_ref, 0, *scratch)
    swap.begin()
    for c in copies:
        c.wait_recv()
    swap.end()
    for c in copies:
        c.wait_send()
    for c in own:
        c.wait()


def prologue(gate_up, down, w, wo, tensor, cid):
    return pl.pallas_call(
        functools.partial(prologue_kernel, tensor),
        in_specs=[ANY] * 4,
        out_specs=[ANY] * 3,
        out_shape=(half_shape(gate_up), shape((tensor, *w.shape), bf16), shape((tensor, *wo.shape), bf16)),
        scratch_shapes=[
            pltpu.SemaphoreType.DMA((2, 2 * (tensor - 1))),
            pltpu.SemaphoreType.DMA((2,)),
            *exchange_scratch(2),
        ],
        compiler_params=pltpu.CompilerParams(collective_id=cid, has_side_effects=True, vmem_limit_bytes=60 << 20),
        cost_estimate=cost(25, 10),
    )(gate_up, down, w, wo)


def exchange_kernel(src, dst, *scratch):
    greet(all_peers())
    swap = Exchange8([src], dst, None, *scratch)
    swap.begin()
    swap.end()


def exchange8(x, cid):
    return pl.pallas_call(
        exchange_kernel,
        in_specs=[ANY],
        out_specs=ANY,
        out_shape=shape(x.shape, x.dtype),
        scratch_shapes=exchange_scratch(1),
        compiler_params=pltpu.CompilerParams(collective_id=cid, has_side_effects=True),
        cost_estimate=cost(18, 10),
    )(x)


class Near:
    def __init__(self, have, got, sems):
        me = lax.axis_index("dp")
        self.have, self.got = have, got
        self.c = [remote(have.at[n], got.at[n], sems, n, "dp", flip(me, m)) for n, m in enumerate((1, 2, 4))]

    def begin(self):
        self.c[0].start()

    def step(self, n):
        self.c[n].wait_recv()
        self.have[n + 1] = self.have[n] + self.got[n]
        if n < 2:
            self.c[n + 1].start()

    def close(self):
        for c in self.c:
            c.wait_send()


def near_scratch(dims):
    return [pltpu.VMEM((4, *dims), f32), pltpu.VMEM((3, *dims), f32), pltpu.SemaphoreType.DMA((2, 3))]


class Far:
    def __init__(self, tensor, value, have, got, sems):
        self.tensor, self.value, self.have, self.got, self.here = tensor, value, have, got, lax.axis_index("tensor")
        self.c = [
            remote(have, got.at[self.here], sems, n, axis, peer) for n, (axis, peer) in enumerate(far_peers(tensor))
        ]

    def begin(self):
        self.have[...] = self.value[...].astype(bf16)
        for c in self.c:
            c.start()
        self.got[self.here] = self.have[...]

    def end(self):
        for c in self.c:
            c.wait_recv()
        total = self.got[0].astype(f32)
        for t in range(1, self.tensor):
            total = total + self.got[t].astype(f32)
        for c in self.c:
            c.wait_send()
        return total


def far_scratch(tensor, dims):
    return [pltpu.VMEM(dims, bf16), pltpu.VMEM((tensor, *dims), bf16), pltpu.SemaphoreType.DMA((2, tensor - 1))]


def final_kernel(
    tensor, comm, g_ref, gp_any, gres_any, tok_any, w_any, yr_any, base_any, pos_ref, par_ref, small_ref,
    zs_ref, igrad_ref, layer_ref, total_ref, nag_ref,
    gp_ref, gres_ref, tok_ref, w_ref, yr_ref, base_ref, lsems, *scratch,
):
    k, d, _ = g_ref.shape
    ntile = SEQ // QT
    pairs = (
        (gp_any, gp_ref), (w_any.at[pl.ds(0, 3)], w_ref), (tok_any, tok_ref), (gres_any, gres_ref), (yr_any, yr_ref),
        (base_any, base_ref),
    )
    loads = [pltpu.make_async_copy(src, dst, lsems.at[n]) for n, (src, dst) in enumerate(pairs)]
    if comm:
        r, f = zs_ref.shape[2:]
        red = Reduce8(lambda s: g_ref.at[:, pl.ds(pl.multiple_of(s * r, r), r), :], scratch[:5], *scratch[5:7])
        sums, smalls = Near(*scratch[7:10]), Far(tensor, small_ref, *scratch[10:13])
        red.load()
        greet(near_peers() + far_peers(tensor))
        red.begin()
        smalls.begin()
    for c in loads:
        c.start()
    ga = par_ref[24:25, :].astype(f32)
    if comm:
        red.first()
        red.second()
    for c in loads[:4]:
        c.wait()
    nag = jnp.zeros((1, d), f32)
    for i in range(ntile):
        rows = pl.ds(i * QT, QT)
        gai = nt(gp_ref[0, rows, :], w_ref[0]) + nt(gp_ref[1, rows, :], w_ref[1])
        gai = gai + nt(gp_ref[2, rows, :], w_ref[2])
        x = tok_ref[rows, :].astype(f32)
        r1 = lax.rsqrt(jnp.mean(x * x, axis=-1, keepdims=True) + EPS)
        nag = nag + jnp.sum(gai * x * r1, axis=0, keepdims=True)
        scaled = gai * ga
        avg = jnp.mean(scaled * x, axis=-1, keepdims=True)
        igrad_ref[rows, :] = gres_ref[rows, :] + r1 * scaled - x * (r1 * r1 * r1 * avg)
        if comm and i == 0:
            red.third()
    if comm:
        sums.have[0] = nag
        sums.begin()
    else:
        nag_ref[...] = nag
        total_ref[...] = small_ref[...]
    for c in loads[4:]:
        c.wait()

    def layer(i):
        rows = pl.ds(i * QT, QT)
        total = base_ref[rows, :]
        for e in range(NF):
            total = total + tn(hot_rows(pos_ref[e, :, rows]), yr_ref[e])
        layer_ref[rows, :] = total.astype(bf16)

    def write(part, total):
        for t in range(tensor):
            zs_ref[t, part] = total[:, :, t * f : (t + 1) * f].astype(bf16)

    for i in range(ntile):
        layer(i)
        if comm and i < 3:
            sums.step(i)
    if not comm:
        return
    for i in range(ntile, 3):
        sums.step(i)
    nag_ref[...] = sums.have[3]
    red.end(write)
    total_ref[...] = smalls.end()
    red.close()
    sums.close()


def last_kernel(tensor, zs_ref, small_ref, dw_ref, out_ref, total_ref, dwx_ref, zr, zsems, *scratch):
    here = lax.axis_index("tensor")
    smalls = Far(tensor, small_ref, *scratch[0:3])
    swap = Exchange8([dw_ref], dwx_ref, None, *scratch[3:5])
    greet(all_peers() + far_peers(tensor))
    copies = [
        remote(zs_ref.at[peer], zr.at[here], zsems, n, axis, peer) for n, (axis, peer) in enumerate(far_peers(tensor))
    ]
    for c in copies:
        c.start()
    smalls.begin()
    swap.begin()
    zr[here] = zs_ref[here]
    for c in copies:
        c.wait_recv()
    total = zr[0].astype(f32)
    for t in range(1, tensor):
        total = total + zr[t].astype(f32)
    out_ref[...] = total
    total_ref[...] = smalls.end()
    for c in copies:
        c.wait_send()
    swap.end()


def last(zs, small, dw, tensor, cid):
    return pl.pallas_call(
        functools.partial(last_kernel, tensor),
        in_specs=[VM] * 2 + [ANY],
        out_specs=[VM] * 2 + [ANY],
        out_shape=(shape(zs.shape[1:], f32), shape(small.shape, f32), shape(dw.shape, dw.dtype)),
        scratch_shapes=[
            pltpu.VMEM(zs.shape, bf16),
            pltpu.SemaphoreType.DMA((2, tensor - 1)),
            *far_scratch(tensor, small.shape),
            *exchange_scratch(1),
        ],
        compiler_params=pltpu.CompilerParams(collective_id=cid, has_side_effects=True, vmem_limit_bytes=60 << 20),
        cost_estimate=cost(18, 10),
    )(zs, small, dw)


def finish(g, gp, gres, tokens, w, yr, base, pos, params, small, tensor, comm, cid):
    k, d, columns = g.shape
    rows = tokens.shape[0]
    r, f = (d // NF if comm else 8), columns // tensor
    once = pltpu.CompilerParams(vmem_limit_bytes=60 << 20)
    if comm:
        once = pltpu.CompilerParams(collective_id=cid, has_side_effects=True, vmem_limit_bytes=60 << 20)
    return pl.pallas_call(
        functools.partial(final_kernel, tensor, comm),
        in_specs=[ANY] * 7 + [VM] * 3,
        out_specs=[VM] * 5,
        out_shape=(
            shape((tensor, k, r, f), bf16), shape((rows, d), f32), shape((rows, d), bf16), shape(small.shape, f32),
            shape((1, d), f32),
        ),
        scratch_shapes=[
            pltpu.VMEM(gp.shape, bf16),
            pltpu.VMEM((rows, d), f32),
            pltpu.VMEM((rows, d), bf16),
            pltpu.VMEM((3, d, columns), bf16),
            pltpu.VMEM(yr.shape, bf16),
            pltpu.VMEM((rows, d), f32),
            pltpu.SemaphoreType.DMA((6,)),
            *reduce_scratch((k, r, columns)),
            *near_scratch((1, d)),
            *far_scratch(tensor, small.shape),
        ],
        compiler_params=once,
        cost_estimate=cost(8, 4),
    )(g, gp, gres, tokens, w, yr, base, pos, params, small)


def fwd_kernel(
    starts_ref, tok_ref, prior_ref, ids_ref, ranks_ref, par_ref, cos_ref, sin_ref, w_ref, pos_ref, ys,
    q_ref, k_ref, v_ref, mixed_ref, lse_ref, nattn_ref, resid_ref, nmoe_ref, base_ref, aux_ref, xr_ref, yr_ref, payr_ref,
    bias_ref, gate_ref, xs, pay, wr_ref, *scratch,
):
    greet(all_peers())
    send_x, send_y = Send8(xs, xr_ref, *scratch[0:2], True), Send8(ys, yr_ref, *scratch[2:4], True)
    swap = Swap8(pay, payr_ref, *scratch[4:6])
    send_y.begin()
    lane = lanes(QT)
    router_rows(par_ref, wr_ref)
    wres = par_ref[32:48, 0:LANES]
    d = tok_ref.shape[1]
    pairs = d // LANES
    ntile = SEQ // QT
    ga, gm = par_ref[24:25, :].astype(f32), par_ref[25:26, :].astype(f32)
    cv = par_ref[26:28, :].astype(f32)
    mask_a, mask_b = head_masks()
    mask16 = (mask_a.astype(bf16), mask_b.astype(bf16))

    def project(i, carry):
        rows = pl.ds(pl.multiple_of(i * QT, QT), QT)
        x = tok_ref[rows, :].astype(f32)
        r1 = lax.rsqrt(jnp.mean(x * x, axis=-1, keepdims=True) + EPS)
        n = (x * r1 * ga).astype(bf16)
        nattn_ref[rows, :] = n
        cosine, sine = cos_ref[rows, :], sin_ref[rows, :]
        for c, out in ((0, q_ref), (1, k_ref), (2, v_ref)):
            proj = nn(n, w_ref[c])
            for p in range(pairs):
                part = proj[:, p * LANES : (p + 1) * LANES]
                if c < 2:
                    part = rot(part, cosine, sine)
                part = part.astype(bf16)
                if c == 0:
                    part = part * jnp.array(HD**-0.5, bf16)
                out[rows, p * LANES : (p + 1) * LANES] = part
        return carry

    lax.fori_loop(0, ntile, project, 0)

    for i in range(ntile):
        lo = i * QT
        width = min(SEQ, lo + 2 * QT) - lo
        rows = pl.ds(lo, QT)
        bias_ref[:, :width] = window_bias(starts_ref, i, width, False)

        def pair(p, lse):
            cols = pl.ds(pl.multiple_of(p * LANES, LANES), LANES)
            q2 = q_ref[rows, cols]
            outs = []
            for h in range(2):
                qh = q2 * mask16[h]
                sb = nt(qh, k_ref[lo : lo + width, cols]) + bias_ref[:, :width]
                m = jnp.max(sb, axis=-1, keepdims=True)
                if lo:
                    sa = nt(qh, k_ref[0:lo, cols])
                    m = jnp.maximum(m, jnp.max(sa, axis=-1, keepdims=True))
                pb = jnp.exp(sb - m)
                total = jnp.sum(pb, axis=-1, keepdims=True)
                acc = nn(pb.astype(bf16), v_ref[lo : lo + width, cols])
                if lo:
                    pa = jnp.exp(sa - m)
                    total = total + jnp.sum(pa, axis=-1, keepdims=True)
                    acc = acc + nn(pa.astype(bf16), v_ref[0:lo, cols])
                outs.append(acc / total)
                lse = jnp.where(lane == 2 * p + h, m + jnp.log(total), lse)
            mixed_ref[rows, cols] = (outs[0] * mask_a + outs[1] * mask_b).astype(bf16)
            return lse

        lse = lax.fori_loop(0, pairs, pair, jnp.zeros((QT, LANES), f32))
        lse_ref[:, rows] = lse.T[0 : lse_ref.shape[0], :]

        x = tok_ref[rows, :].astype(f32)
        resid = x + nt(mixed_ref[rows, :], w_ref[3])
        resid_ref[rows, :] = resid
        r2 = lax.rsqrt(jnp.mean(resid * resid, axis=-1, keepdims=True) + EPS)
        nm = (resid * r2 * gm).astype(bf16)
        nmoe_ref[rows, :] = nm
        raw = nt(nm, wr_ref[...])
        logits = raw + tn(prior_ref[:, rows], wres)
        logits = jnp.where(lane < NF + 2 + NC, logits, -1e30)
        e = jnp.exp(logits - jnp.max(logits, axis=-1, keepdims=True))
        shares = e / jnp.sum(e, axis=-1, keepdims=True)
        chosen, kept = routes(ids_ref, ranks_ref, i)
        gate_ref[:, 0, rows] = shares.T[0:NF, :] * kept[0:NF, :]
        chosen = jnp.concatenate([chosen, jnp.zeros((LANES - 16, QT), f32)], axis=0).T
        gates = shares * chosen
        nv = nm.astype(f32)
        aux = jnp.where(lane < NF + 2 + NC, shares, 0.0) + pltpu.roll(chosen, CHOSEN, 1)
        direct = gates[:, NF + 1 : NF + 2]
        others = None
        for c in range(NC):
            z0, z1 = raw[:, Z0 + 2 * c : Z0 + 2 * c + 1], raw[:, Z0 + 2 * c + 1 : Z0 + 2 * c + 2]
            m0, m1 = 1.0 / (1.0 + jnp.exp(z1 - z0)), 1.0 / (1.0 + jnp.exp(z0 - z1))
            aux = jnp.where(lane == Z0 + 2 * c, m0, aux)
            aux = jnp.where(lane == Z0 + 2 * c + 1, m1, aux)
            w = gates[:, NF + 2 + c : NF + 3 + c]
            direct = direct + w * m0
            term = (w * m1) * cv[c : c + 1, :]
            others = term if others is None else others + term
        aux_ref[rows, :] = aux
        base_ref[rows, :] = resid + direct * nv + others

    for m in (*Send8.order, 0):
        e = flip(send_x.slot, m)
        place = pos_ref[e]
        hot = hot_rows(place)
        xs[m] = nn(hot, nmoe_ref[...]).astype(bf16)
        send_x.start(m)
        pay[e] = jnp.sum(nt(split_rows(gate_ref[e]), hot), axis=0, keepdims=True)
        filled = jnp.minimum(jnp.max(place, axis=1, keepdims=True) + 1.0, float(ROOM))
        pay[NF + e] = jnp.broadcast_to(filled, (1, ROOM))
    swap.begin()
    for send in (send_y, send_x):
        for m in (*Send8.order, 0):
            send.got(m)
        send.close()
    swap.end()


def mid_kernel(
    dxb_ref, ggb_ref, og_any, nmoe_any, resid_any, aux_any, pos_ref, prior_ref, par_ref, count_ref,
    gmo_ref, gres_ref, pgrad_ref, small_ref,
    dxr, ggr, dx_ref, gg_ref, inner_ref, extra_ref, wr_ref, resg_ref, og_ref, nmoe_ref, resid_ref, aux_ref, lsems, *scratch,
):
    pairs = ((og_any, og_ref), (nmoe_any, nmoe_ref), (resid_any, resid_ref), (aux_any, aux_ref))
    loads = [pltpu.make_async_copy(a, b, lsems.at[n]) for n, (a, b) in enumerate(pairs)]
    for c in loads:
        c.start()
    greet(all_peers())
    send, swap = Send8(dxb_ref, dxr, *scratch[0:2], False), Swap8(ggb_ref, ggr, *scratch[2:4])
    swap.begin()
    send.begin()
    gm, cv = par_ref[25:26, :].astype(f32), par_ref[26:28, :].astype(f32)
    wres = par_ref[32:48, 0:LANES]
    router_rows(par_ref, wr_ref)
    lane = lanes(QT)
    small_ref[...] = jnp.zeros_like(small_ref)
    resg_ref[...] = jnp.zeros_like(resg_ref)
    small_ref[28:29, 0:LANES] = jnp.max(jnp.where(count_ref[...] > ROOM, 1.0, 0.0), axis=0, keepdims=True)

    def ahead(i, carry):
        rows = pl.ds(pl.multiple_of(i * QT, QT), QT)
        g16 = og_ref[rows, :]
        g, nv = g16.astype(f32), nmoe_ref[rows, :].astype(f32)
        x = resid_ref[rows, :]
        aux = aux_ref[rows, :]
        chosen = jnp.where(lane < 16, pltpu.roll(aux, LANES - CHOSEN, 1), 0.0)
        gates = jnp.where(lane < NF + 2 + NC, aux, 0.0) * chosen
        copy_inner = jnp.sum(g * nv, axis=-1, keepdims=True)
        inner = jnp.where(lane == NF + 1, copy_inner, 0.0)
        direct = gates[:, NF + 1 : NF + 2]
        extra = jnp.where(lane == 1, lax.rsqrt(jnp.mean(x * x, axis=-1, keepdims=True) + EPS), 0.0)
        cvw = jnp.zeros((QT, LANES), f32)
        for c in range(NC):
            m0, m1 = aux[:, Z0 + 2 * c : Z0 + 2 * c + 1], aux[:, Z0 + 2 * c + 1 : Z0 + 2 * c + 2]
            v_inner = jnp.sum(g * cv[c : c + 1, :], axis=-1, keepdims=True)
            mean = m0 * copy_inner + m1 * v_inner
            inner = jnp.where(lane == NF + 2 + c, mean, inner)
            w = gates[:, NF + 2 + c : NF + 3 + c]
            direct = direct + w * m0
            extra = jnp.where(lane == Z0 + 2 * c, m0 * (w * copy_inner - w * mean), extra)
            extra = jnp.where(lane == Z0 + 2 * c + 1, m1 * (w * v_inner - w * mean), extra)
            cvw = jnp.where(lane == c, w * m1, cvw)
        inner_ref[rows, :] = inner
        extra_ref[rows, :] = jnp.where(lane == 0, direct, extra)
        cv_hi, cv_lo = split(cvw)
        small_ref[24:26, :] += tn(cv_hi, g16)[0:NC] + tn(cv_lo, g16)[0:NC]
        return carry

    for c in loads:
        c.wait()
    lax.fori_loop(0, SEQ // QT, ahead, 0)
    swap.end()
    for n, m in enumerate((0, 1, 2, 3, 4, 5, 6, 7)):
        send.got(m)
        e = flip(send.slot, m)
        hot = hot_rows(pos_ref[e])
        gg_ref[pl.ds(e, 1), :] = jnp.sum(nn(split_rows(ggr[e]), hot), axis=0, keepdims=True)
        part = tn(hot, dxr[e])
        if n:
            dx_ref[...] += part
        else:
            dx_ref[...] = part
    send.close()

    def tile(i, carry):
        rows = pl.ds(pl.multiple_of(i * QT, QT), QT)
        g, n16 = og_ref[rows, :].astype(f32), nmoe_ref[rows, :]
        x = resid_ref[rows, :]
        aux, extra = aux_ref[rows, :], extra_ref[rows, :]
        direct, r2 = extra[:, 0:1], extra[:, 1:2]
        shares = jnp.where(lane < NF + 2 + NC, aux, 0.0)
        chosen = jnp.where(lane < 16, pltpu.roll(aux, LANES - CHOSEN, 1), 0.0)
        inner = jnp.concatenate([gg_ref[:, rows], jnp.zeros((LANES - NF, QT), f32)], axis=0).T
        grad_router = (inner + inner_ref[rows, :]) * chosen
        glog = shares * (grad_router - jnp.sum(shares * grad_router, axis=-1, keepdims=True))
        both_hi, both_lo = split(glog + jnp.where(lane >= Z0, extra, 0.0))
        log_hi, log_lo = split(glog)
        pgrad_ref[:, rows] = nt(wres, log_hi) + nt(wres, log_lo)
        small_ref[0:24, :] += tn(both_hi, n16)[0:24] + tn(both_lo, n16)[0:24]
        resg_ref[...] += nn(prior_ref[:, rows], log_hi) + nn(prior_ref[:, rows], log_lo)
        gmi = dx_ref[rows, :] + direct * g + nn(both_hi, wr_ref[...]) + nn(both_lo, wr_ref[...])
        small_ref[26:27, :] += jnp.sum(gmi * x * r2, axis=0, keepdims=True)
        scaled = gmi * gm
        avg = jnp.mean(scaled * x, axis=-1, keepdims=True)
        gres = g + r2 * scaled - x * (r2 * r2 * r2 * avg)
        gres_ref[rows, :] = gres
        gmo_ref[rows, :] = gres.astype(bf16)
        return carry

    lax.fori_loop(0, SEQ // QT, tile, 0)
    for n in range(NF + 2 + NC):
        at = n % RES * LANES
        small_ref[29 + n // RES : 30 + n // RES, at : at + LANES] = resg_ref[n : n + 1, :]


def bwd_kernel(
    starts_ref, gmo_ref, mixed_ref, q_any, k_any, v_any, lse_ref, nattn_any, cos_any, sin_any, w_any, small_ref,
    outb_ref, dw_ref,
    wg_ref, gp_ref, outr_ref, total_ref, dwx_ref,
    do_ref, delta_ref, bias_ref, dk_ref, dv_ref, dq_ref, wo_ref, wsem, q_ref, k_ref, v_ref, nattn_ref, cos_ref, sin_ref, lsems,
    *scratch,
):
    late = ((q_any, q_ref), (k_any, k_ref), (v_any, v_ref), (cos_any, cos_ref), (sin_any, sin_ref), (nattn_any, nattn_ref))
    loads = [pltpu.make_async_copy(a, b, lsems.at[n]) for n, (a, b) in enumerate(late)]
    load = pltpu.make_async_copy(w_any.at[pl.ds(3, 1)], wo_ref, wsem)
    load.start()
    send = Send8(outb_ref, outr_ref, *scratch[0:2], False)
    sums = Near(*scratch[2:5])
    sums.have[0] = small_ref[...]
    greet(all_peers())
    sums.begin()
    send.begin()
    swap = Exchange8([dw_ref], dwx_ref, None, *scratch[5:7])
    swap.begin()
    for c in loads:
        c.start()
    d = mixed_ref.shape[1]
    pairs = d // LANES
    ntile = SEQ // QT
    mask_a, mask_b = head_masks()
    mask16 = (mask_a.astype(bf16), mask_b.astype(bf16))
    maskf = (mask_a, mask_b)
    heads = delta_ref.shape[0]
    pick = jnp.where(
        lax.broadcasted_iota(i32, (heads, d), 1) // HD == lax.broadcasted_iota(i32, (heads, d), 0), 1.0, 0.0
    ).astype(bf16)

    load.wait()

    def start(i, carry):
        rows = pl.ds(pl.multiple_of(i * QT, QT), QT)
        do = nn(gmo_ref[rows, :], wo_ref[0]).astype(bf16)
        do_ref[rows, :] = do
        hi, lo = split(do.astype(f32) * mixed_ref[rows, :].astype(f32))
        delta_ref[:, rows] = nt(pick, hi) + nt(pick, lo)
        return carry

    lax.fori_loop(0, ntile, start, 0)
    sums.step(0)
    wg_ref[3] = tn(gmo_ref[...], mixed_ref[...]).astype(wg_ref.dtype)
    for i in range(ntile):
        width = min(SEQ, (i + 2) * QT) - i * QT
        bias_ref[i, 0:width, :] = window_bias(starts_ref, i, width, True)

    def pair(p, carry):
        cols = pl.ds(pl.multiple_of(p * LANES, LANES), LANES)
        dk_ref[...] = jnp.zeros_like(dk_ref)
        dv_ref[...] = jnp.zeros_like(dv_ref)
        for i in range(ntile):
            lo = i * QT
            width = min(SEQ, lo + 2 * QT) - lo
            rows = pl.ds(lo, QT)
            q2, do2 = q_ref[rows, cols], do_ref[rows, cols]
            dq = jnp.zeros((QT, LANES), f32)
            for h in range(2):
                qh, doh = q2 * mask16[h], do2 * mask16[h]
                lse, delta = lse_ref[pl.ds(2 * p + h, 1), rows], delta_ref[pl.ds(2 * p + h, 1), rows]
                spans = [(lo, width, True)] + ([(0, lo, False)] if lo else [])
                for at, size, masked in spans:
                    k2 = k_ref[at : at + size, cols]
                    s = nt(k2, qh)
                    if masked:
                        s = s + bias_ref[i, 0:size, :]
                    prob = jnp.exp(s - lse)
                    ds = (prob * (nt(v_ref[at : at + size, cols], doh) - delta)).astype(bf16)
                    dv_ref[at : at + size, :] += nn(prob.astype(bf16), doh)
                    dk_ref[at : at + size, :] += nn(ds, qh)
                    dq = dq + tn(ds, k2) * maskf[h]
            dq_ref[rows, :] = dq * HD**-0.5
        cosine, sine = cos_ref[...], -sin_ref[...]
        gp_ref[0, :, cols] = rot(dq_ref[...], cosine, sine).astype(bf16)
        gp_ref[1, :, cols] = rot(dk_ref[...], cosine, sine).astype(bf16)
        gp_ref[2, :, cols] = dv_ref[...].astype(bf16)
        return carry

    for c in loads:
        c.wait()
    lax.fori_loop(0, pairs, pair, 0)
    sums.step(1)
    for c in range(3):
        wg_ref[c] = tn(nattn_ref[...], gp_ref[c]).astype(wg_ref.dtype)
    for m in range(NF):
        send.got(m)
    send.close()
    swap.end()
    sums.step(2)
    total_ref[...] = sums.have[3]
    sums.close()


def ffn_tile(x, gate, y, w_ref, acc, eo, dx):
    dy = y.astype(f32)
    ge = (gate * dy).astype(bf16)
    x_t, ge_t = x.T, ge.T
    for c in range(w_ref.shape[0]):
        wg, wu, wd = w_ref[c, 0], w_ref[c, 1], w_ref[c, 2]
        gv, uv = nn(x, wg), nn(x, wu)
        gh = nn(ge, wd)
        sig = 1.0 / (1.0 + jnp.exp(-gv))
        act = gv * sig
        hid = (act * uv).astype(bf16)
        eo = eo + nt(hid, wd)
        gg = (gh * uv * (sig * (1.0 + gv * (1.0 - sig)))).astype(bf16)
        gu = (gh * act).astype(bf16)
        dx = dx + nt(gg, wg) + nt(gu, wu)
        acc[c, 0] += nn(x_t, gg)
        acc[c, 1] += nn(x_t, gu)
        acc[c, 2] += nn(ge_t, hid)
    return eo, dx


def first_kernel(pay_ref, x_ref, y_ref, w_ref, xc_ref, yc_ref, gc_ref, eo_ref, dx_ref, dw_ref, meta_ref, acc):
    d = x_ref.shape[2]
    gates = [pay_ref[g] for g in range(NF)] + [jnp.zeros((LANES - NF, ROOM), f32)]
    columns = jnp.concatenate(gates, axis=0).T
    off = jnp.int32(0)
    for g in range(NF):
        rows = pl.ds(pl.multiple_of(off, 16), ROOM)
        xc_ref[rows, :] = x_ref[g]
        yc_ref[rows, :] = y_ref[g]
        gc_ref[rows, :] = jnp.broadcast_to(columns[:, g : g + 1], (ROOM, LANES))
        meta_ref[g] = off
        off = off + (jnp.max(pay_ref[NF + g]).astype(i32) + 15) // 16 * 16
    rows = pl.ds(pl.multiple_of(off, 16), TM)
    xc_ref[rows, :] = jnp.zeros((TM, d), bf16)
    yc_ref[rows, :] = jnp.zeros((TM, d), bf16)
    gc_ref[rows, :] = jnp.zeros((TM, LANES), f32)
    tiles = jnp.maximum((off + TM - 1) // TM, 1)
    meta_ref[NF] = tiles
    acc[...] = jnp.zeros_like(acc)
    zero = jnp.zeros((TM, d), f32)

    def tile(t, carry):
        rows = pl.ds(pl.multiple_of(t * TM, TM), TM)
        eo_ref[rows, :], dx_ref[rows, :] = ffn_tile(
            xc_ref[rows, :], gc_ref[rows, 0:1], yc_ref[rows, :], w_ref, acc, zero, zero
        )
        return carry

    lax.fori_loop(0, tiles, tile, 0)
    dw_ref[...] = acc[...].astype(bf16)


def second_kernel(
    meta_ref, xc_any, yc_any, gc_any, eo_any, dx_any, w_any, outb_ref, dxb_ref, ggb_ref, dw_ref,
    xc_ref, yc_ref, gc_ref, eo_ref, dx_ref, w_ref, outs, dxs, ggs, acc, sems, wsem,
):
    d = xc_ref.shape[1]
    tiles = meta_ref[NF]
    weights = pltpu.make_async_copy(w_any, w_ref, wsem)
    weights.start()

    def copies(t):
        rows = pl.ds(pl.multiple_of(t * TM, TM), TM)
        pairs = ((xc_any, xc_ref), (yc_any, yc_ref), (gc_any, gc_ref), (eo_any, eo_ref), (dx_any, dx_ref))
        return [pltpu.make_async_copy(a.at[rows, :], b.at[rows, :], sems.at[n, t]) for n, (a, b) in enumerate(pairs)]

    def begin(t, carry):
        for c in copies(t):
            c.start()
        return carry

    lax.fori_loop(0, tiles, begin, 0)
    acc[...] = jnp.zeros_like(acc)
    rows = pl.ds(pl.multiple_of(tiles * TM, TM), ROOM)
    outs[rows, :] = jnp.zeros((ROOM, d), bf16)
    dxs[rows, :] = jnp.zeros((ROOM, d), bf16)
    ggs[rows, :] = jnp.zeros((ROOM, LANES), f32)
    weights.wait()

    def tile(t, carry):
        rows = pl.ds(pl.multiple_of(t * TM, TM), TM)
        for c in copies(t):
            c.wait()
        gate, y = gc_ref[rows, 0:1], yc_ref[rows, :]
        eo, dx = ffn_tile(xc_ref[rows, :], gate, y, w_ref, acc, eo_ref[rows, :], dx_ref[rows, :])
        outs[rows, :] = (gate * eo).astype(bf16)
        dxs[rows, :] = dx.astype(bf16)
        ggs[rows, :] = jnp.broadcast_to(jnp.sum(y.astype(f32) * eo, axis=1, keepdims=True), (TM, LANES))
        return carry

    lax.fori_loop(0, tiles, tile, 0)
    lane = lanes(ROOM)
    columns = jnp.zeros((ROOM, LANES), f32)
    for g in range(NF):
        rows = pl.ds(pl.multiple_of(meta_ref[g], 16), ROOM)
        outb_ref[g] = outs[rows, :]
        dxb_ref[g] = dxs[rows, :]
        columns = jnp.where(lane == g, ggs[rows, :], columns)
    ggb_ref[:, 0, :] = columns.T[0:NF, :]
    dw_ref[...] = acc[...].astype(bf16)


def experts_first(pay, x, y, w):
    groups, _, d = x.shape
    total = groups * ROOM + TM
    return pl.pallas_call(
        first_kernel,
        in_specs=[VM] * 4,
        out_specs=[VM] * 6 + [SM],
        out_shape=(
            shape((total, d), bf16), shape((total, d), bf16), shape((total, LANES), f32), shape((total, d), f32),
            shape((total, d), f32), shape(w.shape, bf16), shape((NF + 1,), i32),
        ),
        scratch_shapes=[pltpu.VMEM(w.shape, f32)],
        compiler_params=pltpu.CompilerParams(vmem_limit_bytes=60 << 20),
        cost_estimate=cost(22, 25),
    )(pay, x, y, w)


def experts_second(meta, xc, yc, gc, eo, dx, w):
    total, d = xc.shape
    blocks = shape((NF, ROOM, d), bf16)
    room = total + ROOM
    return pl.pallas_call(
        second_kernel,
        in_specs=[SM] + [ANY] * 6,
        out_specs=[VM] * 4,
        out_shape=(blocks, blocks, shape((NF, 1, ROOM), f32), shape(w.shape, bf16)),
        scratch_shapes=[
            pltpu.VMEM((total, d), bf16),
            pltpu.VMEM((total, d), bf16),
            pltpu.VMEM((total, LANES), f32),
            pltpu.VMEM((total, d), f32),
            pltpu.VMEM((total, d), f32),
            pltpu.VMEM(w.shape, bf16),
            pltpu.VMEM((room, d), bf16),
            pltpu.VMEM((room, d), bf16),
            pltpu.VMEM((room, LANES), f32),
            pltpu.VMEM(w.shape, f32),
            pltpu.SemaphoreType.DMA((5, total // TM)),
            pltpu.SemaphoreType.DMA,
        ],
        compiler_params=pltpu.CompilerParams(vmem_limit_bytes=60 << 20),
        cost_estimate=cost(22, 25),
    )(meta, xc, yc, gc, eo, dx, w)


def emit_kernel(a_ref, b_ref, wg_ref, small_ref, nag_ref, gu_ref, dn_ref, qkv_ref, wo_ref, rt_ref, rg_ref, cv_ref, cg_ref, na_ref, nm_ref):
    half = a_ref.shape[3]
    for n, ref in ((0, a_ref), (1, b_ref)):
        at = slice(n * half, (n + 1) * half)
        gu_ref[:, 0, :, at] = ref[0:2, 0].astype(f32)
        dn_ref[0, :, at] = ref[2, 0].astype(f32)

    @pl.when(pl.program_id(0) == 0)
    def _():
        qkv_ref[...] = wg_ref[0:3]
        r, f = wg_ref.shape[1:]
        wide = jnp.concatenate([wg_ref[3], jnp.zeros((r, -f % LANES), f32)], axis=1)
        wo_ref[...] = jnp.concatenate([wide, jnp.zeros((-r % LANES, wide.shape[1]), f32)], axis=0).T[0:f, 0:r]
        ne = rg_ref.shape[0]
        rt_ref[...] = small_ref[0:ne, :]
        for c in range(NC):
            cg_ref[c] = small_ref[Z0 + 2 * c : Z0 + 2 * c + 2, :]
        cv_ref[...] = small_ref[24 : 24 + NC, :]
        nm_ref[...] = small_ref[26, :]
        na_ref[...] = nag_ref[0, :]
        for n in range(ne):
            at = n % RES * LANES
            rg_ref[n : n + 1, :] = small_ref[29 + n // RES : 30 + n // RES, at : at + LANES][:, 0:ne]


def emit(dw_a, dw_b, wg, small, nag, ne):
    _, groups, r, half = dw_a.shape
    d = small.shape[1]
    piece = pl.BlockSpec((3, 1, r, half), lambda e: (0, e, 0, 0))
    whole = lambda *dims: pl.BlockSpec(dims, lambda e: (0,) * len(dims))
    rest = [(3, *wg.shape[1:]), wg.shape[:0:-1], (ne, d), (ne, ne), (NC, d), (NC, 2, d), (d,), (d,)]
    return pl.pallas_call(
        emit_kernel,
        grid=(groups,),
        in_specs=[piece, piece, whole(*wg.shape), whole(*small.shape), whole(1, d)],
        out_specs=[
            pl.BlockSpec((2, 1, r, 2 * half), lambda e: (0, e, 0, 0)), pl.BlockSpec((1, r, 2 * half), lambda e: (e, 0, 0)),
            *(whole(*dims) for dims in rest),
        ],
        out_shape=(
            shape((2, groups, r, 2 * half), f32), shape((groups, r, 2 * half), f32), *(shape(dims, f32) for dims in rest),
        ),
        cost_estimate=cost(1, 8),
    )(dw_a, dw_b, wg, small, nag)


def router_rows(par_ref, wr_ref):
    wr_ref[...] = jnp.zeros_like(wr_ref)
    wr_ref[0:16, :] = par_ref[0:16, :]
    wr_ref[16:32, :] = jnp.where(
        lax.broadcasted_iota(i32, (16, par_ref.shape[1]), 0) < 2 * NC, par_ref[16:32, :].astype(f32), 0.0
    ).astype(bf16)


def hot_rows(pos):
    slot = lax.broadcasted_iota(i32, (ROOM, pos.shape[1]), 0).astype(f32)
    return jnp.where(slot == pos, 1.0, 0.0).astype(bf16)


def split_rows(row):
    hi = row.astype(bf16).astype(f32)
    mid = (row - hi).astype(bf16).astype(f32)
    at = lax.broadcasted_iota(i32, (8, row.shape[1]), 0)
    out = jnp.where(at == 0, hi, jnp.where(at == 1, mid, jnp.where(at == 2, row - hi - mid, 0.0)))
    return out.astype(bf16)


def shape(dims, dtype):
    return jax.ShapeDtypeStruct(dims, dtype)


def cost(gflop, mbytes, mexp=0):
    return pl.CostEstimate(flops=int(gflop * 1e9), bytes_accessed=int(mbytes * 1e6), transcendentals=int(mexp * 1e6))


def rms_factor(values):
    return lax.rsqrt(jnp.mean(values * values, axis=-1, keepdims=True) + EPS)


def norm_back(grad, values, factor, gain):
    scaled = grad * gain
    inner = jnp.mean(scaled * values, axis=-1, keepdims=True)
    return factor * scaled - values * factor * factor * factor * inner


def rotary(positions, width):
    place = (jnp.arange(positions) % SEQ).astype(jnp.float32)
    freqs = jnp.power(10000.0, jnp.arange(width // 2).astype(jnp.float32) * (-2.0 / width))
    angles = place[:, None] * freqs[None, :]
    return (jnp.cos(angles)[:, None, :], jnp.sin(angles)[:, None, :])


def rotate(values, cosine, sine):
    half = values.shape[-1] // 2
    front = values[..., :half]
    behind = values[..., half:]
    return jnp.concatenate(
        [front * cosine - behind * sine, behind * cosine + front * sine], axis=-1
    )


def visible(starts):
    position = jnp.arange(SEQ)
    piece_of = jnp.zeros((SEQ,), jnp.int32)
    for index in range(starts.shape[0]):
        inside = (position >= starts[index]) & (position < starts[index] + PIECE)
        piece_of = jnp.where(inside, index + 1, piece_of)
    causal = position[None, :] <= position[:, None]
    same_piece = (piece_of[:, None] > 0) & (piece_of[:, None] == piece_of[None, :])
    return causal | same_piece


def dispatch(route_ids, route_ranks):
    group_rows = route_ids.shape[0]
    retained = (route_ids < NF) & (route_ranks < CAP)
    target = jnp.where(retained, route_ids * CAP + route_ranks, NF * CAP)
    token_index = jnp.broadcast_to(
        jnp.arange(group_rows, dtype=jnp.int32)[:, None], route_ids.shape
    )
    slot_token = (
        jnp.zeros((NF * CAP + 1,), jnp.int32)
        .at[target.reshape(-1)]
        .set(token_index.reshape(-1))[: NF * CAP]
    )
    filled = jnp.zeros((NF * CAP + 1,), jnp.float32).at[target.reshape(-1)].set(1.0)[: NF * CAP]
    return (retained, target, slot_token, filled)


def masked_scores(query, keys, starts):
    scores = jnp.einsum("qhd,khd->hqk", query, keys, preferred_element_type=jnp.float32) * HD ** (
        -0.5
    )
    return jnp.where(visible(starts)[None], scores, -1e30)


def attend_block(parts):
    query, keys, values, starts = parts
    scores = masked_scores(query, keys, starts)
    row_max = jnp.max(scores, axis=-1, keepdims=True)
    denominator = jnp.sum(jnp.exp(scores - row_max), axis=-1, keepdims=True)
    log_total = row_max + jnp.log(denominator)
    shares = jnp.exp(scores - log_total).astype(jnp.bfloat16)
    mixed = jnp.einsum("hqk,khd->qhd", shares, values, preferred_element_type=jnp.float32)
    return (mixed.astype(jnp.bfloat16), log_total)


def attend_back(parts):
    query, keys, values, starts, log_total, grad_out = parts
    shares = jnp.exp(masked_scores(query, keys, starts) - log_total)
    grad_shares = jnp.einsum("qhd,khd->hqk", grad_out, values, preferred_element_type=jnp.float32)
    centre = jnp.sum(shares * grad_shares, axis=-1, keepdims=True)
    grad_scores = (shares * (grad_shares - centre)).astype(jnp.bfloat16)
    factor = HD ** (-0.5)
    grad_query = (
        jnp.einsum("hqk,khd->qhd", grad_scores, keys, preferred_element_type=jnp.float32) * factor
    )
    grad_keys = (
        jnp.einsum("hqk,qhd->khd", grad_scores, query, preferred_element_type=jnp.float32) * factor
    )
    grad_values = jnp.einsum(
        "hqk,qhd->khd", shares.astype(jnp.bfloat16), grad_out, preferred_element_type=jnp.float32
    )
    return (grad_query, grad_keys, grad_values)


def plain_on_device(
    tokens,
    prior_logits,
    expert_ids,
    expert_ranks,
    piece_starts,
    norm_attn,
    qkv_weight,
    out_weight,
    norm_moe,
    router_weight,
    residual_weight,
    const_vectors,
    const_gates,
    w_gate_up,
    w_down,
    out_grad,
):
    highest = lax.Precision.HIGHEST
    local_rows = tokens.shape[0]
    group_rows = expert_ids.shape[0]
    sequences = group_rows // SEQ
    head_count = qkv_weight.shape[2] // HD
    row_start = lax.axis_index("tensor") * local_rows
    seq_shape = (sequences, SEQ, head_count, HD)
    gain_attn = norm_attn.astype(jnp.float32)
    gain_moe = norm_moe.astype(jnp.float32)
    tok_vals = tokens.astype(jnp.float32)
    factor_attn = rms_factor(tok_vals)
    normed_attn = (tok_vals * factor_attn * gain_attn).astype(jnp.bfloat16)
    attn_rows = lax.all_gather(normed_attn, "tensor", axis=0, tiled=True)
    qkv_full, out_full = (
        lax.all_gather(qkv_weight, "dp", axis=1, tiled=True),
        lax.all_gather(out_weight, "dp", axis=1, tiled=True),
    )
    projected = jnp.einsum("gd,cde->cge", attn_rows, qkv_full, preferred_element_type=jnp.float32)
    cosine, sine = rotary(group_rows, HD)
    query = (
        rotate(projected[0].reshape(group_rows, head_count, HD), cosine, sine)
        .astype(jnp.bfloat16)
        .reshape(seq_shape)
    )
    keys = (
        rotate(projected[1].reshape(group_rows, head_count, HD), cosine, sine)
        .astype(jnp.bfloat16)
        .reshape(seq_shape)
    )
    values = projected[2].astype(jnp.bfloat16).reshape(seq_shape)
    mixed, log_total = lax.map(attend_block, (query, keys, values, piece_starts))
    mixed_rows = mixed.reshape(group_rows, head_count * HD)
    attn_part = jnp.dot(mixed_rows, out_full, preferred_element_type=jnp.float32)
    attn_out = lax.psum_scatter(attn_part, "tensor", scatter_dimension=0, tiled=True)
    resid = tok_vals + attn_out
    factor_moe = rms_factor(resid)
    normed_moe = (resid * factor_moe * gain_moe).astype(jnp.bfloat16)
    moe_rows, prior_rows = (
        lax.all_gather(normed_moe, "tensor", axis=0, tiled=True),
        lax.all_gather(prior_logits, "tensor", axis=0, tiled=True),
    )
    logits = jnp.dot(moe_rows, router_weight, preferred_element_type=jnp.float32) + jnp.dot(
        prior_rows, residual_weight, preferred_element_type=jnp.float32
    )
    shares = jax.nn.softmax(logits, axis=-1)
    gates = jnp.take_along_axis(shares, expert_ids, axis=1)
    retained, target, slot_token, filled = dispatch(expert_ids, expert_ranks)
    picker = jnp.minimum(target, NF * CAP - 1)
    slot_gate = (
        jnp.zeros((NF * CAP + 1,), jnp.float32)
        .at[target.reshape(-1)]
        .set(gates.reshape(-1))[: NF * CAP]
        * filled
    )
    expert_rows = (moe_rows[slot_token] * filled[:, None].astype(jnp.bfloat16)).reshape(NF, CAP, -1)
    gate_full, down_full = (
        lax.all_gather(w_gate_up, "dp", axis=2, tiled=True),
        lax.all_gather(w_down, "dp", axis=2, tiled=True),
    )
    gate_up = jnp.einsum(
        "ecd,sedf->secf", expert_rows, gate_full, preferred_element_type=jnp.float32
    )
    sigmoid_vals = jax.nn.sigmoid(gate_up[0])
    activated = gate_up[0] * sigmoid_vals
    hidden = (activated * gate_up[1]).astype(jnp.bfloat16)
    expert_out = jnp.einsum(
        "ecf,efd->ecd", hidden, down_full, preferred_element_type=jnp.float32
    ).reshape(NF * CAP, -1)
    retained_gates = jnp.where(retained, gates, 0.0)
    combined = jnp.sum(retained_gates[:, :, None] * expert_out[picker], axis=1)
    ffn_out = lax.psum_scatter(
        combined.astype(jnp.bfloat16), "tensor", scatter_dimension=0, tiled=True
    ).astype(jnp.float32)
    local_ids = lax.dynamic_slice_in_dim(expert_ids, row_start, local_rows, 0)
    local_shares = lax.dynamic_slice_in_dim(shares, row_start, local_rows, 0)
    local_gates = lax.dynamic_slice_in_dim(gates, row_start, local_rows, 0)
    normed_vals = normed_moe.astype(jnp.float32)
    vectors = const_vectors.astype(jnp.float32)
    gate_mats = const_gates.astype(jnp.float32)
    const_count = vectors.shape[0]
    copy_share = jnp.sum(jnp.where(local_ids == NF + 1, local_gates, 0.0), axis=1)
    const_share = jnp.stack(
        [
            jnp.sum(jnp.where(local_ids == NF + 2 + index, local_gates, 0.0), axis=1)
            for index in range(const_count)
        ],
        axis=1,
    )
    mixing = jax.nn.softmax(
        jnp.einsum("gd,cjd->gcj", normed_vals, gate_mats, precision=highest), axis=-1
    )
    const_out = (
        mixing[:, :, 0:1] * normed_vals[:, None, :] + mixing[:, :, 1:2] * vectors[None, :, :]
    )
    others = copy_share[:, None] * normed_vals + jnp.sum(
        const_share[:, :, None] * const_out, axis=1
    )
    layer_out = (resid + ffn_out + others).astype(jnp.bfloat16)
    grad_out = out_grad.astype(jnp.float32)
    grad_moe_rows = lax.all_gather(out_grad, "tensor", axis=0, tiled=True)
    gate_back, down_back = (
        lax.all_gather(w_gate_up, "dp", axis=2, tiled=True),
        lax.all_gather(w_down, "dp", axis=2, tiled=True),
    )
    slot_grads = grad_moe_rows[slot_token].astype(jnp.float32)
    grad_expert = (slot_gate[:, None] * slot_grads).astype(jnp.bfloat16).reshape(NF, CAP, -1)
    slot_inner = jnp.sum(slot_grads * expert_out, axis=-1)
    gate_grad_ffn = jnp.where(retained, slot_inner[picker], 0.0)
    down_grad = jnp.einsum("ecf,ecd->efd", hidden, grad_expert, preferred_element_type=jnp.float32)
    grad_hidden = jnp.einsum(
        "ecd,efd->ecf", grad_expert, down_back, preferred_element_type=jnp.float32
    )
    slope = sigmoid_vals * (1.0 + gate_up[0] * (1.0 - sigmoid_vals))
    grad_gate_up = jnp.stack([grad_hidden * gate_up[1] * slope, grad_hidden * activated]).astype(
        jnp.bfloat16
    )
    gate_up_grad = jnp.einsum(
        "ecd,secf->sedf", expert_rows, grad_gate_up, preferred_element_type=jnp.float32
    )
    slot_input_grad = jnp.einsum(
        "secf,sedf->ecd", grad_gate_up, gate_back, preferred_element_type=jnp.float32
    ).reshape(NF * CAP, -1)
    grad_ffn_in = jnp.sum(jnp.where(retained[:, :, None], slot_input_grad[picker], 0.0), axis=1)
    gate_up_grad, down_grad = (
        lax.psum_scatter(gate_up_grad, "dp", scatter_dimension=2, tiled=True),
        lax.psum_scatter(down_grad, "dp", scatter_dimension=2, tiled=True),
    )
    grad_ffn_in, gate_grad_ffn = (
        lax.psum_scatter(grad_ffn_in, "tensor", scatter_dimension=0, tiled=True),
        lax.psum_scatter(gate_grad_ffn, "tensor", scatter_dimension=0, tiled=True),
    )
    copy_inner = jnp.sum(grad_out * normed_vals, axis=-1)
    const_inner = jnp.sum(grad_out[:, None, :] * const_out, axis=-1)
    choice_inner = jnp.where(local_ids == NF + 1, copy_inner[:, None], 0.0)
    for index in range(const_count):
        choice_inner = choice_inner + jnp.where(
            local_ids == NF + 2 + index, const_inner[:, index : index + 1], 0.0
        )
    gate_grad = gate_grad_ffn + choice_inner
    expert_range = jnp.arange(shares.shape[1])
    onehot = (local_ids[:, :, None] == expert_range[None, None, :]).astype(jnp.float32)
    grad_router = jnp.sum(onehot * gate_grad[:, :, None], axis=1)
    grad_logits = local_shares * (
        grad_router - jnp.sum(local_shares * grad_router, axis=-1, keepdims=True)
    )
    prior_vals = prior_logits.astype(jnp.float32)
    router_grad = jnp.dot(normed_vals.T, grad_logits, precision=highest)
    residual_grad = jnp.dot(prior_vals.T, grad_logits, precision=highest)
    prior_grad = jnp.dot(grad_logits, residual_weight.astype(jnp.float32).T, precision=highest)
    vector_inner = jnp.dot(grad_out, vectors.T, precision=highest)
    grad_mixing = const_share[:, :, None] * jnp.stack(
        [jnp.broadcast_to(copy_inner[:, None], vector_inner.shape), vector_inner], axis=-1
    )
    grad_blend = mixing * (grad_mixing - jnp.sum(mixing * grad_mixing, axis=-1, keepdims=True))
    const_gate_grad = jnp.einsum("gcj,gd->cjd", grad_blend, normed_vals, precision=highest)
    const_vector_grad = jnp.einsum(
        "gc,gd->cd", const_share * mixing[:, :, 1], grad_out, precision=highest
    )
    direct_share = copy_share + jnp.sum(const_share * mixing[:, :, 0], axis=1)
    grad_moe_in = (
        grad_ffn_in
        + jnp.dot(grad_logits, router_weight.astype(jnp.float32).T, precision=highest)
        + direct_share[:, None] * grad_out
        + jnp.einsum("gcj,cjd->gd", grad_blend, gate_mats, precision=highest)
    )
    norm_moe_grad = jnp.sum(grad_moe_in * resid * factor_moe, axis=0)
    grad_resid = grad_out + norm_back(grad_moe_in, resid, factor_moe, gain_moe)
    grad_mixed_out = grad_resid.astype(jnp.bfloat16)
    grad_attn_rows = lax.all_gather(grad_mixed_out, "tensor", axis=0, tiled=True)
    out_weight_grad = jnp.dot(mixed_rows.T, grad_attn_rows, preferred_element_type=jnp.float32)
    grad_mixed = jnp.dot(grad_attn_rows, out_full.T, preferred_element_type=jnp.float32).astype(
        jnp.bfloat16
    )
    grad_query, grad_keys, grad_values = lax.map(
        attend_back, (query, keys, values, piece_starts, log_total, grad_mixed.reshape(seq_shape))
    )
    grad_query = rotate(grad_query.reshape(group_rows, head_count, HD), cosine, -sine).reshape(
        group_rows, -1
    )
    grad_keys = rotate(grad_keys.reshape(group_rows, head_count, HD), cosine, -sine).reshape(
        group_rows, -1
    )
    grad_proj = jnp.stack([grad_query, grad_keys, grad_values.reshape(group_rows, -1)]).astype(
        jnp.bfloat16
    )
    qkv_grad = jnp.einsum("gd,cge->cde", attn_rows, grad_proj, preferred_element_type=jnp.float32)
    qkv_grad, out_weight_grad = (
        lax.psum_scatter(qkv_grad, "dp", scatter_dimension=1, tiled=True),
        lax.psum_scatter(out_weight_grad, "dp", scatter_dimension=1, tiled=True),
    )
    grad_attn_part = jnp.einsum(
        "cge,cde->gd", grad_proj, qkv_full, preferred_element_type=jnp.float32
    )
    grad_attn_in = lax.psum_scatter(
        grad_attn_part.astype(jnp.bfloat16), "tensor", scatter_dimension=0, tiled=True
    ).astype(jnp.float32)
    norm_attn_grad = jnp.sum(grad_attn_in * tok_vals * factor_attn, axis=0)
    input_grad = grad_resid + norm_back(grad_attn_in, tok_vals, factor_attn, gain_attn)
    summed = lax.psum(
        (
            norm_attn_grad,
            norm_moe_grad,
            router_grad,
            residual_grad,
            const_vector_grad,
            const_gate_grad,
        ),
        ("dp", "tensor"),
    )
    return (
        layer_out,
        input_grad,
        prior_grad,
        summed[0],
        qkv_grad,
        out_weight_grad,
        summed[1],
        summed[2],
        summed[3],
        summed[4],
        summed[5],
        gate_up_grad,
        down_grad,
    )


def on_device(
    dp,
    tensor,
    tokens,
    prior_logits,
    expert_ids,
    expert_ranks,
    piece_starts,
    norm_attn,
    qkv_weight,
    out_weight,
    norm_moe,
    router_weight,
    residual_weight,
    const_vectors,
    const_gates,
    w_gate_up,
    w_down,
    out_grad,
):
    rows, d = tokens.shape
    ne = router_weight.shape[1]
    packs = dp // NF
    groups = None if packs == 1 else [list(range(NF * r, NF * (r + 1))) for r in range(packs)]
    across = None if packs == 1 else [list(range(j, dp, NF)) for j in range(NF)]
    ids, ranks = expert_ids.T, expert_ranks.T
    cosine, sine = (jnp.asarray(t) for t in rotary_tables())
    prior = jnp.pad(prior_logits.T, ((0, 16 - ne), (0, 0)))
    zeros = lambda n: jnp.zeros((n, d), bf16)
    params = jnp.concatenate(
        [
            router_weight.T, zeros(Z0 - ne), const_gates.reshape(2 * NC, d), zeros(8 - 2 * NC), norm_attn[None],
            norm_moe[None], const_vectors, zeros(6 - NC), jnp.pad(residual_weight, ((0, 16 - ne), (0, d - ne))),
        ],
        axis=0,
    )

    w_down_t = w_down.transpose(0, 2, 1)[None]
    shard = w_down.shape[1]
    w_first, zq, zo = prologue(w_gate_up, w_down_t, qkv_weight, out_weight, tensor, 1)
    w_full, w_second, pos, count, ys, slab = gather_weights(
        zq, zo, w_gate_up, w_down_t, ids, ranks, out_grad, packs == 1, 2
    )
    w_attn = lax.all_gather(slab, "dp", axis=1, tiled=True) if packs > 1 else w_full

    def whole(w):
        w = w.reshape(3, -1, w.shape[3])
        if packs > 1:
            w = lax.all_gather(w, "dp", axis=1, tiled=True, axis_index_groups=across)
        return lax.all_gather(w, "tensor", axis=0, tiled=False)

    w_first, w_second = whole(w_first), whole(w_second)

    heads = 16
    blocks = shape((NF, ROOM, d), bf16)
    q, k, v, mixed, lse, nattn, resid, nmoe, base, aux, x_b, y_b, pay = pl.pallas_call(
        fwd_kernel,
        in_specs=[SM] + [VM] * 9 + [ANY],
        out_specs=[VM] * 10 + [ANY] * 3,
        out_shape=(
            shape((rows, d), bf16), shape((rows, d), bf16), shape((rows, d), bf16), shape((rows, d), bf16),
            shape((heads, rows), f32), shape((rows, d), bf16), shape((rows, d), f32), shape((rows, d), bf16),
            shape((rows, d), f32), shape((rows, LANES), f32), blocks, blocks, shape((2 * NF, 1, ROOM), f32),
        ),
        scratch_shapes=[
            pltpu.VMEM((QT, 2 * QT), f32),
            pltpu.VMEM((NF, 1, rows), f32),
            pltpu.VMEM((NF, ROOM, d), bf16),
            pltpu.VMEM((2 * NF, 1, ROOM), f32),
            pltpu.VMEM((LANES, d), bf16),
            *send_scratch(),
            *send_scratch(),
            pltpu.SemaphoreType.DMA((2, 2 * (NF - 1))),
            pltpu.SemaphoreType.DMA((2,)),
        ],
        compiler_params=pltpu.CompilerParams(collective_id=3, has_side_effects=True, vmem_limit_bytes=60 << 20),
        cost_estimate=cost(40, 30, 10),
    )(piece_starts, tokens, prior, ids, ranks, params, cosine, sine, w_attn, pos, ys)

    xc, yc, gc, eo, dx, dw_a, meta = experts_first(pay, x_b, y_b, w_first)
    out_b, dx_b, gg_b, dw_b = experts_second(meta, xc, yc, gc, eo, dx, w_second)

    def owned(dw):
        dw = lax.psum_scatter(dw, "tensor", scatter_dimension=0, tiled=False)
        if packs > 1:
            dw = lax.psum_scatter(dw, "dp", scatter_dimension=1, tiled=True, axis_index_groups=across)
        return dw.reshape(3, NF, -1, dw.shape[-1])

    dw_a = owned(dw_a)

    gmo, gres, pgrad, small = pl.pallas_call(
        mid_kernel,
        in_specs=[ANY] * 6 + [VM] * 4,
        out_specs=[VM] * 4,
        out_shape=(shape((rows, d), bf16), shape((rows, d), f32), shape((16, rows), f32), shape((32, d), f32)),
        scratch_shapes=[
            pltpu.VMEM((NF, ROOM, d), bf16),
            pltpu.VMEM((NF, 1, ROOM), f32),
            pltpu.VMEM((rows, d), f32),
            pltpu.VMEM((NF, rows), f32),
            pltpu.VMEM((rows, LANES), f32),
            pltpu.VMEM((rows, LANES), f32),
            pltpu.VMEM((LANES, d), bf16),
            pltpu.VMEM((16, LANES), f32),
            pltpu.VMEM((rows, d), bf16),
            pltpu.VMEM((rows, d), bf16),
            pltpu.VMEM((rows, d), f32),
            pltpu.VMEM((rows, LANES), f32),
            pltpu.SemaphoreType.DMA((4,)),
            *send_scratch(),
            pltpu.SemaphoreType.DMA((2, NF - 1)),
            pltpu.SemaphoreType.DMA((1,)),
        ],
        compiler_params=pltpu.CompilerParams(collective_id=4, has_side_effects=True, vmem_limit_bytes=60 << 20),
        cost_estimate=cost(4, 4),
    )(dx_b, gg_b, out_grad, nmoe, resid, aux, pos, prior, params, count)
    dw_a, dw_b, gmo = lax.optimization_barrier((dw_a, dw_b, gmo))
    dw_b = owned(dw_b)
    wg, gp, yr, small, dw_a = pl.pallas_call(
        bwd_kernel,
        in_specs=[SM, VM, VM, ANY, ANY, ANY, VM] + [ANY] * 4 + [VM, ANY, ANY],
        out_specs=[VM] * 2 + [ANY, VM, ANY],
        out_shape=(shape((4, d, d), bf16), shape((3, rows, d), bf16), blocks, shape((32, d), f32), shape(dw_a.shape, bf16)),
        scratch_shapes=[
            pltpu.VMEM((rows, d), bf16),
            pltpu.VMEM((heads, rows), f32),
            pltpu.VMEM((rows // QT, 2 * QT, QT), f32),
            pltpu.VMEM((rows, LANES), f32),
            pltpu.VMEM((rows, LANES), f32),
            pltpu.VMEM((rows, LANES), f32),
            pltpu.VMEM((1, d, d), bf16),
            pltpu.SemaphoreType.DMA,
            *[pltpu.VMEM((rows, d), bf16)] * 3,
            pltpu.VMEM((rows, d), bf16),
            *[pltpu.VMEM((rows, LANES), f32)] * 2,
            pltpu.SemaphoreType.DMA((6,)),
            *send_scratch(),
            *near_scratch((32, d)),
            *exchange_scratch(1),
        ],
        compiler_params=pltpu.CompilerParams(collective_id=5, has_side_effects=True, vmem_limit_bytes=60 << 20),
        cost_estimate=cost(8, 4),
    )(piece_starts, gmo, mixed, q, k, v, lse, nattn, cosine, sine, w_attn, small, out_b, dw_a)
    alone = packs == 1
    zs, igrad, layer_out, small, nag = finish(
        wg, gp, gres, tokens, w_attn, yr, base, pos, params, small, tensor, alone, 6
    )
    if alone:
        wg, nag, dw_b = last(zs, nag, dw_b, tensor, 7)
    else:
        wg = lax.psum_scatter(wg, "dp", scatter_dimension=1, tiled=True)
        wg = lax.psum_scatter(wg, "tensor", scatter_dimension=2, tiled=True).astype(f32)
        nag = lax.psum(nag, ("dp", "tensor"))
        small = lax.psum(lax.psum(small, "tensor"), "dp", axis_index_groups=across)
        dw_b = exchange8(dw_b, 7)
    overflow = jnp.sum(small[28:29, 0:LANES]) > 0

    def roomy(args):
        return plain_on_device(*args)

    def packed(args):
        gate_up, down, qkv, wo, router, residual, vectors, blends, gain_attn, gain_moe = emit(dw_a, dw_b, wg, small, nag, ne)
        return (
            layer_out,
            igrad,
            pgrad[0:ne].T,
            gain_attn,
            qkv,
            wo,
            gain_moe,
            router.T,
            residual,
            vectors,
            blends,
            gate_up,
            down.transpose(0, 2, 1),
        )

    args = (
        tokens, prior_logits, expert_ids, expert_ranks, piece_starts, norm_attn, qkv_weight, out_weight, norm_moe,
        router_weight, residual_weight, const_vectors, const_gates, w_gate_up, w_down, out_grad,
    )
    return lax.cond(overflow, roomy, packed, args)


def solution(mesh):
    body = functools.partial(on_device, mesh.shape["dp"], mesh.shape["tensor"])
    rows = P(("dp", "tensor"), None)
    return jax.shard_map(
        body,
        mesh=mesh,
        in_specs=(
            rows, rows, P("dp", None), P("dp", None), P("dp", None), P(), P(None, "dp", "tensor"), P("tensor", "dp"),
            P(), P(), P(), P(), P(), P(None, None, "dp", "tensor"), P(None, "tensor", "dp"), rows,
        ),
        out_specs=(
            rows, rows, rows, P(), P(None, "dp", "tensor"), P("tensor", "dp"), P(), P(), P(), P(), P(),
            P(None, None, "dp", "tensor"), P(None, "tensor", "dp"),
        ),
        check_vma=False,
    )
```

```python
import functools

import jax
import jax.numpy as jnp
import numpy as np
from jax import lax
from jax.experimental import pallas as pl
from jax.experimental.pallas import tpu as pltpu
from jax.sharding import PartitionSpec as P

HD = 64
NF = 8
NC = 2
SEQ = 1024
PIECE = 256
PIECES = 2
CAP = 768
EPS = 1e-06
QT = 256
LANES = 128
TM = 256
ROOM = 256
Z0 = 16
CHOSEN = 32
RES = 6

bf16 = jnp.bfloat16
f32 = jnp.float32
i32 = jnp.int32

VM = pl.BlockSpec(memory_space=pltpu.VMEM)
SM = pl.BlockSpec(memory_space=pltpu.SMEM)
ANY = pl.BlockSpec(memory_space=pl.ANY)


def nn(a, b):
    return lax.dot_general(a, b, (((1,), (0,)), ((), ())), preferred_element_type=f32)


def nt(a, b):
    return lax.dot_general(a, b, (((1,), (1,)), ((), ())), preferred_element_type=f32)


def tn(a, b):
    return lax.dot_general(a, b, (((0,), (0,)), ((), ())), preferred_element_type=f32)


def split(x):
    hi = x.astype(bf16)
    return hi, (x - hi.astype(f32)).astype(bf16)


def lanes(rows):
    return lax.broadcasted_iota(i32, (rows, LANES), 1)


def rot(x, cosine, sine):
    first = lanes(x.shape[0]) % HD < HD // 2
    other = jnp.where(first, pltpu.roll(x, LANES - HD // 2, 1), pltpu.roll(x, HD // 2, 1))
    return x * cosine + other * sine


def head_masks():
    low = lax.broadcasted_iota(i32, (1, LANES), 1) < HD
    a = jnp.where(low, 1.0, 0.0)
    return a, 1.0 - a


def rotary_tables():
    place = np.arange(SEQ, dtype=np.float32)
    half = HD // 2
    freqs = np.power(np.float32(10000.0), np.arange(half, dtype=np.float32) * np.float32(-2.0 / HD)).astype(np.float32)
    angles = (place[:, None] * freqs[None, :]).astype(np.float32).astype(np.float64)
    c, s = np.cos(angles).astype(np.float32), np.sin(angles).astype(np.float32)
    return np.concatenate([c, c, c, c], 1), np.concatenate([-s, s, -s, s], 1)


def window_bias(starts_ref, tile, width, transposed):
    shape = (width, QT) if transposed else (QT, width)
    qpos = lax.broadcasted_iota(i32, shape, 1 if transposed else 0) + tile * QT
    kpos = lax.broadcasted_iota(i32, shape, 0 if transposed else 1) + tile * QT
    seen = jnp.where(kpos <= qpos, 1, 0)
    for piece in range(PIECES):
        s = starts_ref[lax.axis_index("tensor"), piece]
        both = jnp.where(qpos >= s, 1, 0) * jnp.where(qpos < s + PIECE, 1, 0)
        both = both * jnp.where(kpos >= s, 1, 0) * jnp.where(kpos < s + PIECE, 1, 0)
        seen = jnp.maximum(seen, both)
    return jnp.where(seen > 0, 0.0, -1e30)


MESH = pl.DeviceIdType.MESH
GATHER_COPIES = 13
REDUCE_COPIES = 10


def flip(index, m):
    for bit in (1, 2, 4):
        if m & bit:
            index = index + bit - 2 * bit * (index // bit % 2)
    return index


def remote(src, dst, sems, n, axis, peer):
    return pltpu.make_async_remote_copy(
        src_ref=src,
        dst_ref=dst,
        send_sem=sems.at[0, n],
        recv_sem=sems.at[1, n],
        device_id={axis: peer},
        device_id_type=MESH,
    )


def greet(peers):
    barrier = pltpu.get_barrier_semaphore()
    for axis, peer in peers:
        pl.semaphore_signal(barrier, inc=1, device_id={axis: peer}, device_id_type=MESH)
    pl.semaphore_wait(barrier, len(peers))


def near_peers():
    me = lax.axis_index("dp")
    return [("dp", flip(me, m)) for m in (1, 2, 4)]


def far_peers(tensor):
    me = lax.axis_index("tensor")
    return [("tensor", (me + k) % tensor) for k in range(1, tensor)]


class Gather8:
    def __init__(self, src, dst, sems, own_sem):
        me = lax.axis_index("dp")
        slot = me % NF
        nx, ny, nc = flip(me, 2), flip(me, 4), flip(me, 1)
        sx, sy, sd = flip(slot, 2), flip(slot, 4), flip(slot, 6)
        self.own = pltpu.make_async_copy(src(None), dst(slot, None), own_sem)
        go = lambda n, s, d, peer: remote(s, d, sems, n, "dp", peer)
        on = lambda n, s, h, peer: go(n, dst(s, h), dst(s, h), peer)
        self.c = [
            go(0, src(0), dst(slot, 0), nx),
            go(1, src(1), dst(slot, 1), ny),
            go(2, src(1), dst(slot, 1), nx),
            go(3, src(0), dst(slot, 0), ny),
            go(4, src(None), dst(slot, None), nc),
            on(5, sx, 0, ny),
            on(6, sy, 1, nx),
            on(7, sx, 0, nc),
            on(8, sy, 1, nc),
            on(9, sx, 1, nc),
            on(10, sy, 0, nc),
            on(11, sd, 0, nc),
            on(12, sd, 1, nc),
        ]

    def begin(self):
        self.own.start()
        for n in range(5):
            self.c[n].start()

    def forward(self):
        for got, out in ((0, (5, 7)), (1, (6, 8))):
            self.c[got].wait_recv()
            for n in out:
                self.c[n].start()

    def share(self):
        for got, out in ((2, 9), (3, 10)):
            self.c[got].wait_recv()
            self.c[out].start()

    def last(self):
        for got, out in ((5, 11), (6, 12)):
            self.c[got].wait_recv()
            self.c[out].start()

    def end(self):
        for n in (4, 7, 8, 9, 10, 11, 12):
            self.c[n].wait_recv()
        for c in self.c:
            c.wait_send()
        self.own.wait()


def halves(ref, index, rows):
    half = rows // 2
    return lambda s, h: ref.at[s] if h is None else ref.at[s, pl.ds(h * half, half)]


def all_peers():
    me = lax.axis_index("dp")
    return [("dp", flip(me, m)) for m in range(1, NF)]


class Swap8:
    def __init__(self, src, dst, sems, own_sems):
        me = lax.axis_index("dp")
        slot = me % NF
        count = src.shape[0] // NF
        self.own = [
            pltpu.make_async_copy(src.at[NF * i + slot], dst.at[NF * i + slot], own_sems.at[i]) for i in range(count)
        ]
        self.c = [
            remote(
                src.at[NF * i + flip(slot, m)], dst.at[NF * i + slot], sems, (m - 1) * count + i, "dp", flip(me, m)
            )
            for m in range(1, NF)
            for i in range(count)
        ]

    def begin(self):
        for c in self.own + self.c:
            c.start()

    def end(self):
        for c in self.c:
            c.wait_recv()
        for c in self.c:
            c.wait_send()
        for c in self.own:
            c.wait()


def routes(ids_ref, ranks_ref, i):
    start = lax.axis_index("tensor") * SEQ + i * QT
    cols = pl.ds(pl.multiple_of(start, QT), QT)
    at = lax.broadcasted_iota(i32, (16, QT), 0)
    hit0, hit1 = (jnp.where(at == ids_ref[n : n + 1, cols], 1.0, 0.0) for n in range(2))
    keep0, keep1 = (jnp.where(ranks_ref[n : n + 1, cols] < CAP, 1.0, 0.0) for n in range(2))
    return hit0 + hit1, (hit0 * keep0 + hit1 * keep1) * jnp.where(at < NF, 1.0, 0.0)


def weights_kernel(
    gather, zq_ref, zo_ref, gu_ref, dn_ref, ids_ref, ranks_ref, og_ref, out_ref, wx_ref, pos_ref, count_ref, ys_ref, slab, sems,
    own_sem, *scratch,
):
    k, r, _ = slab.shape
    tensor, _, _, f = zq_ref.shape
    for t in range(0, tensor, 2):
        at = slice(t * f, (t + 2) * f)
        for c in range(k - 1):
            slab[c, :, at] = jnp.concatenate([zq_ref[n, c].astype(f32) for n in (t, t + 1)], axis=1).astype(bf16)
        both = jnp.concatenate([zo_ref[n].astype(f32) for n in (t, t + 1)], axis=0)
        wide = jnp.concatenate([both, jnp.zeros((2 * f, -r % LANES), f32)], axis=1)
        slab[k - 1, :, at] = wide.T[0:r, :].astype(bf16)
    greet(all_peers())
    part = lambda h: pl.ds(0, k) if h is None else pl.ds(h * (k // 2), k // 2)
    if gather:
        g = Gather8(
            lambda h: slab.at[part(h)],
            lambda s, h: out_ref.at[part(h), pl.ds(pl.multiple_of(s * r, r), r), :],
            sems,
            own_sem,
        )
        g.begin()
    swap = Exchange8([gu_ref, dn_ref], wx_ref, 1, *scratch)
    swap.begin()
    upper = jnp.where(
        lax.broadcasted_iota(i32, (QT, QT), 0) < lax.broadcasted_iota(i32, (QT, QT), 1), 1.0, 0.0
    ).astype(bf16)
    taken = jnp.zeros((16, 1), f32)
    for i in range(SEQ // QT):
        _, kept = routes(ids_ref, ranks_ref, i)
        pos = jnp.where(kept > 0, nn(kept.astype(bf16), upper) + taken, -1.0)
        pos_ref[:, 0, i * QT : (i + 1) * QT] = pos[0:NF, :]
        taken = taken + jnp.sum(kept, axis=1, keepdims=True)
    count_ref[...] = jnp.broadcast_to(taken, (16, LANES))
    slot = lax.axis_index("dp") % NF

    def pack(*blocks):
        for m in blocks:
            ys_ref[m] = nn(hot_rows(pos_ref[flip(slot, m)]), og_ref[...]).astype(bf16)

    pack(0, 1)
    if gather:
        g.forward()
    pack(2, 3)
    if gather:
        g.share()
    pack(4, 5)
    if gather:
        g.last()
    pack(6, 7)
    if gather:
        g.end()
    swap.end()


def gather_weights(zq, zo, gate_up, down, ids, ranks, og, gather, cid):
    tensor, k, r, f = zq.shape
    k, f = k + 1, tensor * f
    return pl.pallas_call(
        functools.partial(weights_kernel, gather),
        in_specs=[VM] * 2 + [ANY] * 2 + [VM] * 3,
        out_specs=[ANY] * 2 + [VM] * 4,
        out_shape=(
            shape((k, NF * r, f), bf16), half_shape(gate_up), shape((NF, 1, og.shape[0]), f32),
            shape((16, LANES), f32), shape((NF, ROOM, og.shape[1]), bf16),
            shape((k, r, f), bf16),
        ),
        scratch_shapes=[
            pltpu.SemaphoreType.DMA((2, GATHER_COPIES)),
            pltpu.SemaphoreType.DMA,
            *exchange_scratch(2),
        ],
        compiler_params=pltpu.CompilerParams(collective_id=cid, has_side_effects=True, vmem_limit_bytes=60 << 20),
        cost_estimate=cost(35, 10),
    )(zq, zo, gate_up, down, ids, ranks, og)


class Reduce8:
    def __init__(self, view, bufs, sems, lsems):
        self.own, self.away, self.ind, self.inx, self.iny = bufs
        me = lax.axis_index("dp")
        slot = me % NF
        half = self.ind.shape[0] // 2
        a, b = pl.ds(0, half), pl.ds(half, half)
        self.a, self.b = a, b
        nx, ny, nc = flip(me, 2), flip(me, 4), flip(me, 1)
        mine = [flip(slot, m) for m in (6, 2, 4)] + [slot]
        self.loads = [pltpu.make_async_copy(view(s), self.own.at[n % 2], lsems.at[n]) for n, s in enumerate(mine)]
        self.over = [remote(view(flip(s, 1)), self.away.at[n], sems, n, "dp", nc) for n, s in enumerate(mine)]
        go = lambda n, k, i, part, peer: remote(self.away.at[k, part], i.at[part], sems, n, "dp", peer)
        self.da, self.db = go(4, 0, self.ind, a, nx), go(5, 0, self.ind, b, ny)
        self.xa, self.yb = go(6, 1, self.inx, a, nx), go(7, 2, self.iny, b, ny)
        self.ya, self.xb = go(8, 2, self.iny, a, ny), go(9, 1, self.inx, b, nx)

    def load(self):
        self.loads[0].start()
        self.loads[1].start()

    def begin(self):
        for c in self.over:
            c.start()

    def add(self, n, part):
        self.away[n, part] = (self.own[n % 2, part].astype(f32) + self.away[n, part].astype(f32)).astype(bf16)

    def more(self, n, part):
        self.away[n, part] = (self.away[n, part].astype(f32) + self.ind[part].astype(f32)).astype(bf16)

    def ready(self, n):
        self.loads[n].wait()
        self.over[n].wait_recv()

    def first(self):
        self.ready(0)
        self.add(0, self.a)
        self.da.start()
        self.add(0, self.b)
        self.db.start()
        self.loads[2].start()

    def second(self):
        self.ready(1)
        self.add(1, self.a)
        self.xa.start()
        self.add(1, self.b)
        self.loads[3].start()
        self.ready(2)
        self.add(2, self.b)
        self.yb.start()
        self.add(2, self.a)

    def third(self):
        self.da.wait_recv()
        self.more(2, self.a)
        self.ya.start()
        self.db.wait_recv()
        self.more(1, self.b)
        self.xb.start()

    def end(self, write):
        self.ready(3)
        for part, first, second in ((self.a, self.xa, self.ya), (self.b, self.yb, self.xb)):
            first.wait_recv()
            second.wait_recv()
            total = self.own[1, part].astype(f32) + self.away[3, part].astype(f32)
            write(part, total + self.inx[part].astype(f32) + self.iny[part].astype(f32))

    def close(self):
        for c in self.over + [self.da, self.db, self.xa, self.yb, self.ya, self.xb]:
            c.wait_send()


def reduce_scratch(block):
    return [pltpu.VMEM((2, *block), bf16), pltpu.VMEM((4, *block), bf16)] + [pltpu.VMEM(block, bf16)] * 3 + [
        pltpu.SemaphoreType.DMA((2, REDUCE_COPIES)),
        pltpu.SemaphoreType.DMA((4,)),
    ]


class Exchange8:
    def __init__(self, srcs, dst, part, sems, own_sems):
        me = lax.axis_index("dp")
        slot = me % NF
        width = dst.shape[-1]

        def piece(src, e):
            return src.at[:, e] if part is None else src.at[:, e, :, pl.ds(part * width, width)]

        at, pieces = 0, []
        for src in srcs:
            pieces.append((src, pl.ds(at, src.shape[0])))
            at += src.shape[0]
        self.own = [
            pltpu.make_async_copy(piece(src, slot), dst.at[rows, slot], own_sems.at[i])
            for i, (src, rows) in enumerate(pieces)
        ]
        self.c = [
            remote(
                piece(src, flip(slot, m)), dst.at[rows, slot], sems, (m - 1) * len(srcs) + i, "dp", flip(me, m)
            )
            for m in (6, 7, 2, 3, 4, 5, 1)
            for i, (src, rows) in enumerate(pieces)
        ]

    def begin(self):
        for c in self.c + self.own:
            c.start()

    def end(self):
        for c in self.c:
            c.wait_recv()
        for c in self.c:
            c.wait_send()
        for c in self.own:
            c.wait()


class Send8:
    order = (6, 7, 2, 3, 4, 5, 1)

    def __init__(self, src, dst, sems, own_sem, packed):
        me = lax.axis_index("dp")
        slot = me % NF
        at = lambda m: src.at[m] if packed else src.at[flip(slot, m)]
        self.slot = slot
        self.own = pltpu.make_async_copy(at(0), dst.at[slot], own_sem)
        self.c = {m: remote(at(m), dst.at[slot], sems, m - 1, "dp", flip(me, m)) for m in self.order}

    def start(self, m):
        (self.c[m] if m else self.own).start()

    def begin(self):
        for m in (*self.order, 0):
            self.start(m)

    def got(self, m):
        if m:
            self.c[m].wait_recv()
        else:
            self.own.wait()

    def close(self):
        for c in self.c.values():
            c.wait_send()


def send_scratch():
    return [pltpu.SemaphoreType.DMA((2, NF - 1)), pltpu.SemaphoreType.DMA]


def half_shape(gate_up):
    _, groups, r, f = gate_up.shape
    return shape((3, groups, r, f // 2), bf16)


def exchange_scratch(n):
    return [pltpu.SemaphoreType.DMA((2, (NF - 1) * n)), pltpu.SemaphoreType.DMA((n,))]


def prologue_kernel(tensor, gu_ref, dn_ref, w_ref, wo_ref, out_ref, zq_ref, zo_ref, zsems, own_sems, *scratch):
    here = lax.axis_index("tensor")
    pairs = ((w_ref, zq_ref.at[here]), (wo_ref, zo_ref.at[here]))
    own = [pltpu.make_async_copy(src, dst, own_sems.at[i]) for i, (src, dst) in enumerate(pairs)]
    for c in own:
        c.start()
    greet(all_peers() + far_peers(tensor))
    copies = [
        remote(src, dst, zsems, 2 * n + i, axis, peer)
        for n, (axis, peer) in enumerate(far_peers(tensor))
        for i, (src, dst) in enumerate(pairs)
    ]
    for c in copies:
        c.start()
    swap = Exchange8([gu_ref, dn_ref], out_ref, 0, *scratch)
    swap.begin()
    for c in copies:
        c.wait_recv()
    swap.end()
    for c in copies:
        c.wait_send()
    for c in own:
        c.wait()


def prologue(gate_up, down, w, wo, tensor, cid):
    return pl.pallas_call(
        functools.partial(prologue_kernel, tensor),
        in_specs=[ANY] * 4,
        out_specs=[ANY] * 3,
        out_shape=(half_shape(gate_up), shape((tensor, *w.shape), bf16), shape((tensor, *wo.shape), bf16)),
        scratch_shapes=[
            pltpu.SemaphoreType.DMA((2, 2 * (tensor - 1))),
            pltpu.SemaphoreType.DMA((2,)),
            *exchange_scratch(2),
        ],
        compiler_params=pltpu.CompilerParams(collective_id=cid, has_side_effects=True, vmem_limit_bytes=60 << 20),
        cost_estimate=cost(25, 10),
    )(gate_up, down, w, wo)


def exchange_kernel(src, dst, *scratch):
    greet(all_peers())
    swap = Exchange8([src], dst, None, *scratch)
    swap.begin()
    swap.end()


def exchange8(x, cid):
    return pl.pallas_call(
        exchange_kernel,
        in_specs=[ANY],
        out_specs=ANY,
        out_shape=shape(x.shape, x.dtype),
        scratch_shapes=exchange_scratch(1),
        compiler_params=pltpu.CompilerParams(collective_id=cid, has_side_effects=True),
        cost_estimate=cost(18, 10),
    )(x)


class Near:
    def __init__(self, have, got, sems):
        me = lax.axis_index("dp")
        self.slot = me % NF
        self.have, self.got = have, got
        self.c = [
            remote(have, got.at[self.slot], sems, m - 1, "dp", flip(me, m)) for m in (6, 7, 2, 3, 4, 5, 1)
        ]

    def begin(self, value):
        self.have[...] = value.astype(bf16)
        for c in self.c:
            c.start()
        self.got[self.slot] = self.have[...]

    def end(self):
        for c in self.c:
            c.wait_recv()
        total = self.got[0].astype(f32)
        for n in range(1, NF):
            total = total + self.got[n].astype(f32)
        for c in self.c:
            c.wait_send()
        return total


def near_scratch(dims):
    return [pltpu.VMEM(dims, bf16), pltpu.VMEM((NF, *dims), bf16), pltpu.SemaphoreType.DMA((2, NF - 1))]


class Far:
    def __init__(self, tensor, value, have, got, sems):
        self.tensor, self.value, self.have, self.got, self.here = tensor, value, have, got, lax.axis_index("tensor")
        self.c = [
            remote(have, got.at[self.here], sems, n, axis, peer) for n, (axis, peer) in enumerate(far_peers(tensor))
        ]

    def begin(self):
        self.have[...] = self.value[...].astype(bf16)
        for c in self.c:
            c.start()
        self.got[self.here] = self.have[...]

    def end(self):
        for c in self.c:
            c.wait_recv()
        total = self.got[0].astype(f32)
        for t in range(1, self.tensor):
            total = total + self.got[t].astype(f32)
        for c in self.c:
            c.wait_send()
        return total


def far_scratch(tensor, dims):
    return [pltpu.VMEM(dims, bf16), pltpu.VMEM((tensor, *dims), bf16), pltpu.SemaphoreType.DMA((2, tensor - 1))]


def final_kernel(
    tensor, comm, g_ref, gp_any, gres_any, tok_any, w_any, yr_any, base_any, pos_ref, par_ref, small_ref,
    zs_ref, igrad_ref, layer_ref, total_ref, nag_ref,
    gp_ref, gres_ref, tok_ref, w_ref, yr_ref, base_ref, lsems, *scratch,
):
    k, d, _ = g_ref.shape
    ntile = SEQ // QT
    pairs = (
        (gp_any, gp_ref), (w_any.at[pl.ds(0, 3)], w_ref), (tok_any, tok_ref), (gres_any, gres_ref), (yr_any, yr_ref),
        (base_any, base_ref),
    )
    loads = [pltpu.make_async_copy(src, dst, lsems.at[n]) for n, (src, dst) in enumerate(pairs)]
    if comm:
        r, f = zs_ref.shape[2:]
        red = Reduce8(lambda s: g_ref.at[:, pl.ds(pl.multiple_of(s * r, r), r), :], scratch[:5], *scratch[5:7])
        sums, smalls = Near(*scratch[7:10]), Far(tensor, small_ref, *scratch[10:13])
        red.load()
        greet(all_peers() + far_peers(tensor))
        red.begin()
        smalls.begin()
    for c in loads:
        c.start()
    ga = par_ref[24:25, :].astype(f32)
    if comm:
        red.first()
        red.second()
    for c in loads[:4]:
        c.wait()
    nag = jnp.zeros((1, d), f32)
    for i in range(ntile):
        rows = pl.ds(i * QT, QT)
        gai = nt(gp_ref[0, rows, :], w_ref[0]) + nt(gp_ref[1, rows, :], w_ref[1])
        gai = gai + nt(gp_ref[2, rows, :], w_ref[2])
        x = tok_ref[rows, :].astype(f32)
        r1 = lax.rsqrt(jnp.mean(x * x, axis=-1, keepdims=True) + EPS)
        nag = nag + jnp.sum(gai * x * r1, axis=0, keepdims=True)
        scaled = gai * ga
        avg = jnp.mean(scaled * x, axis=-1, keepdims=True)
        igrad_ref[rows, :] = gres_ref[rows, :] + r1 * scaled - x * (r1 * r1 * r1 * avg)
        if comm and i == 0:
            red.third()
    if comm:
        sums.begin(nag)
    else:
        nag_ref[...] = nag
        total_ref[...] = small_ref[...]
    for c in loads[4:]:
        c.wait()

    def layer(i):
        rows = pl.ds(i * QT, QT)
        total = base_ref[rows, :]
        for e in range(NF):
            total = total + tn(hot_rows(pos_ref[e, :, rows]), yr_ref[e])
        layer_ref[rows, :] = total.astype(bf16)

    def write(part, total):
        for t in range(tensor):
            zs_ref[t, part] = total[:, :, t * f : (t + 1) * f].astype(bf16)

    for i in range(ntile):
        layer(i)
    if not comm:
        return
    nag_ref[...] = sums.end()
    red.end(write)
    total_ref[...] = smalls.end()
    red.close()


def last_kernel(tensor, zs_ref, small_ref, dw_ref, out_ref, total_ref, dwx_ref, zr, zsems, *scratch):
    here = lax.axis_index("tensor")
    smalls = Far(tensor, small_ref, *scratch[0:3])
    swap = Exchange8([dw_ref], dwx_ref, None, *scratch[3:5])
    greet(all_peers() + far_peers(tensor))
    copies = [
        remote(zs_ref.at[peer], zr.at[here], zsems, n, axis, peer) for n, (axis, peer) in enumerate(far_peers(tensor))
    ]
    for c in copies:
        c.start()
    smalls.begin()
    swap.begin()
    zr[here] = zs_ref[here]
    for c in copies:
        c.wait_recv()
    total = zr[0].astype(f32)
    for t in range(1, tensor):
        total = total + zr[t].astype(f32)
    out_ref[...] = total
    total_ref[...] = smalls.end()
    for c in copies:
        c.wait_send()
    swap.end()


def last(zs, small, dw, tensor, cid):
    return pl.pallas_call(
        functools.partial(last_kernel, tensor),
        in_specs=[VM] * 2 + [ANY],
        out_specs=[VM] * 2 + [ANY],
        out_shape=(shape(zs.shape[1:], f32), shape(small.shape, f32), shape(dw.shape, dw.dtype)),
        scratch_shapes=[
            pltpu.VMEM(zs.shape, bf16),
            pltpu.SemaphoreType.DMA((2, tensor - 1)),
            *far_scratch(tensor, small.shape),
            *exchange_scratch(1),
        ],
        compiler_params=pltpu.CompilerParams(collective_id=cid, has_side_effects=True, vmem_limit_bytes=60 << 20),
        cost_estimate=cost(18, 10),
    )(zs, small, dw)


def finish(g, gp, gres, tokens, w, yr, base, pos, params, small, tensor, comm, cid):
    k, d, columns = g.shape
    rows = tokens.shape[0]
    r, f = (d // NF if comm else 8), columns // tensor
    once = pltpu.CompilerParams(vmem_limit_bytes=60 << 20)
    if comm:
        once = pltpu.CompilerParams(collective_id=cid, has_side_effects=True, vmem_limit_bytes=60 << 20)
    return pl.pallas_call(
        functools.partial(final_kernel, tensor, comm),
        in_specs=[ANY] * 7 + [VM] * 3,
        out_specs=[VM] * 5,
        out_shape=(
            shape((tensor, k, r, f), bf16), shape((rows, d), f32), shape((rows, d), bf16), shape(small.shape, f32),
            shape((1, d), f32),
        ),
        scratch_shapes=[
            pltpu.VMEM(gp.shape, bf16),
            pltpu.VMEM((rows, d), f32),
            pltpu.VMEM((rows, d), bf16),
            pltpu.VMEM((3, d, columns), bf16),
            pltpu.VMEM(yr.shape, bf16),
            pltpu.VMEM((rows, d), f32),
            pltpu.SemaphoreType.DMA((6,)),
            *reduce_scratch((k, r, columns)),
            *near_scratch((1, d)),
            *far_scratch(tensor, small.shape),
        ],
        compiler_params=once,
        cost_estimate=cost(8, 4),
    )(g, gp, gres, tokens, w, yr, base, pos, params, small)


def fwd_kernel(
    starts_ref, tok_ref, prior_ref, ids_ref, ranks_ref, par_ref, cos_ref, sin_ref, w_ref, pos_ref, ys,
    q_ref, k_ref, v_ref, mixed_ref, lse_ref, nattn_ref, resid_ref, nmoe_ref, base_ref, aux_ref, xr_ref, yr_ref, payr_ref,
    bias_ref, gate_ref, xs, pay, wr_ref, *scratch,
):
    greet(all_peers())
    send_x, send_y = Send8(xs, xr_ref, *scratch[0:2], True), Send8(ys, yr_ref, *scratch[2:4], True)
    swap = Swap8(pay, payr_ref, *scratch[4:6])
    send_y.begin()
    lane = lanes(QT)
    router_rows(par_ref, wr_ref)
    wres = par_ref[32:48, 0:LANES]
    d = tok_ref.shape[1]
    pairs = d // LANES
    ntile = SEQ // QT
    ga, gm = par_ref[24:25, :].astype(f32), par_ref[25:26, :].astype(f32)
    cv = par_ref[26:28, :].astype(f32)
    mask_a, mask_b = head_masks()
    mask16 = (mask_a.astype(bf16), mask_b.astype(bf16))

    def project(i, carry):
        rows = pl.ds(pl.multiple_of(i * QT, QT), QT)
        x = tok_ref[rows, :].astype(f32)
        r1 = lax.rsqrt(jnp.mean(x * x, axis=-1, keepdims=True) + EPS)
        n = (x * r1 * ga).astype(bf16)
        nattn_ref[rows, :] = n
        cosine, sine = cos_ref[rows, :], sin_ref[rows, :]
        for c, out in ((0, q_ref), (1, k_ref), (2, v_ref)):
            proj = nn(n, w_ref[c])
            for p in range(pairs):
                part = proj[:, p * LANES : (p + 1) * LANES]
                if c < 2:
                    part = rot(part, cosine, sine)
                part = part.astype(bf16)
                if c == 0:
                    part = part * jnp.array(HD**-0.5, bf16)
                out[rows, p * LANES : (p + 1) * LANES] = part
        return carry

    lax.fori_loop(0, ntile, project, 0)

    for i in range(ntile):
        lo = i * QT
        width = min(SEQ, lo + 2 * QT) - lo
        rows = pl.ds(lo, QT)
        bias_ref[:, :width] = window_bias(starts_ref, i, width, False)

        def pair(p, lse):
            cols = pl.ds(pl.multiple_of(p * LANES, LANES), LANES)
            q2 = q_ref[rows, cols]
            outs = []
            for h in range(2):
                qh = q2 * mask16[h]
                sb = nt(qh, k_ref[lo : lo + width, cols]) + bias_ref[:, :width]
                m = jnp.max(sb, axis=-1, keepdims=True)
                if lo:
                    sa = nt(qh, k_ref[0:lo, cols])
                    m = jnp.maximum(m, jnp.max(sa, axis=-1, keepdims=True))
                pb = jnp.exp(sb - m)
                total = jnp.sum(pb, axis=-1, keepdims=True)
                acc = nn(pb.astype(bf16), v_ref[lo : lo + width, cols])
                if lo:
                    pa = jnp.exp(sa - m)
                    total = total + jnp.sum(pa, axis=-1, keepdims=True)
                    acc = acc + nn(pa.astype(bf16), v_ref[0:lo, cols])
                outs.append(acc / total)
                lse = jnp.where(lane == 2 * p + h, m + jnp.log(total), lse)
            mixed_ref[rows, cols] = (outs[0] * mask_a + outs[1] * mask_b).astype(bf16)
            return lse

        lse = lax.fori_loop(0, pairs, pair, jnp.zeros((QT, LANES), f32))
        lse_ref[:, rows] = lse.T[0 : lse_ref.shape[0], :]

        x = tok_ref[rows, :].astype(f32)
        resid = x + nt(mixed_ref[rows, :], w_ref[3])
        resid_ref[rows, :] = resid
        r2 = lax.rsqrt(jnp.mean(resid * resid, axis=-1, keepdims=True) + EPS)
        nm = (resid * r2 * gm).astype(bf16)
        nmoe_ref[rows, :] = nm
        raw = nt(nm, wr_ref[...])
        logits = raw + tn(prior_ref[:, rows], wres)
        logits = jnp.where(lane < NF + 2 + NC, logits, -1e30)
        e = jnp.exp(logits - jnp.max(logits, axis=-1, keepdims=True))
        shares = e / jnp.sum(e, axis=-1, keepdims=True)
        chosen, kept = routes(ids_ref, ranks_ref, i)
        gate_ref[:, 0, rows] = shares.T[0:NF, :] * kept[0:NF, :]
        chosen = jnp.concatenate([chosen, jnp.zeros((LANES - 16, QT), f32)], axis=0).T
        gates = shares * chosen
        nv = nm.astype(f32)
        aux = jnp.where(lane < NF + 2 + NC, shares, 0.0) + pltpu.roll(chosen, CHOSEN, 1)
        direct = gates[:, NF + 1 : NF + 2]
        others = None
        for c in range(NC):
            z0, z1 = raw[:, Z0 + 2 * c : Z0 + 2 * c + 1], raw[:, Z0 + 2 * c + 1 : Z0 + 2 * c + 2]
            m0, m1 = 1.0 / (1.0 + jnp.exp(z1 - z0)), 1.0 / (1.0 + jnp.exp(z0 - z1))
            aux = jnp.where(lane == Z0 + 2 * c, m0, aux)
            aux = jnp.where(lane == Z0 + 2 * c + 1, m1, aux)
            w = gates[:, NF + 2 + c : NF + 3 + c]
            direct = direct + w * m0
            term = (w * m1) * cv[c : c + 1, :]
            others = term if others is None else others + term
        aux_ref[rows, :] = aux
        base_ref[rows, :] = resid + direct * nv + others

    for m in (*Send8.order, 0):
        e = flip(send_x.slot, m)
        place = pos_ref[e]
        hot = hot_rows(place)
        xs[m] = nn(hot, nmoe_ref[...]).astype(bf16)
        send_x.start(m)
        pay[e] = jnp.sum(nt(split_rows(gate_ref[e]), hot), axis=0, keepdims=True)
        filled = jnp.minimum(jnp.max(place, axis=1, keepdims=True) + 1.0, float(ROOM))
        pay[NF + e] = jnp.broadcast_to(filled, (1, ROOM))
    swap.begin()
    for send in (send_y, send_x):
        for m in (*Send8.order, 0):
            send.got(m)
        send.close()
    swap.end()


def mid_kernel(
    dxb_ref, ggb_ref, og_any, nmoe_any, resid_any, aux_any, pos_ref, prior_ref, par_ref, count_ref,
    gmo_ref, gres_ref, pgrad_ref, small_ref,
    dxr, ggr, dx_ref, gg_ref, inner_ref, extra_ref, wr_ref, resg_ref, og_ref, nmoe_ref, resid_ref, aux_ref, lsems, *scratch,
):
    pairs = ((og_any, og_ref), (nmoe_any, nmoe_ref), (resid_any, resid_ref), (aux_any, aux_ref))
    loads = [pltpu.make_async_copy(a, b, lsems.at[n]) for n, (a, b) in enumerate(pairs)]
    for c in loads:
        c.start()
    greet(all_peers())
    send, swap = Send8(dxb_ref, dxr, *scratch[0:2], False), Swap8(ggb_ref, ggr, *scratch[2:4])
    swap.begin()
    send.begin()
    gm, cv = par_ref[25:26, :].astype(f32), par_ref[26:28, :].astype(f32)
    wres = par_ref[32:48, 0:LANES]
    router_rows(par_ref, wr_ref)
    lane = lanes(QT)
    small_ref[...] = jnp.zeros_like(small_ref)
    resg_ref[...] = jnp.zeros_like(resg_ref)
    small_ref[28:29, 0:LANES] = jnp.max(jnp.where(count_ref[...] > ROOM, 1.0, 0.0), axis=0, keepdims=True)

    def ahead(i, carry):
        rows = pl.ds(pl.multiple_of(i * QT, QT), QT)
        g16 = og_ref[rows, :]
        g, nv = g16.astype(f32), nmoe_ref[rows, :].astype(f32)
        x = resid_ref[rows, :]
        aux = aux_ref[rows, :]
        chosen = jnp.where(lane < 16, pltpu.roll(aux, LANES - CHOSEN, 1), 0.0)
        gates = jnp.where(lane < NF + 2 + NC, aux, 0.0) * chosen
        copy_inner = jnp.sum(g * nv, axis=-1, keepdims=True)
        inner = jnp.where(lane == NF + 1, copy_inner, 0.0)
        direct = gates[:, NF + 1 : NF + 2]
        extra = jnp.where(lane == 1, lax.rsqrt(jnp.mean(x * x, axis=-1, keepdims=True) + EPS), 0.0)
        cvw = jnp.zeros((QT, LANES), f32)
        for c in range(NC):
            m0, m1 = aux[:, Z0 + 2 * c : Z0 + 2 * c + 1], aux[:, Z0 + 2 * c + 1 : Z0 + 2 * c + 2]
            v_inner = jnp.sum(g * cv[c : c + 1, :], axis=-1, keepdims=True)
            mean = m0 * copy_inner + m1 * v_inner
            inner = jnp.where(lane == NF + 2 + c, mean, inner)
            w = gates[:, NF + 2 + c : NF + 3 + c]
            direct = direct + w * m0
            extra = jnp.where(lane == Z0 + 2 * c, m0 * (w * copy_inner - w * mean), extra)
            extra = jnp.where(lane == Z0 + 2 * c + 1, m1 * (w * v_inner - w * mean), extra)
            cvw = jnp.where(lane == c, w * m1, cvw)
        inner_ref[rows, :] = inner
        extra_ref[rows, :] = jnp.where(lane == 0, direct, extra)
        cv_hi, cv_lo = split(cvw)
        small_ref[24:26, :] += tn(cv_hi, g16)[0:NC] + tn(cv_lo, g16)[0:NC]
        return carry

    for c in loads:
        c.wait()
    lax.fori_loop(0, SEQ // QT, ahead, 0)
    swap.end()
    for n, m in enumerate((0, 1, 2, 3, 4, 5, 6, 7)):
        send.got(m)
        e = flip(send.slot, m)
        hot = hot_rows(pos_ref[e])
        gg_ref[pl.ds(e, 1), :] = jnp.sum(nn(split_rows(ggr[e]), hot), axis=0, keepdims=True)
        part = tn(hot, dxr[e])
        if n:
            dx_ref[...] += part
        else:
            dx_ref[...] = part
    send.close()

    def tile(i, carry):
        rows = pl.ds(pl.multiple_of(i * QT, QT), QT)
        g, n16 = og_ref[rows, :].astype(f32), nmoe_ref[rows, :]
        x = resid_ref[rows, :]
        aux, extra = aux_ref[rows, :], extra_ref[rows, :]
        direct, r2 = extra[:, 0:1], extra[:, 1:2]
        shares = jnp.where(lane < NF + 2 + NC, aux, 0.0)
        chosen = jnp.where(lane < 16, pltpu.roll(aux, LANES - CHOSEN, 1), 0.0)
        inner = jnp.concatenate([gg_ref[:, rows], jnp.zeros((LANES - NF, QT), f32)], axis=0).T
        grad_router = (inner + inner_ref[rows, :]) * chosen
        glog = shares * (grad_router - jnp.sum(shares * grad_router, axis=-1, keepdims=True))
        both_hi, both_lo = split(glog + jnp.where(lane >= Z0, extra, 0.0))
        log_hi, log_lo = split(glog)
        pgrad_ref[:, rows] = nt(wres, log_hi) + nt(wres, log_lo)
        small_ref[0:24, :] += tn(both_hi, n16)[0:24] + tn(both_lo, n16)[0:24]
        resg_ref[...] += nn(prior_ref[:, rows], log_hi) + nn(prior_ref[:, rows], log_lo)
        gmi = dx_ref[rows, :] + direct * g + nn(both_hi, wr_ref[...]) + nn(both_lo, wr_ref[...])
        small_ref[26:27, :] += jnp.sum(gmi * x * r2, axis=0, keepdims=True)
        scaled = gmi * gm
        avg = jnp.mean(scaled * x, axis=-1, keepdims=True)
        gres = g + r2 * scaled - x * (r2 * r2 * r2 * avg)
        gres_ref[rows, :] = gres
        gmo_ref[rows, :] = gres.astype(bf16)
        return carry

    lax.fori_loop(0, SEQ // QT, tile, 0)
    for n in range(NF + 2 + NC):
        at = n % RES * LANES
        small_ref[29 + n // RES : 30 + n // RES, at : at + LANES] = resg_ref[n : n + 1, :]


def bwd_kernel(
    starts_ref, gmo_ref, mixed_ref, q_any, k_any, v_any, lse_ref, nattn_any, cos_any, sin_any, w_any, small_ref,
    outb_ref, dw_ref,
    wg_ref, gp_ref, outr_ref, total_ref, dwx_ref,
    do_ref, delta_ref, bias_ref, dk_ref, dv_ref, dq_ref, wo_ref, wsem, q_ref, k_ref, v_ref, nattn_ref, cos_ref, sin_ref, lsems,
    *scratch,
):
    late = ((q_any, q_ref), (k_any, k_ref), (v_any, v_ref), (cos_any, cos_ref), (sin_any, sin_ref), (nattn_any, nattn_ref))
    loads = [pltpu.make_async_copy(a, b, lsems.at[n]) for n, (a, b) in enumerate(late)]
    load = pltpu.make_async_copy(w_any.at[pl.ds(3, 1)], wo_ref, wsem)
    load.start()
    send = Send8(outb_ref, outr_ref, *scratch[0:2], False)
    sums = Near(*scratch[2:5])
    greet(all_peers())
    sums.begin(small_ref[...])
    send.begin()
    swap = Exchange8([dw_ref], dwx_ref, None, *scratch[5:7])
    swap.begin()
    for c in loads:
        c.start()
    d = mixed_ref.shape[1]
    pairs = d // LANES
    ntile = SEQ // QT
    mask_a, mask_b = head_masks()
    mask16 = (mask_a.astype(bf16), mask_b.astype(bf16))
    maskf = (mask_a, mask_b)
    heads = delta_ref.shape[0]
    pick = jnp.where(
        lax.broadcasted_iota(i32, (heads, d), 1) // HD == lax.broadcasted_iota(i32, (heads, d), 0), 1.0, 0.0
    ).astype(bf16)

    load.wait()

    def start(i, carry):
        rows = pl.ds(pl.multiple_of(i * QT, QT), QT)
        do = nn(gmo_ref[rows, :], wo_ref[0]).astype(bf16)
        do_ref[rows, :] = do
        hi, lo = split(do.astype(f32) * mixed_ref[rows, :].astype(f32))
        delta_ref[:, rows] = nt(pick, hi) + nt(pick, lo)
        return carry

    lax.fori_loop(0, ntile, start, 0)
    wg_ref[3] = tn(gmo_ref[...], mixed_ref[...]).astype(wg_ref.dtype)
    for i in range(ntile):
        width = min(SEQ, (i + 2) * QT) - i * QT
        bias_ref[i, 0:width, :] = window_bias(starts_ref, i, width, True)

    def pair(p, carry):
        cols = pl.ds(pl.multiple_of(p * LANES, LANES), LANES)
        dk_ref[...] = jnp.zeros_like(dk_ref)
        dv_ref[...] = jnp.zeros_like(dv_ref)
        for i in range(ntile):
            lo = i * QT
            width = min(SEQ, lo + 2 * QT) - lo
            rows = pl.ds(lo, QT)
            q2, do2 = q_ref[rows, cols], do_ref[rows, cols]
            dq = jnp.zeros((QT, LANES), f32)
            for h in range(2):
                qh, doh = q2 * mask16[h], do2 * mask16[h]
                lse, delta = lse_ref[pl.ds(2 * p + h, 1), rows], delta_ref[pl.ds(2 * p + h, 1), rows]
                spans = [(lo, width, True)] + ([(0, lo, False)] if lo else [])
                for at, size, masked in spans:
                    k2 = k_ref[at : at + size, cols]
                    s = nt(k2, qh)
                    if masked:
                        s = s + bias_ref[i, 0:size, :]
                    prob = jnp.exp(s - lse)
                    ds = (prob * (nt(v_ref[at : at + size, cols], doh) - delta)).astype(bf16)
                    dv_ref[at : at + size, :] += nn(prob.astype(bf16), doh)
                    dk_ref[at : at + size, :] += nn(ds, qh)
                    dq = dq + tn(ds, k2) * maskf[h]
            dq_ref[rows, :] = dq * HD**-0.5
        cosine, sine = cos_ref[...], -sin_ref[...]
        gp_ref[0, :, cols] = rot(dq_ref[...], cosine, sine).astype(bf16)
        gp_ref[1, :, cols] = rot(dk_ref[...], cosine, sine).astype(bf16)
        gp_ref[2, :, cols] = dv_ref[...].astype(bf16)
        return carry

    for c in loads:
        c.wait()
    lax.fori_loop(0, pairs, pair, 0)
    for c in range(3):
        wg_ref[c] = tn(nattn_ref[...], gp_ref[c]).astype(wg_ref.dtype)
    for m in range(NF):
        send.got(m)
    send.close()
    swap.end()
    total_ref[...] = sums.end()


def ffn_tile(x, gate, y, w_ref, acc, eo, dx):
    dy = y.astype(f32)
    ge = (gate * dy).astype(bf16)
    x_t, ge_t = x.T, ge.T
    for c in range(w_ref.shape[0]):
        wg, wu, wd = w_ref[c, 0], w_ref[c, 1], w_ref[c, 2]
        gv, uv = nn(x, wg), nn(x, wu)
        gh = nn(ge, wd)
        sig = 1.0 / (1.0 + jnp.exp(-gv))
        act = gv * sig
        hid = (act * uv).astype(bf16)
        eo = eo + nt(hid, wd)
        gg = (gh * uv * (sig * (1.0 + gv * (1.0 - sig)))).astype(bf16)
        gu = (gh * act).astype(bf16)
        dx = dx + nt(gg, wg) + nt(gu, wu)
        acc[c, 0] += nn(x_t, gg)
        acc[c, 1] += nn(x_t, gu)
        acc[c, 2] += nn(ge_t, hid)
    return eo, dx


def first_kernel(pay_ref, x_ref, y_ref, w_ref, xc_ref, yc_ref, gc_ref, eo_ref, dx_ref, dw_ref, meta_ref, acc):
    d = x_ref.shape[2]
    gates = [pay_ref[g] for g in range(NF)] + [jnp.zeros((LANES - NF, ROOM), f32)]
    columns = jnp.concatenate(gates, axis=0).T
    off = jnp.int32(0)
    for g in range(NF):
        rows = pl.ds(pl.multiple_of(off, 16), ROOM)
        xc_ref[rows, :] = x_ref[g]
        yc_ref[rows, :] = y_ref[g]
        gc_ref[rows, :] = jnp.broadcast_to(columns[:, g : g + 1], (ROOM, LANES))
        meta_ref[g] = off
        off = off + (jnp.max(pay_ref[NF + g]).astype(i32) + 15) // 16 * 16
    rows = pl.ds(pl.multiple_of(off, 16), TM)
    xc_ref[rows, :] = jnp.zeros((TM, d), bf16)
    yc_ref[rows, :] = jnp.zeros((TM, d), bf16)
    gc_ref[rows, :] = jnp.zeros((TM, LANES), f32)
    tiles = jnp.maximum((off + TM - 1) // TM, 1)
    meta_ref[NF] = tiles
    acc[...] = jnp.zeros_like(acc)
    zero = jnp.zeros((TM, d), f32)

    def tile(t, carry):
        rows = pl.ds(pl.multiple_of(t * TM, TM), TM)
        eo_ref[rows, :], dx_ref[rows, :] = ffn_tile(
            xc_ref[rows, :], gc_ref[rows, 0:1], yc_ref[rows, :], w_ref, acc, zero, zero
        )
        return carry

    lax.fori_loop(0, tiles, tile, 0)
    dw_ref[...] = acc[...].astype(bf16)


def second_kernel(
    meta_ref, xc_any, yc_any, gc_any, eo_any, dx_any, w_any, outb_ref, dxb_ref, ggb_ref, dw_ref,
    xc_ref, yc_ref, gc_ref, eo_ref, dx_ref, w_ref, outs, dxs, ggs, acc, sems, wsem,
):
    d = xc_ref.shape[1]
    tiles = meta_ref[NF]
    weights = pltpu.make_async_copy(w_any, w_ref, wsem)
    weights.start()

    def copies(t):
        rows = pl.ds(pl.multiple_of(t * TM, TM), TM)
        pairs = ((xc_any, xc_ref), (yc_any, yc_ref), (gc_any, gc_ref), (eo_any, eo_ref), (dx_any, dx_ref))
        return [pltpu.make_async_copy(a.at[rows, :], b.at[rows, :], sems.at[n, t]) for n, (a, b) in enumerate(pairs)]

    def begin(t, carry):
        for c in copies(t):
            c.start()
        return carry

    lax.fori_loop(0, tiles, begin, 0)
    acc[...] = jnp.zeros_like(acc)
    rows = pl.ds(pl.multiple_of(tiles * TM, TM), ROOM)
    outs[rows, :] = jnp.zeros((ROOM, d), bf16)
    dxs[rows, :] = jnp.zeros((ROOM, d), bf16)
    ggs[rows, :] = jnp.zeros((ROOM, LANES), f32)
    weights.wait()

    def tile(t, carry):
        rows = pl.ds(pl.multiple_of(t * TM, TM), TM)
        for c in copies(t):
            c.wait()
        gate, y = gc_ref[rows, 0:1], yc_ref[rows, :]
        eo, dx = ffn_tile(xc_ref[rows, :], gate, y, w_ref, acc, eo_ref[rows, :], dx_ref[rows, :])
        outs[rows, :] = (gate * eo).astype(bf16)
        dxs[rows, :] = dx.astype(bf16)
        ggs[rows, :] = jnp.broadcast_to(jnp.sum(y.astype(f32) * eo, axis=1, keepdims=True), (TM, LANES))
        return carry

    lax.fori_loop(0, tiles, tile, 0)
    lane = lanes(ROOM)
    columns = jnp.zeros((ROOM, LANES), f32)
    for g in range(NF):
        rows = pl.ds(pl.multiple_of(meta_ref[g], 16), ROOM)
        outb_ref[g] = outs[rows, :]
        dxb_ref[g] = dxs[rows, :]
        columns = jnp.where(lane == g, ggs[rows, :], columns)
    ggb_ref[:, 0, :] = columns.T[0:NF, :]
    dw_ref[...] = acc[...].astype(bf16)


def experts_first(pay, x, y, w):
    groups, _, d = x.shape
    total = groups * ROOM + TM
    return pl.pallas_call(
        first_kernel,
        in_specs=[VM] * 4,
        out_specs=[VM] * 6 + [SM],
        out_shape=(
            shape((total, d), bf16), shape((total, d), bf16), shape((total, LANES), f32), shape((total, d), f32),
            shape((total, d), f32), shape(w.shape, bf16), shape((NF + 1,), i32),
        ),
        scratch_shapes=[pltpu.VMEM(w.shape, f32)],
        compiler_params=pltpu.CompilerParams(vmem_limit_bytes=60 << 20),
        cost_estimate=cost(22, 25),
    )(pay, x, y, w)


def experts_second(meta, xc, yc, gc, eo, dx, w):
    total, d = xc.shape
    blocks = shape((NF, ROOM, d), bf16)
    room = total + ROOM
    return pl.pallas_call(
        second_kernel,
        in_specs=[SM] + [ANY] * 6,
        out_specs=[VM] * 4,
        out_shape=(blocks, blocks, shape((NF, 1, ROOM), f32), shape(w.shape, bf16)),
        scratch_shapes=[
            pltpu.VMEM((total, d), bf16),
            pltpu.VMEM((total, d), bf16),
            pltpu.VMEM((total, LANES), f32),
            pltpu.VMEM((total, d), f32),
            pltpu.VMEM((total, d), f32),
            pltpu.VMEM(w.shape, bf16),
            pltpu.VMEM((room, d), bf16),
            pltpu.VMEM((room, d), bf16),
            pltpu.VMEM((room, LANES), f32),
            pltpu.VMEM(w.shape, f32),
            pltpu.SemaphoreType.DMA((5, total // TM)),
            pltpu.SemaphoreType.DMA,
        ],
        compiler_params=pltpu.CompilerParams(vmem_limit_bytes=60 << 20),
        cost_estimate=cost(22, 25),
    )(meta, xc, yc, gc, eo, dx, w)


def emit_kernel(a_ref, b_ref, wg_ref, small_ref, nag_ref, gu_ref, dn_ref, qkv_ref, wo_ref, rt_ref, rg_ref, cv_ref, cg_ref, na_ref, nm_ref):
    half = a_ref.shape[3]
    for n, ref in ((0, a_ref), (1, b_ref)):
        at = slice(n * half, (n + 1) * half)
        gu_ref[:, 0, :, at] = ref[0:2, 0].astype(f32)
        dn_ref[0, :, at] = ref[2, 0].astype(f32)

    @pl.when(pl.program_id(0) == 0)
    def _():
        qkv_ref[...] = wg_ref[0:3]
        r, f = wg_ref.shape[1:]
        wide = jnp.concatenate([wg_ref[3], jnp.zeros((r, -f % LANES), f32)], axis=1)
        wo_ref[...] = jnp.concatenate([wide, jnp.zeros((-r % LANES, wide.shape[1]), f32)], axis=0).T[0:f, 0:r]
        ne = rg_ref.shape[0]
        rt_ref[...] = small_ref[0:ne, :]
        for c in range(NC):
            cg_ref[c] = small_ref[Z0 + 2 * c : Z0 + 2 * c + 2, :]
        cv_ref[...] = small_ref[24 : 24 + NC, :]
        nm_ref[...] = small_ref[26, :]
        na_ref[...] = nag_ref[0, :]
        for n in range(ne):
            at = n % RES * LANES
            rg_ref[n : n + 1, :] = small_ref[29 + n // RES : 30 + n // RES, at : at + LANES][:, 0:ne]


def emit(dw_a, dw_b, wg, small, nag, ne):
    _, groups, r, half = dw_a.shape
    d = small.shape[1]
    piece = pl.BlockSpec((3, 1, r, half), lambda e: (0, e, 0, 0))
    whole = lambda *dims: pl.BlockSpec(dims, lambda e: (0,) * len(dims))
    rest = [(3, *wg.shape[1:]), wg.shape[:0:-1], (ne, d), (ne, ne), (NC, d), (NC, 2, d), (d,), (d,)]
    return pl.pallas_call(
        emit_kernel,
        grid=(groups,),
        in_specs=[piece, piece, whole(*wg.shape), whole(*small.shape), whole(1, d)],
        out_specs=[
            pl.BlockSpec((2, 1, r, 2 * half), lambda e: (0, e, 0, 0)), pl.BlockSpec((1, r, 2 * half), lambda e: (e, 0, 0)),
            *(whole(*dims) for dims in rest),
        ],
        out_shape=(
            shape((2, groups, r, 2 * half), f32), shape((groups, r, 2 * half), f32), *(shape(dims, f32) for dims in rest),
        ),
        cost_estimate=cost(1, 8),
    )(dw_a, dw_b, wg, small, nag)


def router_rows(par_ref, wr_ref):
    wr_ref[...] = jnp.zeros_like(wr_ref)
    wr_ref[0:16, :] = par_ref[0:16, :]
    wr_ref[16:32, :] = jnp.where(
        lax.broadcasted_iota(i32, (16, par_ref.shape[1]), 0) < 2 * NC, par_ref[16:32, :].astype(f32), 0.0
    ).astype(bf16)


def hot_rows(pos):
    slot = lax.broadcasted_iota(i32, (ROOM, pos.shape[1]), 0).astype(f32)
    return jnp.where(slot == pos, 1.0, 0.0).astype(bf16)


def split_rows(row):
    hi = row.astype(bf16).astype(f32)
    mid = (row - hi).astype(bf16).astype(f32)
    at = lax.broadcasted_iota(i32, (8, row.shape[1]), 0)
    out = jnp.where(at == 0, hi, jnp.where(at == 1, mid, jnp.where(at == 2, row - hi - mid, 0.0)))
    return out.astype(bf16)


def shape(dims, dtype):
    return jax.ShapeDtypeStruct(dims, dtype)


def cost(gflop, mbytes, mexp=0):
    return pl.CostEstimate(flops=int(gflop * 1e9), bytes_accessed=int(mbytes * 1e6), transcendentals=int(mexp * 1e6))


def rms_factor(values):
    return lax.rsqrt(jnp.mean(values * values, axis=-1, keepdims=True) + EPS)


def norm_back(grad, values, factor, gain):
    scaled = grad * gain
    inner = jnp.mean(scaled * values, axis=-1, keepdims=True)
    return factor * scaled - values * factor * factor * factor * inner


def rotary(positions, width):
    place = (jnp.arange(positions) % SEQ).astype(jnp.float32)
    freqs = jnp.power(10000.0, jnp.arange(width // 2).astype(jnp.float32) * (-2.0 / width))
    angles = place[:, None] * freqs[None, :]
    return (jnp.cos(angles)[:, None, :], jnp.sin(angles)[:, None, :])


def rotate(values, cosine, sine):
    half = values.shape[-1] // 2
    front = values[..., :half]
    behind = values[..., half:]
    return jnp.concatenate(
        [front * cosine - behind * sine, behind * cosine + front * sine], axis=-1
    )


def visible(starts):
    position = jnp.arange(SEQ)
    piece_of = jnp.zeros((SEQ,), jnp.int32)
    for index in range(starts.shape[0]):
        inside = (position >= starts[index]) & (position < starts[index] + PIECE)
        piece_of = jnp.where(inside, index + 1, piece_of)
    causal = position[None, :] <= position[:, None]
    same_piece = (piece_of[:, None] > 0) & (piece_of[:, None] == piece_of[None, :])
    return causal | same_piece


def dispatch(route_ids, route_ranks):
    group_rows = route_ids.shape[0]
    retained = (route_ids < NF) & (route_ranks < CAP)
    target = jnp.where(retained, route_ids * CAP + route_ranks, NF * CAP)
    token_index = jnp.broadcast_to(
        jnp.arange(group_rows, dtype=jnp.int32)[:, None], route_ids.shape
    )
    slot_token = (
        jnp.zeros((NF * CAP + 1,), jnp.int32)
        .at[target.reshape(-1)]
        .set(token_index.reshape(-1))[: NF * CAP]
    )
    filled = jnp.zeros((NF * CAP + 1,), jnp.float32).at[target.reshape(-1)].set(1.0)[: NF * CAP]
    return (retained, target, slot_token, filled)


def masked_scores(query, keys, starts):
    scores = jnp.einsum("qhd,khd->hqk", query, keys, preferred_element_type=jnp.float32) * HD ** (
        -0.5
    )
    return jnp.where(visible(starts)[None], scores, -1e30)


def attend_block(parts):
    query, keys, values, starts = parts
    scores = masked_scores(query, keys, starts)
    row_max = jnp.max(scores, axis=-1, keepdims=True)
    denominator = jnp.sum(jnp.exp(scores - row_max), axis=-1, keepdims=True)
    log_total = row_max + jnp.log(denominator)
    shares = jnp.exp(scores - log_total).astype(jnp.bfloat16)
    mixed = jnp.einsum("hqk,khd->qhd", shares, values, preferred_element_type=jnp.float32)
    return (mixed.astype(jnp.bfloat16), log_total)


def attend_back(parts):
    query, keys, values, starts, log_total, grad_out = parts
    shares = jnp.exp(masked_scores(query, keys, starts) - log_total)
    grad_shares = jnp.einsum("qhd,khd->hqk", grad_out, values, preferred_element_type=jnp.float32)
    centre = jnp.sum(shares * grad_shares, axis=-1, keepdims=True)
    grad_scores = (shares * (grad_shares - centre)).astype(jnp.bfloat16)
    factor = HD ** (-0.5)
    grad_query = (
        jnp.einsum("hqk,khd->qhd", grad_scores, keys, preferred_element_type=jnp.float32) * factor
    )
    grad_keys = (
        jnp.einsum("hqk,qhd->khd", grad_scores, query, preferred_element_type=jnp.float32) * factor
    )
    grad_values = jnp.einsum(
        "hqk,qhd->khd", shares.astype(jnp.bfloat16), grad_out, preferred_element_type=jnp.float32
    )
    return (grad_query, grad_keys, grad_values)


def plain_on_device(
    tokens,
    prior_logits,
    expert_ids,
    expert_ranks,
    piece_starts,
    norm_attn,
    qkv_weight,
    out_weight,
    norm_moe,
    router_weight,
    residual_weight,
    const_vectors,
    const_gates,
    w_gate_up,
    w_down,
    out_grad,
):
    highest = lax.Precision.HIGHEST
    local_rows = tokens.shape[0]
    group_rows = expert_ids.shape[0]
    sequences = group_rows // SEQ
    head_count = qkv_weight.shape[2] // HD
    row_start = lax.axis_index("tensor") * local_rows
    seq_shape = (sequences, SEQ, head_count, HD)
    gain_attn = norm_attn.astype(jnp.float32)
    gain_moe = norm_moe.astype(jnp.float32)
    tok_vals = tokens.astype(jnp.float32)
    factor_attn = rms_factor(tok_vals)
    normed_attn = (tok_vals * factor_attn * gain_attn).astype(jnp.bfloat16)
    attn_rows = lax.all_gather(normed_attn, "tensor", axis=0, tiled=True)
    qkv_full, out_full = (
        lax.all_gather(qkv_weight, "dp", axis=1, tiled=True),
        lax.all_gather(out_weight, "dp", axis=1, tiled=True),
    )
    projected = jnp.einsum("gd,cde->cge", attn_rows, qkv_full, preferred_element_type=jnp.float32)
    cosine, sine = rotary(group_rows, HD)
    query = (
        rotate(projected[0].reshape(group_rows, head_count, HD), cosine, sine)
        .astype(jnp.bfloat16)
        .reshape(seq_shape)
    )
    keys = (
        rotate(projected[1].reshape(group_rows, head_count, HD), cosine, sine)
        .astype(jnp.bfloat16)
        .reshape(seq_shape)
    )
    values = projected[2].astype(jnp.bfloat16).reshape(seq_shape)
    mixed, log_total = lax.map(attend_block, (query, keys, values, piece_starts))
    mixed_rows = mixed.reshape(group_rows, head_count * HD)
    attn_part = jnp.dot(mixed_rows, out_full, preferred_element_type=jnp.float32)
    attn_out = lax.psum_scatter(attn_part, "tensor", scatter_dimension=0, tiled=True)
    resid = tok_vals + attn_out
    factor_moe = rms_factor(resid)
    normed_moe = (resid * factor_moe * gain_moe).astype(jnp.bfloat16)
    moe_rows, prior_rows = (
        lax.all_gather(normed_moe, "tensor", axis=0, tiled=True),
        lax.all_gather(prior_logits, "tensor", axis=0, tiled=True),
    )
    logits = jnp.dot(moe_rows, router_weight, preferred_element_type=jnp.float32) + jnp.dot(
        prior_rows, residual_weight, preferred_element_type=jnp.float32
    )
    shares = jax.nn.softmax(logits, axis=-1)
    gates = jnp.take_along_axis(shares, expert_ids, axis=1)
    retained, target, slot_token, filled = dispatch(expert_ids, expert_ranks)
    picker = jnp.minimum(target, NF * CAP - 1)
    slot_gate = (
        jnp.zeros((NF * CAP + 1,), jnp.float32)
        .at[target.reshape(-1)]
        .set(gates.reshape(-1))[: NF * CAP]
        * filled
    )
    expert_rows = (moe_rows[slot_token] * filled[:, None].astype(jnp.bfloat16)).reshape(NF, CAP, -1)
    gate_full, down_full = (
        lax.all_gather(w_gate_up, "dp", axis=2, tiled=True),
        lax.all_gather(w_down, "dp", axis=2, tiled=True),
    )
    gate_up = jnp.einsum(
        "ecd,sedf->secf", expert_rows, gate_full, preferred_element_type=jnp.float32
    )
    sigmoid_vals = jax.nn.sigmoid(gate_up[0])
    activated = gate_up[0] * sigmoid_vals
    hidden = (activated * gate_up[1]).astype(jnp.bfloat16)
    expert_out = jnp.einsum(
        "ecf,efd->ecd", hidden, down_full, preferred_element_type=jnp.float32
    ).reshape(NF * CAP, -1)
    retained_gates = jnp.where(retained, gates, 0.0)
    combined = jnp.sum(retained_gates[:, :, None] * expert_out[picker], axis=1)
    ffn_out = lax.psum_scatter(
        combined.astype(jnp.bfloat16), "tensor", scatter_dimension=0, tiled=True
    ).astype(jnp.float32)
    local_ids = lax.dynamic_slice_in_dim(expert_ids, row_start, local_rows, 0)
    local_shares = lax.dynamic_slice_in_dim(shares, row_start, local_rows, 0)
    local_gates = lax.dynamic_slice_in_dim(gates, row_start, local_rows, 0)
    normed_vals = normed_moe.astype(jnp.float32)
    vectors = const_vectors.astype(jnp.float32)
    gate_mats = const_gates.astype(jnp.float32)
    const_count = vectors.shape[0]
    copy_share = jnp.sum(jnp.where(local_ids == NF + 1, local_gates, 0.0), axis=1)
    const_share = jnp.stack(
        [
            jnp.sum(jnp.where(local_ids == NF + 2 + index, local_gates, 0.0), axis=1)
            for index in range(const_count)
        ],
        axis=1,
    )
    mixing = jax.nn.softmax(
        jnp.einsum("gd,cjd->gcj", normed_vals, gate_mats, precision=highest), axis=-1
    )
    const_out = (
        mixing[:, :, 0:1] * normed_vals[:, None, :] + mixing[:, :, 1:2] * vectors[None, :, :]
    )
    others = copy_share[:, None] * normed_vals + jnp.sum(
        const_share[:, :, None] * const_out, axis=1
    )
    layer_out = (resid + ffn_out + others).astype(jnp.bfloat16)
    grad_out = out_grad.astype(jnp.float32)
    grad_moe_rows = lax.all_gather(out_grad, "tensor", axis=0, tiled=True)
    gate_back, down_back = (
        lax.all_gather(w_gate_up, "dp", axis=2, tiled=True),
        lax.all_gather(w_down, "dp", axis=2, tiled=True),
    )
    slot_grads = grad_moe_rows[slot_token].astype(jnp.float32)
    grad_expert = (slot_gate[:, None] * slot_grads).astype(jnp.bfloat16).reshape(NF, CAP, -1)
    slot_inner = jnp.sum(slot_grads * expert_out, axis=-1)
    gate_grad_ffn = jnp.where(retained, slot_inner[picker], 0.0)
    down_grad = jnp.einsum("ecf,ecd->efd", hidden, grad_expert, preferred_element_type=jnp.float32)
    grad_hidden = jnp.einsum(
        "ecd,efd->ecf", grad_expert, down_back, preferred_element_type=jnp.float32
    )
    slope = sigmoid_vals * (1.0 + gate_up[0] * (1.0 - sigmoid_vals))
    grad_gate_up = jnp.stack([grad_hidden * gate_up[1] * slope, grad_hidden * activated]).astype(
        jnp.bfloat16
    )
    gate_up_grad = jnp.einsum(
        "ecd,secf->sedf", expert_rows, grad_gate_up, preferred_element_type=jnp.float32
    )
    slot_input_grad = jnp.einsum(
        "secf,sedf->ecd", grad_gate_up, gate_back, preferred_element_type=jnp.float32
    ).reshape(NF * CAP, -1)
    grad_ffn_in = jnp.sum(jnp.where(retained[:, :, None], slot_input_grad[picker], 0.0), axis=1)
    gate_up_grad, down_grad = (
        lax.psum_scatter(gate_up_grad, "dp", scatter_dimension=2, tiled=True),
        lax.psum_scatter(down_grad, "dp", scatter_dimension=2, tiled=True),
    )
    grad_ffn_in, gate_grad_ffn = (
        lax.psum_scatter(grad_ffn_in, "tensor", scatter_dimension=0, tiled=True),
        lax.psum_scatter(gate_grad_ffn, "tensor", scatter_dimension=0, tiled=True),
    )
    copy_inner = jnp.sum(grad_out * normed_vals, axis=-1)
    const_inner = jnp.sum(grad_out[:, None, :] * const_out, axis=-1)
    choice_inner = jnp.where(local_ids == NF + 1, copy_inner[:, None], 0.0)
    for index in range(const_count):
        choice_inner = choice_inner + jnp.where(
            local_ids == NF + 2 + index, const_inner[:, index : index + 1], 0.0
        )
    gate_grad = gate_grad_ffn + choice_inner
    expert_range = jnp.arange(shares.shape[1])
    onehot = (local_ids[:, :, None] == expert_range[None, None, :]).astype(jnp.float32)
    grad_router = jnp.sum(onehot * gate_grad[:, :, None], axis=1)
    grad_logits = local_shares * (
        grad_router - jnp.sum(local_shares * grad_router, axis=-1, keepdims=True)
    )
    prior_vals = prior_logits.astype(jnp.float32)
    router_grad = jnp.dot(normed_vals.T, grad_logits, precision=highest)
    residual_grad = jnp.dot(prior_vals.T, grad_logits, precision=highest)
    prior_grad = jnp.dot(grad_logits, residual_weight.astype(jnp.float32).T, precision=highest)
    vector_inner = jnp.dot(grad_out, vectors.T, precision=highest)
    grad_mixing = const_share[:, :, None] * jnp.stack(
        [jnp.broadcast_to(copy_inner[:, None], vector_inner.shape), vector_inner], axis=-1
    )
    grad_blend = mixing * (grad_mixing - jnp.sum(mixing * grad_mixing, axis=-1, keepdims=True))
    const_gate_grad = jnp.einsum("gcj,gd->cjd", grad_blend, normed_vals, precision=highest)
    const_vector_grad = jnp.einsum(
        "gc,gd->cd", const_share * mixing[:, :, 1], grad_out, precision=highest
    )
    direct_share = copy_share + jnp.sum(const_share * mixing[:, :, 0], axis=1)
    grad_moe_in = (
        grad_ffn_in
        + jnp.dot(grad_logits, router_weight.astype(jnp.float32).T, precision=highest)
        + direct_share[:, None] * grad_out
        + jnp.einsum("gcj,cjd->gd", grad_blend, gate_mats, precision=highest)
    )
    norm_moe_grad = jnp.sum(grad_moe_in * resid * factor_moe, axis=0)
    grad_resid = grad_out + norm_back(grad_moe_in, resid, factor_moe, gain_moe)
    grad_mixed_out = grad_resid.astype(jnp.bfloat16)
    grad_attn_rows = lax.all_gather(grad_mixed_out, "tensor", axis=0, tiled=True)
    out_weight_grad = jnp.dot(mixed_rows.T, grad_attn_rows, preferred_element_type=jnp.float32)
    grad_mixed = jnp.dot(grad_attn_rows, out_full.T, preferred_element_type=jnp.float32).astype(
        jnp.bfloat16
    )
    grad_query, grad_keys, grad_values = lax.map(
        attend_back, (query, keys, values, piece_starts, log_total, grad_mixed.reshape(seq_shape))
    )
    grad_query = rotate(grad_query.reshape(group_rows, head_count, HD), cosine, -sine).reshape(
        group_rows, -1
    )
    grad_keys = rotate(grad_keys.reshape(group_rows, head_count, HD), cosine, -sine).reshape(
        group_rows, -1
    )
    grad_proj = jnp.stack([grad_query, grad_keys, grad_values.reshape(group_rows, -1)]).astype(
        jnp.bfloat16
    )
    qkv_grad = jnp.einsum("gd,cge->cde", attn_rows, grad_proj, preferred_element_type=jnp.float32)
    qkv_grad, out_weight_grad = (
        lax.psum_scatter(qkv_grad, "dp", scatter_dimension=1, tiled=True),
        lax.psum_scatter(out_weight_grad, "dp", scatter_dimension=1, tiled=True),
    )
    grad_attn_part = jnp.einsum(
        "cge,cde->gd", grad_proj, qkv_full, preferred_element_type=jnp.float32
    )
    grad_attn_in = lax.psum_scatter(
        grad_attn_part.astype(jnp.bfloat16), "tensor", scatter_dimension=0, tiled=True
    ).astype(jnp.float32)
    norm_attn_grad = jnp.sum(grad_attn_in * tok_vals * factor_attn, axis=0)
    input_grad = grad_resid + norm_back(grad_attn_in, tok_vals, factor_attn, gain_attn)
    summed = lax.psum(
        (
            norm_attn_grad,
            norm_moe_grad,
            router_grad,
            residual_grad,
            const_vector_grad,
            const_gate_grad,
        ),
        ("dp", "tensor"),
    )
    return (
        layer_out,
        input_grad,
        prior_grad,
        summed[0],
        qkv_grad,
        out_weight_grad,
        summed[1],
        summed[2],
        summed[3],
        summed[4],
        summed[5],
        gate_up_grad,
        down_grad,
    )


def on_device(
    dp,
    tensor,
    tokens,
    prior_logits,
    expert_ids,
    expert_ranks,
    piece_starts,
    norm_attn,
    qkv_weight,
    out_weight,
    norm_moe,
    router_weight,
    residual_weight,
    const_vectors,
    const_gates,
    w_gate_up,
    w_down,
    out_grad,
):
    rows, d = tokens.shape
    ne = router_weight.shape[1]
    packs = dp // NF
    groups = None if packs == 1 else [list(range(NF * r, NF * (r + 1))) for r in range(packs)]
    across = None if packs == 1 else [list(range(j, dp, NF)) for j in range(NF)]
    ids, ranks = expert_ids.T, expert_ranks.T
    cosine, sine = (jnp.asarray(t) for t in rotary_tables())
    prior = jnp.pad(prior_logits.T, ((0, 16 - ne), (0, 0)))
    zeros = lambda n: jnp.zeros((n, d), bf16)
    params = jnp.concatenate(
        [
            router_weight.T, zeros(Z0 - ne), const_gates.reshape(2 * NC, d), zeros(8 - 2 * NC), norm_attn[None],
            norm_moe[None], const_vectors, zeros(6 - NC), jnp.pad(residual_weight, ((0, 16 - ne), (0, d - ne))),
        ],
        axis=0,
    )

    w_down_t = w_down.transpose(0, 2, 1)[None]
    shard = w_down.shape[1]
    w_first, zq, zo = prologue(w_gate_up, w_down_t, qkv_weight, out_weight, tensor, 1)
    w_full, w_second, pos, count, ys, slab = gather_weights(
        zq, zo, w_gate_up, w_down_t, ids, ranks, out_grad, packs == 1, 2
    )
    w_attn = lax.all_gather(slab, "dp", axis=1, tiled=True) if packs > 1 else w_full

    def whole(w):
        w = w.reshape(3, -1, w.shape[3])
        if packs > 1:
            w = lax.all_gather(w, "dp", axis=1, tiled=True, axis_index_groups=across)
        return lax.all_gather(w, "tensor", axis=0, tiled=False)

    w_first, w_second = whole(w_first), whole(w_second)

    heads = 16
    blocks = shape((NF, ROOM, d), bf16)
    q, k, v, mixed, lse, nattn, resid, nmoe, base, aux, x_b, y_b, pay = pl.pallas_call(
        fwd_kernel,
        in_specs=[SM] + [VM] * 9 + [ANY],
        out_specs=[VM] * 10 + [ANY] * 3,
        out_shape=(
            shape((rows, d), bf16), shape((rows, d), bf16), shape((rows, d), bf16), shape((rows, d), bf16),
            shape((heads, rows), f32), shape((rows, d), bf16), shape((rows, d), f32), shape((rows, d), bf16),
            shape((rows, d), f32), shape((rows, LANES), f32), blocks, blocks, shape((2 * NF, 1, ROOM), f32),
        ),
        scratch_shapes=[
            pltpu.VMEM((QT, 2 * QT), f32),
            pltpu.VMEM((NF, 1, rows), f32),
            pltpu.VMEM((NF, ROOM, d), bf16),
            pltpu.VMEM((2 * NF, 1, ROOM), f32),
            pltpu.VMEM((LANES, d), bf16),
            *send_scratch(),
            *send_scratch(),
            pltpu.SemaphoreType.DMA((2, 2 * (NF - 1))),
            pltpu.SemaphoreType.DMA((2,)),
        ],
        compiler_params=pltpu.CompilerParams(collective_id=3, has_side_effects=True, vmem_limit_bytes=60 << 20),
        cost_estimate=cost(40, 30, 10),
    )(piece_starts, tokens, prior, ids, ranks, params, cosine, sine, w_attn, pos, ys)

    xc, yc, gc, eo, dx, dw_a, meta = experts_first(pay, x_b, y_b, w_first)
    out_b, dx_b, gg_b, dw_b = experts_second(meta, xc, yc, gc, eo, dx, w_second)

    def owned(dw):
        dw = lax.psum_scatter(dw, "tensor", scatter_dimension=0, tiled=False)
        if packs > 1:
            dw = lax.psum_scatter(dw, "dp", scatter_dimension=1, tiled=True, axis_index_groups=across)
        return dw.reshape(3, NF, -1, dw.shape[-1])

    dw_a = owned(dw_a)

    gmo, gres, pgrad, small = pl.pallas_call(
        mid_kernel,
        in_specs=[ANY] * 6 + [VM] * 4,
        out_specs=[VM] * 4,
        out_shape=(shape((rows, d), bf16), shape((rows, d), f32), shape((16, rows), f32), shape((32, d), f32)),
        scratch_shapes=[
            pltpu.VMEM((NF, ROOM, d), bf16),
            pltpu.VMEM((NF, 1, ROOM), f32),
            pltpu.VMEM((rows, d), f32),
            pltpu.VMEM((NF, rows), f32),
            pltpu.VMEM((rows, LANES), f32),
            pltpu.VMEM((rows, LANES), f32),
            pltpu.VMEM((LANES, d), bf16),
            pltpu.VMEM((16, LANES), f32),
            pltpu.VMEM((rows, d), bf16),
            pltpu.VMEM((rows, d), bf16),
            pltpu.VMEM((rows, d), f32),
            pltpu.VMEM((rows, LANES), f32),
            pltpu.SemaphoreType.DMA((4,)),
            *send_scratch(),
            pltpu.SemaphoreType.DMA((2, NF - 1)),
            pltpu.SemaphoreType.DMA((1,)),
        ],
        compiler_params=pltpu.CompilerParams(collective_id=4, has_side_effects=True, vmem_limit_bytes=60 << 20),
        cost_estimate=cost(4, 4),
    )(dx_b, gg_b, out_grad, nmoe, resid, aux, pos, prior, params, count)
    dw_a, dw_b, gmo = lax.optimization_barrier((dw_a, dw_b, gmo))
    dw_b = owned(dw_b)
    wg, gp, yr, small, dw_a = pl.pallas_call(
        bwd_kernel,
        in_specs=[SM, VM, VM, ANY, ANY, ANY, VM] + [ANY] * 4 + [VM, ANY, ANY],
        out_specs=[VM] * 2 + [ANY, VM, ANY],
        out_shape=(shape((4, d, d), bf16), shape((3, rows, d), bf16), blocks, shape((32, d), f32), shape(dw_a.shape, bf16)),
        scratch_shapes=[
            pltpu.VMEM((rows, d), bf16),
            pltpu.VMEM((heads, rows), f32),
            pltpu.VMEM((rows // QT, 2 * QT, QT), f32),
            pltpu.VMEM((rows, LANES), f32),
            pltpu.VMEM((rows, LANES), f32),
            pltpu.VMEM((rows, LANES), f32),
            pltpu.VMEM((1, d, d), bf16),
            pltpu.SemaphoreType.DMA,
            *[pltpu.VMEM((rows, d), bf16)] * 3,
            pltpu.VMEM((rows, d), bf16),
            *[pltpu.VMEM((rows, LANES), f32)] * 2,
            pltpu.SemaphoreType.DMA((6,)),
            *send_scratch(),
            *near_scratch((32, d)),
            *exchange_scratch(1),
        ],
        compiler_params=pltpu.CompilerParams(collective_id=5, has_side_effects=True, vmem_limit_bytes=60 << 20),
        cost_estimate=cost(8, 4),
    )(piece_starts, gmo, mixed, q, k, v, lse, nattn, cosine, sine, w_attn, small, out_b, dw_a)
    alone = packs == 1
    zs, igrad, layer_out, small, nag = finish(
        wg, gp, gres, tokens, w_attn, yr, base, pos, params, small, tensor, alone, 6
    )
    if alone:
        wg, nag, dw_b = last(zs, nag, dw_b, tensor, 7)
    else:
        wg = lax.psum_scatter(wg, "dp", scatter_dimension=1, tiled=True)
        wg = lax.psum_scatter(wg, "tensor", scatter_dimension=2, tiled=True).astype(f32)
        nag = lax.psum(nag, ("dp", "tensor"))
        small = lax.psum(lax.psum(small, "tensor"), "dp", axis_index_groups=across)
        dw_b = exchange8(dw_b, 7)
    overflow = jnp.sum(small[28:29, 0:LANES]) > 0

    def roomy(args):
        return plain_on_device(*args)

    def packed(args):
        gate_up, down, qkv, wo, router, residual, vectors, blends, gain_attn, gain_moe = emit(dw_a, dw_b, wg, small, nag, ne)
        return (
            layer_out,
            igrad,
            pgrad[0:ne].T,
            gain_attn,
            qkv,
            wo,
            gain_moe,
            router.T,
            residual,
            vectors,
            blends,
            gate_up,
            down.transpose(0, 2, 1),
        )

    args = (
        tokens, prior_logits, expert_ids, expert_ranks, piece_starts, norm_attn, qkv_weight, out_weight, norm_moe,
        router_weight, residual_weight, const_vectors, const_gates, w_gate_up, w_down, out_grad,
    )
    return lax.cond(overflow, roomy, packed, args)


def solution(mesh):
    body = functools.partial(on_device, mesh.shape["dp"], mesh.shape["tensor"])
    rows = P(("dp", "tensor"), None)
    return jax.shard_map(
        body,
        mesh=mesh,
        in_specs=(
            rows, rows, P("dp", None), P("dp", None), P("dp", None), P(), P(None, "dp", "tensor"), P("tensor", "dp"),
            P(), P(), P(), P(), P(), P(None, None, "dp", "tensor"), P(None, "tensor", "dp"), rows,
        ),
        out_specs=(
            rows, rows, rows, P(), P(None, "dp", "tensor"), P("tensor", "dp"), P(), P(), P(), P(), P(),
            P(None, None, "dp", "tensor"), P(None, "tensor", "dp"),
        ),
        check_vma=False,
    )
```

```python
import functools

import jax
import jax.numpy as jnp
import numpy as np
from jax import lax
from jax.experimental import pallas as pl
from jax.experimental.pallas import tpu as pltpu
from jax.sharding import PartitionSpec as P

HD = 64
NF = 8
NC = 2
SEQ = 1024
PIECE = 256
PIECES = 2
CAP = 768
EPS = 1e-06
QT = 256
LANES = 128
TM = 256
ROOM = 256
Z0 = 16
CHOSEN = 32
RES = 6

bf16 = jnp.bfloat16
f32 = jnp.float32
i32 = jnp.int32

VM = pl.BlockSpec(memory_space=pltpu.VMEM)
SM = pl.BlockSpec(memory_space=pltpu.SMEM)
ANY = pl.BlockSpec(memory_space=pl.ANY)


def nn(a, b):
    return lax.dot_general(a, b, (((1,), (0,)), ((), ())), preferred_element_type=f32)


def nt(a, b):
    return lax.dot_general(a, b, (((1,), (1,)), ((), ())), preferred_element_type=f32)


def tn(a, b):
    return lax.dot_general(a, b, (((0,), (0,)), ((), ())), preferred_element_type=f32)


def split(x):
    hi = x.astype(bf16)
    return hi, (x - hi.astype(f32)).astype(bf16)


def lanes(rows):
    return lax.broadcasted_iota(i32, (rows, LANES), 1)


def rot(x, cosine, sine):
    first = lanes(x.shape[0]) % HD < HD // 2
    other = jnp.where(first, pltpu.roll(x, LANES - HD // 2, 1), pltpu.roll(x, HD // 2, 1))
    return x * cosine + other * sine


def head_masks():
    low = lax.broadcasted_iota(i32, (1, LANES), 1) < HD
    a = jnp.where(low, 1.0, 0.0)
    return a, 1.0 - a


def rotary_tables():
    place = np.arange(SEQ, dtype=np.float32)
    half = HD // 2
    freqs = np.power(np.float32(10000.0), np.arange(half, dtype=np.float32) * np.float32(-2.0 / HD)).astype(np.float32)
    angles = (place[:, None] * freqs[None, :]).astype(np.float32).astype(np.float64)
    c, s = np.cos(angles).astype(np.float32), np.sin(angles).astype(np.float32)
    return np.concatenate([c, c, c, c], 1), np.concatenate([-s, s, -s, s], 1)


def window_bias(starts_ref, tile, width, transposed):
    shape = (width, QT) if transposed else (QT, width)
    qpos = lax.broadcasted_iota(i32, shape, 1 if transposed else 0) + tile * QT
    kpos = lax.broadcasted_iota(i32, shape, 0 if transposed else 1) + tile * QT
    seen = jnp.where(kpos <= qpos, 1, 0)
    for piece in range(PIECES):
        s = starts_ref[lax.axis_index("tensor"), piece]
        both = jnp.where(qpos >= s, 1, 0) * jnp.where(qpos < s + PIECE, 1, 0)
        both = both * jnp.where(kpos >= s, 1, 0) * jnp.where(kpos < s + PIECE, 1, 0)
        seen = jnp.maximum(seen, both)
    return jnp.where(seen > 0, 0.0, -1e30)


MESH = pl.DeviceIdType.MESH
GATHER_COPIES = 13
REDUCE_COPIES = 10


def flip(index, m):
    for bit in (1, 2, 4):
        if m & bit:
            index = index + bit - 2 * bit * (index // bit % 2)
    return index


def remote(src, dst, sems, n, axis, peer):
    return pltpu.make_async_remote_copy(
        src_ref=src,
        dst_ref=dst,
        send_sem=sems.at[0, n],
        recv_sem=sems.at[1, n],
        device_id={axis: peer},
        device_id_type=MESH,
    )


def greet(peers):
    barrier = pltpu.get_barrier_semaphore()
    for axis, peer in peers:
        pl.semaphore_signal(barrier, inc=1, device_id={axis: peer}, device_id_type=MESH)
    pl.semaphore_wait(barrier, len(peers))


def near_peers():
    me = lax.axis_index("dp")
    return [("dp", flip(me, m)) for m in (1, 2, 4)]


def far_peers(tensor):
    me = lax.axis_index("tensor")
    return [("tensor", (me + k) % tensor) for k in range(1, tensor)]


class Gather8:
    def __init__(self, src, dst, sems, own_sem):
        me = lax.axis_index("dp")
        slot = me % NF
        nx, ny, nc = flip(me, 2), flip(me, 4), flip(me, 1)
        sx, sy, sd = flip(slot, 2), flip(slot, 4), flip(slot, 6)
        self.own = pltpu.make_async_copy(src(None), dst(slot, None), own_sem)
        go = lambda n, s, d, peer: remote(s, d, sems, n, "dp", peer)
        on = lambda n, s, h, peer: go(n, dst(s, h), dst(s, h), peer)
        self.c = [
            go(0, src(0), dst(slot, 0), nx),
            go(1, src(1), dst(slot, 1), ny),
            go(2, src(1), dst(slot, 1), nx),
            go(3, src(0), dst(slot, 0), ny),
            go(4, src(None), dst(slot, None), nc),
            on(5, sx, 0, ny),
            on(6, sy, 1, nx),
            on(7, sx, 0, nc),
            on(8, sy, 1, nc),
            on(9, sx, 1, nc),
            on(10, sy, 0, nc),
            on(11, sd, 0, nc),
            on(12, sd, 1, nc),
        ]

    def begin(self):
        self.own.start()
        for n in range(5):
            self.c[n].start()

    def forward(self):
        for got, out in ((0, (5, 7)), (1, (6, 8))):
            self.c[got].wait_recv()
            for n in out:
                self.c[n].start()

    def share(self):
        for got, out in ((2, 9), (3, 10)):
            self.c[got].wait_recv()
            self.c[out].start()

    def last(self):
        for got, out in ((5, 11), (6, 12)):
            self.c[got].wait_recv()
            self.c[out].start()

    def end(self):
        for n in (4, 7, 8, 9, 10, 11, 12):
            self.c[n].wait_recv()
        for c in self.c:
            c.wait_send()
        self.own.wait()


def halves(ref, index, rows):
    half = rows // 2
    return lambda s, h: ref.at[s] if h is None else ref.at[s, pl.ds(h * half, half)]


def all_peers():
    me = lax.axis_index("dp")
    return [("dp", flip(me, m)) for m in range(1, NF)]


class Swap8:
    def __init__(self, src, dst, sems, own_sems):
        me = lax.axis_index("dp")
        slot = me % NF
        count = src.shape[0] // NF
        self.own = [
            pltpu.make_async_copy(src.at[NF * i + slot], dst.at[NF * i + slot], own_sems.at[i]) for i in range(count)
        ]
        self.c = [
            remote(
                src.at[NF * i + flip(slot, m)], dst.at[NF * i + slot], sems, (m - 1) * count + i, "dp", flip(me, m)
            )
            for m in range(1, NF)
            for i in range(count)
        ]

    def begin(self):
        for c in self.own + self.c:
            c.start()

    def end(self):
        for c in self.c:
            c.wait_recv()
        for c in self.c:
            c.wait_send()
        for c in self.own:
            c.wait()


def routes(ids_ref, ranks_ref, i):
    start = lax.axis_index("tensor") * SEQ + i * QT
    cols = pl.ds(pl.multiple_of(start, QT), QT)
    at = lax.broadcasted_iota(i32, (16, QT), 0)
    hit0, hit1 = (jnp.where(at == ids_ref[n : n + 1, cols], 1.0, 0.0) for n in range(2))
    keep0, keep1 = (jnp.where(ranks_ref[n : n + 1, cols] < CAP, 1.0, 0.0) for n in range(2))
    return hit0 + hit1, (hit0 * keep0 + hit1 * keep1) * jnp.where(at < NF, 1.0, 0.0)


def weights_kernel(
    gather, zq_ref, zo_ref, gu_ref, dn_ref, ids_ref, ranks_ref, og_ref, out_ref, wx_ref, pos_ref, count_ref, ys_ref, slab, sems,
    own_sem, *scratch,
):
    k, r, _ = slab.shape
    tensor, _, _, f = zq_ref.shape
    for t in range(0, tensor, 2):
        at = slice(t * f, (t + 2) * f)
        for c in range(k - 1):
            slab[c, :, at] = jnp.concatenate([zq_ref[n, c].astype(f32) for n in (t, t + 1)], axis=1).astype(bf16)
        both = jnp.concatenate([zo_ref[n].astype(f32) for n in (t, t + 1)], axis=0)
        wide = jnp.concatenate([both, jnp.zeros((2 * f, -r % LANES), f32)], axis=1)
        slab[k - 1, :, at] = wide.T[0:r, :].astype(bf16)
    greet(all_peers())
    part = lambda h: pl.ds(0, k) if h is None else pl.ds(h * (k // 2), k // 2)
    if gather:
        g = Gather8(
            lambda h: slab.at[part(h)],
            lambda s, h: out_ref.at[part(h), pl.ds(pl.multiple_of(s * r, r), r), :],
            sems,
            own_sem,
        )
        g.begin()
    swap = Exchange8([gu_ref, dn_ref], wx_ref, 1, *scratch)
    swap.begin()
    upper = jnp.where(
        lax.broadcasted_iota(i32, (QT, QT), 0) < lax.broadcasted_iota(i32, (QT, QT), 1), 1.0, 0.0
    ).astype(bf16)
    taken = jnp.zeros((16, 1), f32)
    for i in range(SEQ // QT):
        _, kept = routes(ids_ref, ranks_ref, i)
        pos = jnp.where(kept > 0, nn(kept.astype(bf16), upper) + taken, -1.0)
        pos_ref[:, 0, i * QT : (i + 1) * QT] = pos[0:NF, :]
        taken = taken + jnp.sum(kept, axis=1, keepdims=True)
    count_ref[...] = jnp.broadcast_to(taken, (16, LANES))
    slot = lax.axis_index("dp") % NF

    def pack(*blocks):
        for m in blocks:
            ys_ref[m] = nn(hot_rows(pos_ref[flip(slot, m)]), og_ref[...]).astype(bf16)

    pack(0, 1)
    if gather:
        g.forward()
    pack(2, 3)
    if gather:
        g.share()
    pack(4, 5)
    if gather:
        g.last()
    pack(6, 7)
    if gather:
        g.end()
    swap.end()


def gather_weights(zq, zo, gate_up, down, ids, ranks, og, gather, cid):
    tensor, k, r, f = zq.shape
    k, f = k + 1, tensor * f
    return pl.pallas_call(
        functools.partial(weights_kernel, gather),
        in_specs=[VM] * 2 + [ANY] * 2 + [VM] * 3,
        out_specs=[ANY] * 2 + [VM] * 4,
        out_shape=(
            shape((k, NF * r, f), bf16), half_shape(gate_up), shape((NF, 1, og.shape[0]), f32),
            shape((16, LANES), f32), shape((NF, ROOM, og.shape[1]), bf16),
            shape((k, r, f), bf16),
        ),
        scratch_shapes=[
            pltpu.SemaphoreType.DMA((2, GATHER_COPIES)),
            pltpu.SemaphoreType.DMA,
            *exchange_scratch(2),
        ],
        compiler_params=pltpu.CompilerParams(collective_id=cid, has_side_effects=True, vmem_limit_bytes=60 << 20),
        cost_estimate=cost(35, 10),
    )(zq, zo, gate_up, down, ids, ranks, og)


class Reduce8:
    def __init__(self, view, bufs, sems, lsems):
        self.own, self.away, self.ind, self.inx, self.iny = bufs
        me = lax.axis_index("dp")
        slot = me % NF
        half = self.ind.shape[0] // 2
        a, b = pl.ds(0, half), pl.ds(half, half)
        self.a, self.b = a, b
        nx, ny, nc = flip(me, 2), flip(me, 4), flip(me, 1)
        mine = [flip(slot, m) for m in (6, 2, 4)] + [slot]
        self.loads = [pltpu.make_async_copy(view(s), self.own.at[n % 2], lsems.at[n]) for n, s in enumerate(mine)]
        self.over = [remote(view(flip(s, 1)), self.away.at[n], sems, n, "dp", nc) for n, s in enumerate(mine)]
        go = lambda n, k, i, part, peer: remote(self.away.at[k, part], i.at[part], sems, n, "dp", peer)
        self.da, self.db = go(4, 0, self.ind, a, nx), go(5, 0, self.ind, b, ny)
        self.xa, self.yb = go(6, 1, self.inx, a, nx), go(7, 2, self.iny, b, ny)
        self.ya, self.xb = go(8, 2, self.iny, a, ny), go(9, 1, self.inx, b, nx)

    def load(self):
        self.loads[0].start()
        self.loads[1].start()

    def begin(self):
        for c in self.over:
            c.start()

    def add(self, n, part):
        self.away[n, part] = (self.own[n % 2, part].astype(f32) + self.away[n, part].astype(f32)).astype(bf16)

    def more(self, n, part):
        self.away[n, part] = (self.away[n, part].astype(f32) + self.ind[part].astype(f32)).astype(bf16)

    def ready(self, n):
        self.loads[n].wait()
        self.over[n].wait_recv()

    def first(self):
        self.ready(0)
        self.add(0, self.a)
        self.da.start()
        self.add(0, self.b)
        self.db.start()
        self.loads[2].start()

    def second(self):
        self.ready(1)
        self.add(1, self.a)
        self.xa.start()
        self.add(1, self.b)
        self.loads[3].start()
        self.ready(2)
        self.add(2, self.b)
        self.yb.start()
        self.add(2, self.a)

    def third(self):
        self.da.wait_recv()
        self.more(2, self.a)
        self.ya.start()
        self.db.wait_recv()
        self.more(1, self.b)
        self.xb.start()

    def end(self, write):
        self.ready(3)
        for part, first, second in ((self.a, self.xa, self.ya), (self.b, self.yb, self.xb)):
            first.wait_recv()
            second.wait_recv()
            total = self.own[1, part].astype(f32) + self.away[3, part].astype(f32)
            write(part, total + self.inx[part].astype(f32) + self.iny[part].astype(f32))

    def close(self):
        for c in self.over + [self.da, self.db, self.xa, self.yb, self.ya, self.xb]:
            c.wait_send()


def reduce_scratch(block):
    return [pltpu.VMEM((2, *block), bf16), pltpu.VMEM((4, *block), bf16)] + [pltpu.VMEM(block, bf16)] * 3 + [
        pltpu.SemaphoreType.DMA((2, REDUCE_COPIES)),
        pltpu.SemaphoreType.DMA((4,)),
    ]


class Exchange8:
    def __init__(self, srcs, dst, part, sems, own_sems):
        me = lax.axis_index("dp")
        slot = me % NF
        width = dst.shape[-1]

        def piece(src, e):
            return src.at[:, e] if part is None else src.at[:, e, :, pl.ds(part * width, width)]

        at, pieces = 0, []
        for src in srcs:
            pieces.append((src, pl.ds(at, src.shape[0])))
            at += src.shape[0]
        self.own = [
            pltpu.make_async_copy(piece(src, slot), dst.at[rows, slot], own_sems.at[i])
            for i, (src, rows) in enumerate(pieces)
        ]
        self.c = [
            remote(
                piece(src, flip(slot, m)), dst.at[rows, slot], sems, (m - 1) * len(srcs) + i, "dp", flip(me, m)
            )
            for m in (6, 7, 2, 3, 4, 5, 1)
            for i, (src, rows) in enumerate(pieces)
        ]

    def begin(self):
        for c in self.c + self.own:
            c.start()

    def end(self):
        for c in self.c:
            c.wait_recv()
        for c in self.c:
            c.wait_send()
        for c in self.own:
            c.wait()


class Send8:
    order = (6, 7, 2, 3, 4, 5, 1)

    def __init__(self, src, dst, sems, own_sem, packed):
        me = lax.axis_index("dp")
        slot = me % NF
        at = lambda m: src.at[m] if packed else src.at[flip(slot, m)]
        self.slot = slot
        self.own = pltpu.make_async_copy(at(0), dst.at[slot], own_sem)
        self.c = {m: remote(at(m), dst.at[slot], sems, m - 1, "dp", flip(me, m)) for m in self.order}

    def start(self, m):
        (self.c[m] if m else self.own).start()

    def begin(self):
        for m in (*self.order, 0):
            self.start(m)

    def got(self, m):
        if m:
            self.c[m].wait_recv()
        else:
            self.own.wait()

    def close(self):
        for c in self.c.values():
            c.wait_send()


def send_scratch():
    return [pltpu.SemaphoreType.DMA((2, NF - 1)), pltpu.SemaphoreType.DMA]


def half_shape(gate_up):
    _, groups, r, f = gate_up.shape
    return shape((3, groups, r, f // 2), bf16)


def exchange_scratch(n):
    return [pltpu.SemaphoreType.DMA((2, (NF - 1) * n)), pltpu.SemaphoreType.DMA((n,))]


def prologue_kernel(tensor, gu_ref, dn_ref, w_ref, wo_ref, out_ref, zq_ref, zo_ref, zsems, own_sems, *scratch):
    here = lax.axis_index("tensor")
    pairs = ((w_ref, zq_ref.at[here]), (wo_ref, zo_ref.at[here]))
    own = [pltpu.make_async_copy(src, dst, own_sems.at[i]) for i, (src, dst) in enumerate(pairs)]
    for c in own:
        c.start()
    greet(all_peers() + far_peers(tensor))
    copies = [
        remote(src, dst, zsems, 2 * n + i, axis, peer)
        for n, (axis, peer) in enumerate(far_peers(tensor))
        for i, (src, dst) in enumerate(pairs)
    ]
    for c in copies:
        c.start()
    swap = Exchange8([gu_ref, dn_ref], out_ref, 0, *scratch)
    swap.begin()
    for c in copies:
        c.wait_recv()
    swap.end()
    for c in copies:
        c.wait_send()
    for c in own:
        c.wait()


def prologue(gate_up, down, w, wo, tensor, cid):
    return pl.pallas_call(
        functools.partial(prologue_kernel, tensor),
        in_specs=[ANY] * 4,
        out_specs=[ANY] * 3,
        out_shape=(half_shape(gate_up), shape((tensor, *w.shape), bf16), shape((tensor, *wo.shape), bf16)),
        scratch_shapes=[
            pltpu.SemaphoreType.DMA((2, 2 * (tensor - 1))),
            pltpu.SemaphoreType.DMA((2,)),
            *exchange_scratch(2),
        ],
        compiler_params=pltpu.CompilerParams(collective_id=cid, has_side_effects=True, vmem_limit_bytes=60 << 20),
        cost_estimate=cost(25, 10),
    )(gate_up, down, w, wo)


def exchange_kernel(src, dst, *scratch):
    greet(all_peers())
    swap = Exchange8([src], dst, None, *scratch)
    swap.begin()
    swap.end()


def exchange8(x, cid):
    return pl.pallas_call(
        exchange_kernel,
        in_specs=[ANY],
        out_specs=ANY,
        out_shape=shape(x.shape, x.dtype),
        scratch_shapes=exchange_scratch(1),
        compiler_params=pltpu.CompilerParams(collective_id=cid, has_side_effects=True),
        cost_estimate=cost(18, 10),
    )(x)


class Near:
    def __init__(self, have, got, sems):
        me = lax.axis_index("dp")
        self.slot = me % NF
        self.have, self.got = have, got
        self.c = [
            remote(have, got.at[self.slot], sems, m - 1, "dp", flip(me, m)) for m in (6, 7, 2, 3, 4, 5, 1)
        ]

    def begin(self, value):
        self.have[...] = value.astype(bf16)
        for c in self.c:
            c.start()
        self.got[self.slot] = self.have[...]

    def end(self):
        for c in self.c:
            c.wait_recv()
        total = self.got[0].astype(f32)
        for n in range(1, NF):
            total = total + self.got[n].astype(f32)
        for c in self.c:
            c.wait_send()
        return total


def near_scratch(dims):
    return [pltpu.VMEM(dims, bf16), pltpu.VMEM((NF, *dims), bf16), pltpu.SemaphoreType.DMA((2, NF - 1))]


class Far:
    def __init__(self, tensor, value, have, got, sems):
        self.tensor, self.value, self.have, self.got, self.here = tensor, value, have, got, lax.axis_index("tensor")
        self.c = [
            remote(have, got.at[self.here], sems, n, axis, peer) for n, (axis, peer) in enumerate(far_peers(tensor))
        ]

    def begin(self):
        self.have[...] = self.value[...].astype(bf16)
        for c in self.c:
            c.start()
        self.got[self.here] = self.have[...]

    def end(self):
        for c in self.c:
            c.wait_recv()
        total = self.got[0].astype(f32)
        for t in range(1, self.tensor):
            total = total + self.got[t].astype(f32)
        for c in self.c:
            c.wait_send()
        return total


def far_scratch(tensor, dims):
    return [pltpu.VMEM(dims, bf16), pltpu.VMEM((tensor, *dims), bf16), pltpu.SemaphoreType.DMA((2, tensor - 1))]


def final_kernel(
    tensor, comm, g_ref, gp_any, gres_any, tok_any, w_any, yr_any, base_any, pos_ref, par_ref, small_ref,
    zs_ref, igrad_ref, layer_ref, total_ref, nag_ref,
    gp_ref, gres_ref, tok_ref, w_ref, yr_ref, base_ref, lsems, *scratch,
):
    k, d, _ = g_ref.shape
    ntile = SEQ // QT
    pairs = (
        (gp_any, gp_ref), (w_any.at[pl.ds(0, 3)], w_ref), (tok_any, tok_ref), (gres_any, gres_ref), (yr_any, yr_ref),
        (base_any, base_ref),
    )
    loads = [pltpu.make_async_copy(src, dst, lsems.at[n]) for n, (src, dst) in enumerate(pairs)]
    if comm:
        r, f = zs_ref.shape[2:]
        red = Reduce8(lambda s: g_ref.at[:, pl.ds(pl.multiple_of(s * r, r), r), :], scratch[:5], *scratch[5:7])
        sums, smalls = Near(*scratch[7:10]), Far(tensor, small_ref, *scratch[10:13])
        red.load()
        greet(all_peers() + far_peers(tensor))
        red.begin()
        smalls.begin()
    for c in loads:
        c.start()
    ga = par_ref[24:25, :].astype(f32)
    if comm:
        red.first()
        red.second()
    for c in loads[:4]:
        c.wait()
    nag = jnp.zeros((1, d), f32)
    for i in range(ntile):
        rows = pl.ds(i * QT, QT)
        gai = nt(gp_ref[0, rows, :], w_ref[0]) + nt(gp_ref[1, rows, :], w_ref[1])
        gai = gai + nt(gp_ref[2, rows, :], w_ref[2])
        x = tok_ref[rows, :].astype(f32)
        r1 = lax.rsqrt(jnp.mean(x * x, axis=-1, keepdims=True) + EPS)
        nag = nag + jnp.sum(gai * x * r1, axis=0, keepdims=True)
        scaled = gai * ga
        avg = jnp.mean(scaled * x, axis=-1, keepdims=True)
        igrad_ref[rows, :] = gres_ref[rows, :] + r1 * scaled - x * (r1 * r1 * r1 * avg)
        if comm and i == 0:
            red.third()
    if comm:
        sums.begin(nag)
    else:
        nag_ref[...] = nag
        total_ref[...] = small_ref[...]
    for c in loads[4:]:
        c.wait()

    def layer(i):
        rows = pl.ds(i * QT, QT)
        total = base_ref[rows, :]
        for e in range(NF):
            total = total + tn(hot_rows(pos_ref[e, :, rows]), yr_ref[e])
        layer_ref[rows, :] = total.astype(bf16)

    def write(part, total):
        for t in range(tensor):
            zs_ref[t, part] = total[:, :, t * f : (t + 1) * f].astype(bf16)

    for i in range(ntile):
        layer(i)
    if not comm:
        return
    nag_ref[...] = sums.end()
    red.end(write)
    total_ref[...] = smalls.end()
    red.close()


def last_kernel(tensor, zs_ref, small_ref, dw_ref, out_ref, total_ref, dwx_ref, zr, zsems, *scratch):
    here = lax.axis_index("tensor")
    smalls = Far(tensor, small_ref, *scratch[0:3])
    swap = Exchange8([dw_ref], dwx_ref, None, *scratch[3:5])
    greet(all_peers() + far_peers(tensor))
    copies = [
        remote(zs_ref.at[peer], zr.at[here], zsems, n, axis, peer) for n, (axis, peer) in enumerate(far_peers(tensor))
    ]
    for c in copies:
        c.start()
    smalls.begin()
    swap.begin()
    zr[here] = zs_ref[here]
    for c in copies:
        c.wait_recv()
    total = zr[0].astype(f32)
    for t in range(1, tensor):
        total = total + zr[t].astype(f32)
    out_ref[...] = total
    total_ref[...] = smalls.end()
    for c in copies:
        c.wait_send()
    swap.end()


def last(zs, small, dw, tensor, cid):
    return pl.pallas_call(
        functools.partial(last_kernel, tensor),
        in_specs=[VM] * 2 + [ANY],
        out_specs=[VM] * 2 + [ANY],
        out_shape=(shape(zs.shape[1:], f32), shape(small.shape, f32), shape(dw.shape, dw.dtype)),
        scratch_shapes=[
            pltpu.VMEM(zs.shape, bf16),
            pltpu.SemaphoreType.DMA((2, tensor - 1)),
            *far_scratch(tensor, small.shape),
            *exchange_scratch(1),
        ],
        compiler_params=pltpu.CompilerParams(collective_id=cid, has_side_effects=True, vmem_limit_bytes=60 << 20),
        cost_estimate=cost(18, 10),
    )(zs, small, dw)


def finish(g, gp, gres, tokens, w, yr, base, pos, params, small, tensor, comm, cid):
    k, d, columns = g.shape
    rows = tokens.shape[0]
    r, f = (d // NF if comm else 8), columns // tensor
    once = pltpu.CompilerParams(vmem_limit_bytes=60 << 20)
    if comm:
        once = pltpu.CompilerParams(collective_id=cid, has_side_effects=True, vmem_limit_bytes=60 << 20)
    return pl.pallas_call(
        functools.partial(final_kernel, tensor, comm),
        in_specs=[ANY] * 7 + [VM] * 3,
        out_specs=[VM] * 5,
        out_shape=(
            shape((tensor, k, r, f), bf16), shape((rows, d), f32), shape((rows, d), bf16), shape(small.shape, f32),
            shape((1, d), f32),
        ),
        scratch_shapes=[
            pltpu.VMEM(gp.shape, bf16),
            pltpu.VMEM((rows, d), f32),
            pltpu.VMEM((rows, d), bf16),
            pltpu.VMEM((3, d, columns), bf16),
            pltpu.VMEM(yr.shape, bf16),
            pltpu.VMEM((rows, d), f32),
            pltpu.SemaphoreType.DMA((6,)),
            *reduce_scratch((k, r, columns)),
            *near_scratch((1, d)),
            *far_scratch(tensor, small.shape),
        ],
        compiler_params=once,
        cost_estimate=cost(8, 4),
    )(g, gp, gres, tokens, w, yr, base, pos, params, small)


def fwd_kernel(
    starts_ref, tok_ref, prior_ref, ids_ref, ranks_ref, par_ref, cos_ref, sin_ref, w_ref, pos_ref, ys,
    q_ref, k_ref, v_ref, mixed_ref, lse_ref, nattn_ref, resid_ref, nmoe_ref, base_ref, aux_ref, xr_ref, yr_ref, payr_ref,
    bias_ref, gate_ref, xs, pay, wr_ref, *scratch,
):
    greet(all_peers())
    send_x, send_y = Send8(xs, xr_ref, *scratch[0:2], True), Send8(ys, yr_ref, *scratch[2:4], True)
    swap = Swap8(pay, payr_ref, *scratch[4:6])
    send_y.begin()
    lane = lanes(QT)
    router_rows(par_ref, wr_ref)
    wres = par_ref[32:48, 0:LANES]
    d = tok_ref.shape[1]
    pairs = d // LANES
    ntile = SEQ // QT
    ga, gm = par_ref[24:25, :].astype(f32), par_ref[25:26, :].astype(f32)
    cv = par_ref[26:28, :].astype(f32)
    mask_a, mask_b = head_masks()
    mask16 = (mask_a.astype(bf16), mask_b.astype(bf16))

    def project(i, carry):
        rows = pl.ds(pl.multiple_of(i * QT, QT), QT)
        x = tok_ref[rows, :].astype(f32)
        r1 = lax.rsqrt(jnp.mean(x * x, axis=-1, keepdims=True) + EPS)
        n = (x * r1 * ga).astype(bf16)
        nattn_ref[rows, :] = n
        cosine, sine = cos_ref[rows, :], sin_ref[rows, :]
        for c, out in ((0, q_ref), (1, k_ref), (2, v_ref)):
            proj = nn(n, w_ref[c])
            for p in range(pairs):
                part = proj[:, p * LANES : (p + 1) * LANES]
                if c < 2:
                    part = rot(part, cosine, sine)
                part = part.astype(bf16)
                if c == 0:
                    part = part * jnp.array(HD**-0.5, bf16)
                out[rows, p * LANES : (p + 1) * LANES] = part
        return carry

    lax.fori_loop(0, ntile, project, 0)

    for i in range(ntile):
        lo = i * QT
        width = min(SEQ, lo + 2 * QT) - lo
        rows = pl.ds(lo, QT)
        bias_ref[:, :width] = window_bias(starts_ref, i, width, False)

        def pair(p, lse):
            cols = pl.ds(pl.multiple_of(p * LANES, LANES), LANES)
            q2 = q_ref[rows, cols]
            outs = []
            for h in range(2):
                qh = q2 * mask16[h]
                sb = nt(qh, k_ref[lo : lo + width, cols]) + bias_ref[:, :width]
                m = jnp.max(sb, axis=-1, keepdims=True)
                if lo:
                    sa = nt(qh, k_ref[0:lo, cols])
                    m = jnp.maximum(m, jnp.max(sa, axis=-1, keepdims=True))
                pb = jnp.exp(sb - m)
                total = jnp.sum(pb, axis=-1, keepdims=True)
                acc = nn(pb.astype(bf16), v_ref[lo : lo + width, cols])
                if lo:
                    pa = jnp.exp(sa - m)
                    total = total + jnp.sum(pa, axis=-1, keepdims=True)
                    acc = acc + nn(pa.astype(bf16), v_ref[0:lo, cols])
                outs.append(acc / total)
                lse = jnp.where(lane == 2 * p + h, m + jnp.log(total), lse)
            mixed_ref[rows, cols] = (outs[0] * mask_a + outs[1] * mask_b).astype(bf16)
            return lse

        lse = lax.fori_loop(0, pairs, pair, jnp.zeros((QT, LANES), f32))
        lse_ref[:, rows] = lse.T[0 : lse_ref.shape[0], :]

        x = tok_ref[rows, :].astype(f32)
        resid = x + nt(mixed_ref[rows, :], w_ref[3])
        resid_ref[rows, :] = resid
        r2 = lax.rsqrt(jnp.mean(resid * resid, axis=-1, keepdims=True) + EPS)
        nm = (resid * r2 * gm).astype(bf16)
        nmoe_ref[rows, :] = nm
        raw = nt(nm, wr_ref[...])
        logits = raw + tn(prior_ref[:, rows], wres)
        logits = jnp.where(lane < NF + 2 + NC, logits, -1e30)
        e = jnp.exp(logits - jnp.max(logits, axis=-1, keepdims=True))
        shares = e / jnp.sum(e, axis=-1, keepdims=True)
        chosen, kept = routes(ids_ref, ranks_ref, i)
        gate_ref[:, 0, rows] = shares.T[0:NF, :] * kept[0:NF, :]
        chosen = jnp.concatenate([chosen, jnp.zeros((LANES - 16, QT), f32)], axis=0).T
        gates = shares * chosen
        nv = nm.astype(f32)
        aux = jnp.where(lane < NF + 2 + NC, shares, 0.0) + pltpu.roll(chosen, CHOSEN, 1)
        direct = gates[:, NF + 1 : NF + 2]
        others = None
        for c in range(NC):
            z0, z1 = raw[:, Z0 + 2 * c : Z0 + 2 * c + 1], raw[:, Z0 + 2 * c + 1 : Z0 + 2 * c + 2]
            m0, m1 = 1.0 / (1.0 + jnp.exp(z1 - z0)), 1.0 / (1.0 + jnp.exp(z0 - z1))
            aux = jnp.where(lane == Z0 + 2 * c, m0, aux)
            aux = jnp.where(lane == Z0 + 2 * c + 1, m1, aux)
            w = gates[:, NF + 2 + c : NF + 3 + c]
            direct = direct + w * m0
            term = (w * m1) * cv[c : c + 1, :]
            others = term if others is None else others + term
        aux_ref[rows, :] = aux
        base_ref[rows, :] = resid + direct * nv + others

    for m in (*Send8.order, 0):
        e = flip(send_x.slot, m)
        place = pos_ref[e]
        hot = hot_rows(place)
        xs[m] = nn(hot, nmoe_ref[...]).astype(bf16)
        send_x.start(m)
        pay[e] = jnp.sum(nt(split_rows(gate_ref[e]), hot), axis=0, keepdims=True)
        filled = jnp.minimum(jnp.max(place, axis=1, keepdims=True) + 1.0, float(ROOM))
        pay[NF + e] = jnp.broadcast_to(filled, (1, ROOM))
    swap.begin()
    for send in (send_y, send_x):
        for m in (*Send8.order, 0):
            send.got(m)
        send.close()
    swap.end()


def mid_kernel(
    dxb_ref, ggb_ref, og_any, nmoe_any, resid_any, aux_any, pos_ref, prior_ref, par_ref, count_ref,
    gmo_ref, gres_ref, pgrad_ref, small_ref,
    dxr, ggr, dx_ref, gg_ref, inner_ref, extra_ref, wr_ref, resg_ref, og_ref, nmoe_ref, resid_ref, aux_ref, lsems, *scratch,
):
    pairs = ((og_any, og_ref), (nmoe_any, nmoe_ref), (resid_any, resid_ref), (aux_any, aux_ref))
    loads = [pltpu.make_async_copy(a, b, lsems.at[n]) for n, (a, b) in enumerate(pairs)]
    for c in loads:
        c.start()
    greet(all_peers())
    send, swap = Send8(dxb_ref, dxr, *scratch[0:2], False), Swap8(ggb_ref, ggr, *scratch[2:4])
    swap.begin()
    send.begin()
    gm, cv = par_ref[25:26, :].astype(f32), par_ref[26:28, :].astype(f32)
    wres = par_ref[32:48, 0:LANES]
    router_rows(par_ref, wr_ref)
    lane = lanes(QT)
    small_ref[...] = jnp.zeros_like(small_ref)
    resg_ref[...] = jnp.zeros_like(resg_ref)
    small_ref[28:29, 0:LANES] = jnp.max(jnp.where(count_ref[...] > ROOM, 1.0, 0.0), axis=0, keepdims=True)

    def ahead(i, carry):
        rows = pl.ds(pl.multiple_of(i * QT, QT), QT)
        g16 = og_ref[rows, :]
        g, nv = g16.astype(f32), nmoe_ref[rows, :].astype(f32)
        x = resid_ref[rows, :]
        aux = aux_ref[rows, :]
        chosen = jnp.where(lane < 16, pltpu.roll(aux, LANES - CHOSEN, 1), 0.0)
        gates = jnp.where(lane < NF + 2 + NC, aux, 0.0) * chosen
        copy_inner = jnp.sum(g * nv, axis=-1, keepdims=True)
        inner = jnp.where(lane == NF + 1, copy_inner, 0.0)
        direct = gates[:, NF + 1 : NF + 2]
        extra = jnp.where(lane == 1, lax.rsqrt(jnp.mean(x * x, axis=-1, keepdims=True) + EPS), 0.0)
        cvw = jnp.zeros((QT, LANES), f32)
        for c in range(NC):
            m0, m1 = aux[:, Z0 + 2 * c : Z0 + 2 * c + 1], aux[:, Z0 + 2 * c + 1 : Z0 + 2 * c + 2]
            v_inner = jnp.sum(g * cv[c : c + 1, :], axis=-1, keepdims=True)
            mean = m0 * copy_inner + m1 * v_inner
            inner = jnp.where(lane == NF + 2 + c, mean, inner)
            w = gates[:, NF + 2 + c : NF + 3 + c]
            direct = direct + w * m0
            extra = jnp.where(lane == Z0 + 2 * c, m0 * (w * copy_inner - w * mean), extra)
            extra = jnp.where(lane == Z0 + 2 * c + 1, m1 * (w * v_inner - w * mean), extra)
            cvw = jnp.where(lane == c, w * m1, cvw)
        inner_ref[rows, :] = inner
        extra_ref[rows, :] = jnp.where(lane == 0, direct, extra)
        cv_hi, cv_lo = split(cvw)
        small_ref[24:26, :] += tn(cv_hi, g16)[0:NC] + tn(cv_lo, g16)[0:NC]
        return carry

    for c in loads:
        c.wait()
    lax.fori_loop(0, SEQ // QT, ahead, 0)
    swap.end()
    for n, m in enumerate((0, 1, 2, 3, 4, 5, 6, 7)):
        send.got(m)
        e = flip(send.slot, m)
        hot = hot_rows(pos_ref[e])
        gg_ref[pl.ds(e, 1), :] = jnp.sum(nn(split_rows(ggr[e]), hot), axis=0, keepdims=True)
        part = tn(hot, dxr[e])
        if n:
            dx_ref[...] += part
        else:
            dx_ref[...] = part
    send.close()

    def tile(i, carry):
        rows = pl.ds(pl.multiple_of(i * QT, QT), QT)
        g, n16 = og_ref[rows, :].astype(f32), nmoe_ref[rows, :]
        x = resid_ref[rows, :]
        aux, extra = aux_ref[rows, :], extra_ref[rows, :]
        direct, r2 = extra[:, 0:1], extra[:, 1:2]
        shares = jnp.where(lane < NF + 2 + NC, aux, 0.0)
        chosen = jnp.where(lane < 16, pltpu.roll(aux, LANES - CHOSEN, 1), 0.0)
        inner = jnp.concatenate([gg_ref[:, rows], jnp.zeros((LANES - NF, QT), f32)], axis=0).T
        grad_router = (inner + inner_ref[rows, :]) * chosen
        glog = shares * (grad_router - jnp.sum(shares * grad_router, axis=-1, keepdims=True))
        both_hi, both_lo = split(glog + jnp.where(lane >= Z0, extra, 0.0))
        log_hi, log_lo = split(glog)
        pgrad_ref[:, rows] = nt(wres, log_hi) + nt(wres, log_lo)
        small_ref[0:24, :] += tn(both_hi, n16)[0:24] + tn(both_lo, n16)[0:24]
        resg_ref[...] += nn(prior_ref[:, rows], log_hi) + nn(prior_ref[:, rows], log_lo)
        gmi = dx_ref[rows, :] + direct * g + nn(both_hi, wr_ref[...]) + nn(both_lo, wr_ref[...])
        small_ref[26:27, :] += jnp.sum(gmi * x * r2, axis=0, keepdims=True)
        scaled = gmi * gm
        avg = jnp.mean(scaled * x, axis=-1, keepdims=True)
        gres = g + r2 * scaled - x * (r2 * r2 * r2 * avg)
        gres_ref[rows, :] = gres
        gmo_ref[rows, :] = gres.astype(bf16)
        return carry

    lax.fori_loop(0, SEQ // QT, tile, 0)
    for n in range(NF + 2 + NC):
        at = n % RES * LANES
        small_ref[29 + n // RES : 30 + n // RES, at : at + LANES] = resg_ref[n : n + 1, :]


def bwd_kernel(
    starts_ref, gmo_ref, mixed_ref, q_any, k_any, v_any, lse_ref, nattn_any, cos_any, sin_any, w_any, small_ref,
    outb_ref, dw_ref,
    wg_ref, gp_ref, outr_ref, total_ref, dwx_ref,
    do_ref, delta_ref, bias_ref, dk_ref, dv_ref, dq_ref, wo_ref, wsem, q_ref, k_ref, v_ref, nattn_ref, cos_ref, sin_ref, lsems,
    *scratch,
):
    late = ((q_any, q_ref), (k_any, k_ref), (v_any, v_ref), (cos_any, cos_ref), (sin_any, sin_ref), (nattn_any, nattn_ref))
    loads = [pltpu.make_async_copy(a, b, lsems.at[n]) for n, (a, b) in enumerate(late)]
    load = pltpu.make_async_copy(w_any.at[pl.ds(3, 1)], wo_ref, wsem)
    load.start()
    send = Send8(outb_ref, outr_ref, *scratch[0:2], False)
    sums = Near(*scratch[2:5])
    greet(all_peers())
    sums.begin(small_ref[...])
    send.begin()
    swap = Exchange8([dw_ref], dwx_ref, None, *scratch[5:7])
    swap.begin()
    for c in loads:
        c.start()
    d = mixed_ref.shape[1]
    pairs = d // LANES
    ntile = SEQ // QT
    mask_a, mask_b = head_masks()
    mask16 = (mask_a.astype(bf16), mask_b.astype(bf16))
    maskf = (mask_a, mask_b)
    heads = delta_ref.shape[0]
    pick = jnp.where(
        lax.broadcasted_iota(i32, (heads, d), 1) // HD == lax.broadcasted_iota(i32, (heads, d), 0), 1.0, 0.0
    ).astype(bf16)

    load.wait()

    def start(i, carry):
        rows = pl.ds(pl.multiple_of(i * QT, QT), QT)
        do = nn(gmo_ref[rows, :], wo_ref[0]).astype(bf16)
        do_ref[rows, :] = do
        hi, lo = split(do.astype(f32) * mixed_ref[rows, :].astype(f32))
        delta_ref[:, rows] = nt(pick, hi) + nt(pick, lo)
        return carry

    lax.fori_loop(0, ntile, start, 0)
    wg_ref[3] = tn(gmo_ref[...], mixed_ref[...]).astype(wg_ref.dtype)
    for i in range(ntile):
        width = min(SEQ, (i + 2) * QT) - i * QT
        bias_ref[i, 0:width, :] = window_bias(starts_ref, i, width, True)

    def pair(p, carry):
        cols = pl.ds(pl.multiple_of(p * LANES, LANES), LANES)
        dk_ref[...] = jnp.zeros_like(dk_ref)
        dv_ref[...] = jnp.zeros_like(dv_ref)
        for i in range(ntile):
            lo = i * QT
            width = min(SEQ, lo + 2 * QT) - lo
            rows = pl.ds(lo, QT)
            q2, do2 = q_ref[rows, cols], do_ref[rows, cols]
            dq = jnp.zeros((QT, LANES), f32)
            for h in range(2):
                qh, doh = q2 * mask16[h], do2 * mask16[h]
                lse, delta = lse_ref[pl.ds(2 * p + h, 1), rows], delta_ref[pl.ds(2 * p + h, 1), rows]
                spans = [(lo, width, True)] + ([(0, lo, False)] if lo else [])
                for at, size, masked in spans:
                    k2 = k_ref[at : at + size, cols]
                    s = nt(k2, qh)
                    if masked:
                        s = s + bias_ref[i, 0:size, :]
                    prob = jnp.exp(s - lse)
                    ds = (prob * (nt(v_ref[at : at + size, cols], doh) - delta)).astype(bf16)
                    dv_ref[at : at + size, :] += nn(prob.astype(bf16), doh)
                    dk_ref[at : at + size, :] += nn(ds, qh)
                    dq = dq + tn(ds, k2) * maskf[h]
            dq_ref[rows, :] = dq * HD**-0.5
        cosine, sine = cos_ref[...], -sin_ref[...]
        gp_ref[0, :, cols] = rot(dq_ref[...], cosine, sine).astype(bf16)
        gp_ref[1, :, cols] = rot(dk_ref[...], cosine, sine).astype(bf16)
        gp_ref[2, :, cols] = dv_ref[...].astype(bf16)
        return carry

    for c in loads:
        c.wait()
    lax.fori_loop(0, pairs, pair, 0)
    for c in range(3):
        wg_ref[c] = tn(nattn_ref[...], gp_ref[c]).astype(wg_ref.dtype)
    for m in range(NF):
        send.got(m)
    send.close()
    swap.end()
    total_ref[...] = sums.end()


def ffn_tile(x, gate, y, w_ref, acc, eo, dx):
    dy = y.astype(f32)
    ge = (gate * dy).astype(bf16)
    x_t, ge_t = x.T, ge.T
    for c in range(w_ref.shape[0]):
        wg, wu, wd = w_ref[c, 0], w_ref[c, 1], w_ref[c, 2]
        gv, uv = nn(x, wg), nn(x, wu)
        gh = nn(ge, wd)
        sig = 1.0 / (1.0 + jnp.exp(-gv))
        act = gv * sig
        hid = (act * uv).astype(bf16)
        eo = eo + nt(hid, wd)
        gg = (gh * uv * (sig * (1.0 + gv * (1.0 - sig)))).astype(bf16)
        gu = (gh * act).astype(bf16)
        dx = dx + nt(gg, wg) + nt(gu, wu)
        acc[c, 0] += nn(x_t, gg)
        acc[c, 1] += nn(x_t, gu)
        acc[c, 2] += nn(ge_t, hid)
    return eo, dx


def first_kernel(pay_ref, x_ref, y_ref, w_ref, xc_ref, yc_ref, gc_ref, eo_ref, dx_ref, dw_ref, meta_ref, acc):
    d = x_ref.shape[2]
    gates = [pay_ref[g] for g in range(NF)] + [jnp.zeros((LANES - NF, ROOM), f32)]
    columns = jnp.concatenate(gates, axis=0).T
    off = jnp.int32(0)
    for g in range(NF):
        rows = pl.ds(pl.multiple_of(off, 16), ROOM)
        xc_ref[rows, :] = x_ref[g]
        yc_ref[rows, :] = y_ref[g]
        gc_ref[rows, :] = jnp.broadcast_to(columns[:, g : g + 1], (ROOM, LANES))
        meta_ref[g] = off
        off = off + (jnp.max(pay_ref[NF + g]).astype(i32) + 15) // 16 * 16
    rows = pl.ds(pl.multiple_of(off, 16), TM)
    xc_ref[rows, :] = jnp.zeros((TM, d), bf16)
    yc_ref[rows, :] = jnp.zeros((TM, d), bf16)
    gc_ref[rows, :] = jnp.zeros((TM, LANES), f32)
    tiles = jnp.maximum((off + TM - 1) // TM, 1)
    meta_ref[NF] = tiles
    acc[...] = jnp.zeros_like(acc)
    zero = jnp.zeros((TM, d), f32)

    def tile(t, carry):
        rows = pl.ds(pl.multiple_of(t * TM, TM), TM)
        eo_ref[rows, :], dx_ref[rows, :] = ffn_tile(
            xc_ref[rows, :], gc_ref[rows, 0:1], yc_ref[rows, :], w_ref, acc, zero, zero
        )
        return carry

    lax.fori_loop(0, tiles, tile, 0)
    dw_ref[...] = acc[...].astype(bf16)


def second_kernel(
    meta_ref, xc_any, yc_any, gc_any, eo_any, dx_any, w_any, outb_ref, dxb_ref, ggb_ref, dw_ref,
    xc_ref, yc_ref, gc_ref, eo_ref, dx_ref, w_ref, outs, dxs, ggs, acc, sems, wsem,
):
    d = xc_ref.shape[1]
    tiles = meta_ref[NF]
    weights = pltpu.make_async_copy(w_any, w_ref, wsem)
    weights.start()

    def copies(t):
        rows = pl.ds(pl.multiple_of(t * TM, TM), TM)
        pairs = ((xc_any, xc_ref), (yc_any, yc_ref), (gc_any, gc_ref), (eo_any, eo_ref), (dx_any, dx_ref))
        return [pltpu.make_async_copy(a.at[rows, :], b.at[rows, :], sems.at[n, t]) for n, (a, b) in enumerate(pairs)]

    def begin(t, carry):
        for c in copies(t):
            c.start()
        return carry

    lax.fori_loop(0, tiles, begin, 0)
    acc[...] = jnp.zeros_like(acc)
    rows = pl.ds(pl.multiple_of(tiles * TM, TM), ROOM)
    outs[rows, :] = jnp.zeros((ROOM, d), bf16)
    dxs[rows, :] = jnp.zeros((ROOM, d), bf16)
    ggs[rows, :] = jnp.zeros((ROOM, LANES), f32)
    weights.wait()

    def tile(t, carry):
        rows = pl.ds(pl.multiple_of(t * TM, TM), TM)
        for c in copies(t):
            c.wait()
        gate, y = gc_ref[rows, 0:1], yc_ref[rows, :]
        eo, dx = ffn_tile(xc_ref[rows, :], gate, y, w_ref, acc, eo_ref[rows, :], dx_ref[rows, :])
        outs[rows, :] = (gate * eo).astype(bf16)
        dxs[rows, :] = dx.astype(bf16)
        ggs[rows, :] = jnp.broadcast_to(jnp.sum(y.astype(f32) * eo, axis=1, keepdims=True), (TM, LANES))
        return carry

    lax.fori_loop(0, tiles, tile, 0)
    lane = lanes(ROOM)
    columns = jnp.zeros((ROOM, LANES), f32)
    for g in range(NF):
        rows = pl.ds(pl.multiple_of(meta_ref[g], 16), ROOM)
        outb_ref[g] = outs[rows, :]
        dxb_ref[g] = dxs[rows, :]
        columns = jnp.where(lane == g, ggs[rows, :], columns)
    ggb_ref[:, 0, :] = columns.T[0:NF, :]
    dw_ref[...] = acc[...].astype(bf16)


def experts_first(pay, x, y, w):
    groups, _, d = x.shape
    total = groups * ROOM + TM
    return pl.pallas_call(
        first_kernel,
        in_specs=[VM] * 4,
        out_specs=[VM] * 6 + [SM],
        out_shape=(
            shape((total, d), bf16), shape((total, d), bf16), shape((total, LANES), f32), shape((total, d), f32),
            shape((total, d), f32), shape(w.shape, bf16), shape((NF + 1,), i32),
        ),
        scratch_shapes=[pltpu.VMEM(w.shape, f32)],
        compiler_params=pltpu.CompilerParams(vmem_limit_bytes=60 << 20),
        cost_estimate=cost(22, 25),
    )(pay, x, y, w)


def experts_second(meta, xc, yc, gc, eo, dx, w):
    total, d = xc.shape
    blocks = shape((NF, ROOM, d), bf16)
    room = total + ROOM
    return pl.pallas_call(
        second_kernel,
        in_specs=[SM] + [ANY] * 6,
        out_specs=[VM] * 4,
        out_shape=(blocks, blocks, shape((NF, 1, ROOM), f32), shape(w.shape, bf16)),
        scratch_shapes=[
            pltpu.VMEM((total, d), bf16),
            pltpu.VMEM((total, d), bf16),
            pltpu.VMEM((total, LANES), f32),
            pltpu.VMEM((total, d), f32),
            pltpu.VMEM((total, d), f32),
            pltpu.VMEM(w.shape, bf16),
            pltpu.VMEM((room, d), bf16),
            pltpu.VMEM((room, d), bf16),
            pltpu.VMEM((room, LANES), f32),
            pltpu.VMEM(w.shape, f32),
            pltpu.SemaphoreType.DMA((5, total // TM)),
            pltpu.SemaphoreType.DMA,
        ],
        compiler_params=pltpu.CompilerParams(vmem_limit_bytes=60 << 20),
        cost_estimate=cost(22, 25),
    )(meta, xc, yc, gc, eo, dx, w)


def emit_kernel(a_ref, b_ref, wg_ref, small_ref, nag_ref, gu_ref, dn_ref, qkv_ref, wo_ref, rt_ref, rg_ref, cv_ref, cg_ref, na_ref, nm_ref):
    half = a_ref.shape[3]
    for n, ref in ((0, a_ref), (1, b_ref)):
        at = slice(n * half, (n + 1) * half)
        gu_ref[:, :, :, at] = ref[0:2].astype(f32)
        dn_ref[:, :, at] = ref[2].astype(f32)

    @pl.when(pl.program_id(0) == 0)
    def _():
        qkv_ref[...] = wg_ref[0:3]
        r, f = wg_ref.shape[1:]
        wide = jnp.concatenate([wg_ref[3], jnp.zeros((r, -f % LANES), f32)], axis=1)
        wo_ref[...] = jnp.concatenate([wide, jnp.zeros((-r % LANES, wide.shape[1]), f32)], axis=0).T[0:f, 0:r]
        ne = rg_ref.shape[0]
        rt_ref[...] = small_ref[0:ne, :]
        for c in range(NC):
            cg_ref[c] = small_ref[Z0 + 2 * c : Z0 + 2 * c + 2, :]
        cv_ref[...] = small_ref[24 : 24 + NC, :]
        nm_ref[...] = small_ref[26, :]
        na_ref[...] = nag_ref[0, :]
        for n in range(ne):
            at = n % RES * LANES
            rg_ref[n : n + 1, :] = small_ref[29 + n // RES : 30 + n // RES, at : at + LANES][:, 0:ne]


def emit(dw_a, dw_b, wg, small, nag, ne):
    _, groups, r, half = dw_a.shape
    d = small.shape[1]
    some = 2
    piece = pl.BlockSpec((3, some, r, half), lambda e: (0, e, 0, 0))
    whole = lambda *dims: pl.BlockSpec(dims, lambda e: (0,) * len(dims))
    rest = [(3, *wg.shape[1:]), wg.shape[:0:-1], (ne, d), (ne, ne), (NC, d), (NC, 2, d), (d,), (d,)]
    return pl.pallas_call(
        emit_kernel,
        grid=(groups // some,),
        in_specs=[piece, piece, whole(*wg.shape), whole(*small.shape), whole(1, d)],
        out_specs=[
            pl.BlockSpec((2, some, r, 2 * half), lambda e: (0, e, 0, 0)),
            pl.BlockSpec((some, r, 2 * half), lambda e: (e, 0, 0)),
            *(whole(*dims) for dims in rest),
        ],
        out_shape=(
            shape((2, groups, r, 2 * half), f32), shape((groups, r, 2 * half), f32), *(shape(dims, f32) for dims in rest),
        ),
        cost_estimate=cost(1, 8),
    )(dw_a, dw_b, wg, small, nag)


def router_rows(par_ref, wr_ref):
    wr_ref[...] = jnp.zeros_like(wr_ref)
    wr_ref[0:16, :] = par_ref[0:16, :]
    wr_ref[16:32, :] = jnp.where(
        lax.broadcasted_iota(i32, (16, par_ref.shape[1]), 0) < 2 * NC, par_ref[16:32, :].astype(f32), 0.0
    ).astype(bf16)


def hot_rows(pos):
    slot = lax.broadcasted_iota(i32, (ROOM, pos.shape[1]), 0).astype(f32)
    return jnp.where(slot == pos, 1.0, 0.0).astype(bf16)


def split_rows(row):
    hi = row.astype(bf16).astype(f32)
    mid = (row - hi).astype(bf16).astype(f32)
    at = lax.broadcasted_iota(i32, (8, row.shape[1]), 0)
    out = jnp.where(at == 0, hi, jnp.where(at == 1, mid, jnp.where(at == 2, row - hi - mid, 0.0)))
    return out.astype(bf16)


def shape(dims, dtype):
    return jax.ShapeDtypeStruct(dims, dtype)


def cost(gflop, mbytes, mexp=0):
    return pl.CostEstimate(flops=int(gflop * 1e9), bytes_accessed=int(mbytes * 1e6), transcendentals=int(mexp * 1e6))


def rms_factor(values):
    return lax.rsqrt(jnp.mean(values * values, axis=-1, keepdims=True) + EPS)


def norm_back(grad, values, factor, gain):
    scaled = grad * gain
    inner = jnp.mean(scaled * values, axis=-1, keepdims=True)
    return factor * scaled - values * factor * factor * factor * inner


def rotary(positions, width):
    place = (jnp.arange(positions) % SEQ).astype(jnp.float32)
    freqs = jnp.power(10000.0, jnp.arange(width // 2).astype(jnp.float32) * (-2.0 / width))
    angles = place[:, None] * freqs[None, :]
    return (jnp.cos(angles)[:, None, :], jnp.sin(angles)[:, None, :])


def rotate(values, cosine, sine):
    half = values.shape[-1] // 2
    front = values[..., :half]
    behind = values[..., half:]
    return jnp.concatenate(
        [front * cosine - behind * sine, behind * cosine + front * sine], axis=-1
    )


def visible(starts):
    position = jnp.arange(SEQ)
    piece_of = jnp.zeros((SEQ,), jnp.int32)
    for index in range(starts.shape[0]):
        inside = (position >= starts[index]) & (position < starts[index] + PIECE)
        piece_of = jnp.where(inside, index + 1, piece_of)
    causal = position[None, :] <= position[:, None]
    same_piece = (piece_of[:, None] > 0) & (piece_of[:, None] == piece_of[None, :])
    return causal | same_piece


def dispatch(route_ids, route_ranks):
    group_rows = route_ids.shape[0]
    retained = (route_ids < NF) & (route_ranks < CAP)
    target = jnp.where(retained, route_ids * CAP + route_ranks, NF * CAP)
    token_index = jnp.broadcast_to(
        jnp.arange(group_rows, dtype=jnp.int32)[:, None], route_ids.shape
    )
    slot_token = (
        jnp.zeros((NF * CAP + 1,), jnp.int32)
        .at[target.reshape(-1)]
        .set(token_index.reshape(-1))[: NF * CAP]
    )
    filled = jnp.zeros((NF * CAP + 1,), jnp.float32).at[target.reshape(-1)].set(1.0)[: NF * CAP]
    return (retained, target, slot_token, filled)


def masked_scores(query, keys, starts):
    scores = jnp.einsum("qhd,khd->hqk", query, keys, preferred_element_type=jnp.float32) * HD ** (
        -0.5
    )
    return jnp.where(visible(starts)[None], scores, -1e30)


def attend_block(parts):
    query, keys, values, starts = parts
    scores = masked_scores(query, keys, starts)
    row_max = jnp.max(scores, axis=-1, keepdims=True)
    denominator = jnp.sum(jnp.exp(scores - row_max), axis=-1, keepdims=True)
    log_total = row_max + jnp.log(denominator)
    shares = jnp.exp(scores - log_total).astype(jnp.bfloat16)
    mixed = jnp.einsum("hqk,khd->qhd", shares, values, preferred_element_type=jnp.float32)
    return (mixed.astype(jnp.bfloat16), log_total)


def attend_back(parts):
    query, keys, values, starts, log_total, grad_out = parts
    shares = jnp.exp(masked_scores(query, keys, starts) - log_total)
    grad_shares = jnp.einsum("qhd,khd->hqk", grad_out, values, preferred_element_type=jnp.float32)
    centre = jnp.sum(shares * grad_shares, axis=-1, keepdims=True)
    grad_scores = (shares * (grad_shares - centre)).astype(jnp.bfloat16)
    factor = HD ** (-0.5)
    grad_query = (
        jnp.einsum("hqk,khd->qhd", grad_scores, keys, preferred_element_type=jnp.float32) * factor
    )
    grad_keys = (
        jnp.einsum("hqk,qhd->khd", grad_scores, query, preferred_element_type=jnp.float32) * factor
    )
    grad_values = jnp.einsum(
        "hqk,qhd->khd", shares.astype(jnp.bfloat16), grad_out, preferred_element_type=jnp.float32
    )
    return (grad_query, grad_keys, grad_values)


def plain_on_device(
    tokens,
    prior_logits,
    expert_ids,
    expert_ranks,
    piece_starts,
    norm_attn,
    qkv_weight,
    out_weight,
    norm_moe,
    router_weight,
    residual_weight,
    const_vectors,
    const_gates,
    w_gate_up,
    w_down,
    out_grad,
):
    highest = lax.Precision.HIGHEST
    local_rows = tokens.shape[0]
    group_rows = expert_ids.shape[0]
    sequences = group_rows // SEQ
    head_count = qkv_weight.shape[2] // HD
    row_start = lax.axis_index("tensor") * local_rows
    seq_shape = (sequences, SEQ, head_count, HD)
    gain_attn = norm_attn.astype(jnp.float32)
    gain_moe = norm_moe.astype(jnp.float32)
    tok_vals = tokens.astype(jnp.float32)
    factor_attn = rms_factor(tok_vals)
    normed_attn = (tok_vals * factor_attn * gain_attn).astype(jnp.bfloat16)
    attn_rows = lax.all_gather(normed_attn, "tensor", axis=0, tiled=True)
    qkv_full, out_full = (
        lax.all_gather(qkv_weight, "dp", axis=1, tiled=True),
        lax.all_gather(out_weight, "dp", axis=1, tiled=True),
    )
    projected = jnp.einsum("gd,cde->cge", attn_rows, qkv_full, preferred_element_type=jnp.float32)
    cosine, sine = rotary(group_rows, HD)
    query = (
        rotate(projected[0].reshape(group_rows, head_count, HD), cosine, sine)
        .astype(jnp.bfloat16)
        .reshape(seq_shape)
    )
    keys = (
        rotate(projected[1].reshape(group_rows, head_count, HD), cosine, sine)
        .astype(jnp.bfloat16)
        .reshape(seq_shape)
    )
    values = projected[2].astype(jnp.bfloat16).reshape(seq_shape)
    mixed, log_total = lax.map(attend_block, (query, keys, values, piece_starts))
    mixed_rows = mixed.reshape(group_rows, head_count * HD)
    attn_part = jnp.dot(mixed_rows, out_full, preferred_element_type=jnp.float32)
    attn_out = lax.psum_scatter(attn_part, "tensor", scatter_dimension=0, tiled=True)
    resid = tok_vals + attn_out
    factor_moe = rms_factor(resid)
    normed_moe = (resid * factor_moe * gain_moe).astype(jnp.bfloat16)
    moe_rows, prior_rows = (
        lax.all_gather(normed_moe, "tensor", axis=0, tiled=True),
        lax.all_gather(prior_logits, "tensor", axis=0, tiled=True),
    )
    logits = jnp.dot(moe_rows, router_weight, preferred_element_type=jnp.float32) + jnp.dot(
        prior_rows, residual_weight, preferred_element_type=jnp.float32
    )
    shares = jax.nn.softmax(logits, axis=-1)
    gates = jnp.take_along_axis(shares, expert_ids, axis=1)
    retained, target, slot_token, filled = dispatch(expert_ids, expert_ranks)
    picker = jnp.minimum(target, NF * CAP - 1)
    slot_gate = (
        jnp.zeros((NF * CAP + 1,), jnp.float32)
        .at[target.reshape(-1)]
        .set(gates.reshape(-1))[: NF * CAP]
        * filled
    )
    expert_rows = (moe_rows[slot_token] * filled[:, None].astype(jnp.bfloat16)).reshape(NF, CAP, -1)
    gate_full, down_full = (
        lax.all_gather(w_gate_up, "dp", axis=2, tiled=True),
        lax.all_gather(w_down, "dp", axis=2, tiled=True),
    )
    gate_up = jnp.einsum(
        "ecd,sedf->secf", expert_rows, gate_full, preferred_element_type=jnp.float32
    )
    sigmoid_vals = jax.nn.sigmoid(gate_up[0])
    activated = gate_up[0] * sigmoid_vals
    hidden = (activated * gate_up[1]).astype(jnp.bfloat16)
    expert_out = jnp.einsum(
        "ecf,efd->ecd", hidden, down_full, preferred_element_type=jnp.float32
    ).reshape(NF * CAP, -1)
    retained_gates = jnp.where(retained, gates, 0.0)
    combined = jnp.sum(retained_gates[:, :, None] * expert_out[picker], axis=1)
    ffn_out = lax.psum_scatter(
        combined.astype(jnp.bfloat16), "tensor", scatter_dimension=0, tiled=True
    ).astype(jnp.float32)
    local_ids = lax.dynamic_slice_in_dim(expert_ids, row_start, local_rows, 0)
    local_shares = lax.dynamic_slice_in_dim(shares, row_start, local_rows, 0)
    local_gates = lax.dynamic_slice_in_dim(gates, row_start, local_rows, 0)
    normed_vals = normed_moe.astype(jnp.float32)
    vectors = const_vectors.astype(jnp.float32)
    gate_mats = const_gates.astype(jnp.float32)
    const_count = vectors.shape[0]
    copy_share = jnp.sum(jnp.where(local_ids == NF + 1, local_gates, 0.0), axis=1)
    const_share = jnp.stack(
        [
            jnp.sum(jnp.where(local_ids == NF + 2 + index, local_gates, 0.0), axis=1)
            for index in range(const_count)
        ],
        axis=1,
    )
    mixing = jax.nn.softmax(
        jnp.einsum("gd,cjd->gcj", normed_vals, gate_mats, precision=highest), axis=-1
    )
    const_out = (
        mixing[:, :, 0:1] * normed_vals[:, None, :] + mixing[:, :, 1:2] * vectors[None, :, :]
    )
    others = copy_share[:, None] * normed_vals + jnp.sum(
        const_share[:, :, None] * const_out, axis=1
    )
    layer_out = (resid + ffn_out + others).astype(jnp.bfloat16)
    grad_out = out_grad.astype(jnp.float32)
    grad_moe_rows = lax.all_gather(out_grad, "tensor", axis=0, tiled=True)
    gate_back, down_back = (
        lax.all_gather(w_gate_up, "dp", axis=2, tiled=True),
        lax.all_gather(w_down, "dp", axis=2, tiled=True),
    )
    slot_grads = grad_moe_rows[slot_token].astype(jnp.float32)
    grad_expert = (slot_gate[:, None] * slot_grads).astype(jnp.bfloat16).reshape(NF, CAP, -1)
    slot_inner = jnp.sum(slot_grads * expert_out, axis=-1)
    gate_grad_ffn = jnp.where(retained, slot_inner[picker], 0.0)
    down_grad = jnp.einsum("ecf,ecd->efd", hidden, grad_expert, preferred_element_type=jnp.float32)
    grad_hidden = jnp.einsum(
        "ecd,efd->ecf", grad_expert, down_back, preferred_element_type=jnp.float32
    )
    slope = sigmoid_vals * (1.0 + gate_up[0] * (1.0 - sigmoid_vals))
    grad_gate_up = jnp.stack([grad_hidden * gate_up[1] * slope, grad_hidden * activated]).astype(
        jnp.bfloat16
    )
    gate_up_grad = jnp.einsum(
        "ecd,secf->sedf", expert_rows, grad_gate_up, preferred_element_type=jnp.float32
    )
    slot_input_grad = jnp.einsum(
        "secf,sedf->ecd", grad_gate_up, gate_back, preferred_element_type=jnp.float32
    ).reshape(NF * CAP, -1)
    grad_ffn_in = jnp.sum(jnp.where(retained[:, :, None], slot_input_grad[picker], 0.0), axis=1)
    gate_up_grad, down_grad = (
        lax.psum_scatter(gate_up_grad, "dp", scatter_dimension=2, tiled=True),
        lax.psum_scatter(down_grad, "dp", scatter_dimension=2, tiled=True),
    )
    grad_ffn_in, gate_grad_ffn = (
        lax.psum_scatter(grad_ffn_in, "tensor", scatter_dimension=0, tiled=True),
        lax.psum_scatter(gate_grad_ffn, "tensor", scatter_dimension=0, tiled=True),
    )
    copy_inner = jnp.sum(grad_out * normed_vals, axis=-1)
    const_inner = jnp.sum(grad_out[:, None, :] * const_out, axis=-1)
    choice_inner = jnp.where(local_ids == NF + 1, copy_inner[:, None], 0.0)
    for index in range(const_count):
        choice_inner = choice_inner + jnp.where(
            local_ids == NF + 2 + index, const_inner[:, index : index + 1], 0.0
        )
    gate_grad = gate_grad_ffn + choice_inner
    expert_range = jnp.arange(shares.shape[1])
    onehot = (local_ids[:, :, None] == expert_range[None, None, :]).astype(jnp.float32)
    grad_router = jnp.sum(onehot * gate_grad[:, :, None], axis=1)
    grad_logits = local_shares * (
        grad_router - jnp.sum(local_shares * grad_router, axis=-1, keepdims=True)
    )
    prior_vals = prior_logits.astype(jnp.float32)
    router_grad = jnp.dot(normed_vals.T, grad_logits, precision=highest)
    residual_grad = jnp.dot(prior_vals.T, grad_logits, precision=highest)
    prior_grad = jnp.dot(grad_logits, residual_weight.astype(jnp.float32).T, precision=highest)
    vector_inner = jnp.dot(grad_out, vectors.T, precision=highest)
    grad_mixing = const_share[:, :, None] * jnp.stack(
        [jnp.broadcast_to(copy_inner[:, None], vector_inner.shape), vector_inner], axis=-1
    )
    grad_blend = mixing * (grad_mixing - jnp.sum(mixing * grad_mixing, axis=-1, keepdims=True))
    const_gate_grad = jnp.einsum("gcj,gd->cjd", grad_blend, normed_vals, precision=highest)
    const_vector_grad = jnp.einsum(
        "gc,gd->cd", const_share * mixing[:, :, 1], grad_out, precision=highest
    )
    direct_share = copy_share + jnp.sum(const_share * mixing[:, :, 0], axis=1)
    grad_moe_in = (
        grad_ffn_in
        + jnp.dot(grad_logits, router_weight.astype(jnp.float32).T, precision=highest)
        + direct_share[:, None] * grad_out
        + jnp.einsum("gcj,cjd->gd", grad_blend, gate_mats, precision=highest)
    )
    norm_moe_grad = jnp.sum(grad_moe_in * resid * factor_moe, axis=0)
    grad_resid = grad_out + norm_back(grad_moe_in, resid, factor_moe, gain_moe)
    grad_mixed_out = grad_resid.astype(jnp.bfloat16)
    grad_attn_rows = lax.all_gather(grad_mixed_out, "tensor", axis=0, tiled=True)
    out_weight_grad = jnp.dot(mixed_rows.T, grad_attn_rows, preferred_element_type=jnp.float32)
    grad_mixed = jnp.dot(grad_attn_rows, out_full.T, preferred_element_type=jnp.float32).astype(
        jnp.bfloat16
    )
    grad_query, grad_keys, grad_values = lax.map(
        attend_back, (query, keys, values, piece_starts, log_total, grad_mixed.reshape(seq_shape))
    )
    grad_query = rotate(grad_query.reshape(group_rows, head_count, HD), cosine, -sine).reshape(
        group_rows, -1
    )
    grad_keys = rotate(grad_keys.reshape(group_rows, head_count, HD), cosine, -sine).reshape(
        group_rows, -1
    )
    grad_proj = jnp.stack([grad_query, grad_keys, grad_values.reshape(group_rows, -1)]).astype(
        jnp.bfloat16
    )
    qkv_grad = jnp.einsum("gd,cge->cde", attn_rows, grad_proj, preferred_element_type=jnp.float32)
    qkv_grad, out_weight_grad = (
        lax.psum_scatter(qkv_grad, "dp", scatter_dimension=1, tiled=True),
        lax.psum_scatter(out_weight_grad, "dp", scatter_dimension=1, tiled=True),
    )
    grad_attn_part = jnp.einsum(
        "cge,cde->gd", grad_proj, qkv_full, preferred_element_type=jnp.float32
    )
    grad_attn_in = lax.psum_scatter(
        grad_attn_part.astype(jnp.bfloat16), "tensor", scatter_dimension=0, tiled=True
    ).astype(jnp.float32)
    norm_attn_grad = jnp.sum(grad_attn_in * tok_vals * factor_attn, axis=0)
    input_grad = grad_resid + norm_back(grad_attn_in, tok_vals, factor_attn, gain_attn)
    summed = lax.psum(
        (
            norm_attn_grad,
            norm_moe_grad,
            router_grad,
            residual_grad,
            const_vector_grad,
            const_gate_grad,
        ),
        ("dp", "tensor"),
    )
    return (
        layer_out,
        input_grad,
        prior_grad,
        summed[0],
        qkv_grad,
        out_weight_grad,
        summed[1],
        summed[2],
        summed[3],
        summed[4],
        summed[5],
        gate_up_grad,
        down_grad,
    )


def on_device(
    dp,
    tensor,
    tokens,
    prior_logits,
    expert_ids,
    expert_ranks,
    piece_starts,
    norm_attn,
    qkv_weight,
    out_weight,
    norm_moe,
    router_weight,
    residual_weight,
    const_vectors,
    const_gates,
    w_gate_up,
    w_down,
    out_grad,
):
    rows, d = tokens.shape
    ne = router_weight.shape[1]
    packs = dp // NF
    groups = None if packs == 1 else [list(range(NF * r, NF * (r + 1))) for r in range(packs)]
    across = None if packs == 1 else [list(range(j, dp, NF)) for j in range(NF)]
    ids, ranks = expert_ids.T, expert_ranks.T
    cosine, sine = (jnp.asarray(t) for t in rotary_tables())
    prior = jnp.pad(prior_logits.T, ((0, 16 - ne), (0, 0)))
    zeros = lambda n: jnp.zeros((n, d), bf16)
    params = jnp.concatenate(
        [
            router_weight.T, zeros(Z0 - ne), const_gates.reshape(2 * NC, d), zeros(8 - 2 * NC), norm_attn[None],
            norm_moe[None], const_vectors, zeros(6 - NC), jnp.pad(residual_weight, ((0, 16 - ne), (0, d - ne))),
        ],
        axis=0,
    )

    w_down_t = w_down.transpose(0, 2, 1)[None]
    shard = w_down.shape[1]
    w_first, zq, zo = prologue(w_gate_up, w_down_t, qkv_weight, out_weight, tensor, 1)
    w_full, w_second, pos, count, ys, slab = gather_weights(
        zq, zo, w_gate_up, w_down_t, ids, ranks, out_grad, packs == 1, 2
    )
    w_attn = lax.all_gather(slab, "dp", axis=1, tiled=True) if packs > 1 else w_full

    def whole(w):
        w = w.reshape(3, -1, w.shape[3])
        if packs > 1:
            w = lax.all_gather(w, "dp", axis=1, tiled=True, axis_index_groups=across)
        return lax.all_gather(w, "tensor", axis=0, tiled=False)

    w_first, w_second = whole(w_first), whole(w_second)

    heads = 16
    blocks = shape((NF, ROOM, d), bf16)
    q, k, v, mixed, lse, nattn, resid, nmoe, base, aux, x_b, y_b, pay = pl.pallas_call(
        fwd_kernel,
        in_specs=[SM] + [VM] * 9 + [ANY],
        out_specs=[VM] * 10 + [ANY] * 3,
        out_shape=(
            shape((rows, d), bf16), shape((rows, d), bf16), shape((rows, d), bf16), shape((rows, d), bf16),
            shape((heads, rows), f32), shape((rows, d), bf16), shape((rows, d), f32), shape((rows, d), bf16),
            shape((rows, d), f32), shape((rows, LANES), f32), blocks, blocks, shape((2 * NF, 1, ROOM), f32),
        ),
        scratch_shapes=[
            pltpu.VMEM((QT, 2 * QT), f32),
            pltpu.VMEM((NF, 1, rows), f32),
            pltpu.VMEM((NF, ROOM, d), bf16),
            pltpu.VMEM((2 * NF, 1, ROOM), f32),
            pltpu.VMEM((LANES, d), bf16),
            *send_scratch(),
            *send_scratch(),
            pltpu.SemaphoreType.DMA((2, 2 * (NF - 1))),
            pltpu.SemaphoreType.DMA((2,)),
        ],
        compiler_params=pltpu.CompilerParams(collective_id=3, has_side_effects=True, vmem_limit_bytes=60 << 20),
        cost_estimate=cost(40, 30, 10),
    )(piece_starts, tokens, prior, ids, ranks, params, cosine, sine, w_attn, pos, ys)

    xc, yc, gc, eo, dx, dw_a, meta = experts_first(pay, x_b, y_b, w_first)
    out_b, dx_b, gg_b, dw_b = experts_second(meta, xc, yc, gc, eo, dx, w_second)

    def owned(dw):
        dw = lax.psum_scatter(dw, "tensor", scatter_dimension=0, tiled=False)
        if packs > 1:
            dw = lax.psum_scatter(dw, "dp", scatter_dimension=1, tiled=True, axis_index_groups=across)
        return dw.reshape(3, NF, -1, dw.shape[-1])

    dw_a = owned(dw_a)

    gmo, gres, pgrad, small = pl.pallas_call(
        mid_kernel,
        in_specs=[ANY] * 6 + [VM] * 4,
        out_specs=[VM] * 4,
        out_shape=(shape((rows, d), bf16), shape((rows, d), f32), shape((16, rows), f32), shape((32, d), f32)),
        scratch_shapes=[
            pltpu.VMEM((NF, ROOM, d), bf16),
            pltpu.VMEM((NF, 1, ROOM), f32),
            pltpu.VMEM((rows, d), f32),
            pltpu.VMEM((NF, rows), f32),
            pltpu.VMEM((rows, LANES), f32),
            pltpu.VMEM((rows, LANES), f32),
            pltpu.VMEM((LANES, d), bf16),
            pltpu.VMEM((16, LANES), f32),
            pltpu.VMEM((rows, d), bf16),
            pltpu.VMEM((rows, d), bf16),
            pltpu.VMEM((rows, d), f32),
            pltpu.VMEM((rows, LANES), f32),
            pltpu.SemaphoreType.DMA((4,)),
            *send_scratch(),
            pltpu.SemaphoreType.DMA((2, NF - 1)),
            pltpu.SemaphoreType.DMA((1,)),
        ],
        compiler_params=pltpu.CompilerParams(collective_id=4, has_side_effects=True, vmem_limit_bytes=60 << 20),
        cost_estimate=cost(4, 4),
    )(dx_b, gg_b, out_grad, nmoe, resid, aux, pos, prior, params, count)
    dw_a, dw_b, gmo = lax.optimization_barrier((dw_a, dw_b, gmo))
    dw_b = owned(dw_b)
    wg, gp, yr, small, dw_a = pl.pallas_call(
        bwd_kernel,
        in_specs=[SM, VM, VM, ANY, ANY, ANY, VM] + [ANY] * 4 + [VM, ANY, ANY],
        out_specs=[VM] * 2 + [ANY, VM, ANY],
        out_shape=(shape((4, d, d), bf16), shape((3, rows, d), bf16), blocks, shape((32, d), f32), shape(dw_a.shape, bf16)),
        scratch_shapes=[
            pltpu.VMEM((rows, d), bf16),
            pltpu.VMEM((heads, rows), f32),
            pltpu.VMEM((rows // QT, 2 * QT, QT), f32),
            pltpu.VMEM((rows, LANES), f32),
            pltpu.VMEM((rows, LANES), f32),
            pltpu.VMEM((rows, LANES), f32),
            pltpu.VMEM((1, d, d), bf16),
            pltpu.SemaphoreType.DMA,
            *[pltpu.VMEM((rows, d), bf16)] * 3,
            pltpu.VMEM((rows, d), bf16),
            *[pltpu.VMEM((rows, LANES), f32)] * 2,
            pltpu.SemaphoreType.DMA((6,)),
            *send_scratch(),
            *near_scratch((32, d)),
            *exchange_scratch(1),
        ],
        compiler_params=pltpu.CompilerParams(collective_id=5, has_side_effects=True, vmem_limit_bytes=60 << 20),
        cost_estimate=cost(8, 4),
    )(piece_starts, gmo, mixed, q, k, v, lse, nattn, cosine, sine, w_attn, small, out_b, dw_a)
    alone = packs == 1
    zs, igrad, layer_out, small, nag = finish(
        wg, gp, gres, tokens, w_attn, yr, base, pos, params, small, tensor, alone, 6
    )
    if alone:
        wg, nag, dw_b = last(zs, nag, dw_b, tensor, 7)
    else:
        wg = lax.psum_scatter(wg, "dp", scatter_dimension=1, tiled=True)
        wg = lax.psum_scatter(wg, "tensor", scatter_dimension=2, tiled=True).astype(f32)
        nag = lax.psum(nag, ("dp", "tensor"))
        small = lax.psum(lax.psum(small, "tensor"), "dp", axis_index_groups=across)
        dw_b = exchange8(dw_b, 7)
    overflow = jnp.sum(small[28:29, 0:LANES]) > 0

    def roomy(args):
        return plain_on_device(*args)

    def packed(args):
        gate_up, down, qkv, wo, router, residual, vectors, blends, gain_attn, gain_moe = emit(dw_a, dw_b, wg, small, nag, ne)
        return (
            layer_out,
            igrad,
            pgrad[0:ne].T,
            gain_attn,
            qkv,
            wo,
            gain_moe,
            router.T,
            residual,
            vectors,
            blends,
            gate_up,
            down.transpose(0, 2, 1),
        )

    args = (
        tokens, prior_logits, expert_ids, expert_ranks, piece_starts, norm_attn, qkv_weight, out_weight, norm_moe,
        router_weight, residual_weight, const_vectors, const_gates, w_gate_up, w_down, out_grad,
    )
    return lax.cond(overflow, roomy, packed, args)


def solution(mesh):
    body = functools.partial(on_device, mesh.shape["dp"], mesh.shape["tensor"])
    rows = P(("dp", "tensor"), None)
    return jax.shard_map(
        body,
        mesh=mesh,
        in_specs=(
            rows, rows, P("dp", None), P("dp", None), P("dp", None), P(), P(None, "dp", "tensor"), P("tensor", "dp"),
            P(), P(), P(), P(), P(), P(None, None, "dp", "tensor"), P(None, "tensor", "dp"), rows,
        ),
        out_specs=(
            rows, rows, rows, P(), P(None, "dp", "tensor"), P("tensor", "dp"), P(), P(), P(), P(), P(),
            P(None, None, "dp", "tensor"), P(None, "tensor", "dp"),
        ),
        check_vma=False,
    )
```
